128 devices in a mesh: lat: 4 (over x_lo, core), lon: 32 (over x_hi, y, z).
Axes of the slice: x: 4 (x_hi: 2, x_lo: 2; x = x_hi * 2 + x_lo), y: 4, z: 4, core: 2. Of those that a mesh axis runs over, the one named last changes fastest.
Arguments:
- tokens: bfloat16 [128, 512, 512], P('lat', 'lon'), may hold values from -6 to 6
- labels: int32 [128, 512], P('lat', 'lon'), may hold values from 0 to 3
- offsets: int32 [2], replicated, may hold values from 1 to 7, as said below
- gain_attn: float32 [512], replicated, may hold values from 0.1 to 1.9
- w_qkv: bfloat16 [512, 1536], replicated, may hold values from -0.25 to 0.25
- w_proj: bfloat16 [512, 512], replicated, may hold values from -0.25 to 0.25
- gain_ffn: float32 [512], replicated, may hold values from 0.1 to 1.9
- w_fc1: bfloat16 [512, 2048], replicated, may hold values from -0.25 to 0.25
- w_fc2: bfloat16 [2048, 512], replicated, may hold values from -0.125 to 0.125
- gain_merge: float32 [2048], replicated, may hold values from 0.1 to 1.9
- w_merge: bfloat16 [2048, 1024], replicated, may hold values from -0.125 to 0.125
- gain_mlp: float32 [1024], replicated, may hold values from 0.1 to 1.9
- w_first: bfloat16 [1024, 4096], P('lat', 'lon'), may hold values from -0.1875 to 0.1875
- w_second: bfloat16 [4096, 1024], P('lon', 'lat'), may hold values from -0.09375 to 0.09375
- w_up: bfloat16 [1024, 2048], replicated, may hold values from -0.1875 to 0.1875
- cotangent: bfloat16 [128, 512, 512], P('lat', 'lon'), may hold values from -6 to 6
Outputs:
- field_out: bfloat16 [128, 512, 512], P('lat', 'lon')
- grad_in: bfloat16 [128, 512, 512], P('lat', 'lon')
The draws below stay inside these ranges and needn't reach their ends.
Inputs may be any that keep to these rules, and one draw needn't show every extreme that they name: One of the two offsets equals 7.
All inputs are finite; a program needn't handle non-finite values.
Results may differ from the reference program's by a relative error of at most 0.024.
Values may be sent and summed in bfloat16 or wider, within the bound.
No kernel may reach another device: no remote copies, remote signals or barrier semaphores. Data moves between devices by JAX's collectives and lax.ppermute only.
A program may use at most 192 MiB of HBM per device.

```python
import jax
import jax.numpy as jnp
from jax import lax

D = 512
HEADS = 8
FFN = 2048
D2 = 1024
FF2 = 4096
WIN = 8
NLAT = 128
NLON = 512


def draw_offsets(key, part):
    key = jax.random.fold_in(key, 7)
    chooser_key, second_key = jax.random.split(key)
    chooser = jax.random.randint(chooser_key, (), 0, 2)
    second_offset = jax.random.randint(second_key, (), 1, WIN)
    largest = jnp.int32(WIN - 1)
    first_form = jnp.stack([largest, second_offset])
    other_form = jnp.stack([second_offset, largest])
    return jnp.where(chooser == 0, first_form, other_form).astype(jnp.int32)


def set_ends(drawn, key, low, high):
    longest = drawn.shape.index(max(drawn.shape))
    spots = []
    for shift in (0, 1):
        where = [jax.random.randint(jax.random.fold_in(key, axis), (), 0, length) for axis, length in enumerate(drawn.shape)]
        where[longest] = (where[longest] + shift) % drawn.shape[longest]
        spots.append(tuple(where))
    return drawn.at[spots[0]].set(low).at[spots[1]].set(high)


def shard_levels(stream_key, dims, cuts, least, high):
    factor_of = 1.0
    for dim, parts in cuts:
        heights = jax.random.uniform(jax.random.fold_in(jax.random.fold_in(stream_key, 6), dim), (parts,), jnp.float32, least / len(cuts), high / len(cuts))
        factor_of = factor_of * jnp.repeat(jnp.exp(heights), dims[dim] // parts).reshape((-1,) + (1,) * (len(dims) - 1 - dim))
    return factor_of


def noise(rng, extent, deviation, reach, pieces=(), kind=jnp.bfloat16):
    level = shard_levels(rng, extent, pieces, -0.22, 0.18) if pieces else 1.0
    drawn = jax.random.normal(rng, extent, jnp.float32) * deviation * level
    return jnp.minimum(jnp.maximum(drawn, -reach), reach).astype(kind)


def setup_inputs(seed: int = 0) -> dict:
    arg_keys = jax.random.split(jax.random.key(seed), 17)
    tokens = noise(arg_keys[0], (NLAT, NLON, D), 1.0, 6.0, ((0, 4), (1, 32)))
    labels = set_ends(jax.random.randint(arg_keys[1], (NLAT, NLON), 0, 4), jax.random.fold_in(arg_keys[1], 1), 0, 3).astype(jnp.int32)
    offsets = draw_offsets(jax.random.fold_in(arg_keys[16], 71), 0)
    gain_attn = jnp.clip(1.0 + 0.18 * jax.random.normal(arg_keys[3], (D,), jnp.float32), 0.1, 1.9)
    w_qkv = noise(arg_keys[4], (D, 3 * D), D ** -0.5, 0.25)
    w_proj = noise(arg_keys[5], (D, D), D ** -0.5, 0.25)
    gain_ffn = jnp.clip(1.0 + 0.18 * jax.random.normal(arg_keys[6], (D,), jnp.float32), 0.1, 1.9)
    w_fc1 = noise(arg_keys[7], (D, FFN), D ** -0.5, 0.25)
    w_fc2 = noise(arg_keys[8], (FFN, D), FFN ** -0.5, 0.125)
    gain_merge = jnp.clip(1.0 + 0.18 * jax.random.normal(arg_keys[9], (4 * D,), jnp.float32), 0.1, 1.9)
    w_merge = noise(arg_keys[10], (4 * D, D2), (4 * D) ** -0.5, 0.125)
    gain_mlp = jnp.clip(1.0 + 0.18 * jax.random.normal(arg_keys[11], (D2,), jnp.float32), 0.1, 1.9)
    w_first = noise(arg_keys[12], (D2, FF2), D2 ** -0.5, 0.1875, ((0, 4), (1, 32)))
    w_second = noise(arg_keys[13], (FF2, D2), FF2 ** -0.5, 0.09375, ((0, 32), (1, 4)))
    w_up = noise(arg_keys[14], (D2, 4 * D), D2 ** -0.5, 0.1875)
    cotangent = noise(arg_keys[15], (NLAT, NLON, D), 1.0, 6.0, ((0, 4), (1, 32)))
    return {"tokens": tokens, "labels": labels, "offsets": offsets, "gain_attn": gain_attn, "w_qkv": w_qkv, "w_proj": w_proj, "gain_ffn": gain_ffn, "w_fc1": w_fc1, "w_fc2": w_fc2, "gain_merge": gain_merge, "w_merge": w_merge, "gain_mlp": gain_mlp, "w_first": w_first, "w_second": w_second, "w_up": w_up, "cotangent": cotangent}


EPS = 1e-05

def matmul(operand, matrix):
    flattened = operand.reshape(-1, operand.shape[-1])
    result = jnp.dot(flattened, matrix, preferred_element_type=jnp.float32)
    return result.reshape(operand.shape[:-1] + (matrix.shape[1],))

def matmul_t(operand, matrix):
    flattened = operand.reshape(-1, operand.shape[-1])
    result = jnp.dot(flattened, matrix.T, preferred_element_type=jnp.float32)
    return result.reshape(operand.shape[:-1] + (matrix.shape[0],))

def norm_forward(source, scales):
    average = lax.optimization_barrier(jnp.mean(source, -1, keepdims=True))
    centred = source - average
    inverse = lax.rsqrt(lax.optimization_barrier(jnp.mean(centred * centred, -1, keepdims=True)) + EPS)
    return centred * inverse * scales

def norm_backward(source, scales, upstream):
    average = lax.optimization_barrier(jnp.mean(source, -1, keepdims=True))
    centred = source - average
    inverse = lax.rsqrt(lax.optimization_barrier(jnp.mean(centred * centred, -1, keepdims=True)) + EPS)
    normal_part = centred * inverse
    scaled = upstream * scales
    return inverse * (scaled - lax.optimization_barrier(jnp.mean(scaled, -1, keepdims=True)) - normal_part * lax.optimization_barrier(jnp.mean(scaled * normal_part, -1, keepdims=True)))

def gelu_grad(preact, upstream):
    return jax.vjp(jax.nn.gelu, preact)[1](upstream)[0]

def merge_patches(block):
    row_count, col_count, channels = block.shape
    return block.reshape(row_count // 2, 2, col_count // 2, 2, channels).transpose(0, 2, 3, 1, 4).reshape(row_count // 2, col_count // 2, 4 * channels)

def split_patches(merged):
    row_half, col_half, wide_channels = merged.shape
    channels = wide_channels // 4
    return merged.reshape(row_half, col_half, 2, 2, channels).transpose(0, 3, 1, 2, 4).reshape(2 * row_half, 2 * col_half, channels)

def to_windows(source):
    row_count, col_count = (source.shape[0], source.shape[1])
    trailing = source.shape[2:]
    extra = tuple(range(4, 4 + len(trailing)))
    shaped = source.reshape((row_count // WIN, WIN, col_count // WIN, WIN) + trailing)
    return shaped.transpose((0, 2, 1, 3) + extra).reshape((-1, WIN * WIN) + trailing)

def from_windows(windows, row_count, col_count):
    trailing = windows.shape[2:]
    extra = tuple(range(4, 4 + len(trailing)))
    shaped = windows.reshape((row_count // WIN, col_count // WIN, WIN, WIN) + trailing)
    return shaped.transpose((0, 2, 1, 3) + extra).reshape((row_count, col_count) + trailing)

def attend_forward(shifted, shifted_labels, sides, w_qkv, w_proj):
    row_count, col_count, channels = shifted.shape
    head_size = channels // HEADS
    qkv_rounded = matmul(shifted, w_qkv).astype(jnp.bfloat16)
    windows = to_windows(qkv_rounded)
    window_count, window_size = (windows.shape[0], windows.shape[1])
    queries = windows[..., :channels].reshape(window_count, window_size, HEADS, head_size).astype(jnp.float32)
    key_rows = windows[..., channels:2 * channels].reshape(window_count, window_size, HEADS, head_size).astype(jnp.float32)
    values = windows[..., 2 * channels:].reshape(window_count, window_size, HEADS, head_size).astype(jnp.float32)
    scores = jnp.einsum('nqhd,nkhd->nhqk', queries, key_rows) / jnp.sqrt(jnp.float32(head_size))
    win_labels = to_windows(shifted_labels)
    win_sides = to_windows(sides)
    allowed = (win_labels[:, :, None] == win_labels[:, None, :]) & (win_sides[:, :, None] == win_sides[:, None, :])
    exponent = jnp.where(allowed[:, None], jnp.exp(scores), 0.0)
    weights = exponent / lax.optimization_barrier(jnp.sum(exponent, -1, keepdims=True))
    probs = weights.astype(jnp.bfloat16)
    mixed = jnp.einsum('nhqk,nkhd->nqhd', probs.astype(jnp.float32), values).astype(jnp.bfloat16)
    attn_rounded = matmul(mixed.reshape(window_count, window_size, channels), w_proj).astype(jnp.bfloat16)
    return (from_windows(attn_rounded, row_count, col_count), (queries, key_rows, values, weights, probs))

def attend_backward(upstream, stash_attn, w_qkv, w_proj):
    queries, key_rows, values, weights, probs = stash_attn
    row_count, col_count, channels = upstream.shape
    head_size = channels // HEADS
    up_windows = to_windows(upstream)
    window_count, window_size = (up_windows.shape[0], up_windows.shape[1])
    g_mixed = matmul_t(up_windows, w_proj).reshape(window_count, window_size, HEADS, head_size)
    g_probs = jnp.einsum('nqhd,nkhd->nhqk', g_mixed, values)
    g_values = jnp.einsum('nhqk,nqhd->nkhd', probs.astype(jnp.float32), g_mixed)
    g_scores = weights * (g_probs - lax.optimization_barrier(jnp.sum(weights * g_probs, -1, keepdims=True))) / jnp.sqrt(jnp.float32(head_size))
    g_queries = jnp.einsum('nhqk,nkhd->nqhd', g_scores, key_rows)
    g_keys = jnp.einsum('nhqk,nqhd->nkhd', g_scores, queries)
    flat_shape = (window_count, window_size, channels)
    g_qkv = jnp.concatenate([g_queries.reshape(flat_shape), g_keys.reshape(flat_shape), g_values.reshape(flat_shape)], -1).astype(jnp.bfloat16)
    g_shifted = matmul_t(g_qkv, w_qkv).astype(jnp.bfloat16)
    return from_windows(g_shifted, row_count, col_count)

def reference(tokens, labels, offsets, gain_attn, w_qkv, w_proj, gain_ffn, w_fc1, w_fc2, gain_merge, w_merge, gain_mlp, w_first, w_second, w_up, cotangent):
    lat_shift = offsets[0]
    lon_shift = offsets[1]
    wide = tokens.astype(jnp.float32)
    normed = norm_forward(wide, gain_attn).astype(jnp.bfloat16)
    shifted = jnp.roll(normed, (-lat_shift, -lon_shift), axis=(0, 1))
    shifted_labels = jnp.roll(labels, (-lat_shift, -lon_shift), axis=(0, 1))
    row_ids = jnp.arange(NLAT, dtype=jnp.int32)
    sides = jnp.broadcast_to((row_ids + lat_shift >= NLAT).astype(jnp.int32)[:, None], (NLAT, NLON))
    shifted_attn, stash_attn = attend_forward(shifted, shifted_labels, sides, w_qkv, w_proj)
    attended = jnp.roll(shifted_attn, (lat_shift, lon_shift), axis=(0, 1))
    resid = (wide + attended.astype(jnp.float32)).astype(jnp.bfloat16)
    resid_wide = resid.astype(jnp.float32)
    ffn_in = norm_forward(resid_wide, gain_ffn).astype(jnp.bfloat16)
    ffn_pre = matmul(ffn_in, w_fc1)
    ffn_hid = jax.nn.gelu(ffn_pre).astype(jnp.bfloat16)
    block = (resid_wide + matmul(ffn_hid, w_fc2)).astype(jnp.bfloat16)
    merged = merge_patches(block).astype(jnp.float32)
    merge_in = norm_forward(merged, gain_merge).astype(jnp.bfloat16)
    coarse = matmul(merge_in, w_merge).astype(jnp.bfloat16)
    coarse_wide = coarse.astype(jnp.float32)
    coarse_in = norm_forward(coarse_wide, gain_mlp).astype(jnp.bfloat16)
    mlp_pre = matmul(coarse_in, w_first)
    mlp_hid = jax.nn.gelu(mlp_pre).astype(jnp.bfloat16)
    deep = (coarse_wide + matmul(mlp_hid, w_second)).astype(jnp.bfloat16)
    upward = matmul(deep, w_up)
    field_out = (block.astype(jnp.float32) + split_patches(upward)).astype(jnp.bfloat16)
    g_deep = matmul_t(merge_patches(cotangent), w_up).astype(jnp.bfloat16)
    g_hid = matmul_t(g_deep, w_second)
    g_pre = gelu_grad(mlp_pre, g_hid).astype(jnp.bfloat16)
    g_cin = matmul_t(g_pre, w_first).astype(jnp.bfloat16)
    g_coarse = (g_deep.astype(jnp.float32) + norm_backward(coarse_wide, gain_mlp, g_cin.astype(jnp.float32))).astype(jnp.bfloat16)
    g_merged = norm_backward(merged, gain_merge, matmul_t(g_coarse, w_merge))
    g_block = (cotangent.astype(jnp.float32) + split_patches(g_merged)).astype(jnp.bfloat16)
    g_fhid = matmul_t(g_block, w_fc2)
    g_fpre = gelu_grad(ffn_pre, g_fhid).astype(jnp.bfloat16)
    g_fin = matmul_t(g_fpre, w_fc1).astype(jnp.bfloat16)
    g_resid = (g_block.astype(jnp.float32) + norm_backward(resid_wide, gain_ffn, g_fin.astype(jnp.float32))).astype(jnp.bfloat16)
    g_shift_attn = jnp.roll(g_resid, (-lat_shift, -lon_shift), axis=(0, 1))
    g_shifted = attend_backward(g_shift_attn, stash_attn, w_qkv, w_proj)
    g_normed = jnp.roll(g_shifted, (lat_shift, lon_shift), axis=(0, 1))
    grad_in = (g_resid.astype(jnp.float32) + norm_backward(wide, gain_attn, g_normed.astype(jnp.float32))).astype(jnp.bfloat16)
    return (field_out, grad_in)
```

```python
import jax
import jax.numpy as jnp
from jax import lax
from jax.experimental import pallas as pl
from jax.experimental.pallas import tpu as pltpu
from jax.sharding import PartitionSpec as P

BF = jnp.bfloat16
F32 = jnp.float32
EPS = 1e-05
NT = (((1,), (1,)), ((), ()))
TN = (((0,), (0,)), ((), ()))
GELU_C = 0.7978845608028654
GELU_A = 0.044715


def dot(a, b):
    return jnp.dot(a, b, preferred_element_type=F32)


def dot_nt(a, b):
    return lax.dot_general(a, b, NT, preferred_element_type=F32)


def dot_tn(a, b):
    return lax.dot_general(a, b, TN, preferred_element_type=F32)


def normalise(v):
    mean = jnp.mean(v, -1, keepdims=True)
    c = v - mean
    r = lax.rsqrt(jnp.mean(c * c, -1, keepdims=True) + EPS)
    return c * r, r


def norm_back(v, gain, t):
    xh, r = normalise(v)
    s = t * gain
    return r * (s - jnp.mean(s, -1, keepdims=True) - xh * jnp.mean(s * xh, -1, keepdims=True))


def gelu_both(x):
    x2 = x * x
    t = jnp.tanh(GELU_C * x * (1.0 + GELU_A * x2))
    half = 0.5 * (1.0 + t)
    slope = half + 0.5 * x * (1.0 - t * t) * (GELU_C * (1.0 + 3.0 * GELU_A * x2))
    return x * half, slope


def head_masks():
    lane = lax.broadcasted_iota(jnp.int32, (1, 256), 1) // 64
    return [(lane == h).astype(F32).astype(BF) for h in range(4)]


def block_ones():
    r = lax.broadcasted_iota(jnp.int32, (256, 256), 0) // 64
    c = lax.broadcasted_iota(jnp.int32, (256, 256), 1) // 64
    return (r == c).astype(F32).astype(BF)


def spread(x, masks):
    return jnp.concatenate([x * m for m in masks], 0)


def collect(big, masks):
    out = None
    for h, m in enumerate(masks):
        term = big[64 * h : 64 * h + 64] * m.astype(F32)
        out = term if out is None else out + term
    return out


def fill_grid(grid, b, left, own, right, up, down):
    def moved(line):
        return pltpu.roll(line.astype(F32), 32 - b, 0)[:24]

    def row(r, carry):
        grid[8 + r] = moved(
            jnp.concatenate([left[r].astype(F32), own[r].astype(F32), right[r].astype(F32)], 0)
        )
        return carry

    lax.fori_loop(0, 32, row, 0, unroll=4)

    def edge(r, carry):
        grid[r] = moved(up[r])
        grid[40 + r] = moved(down[r])
        return carry

    lax.fori_loop(0, 8, edge, 0, unroll=2)


def place_back(back, r, a, b):
    return pltpu.roll(back[8 - a + r], 16 + b, 0)[:16]


def attn_fwd_kernel(
    place, left, own, right, up, down, gain, w_qkv, w_proj,
    qkv_out, probs_out, resid_out,
    grid, codes, back, mixed,
):
    a, b, d = place[0], place[1], place[2]
    fill_grid(grid, b, left, own, right, up, down)
    slab = jnp.concatenate([v[32].astype(F32) for v in (left, own, right)], 0)
    slab = pltpu.roll(slab, 32 - b, 0)[:24]
    first = jnp.where(d == 0, 4.0, 0.0).astype(F32)
    last = jnp.where(d == 3, 4.0, 0.0).astype(F32)
    slab_up = pltpu.roll(up[8].astype(F32) + first, 32 - b, 0)[:24]
    slab_down = pltpu.roll(down[8].astype(F32) + last, 32 - b, 0)[:24]
    for r in range(32):
        codes[8 + r] = jnp.broadcast_to(slab[:, r : r + 1], (24, 128))
    for r in range(8):
        codes[r] = jnp.broadcast_to(slab_up[:, 24 + r : 25 + r], (24, 128))
        codes[40 + r] = jnp.broadcast_to(slab_down[:, r : r + 1], (24, 128))
    masks = head_masks()
    ones = block_ones()

    def band(wi, carry):
        rows = pl.multiple_of(wi * 192, 192)
        normed = []
        for wj in range(3):
            x = grid[pl.ds(a + 8 * wi, 8), 8 * wj : 8 * wj + 8, :].reshape(64, 512)
            xh, _ = normalise(x)
            normed.append((xh * gain[...]).astype(BF))
        qkv = dot(jnp.concatenate(normed, 0), w_qkv[...]).astype(BF)
        qkv_out[pl.ds(rows, 192), :] = qkv
        for wj in range(3):
            col = codes[pl.ds(a + 8 * wi, 8), 8 * wj : 8 * wj + 8, :].reshape(64, 128)
            row = col.T[0:1, 0:64]
            same = jnp.concatenate([col, col], 1) == jnp.concatenate([row] * 4, 1)
            win = qkv[64 * wj : 64 * wj + 64]
            for c in range(2):
                lo = 256 * c
                q = win[:, lo : lo + 256]
                kbig = spread(win[:, 512 + lo : 768 + lo], masks)
                vbig = spread(win[:, 1024 + lo : 1280 + lo], masks)
                e = jnp.where(same, jnp.exp(dot_nt(q, kbig) * 0.125), 0.0)
                total = dot(e.astype(BF), ones)
                p = (e / total).astype(BF)
                probs_out[pl.ds(rows + 64 * wj, 64), lo : lo + 256] = p
                mixed[64 * wj : 64 * wj + 64, lo : lo + 256] = dot(p, vbig).astype(BF)
        att = dot(mixed[...], w_proj[...]).astype(BF).astype(F32)
        for wj in range(3):
            back[pl.ds(8 * wi, 8), 8 * wj : 8 * wj + 8, :] = att[64 * wj : 64 * wj + 64].reshape(
                8, 8, 512
            )
        return carry

    lax.fori_loop(0, 5, band, 0)

    def finish(r, carry):
        moved = place_back(back, r, a, b)
        resid_out[r] = (own[r].astype(F32) + moved).astype(BF)
        return carry

    lax.fori_loop(0, 32, finish, 0, unroll=4)


VM = pl.BlockSpec(memory_space=pltpu.VMEM)
SM = pl.BlockSpec(memory_space=pltpu.SMEM)


def params(mib):
    return pltpu.CompilerParams(vmem_limit_bytes=mib * 2**20)


def attn_fwd(place, left, own, right, up, down, gain, w_qkv, w_proj):
    return pl.pallas_call(
        attn_fwd_kernel,
        out_shape=(
            jax.ShapeDtypeStruct((960, 1536), BF),
            jax.ShapeDtypeStruct((960, 512), BF),
            jax.ShapeDtypeStruct((32, 16, 512), BF),
        ),
        in_specs=[SM] + [VM] * 8,
        out_specs=(VM, VM, VM),
        scratch_shapes=[
            pltpu.VMEM((48, 24, 512), F32),
            pltpu.VMEM((48, 24, 128), F32),
            pltpu.VMEM((40, 24, 512), F32),
            pltpu.VMEM((192, 512), BF),
        ],
        compiler_params=params(40),
        cost_estimate=pl.CostEstimate(flops=2 * 10**9, bytes_accessed=10 * 2**20, transcendentals=10**6),
        name="attn_fwd",
    )(place, left, own, right, up, down, gain, w_qkv, w_proj)


def attn_bwd_kernel(
    place, left, own, right, up, down, qkv, probs, w_proj, w_qkv, tokens, gain,
    grad_out,
    grid, back, g_qkv,
):
    a, b = place[0], place[1]
    fill_grid(grid, b, left, own, right, up, down)
    masks = head_masks()
    ones = block_ones()

    def band(wi, carry):
        rows = pl.multiple_of(wi * 192, 192)
        ups = []
        for wj in range(3):
            x = grid[pl.ds(a + 8 * wi, 8), 8 * wj : 8 * wj + 8, :].reshape(64, 512)
            ups.append(x.astype(BF))
        g_mixed = dot_nt(jnp.concatenate(ups, 0), w_proj[...]).astype(BF)
        for wj in range(3):
            at = pl.ds(rows + 64 * wj, 64)
            for c in range(2):
                lo = 256 * c
                q = qkv[at, lo : lo + 256]
                kbig = spread(qkv[at, 512 + lo : 768 + lo], masks)
                vbig = spread(qkv[at, 1024 + lo : 1280 + lo], masks)
                p = probs[at, lo : lo + 256]
                g = g_mixed[64 * wj : 64 * wj + 64, lo : lo + 256]
                g_probs = dot_nt(g, vbig)
                wide_p = p.astype(F32)
                total = dot((wide_p * g_probs).astype(BF), ones)
                g_score = (wide_p * (g_probs - total) * 0.125).astype(BF)
                g_q = dot(g_score, kbig)
                g_k = collect(dot_tn(g_score, q), masks)
                g_v = collect(dot_tn(p, g), masks)
                out = slice(64 * wj, 64 * wj + 64)
                g_qkv[out, lo : lo + 256] = g_q.astype(BF)
                g_qkv[out, 512 + lo : 768 + lo] = g_k.astype(BF)
                g_qkv[out, 1024 + lo : 1280 + lo] = g_v.astype(BF)
        g_shift = dot_nt(g_qkv[...], w_qkv[...]).astype(BF).astype(F32)
        for wj in range(3):
            back[pl.ds(8 * wi, 8), 8 * wj : 8 * wj + 8, :] = g_shift[
                64 * wj : 64 * wj + 64
            ].reshape(8, 8, 512)
        return carry

    lax.fori_loop(0, 5, band, 0)

    def finish(r, carry):
        moved = place_back(back, r, a, b)
        part = norm_back(tokens[r].astype(F32), gain[...], moved)
        grad_out[r] = (own[r].astype(F32) + part).astype(BF)
        return carry

    lax.fori_loop(0, 32, finish, 0, unroll=4)


def attn_bwd(place, left, own, right, up, down, qkv, probs, w_proj, w_qkv, tokens, gain):
    return pl.pallas_call(
        attn_bwd_kernel,
        out_shape=jax.ShapeDtypeStruct((32, 16, 512), BF),
        in_specs=[SM] + [VM] * 11,
        out_specs=VM,
        scratch_shapes=[
            pltpu.VMEM((48, 24, 512), F32),
            pltpu.VMEM((40, 24, 512), F32),
            pltpu.VMEM((192, 1536), BF),
        ],
        compiler_params=params(40),
        cost_estimate=pl.CostEstimate(flops=4 * 10**9, bytes_accessed=10 * 2**20, transcendentals=0),
        name="attn_bwd",
    )(place, left, own, right, up, down, qkv, probs, w_proj, w_qkv, tokens, gain)


def set_fine(fine, value):
    for lane in range(4):
        fine[lane] = value[:, 128 * lane : 128 * lane + 128]


def get_fine(fine):
    return jnp.concatenate([fine[lane] for lane in range(4)], 1)


def patch_parts(fine):
    parts = {}
    for s in range(2):
        lanes = [fine[lane, pl.ds(s, 256, 2), :] for lane in range(4)]
        half = jnp.concatenate(lanes, 1).reshape(16, 2, 8, 512)
        for r in range(2):
            parts[r + 2 * s] = half[:, r].reshape(128, 512)
    return [parts[k] for k in range(4)]


def unpatch(fine, parts):
    for s in range(2):
        pair = [parts[r + 2 * s].reshape(16, 1, 8, 512) for r in range(2)]
        half = jnp.concatenate(pair, 1).reshape(256, 512)
        for lane in range(4):
            fine[lane, pl.ds(s, 256, 2), :] = half[:, 128 * lane : 128 * lane + 128]


def joint_normalise(parts):
    mean = sum(jnp.sum(p, -1, keepdims=True) for p in parts) / 2048.0
    cent = [p - mean for p in parts]
    var = sum(jnp.sum(c * c, -1, keepdims=True) for c in cent) / 2048.0
    r = lax.rsqrt(var + EPS)
    return [c * r for c in cent], r


def ffn_fwd_kernel(
    resid, gain_ffn, w_fc1, w_fc2, gain_merge, w_merge, gain_mlp,
    slope_out, block_out, coarse_out, cin_out,
    ffn_in, acc, merge_in, cacc, fine,
):
    n = pl.program_id(0)

    @pl.when(n == 0)
    def _():
        xh, _ = normalise(resid[...].astype(F32))
        ffn_in[...] = (xh * gain_ffn[...]).astype(BF)
        acc[...] = resid[...].astype(F32)

    @pl.when(n < 4)
    def _():
        for m in range(2):
            rows = slice(256 * m, 256 * m + 256)
            hid, slope = gelu_both(dot(ffn_in[rows, :], w_fc1[...]))
            slope_out[rows, :] = slope.astype(BF)
            acc[rows, :] += dot(hid.astype(BF), w_fc2[...])

    @pl.when(n == 3)
    def _():
        block = acc[...].astype(BF)
        block_out[...] = block
        set_fine(fine, block.astype(F32))
        xhs, _ = joint_normalise(patch_parts(fine))
        for k in range(4):
            merge_in[k] = (xhs[k] * gain_merge[:, 512 * k : 512 * k + 512]).astype(BF)
        cacc[...] = jnp.zeros_like(cacc)

    @pl.when(n >= 4)
    def _():
        cacc[...] += dot(merge_in[n - 4], w_merge[...])

    @pl.when(n == 7)
    def _():
        coarse = cacc[...].astype(BF)
        coarse_out[...] = coarse
        xh, _ = normalise(coarse.astype(F32))
        cin_out[...] = (xh * gain_mlp[...]).astype(BF)


def whole(shape):
    return pl.BlockSpec(shape, lambda n: (0,) * len(shape))


def ffn_fwd(resid, gain_ffn, w_fc1, w_fc2, gain_merge, w_merge, gain_mlp):
    early = lambda n: jnp.minimum(n, 3)
    late = lambda n: jnp.maximum(n - 4, 0)
    return pl.pallas_call(
        ffn_fwd_kernel,
        grid=(8,),
        out_shape=(
            jax.ShapeDtypeStruct((512, 2048), BF),
            jax.ShapeDtypeStruct((512, 512), BF),
            jax.ShapeDtypeStruct((128, 1024), BF),
            jax.ShapeDtypeStruct((128, 1024), BF),
        ),
        in_specs=[
            whole((512, 512)),
            whole((1, 512)),
            pl.BlockSpec((512, 512), lambda n: (0, early(n))),
            pl.BlockSpec((512, 512), lambda n: (early(n), 0)),
            whole((1, 2048)),
            pl.BlockSpec((512, 1024), lambda n: (late(n), 0)),
            whole((1, 1024)),
        ],
        out_specs=(
            pl.BlockSpec((512, 512), lambda n: (0, early(n))),
            whole((512, 512)),
            whole((128, 1024)),
            whole((128, 1024)),
        ),
        scratch_shapes=[
            pltpu.VMEM((512, 512), BF),
            pltpu.VMEM((512, 512), F32),
            pltpu.VMEM((4, 128, 512), BF),
            pltpu.VMEM((128, 1024), F32),
            pltpu.VMEM((4, 512, 128), F32),
        ],
        compiler_params=params(32),
        cost_estimate=pl.CostEstimate(flops=3 * 10**9, bytes_accessed=12 * 2**20, transcendentals=10**6),
        name="ffn_fwd",
    )(resid, gain_ffn, w_fc1, w_fc2, gain_merge, w_merge, gain_mlp)


def mlp_kernel(
    c0, c1, c2, c3, d0, d1, d2, d3,
    a0, a1, a2, a3, a4, b0, b1, b2, b3, b4,
    gcin_out, down_out,
    cs, ds, gacc, dacc,
):
    for k, (c, g) in enumerate(((c0, d0), (c1, d1), (c2, d2), (c3, d3))):
        cs[128 * k : 128 * k + 128] = c[...]
        ds[128 * k : 128 * k + 128] = g[...]
    firsts = [a0[...], a1[...], a2[...], jnp.concatenate([a3[...], a4[...]], 0)]
    for y in range(4):
        at = slice(64 * y, 64 * y + 64)
        fourth = b3[at] if y < 2 else b4[64 * y - 128 : 64 * y - 64]
        first = firsts[y]
        second = jnp.concatenate([b0[at], b1[at], b2[at], fourth], 0)
        for m in range(2):
            rows = slice(256 * m, 256 * m + 256)
            hid, slope = gelu_both(dot_nt(cs[rows], first))
            g_pre = (dot_nt(ds[rows], second) * slope).astype(BF)
            g_cin = dot(g_pre, first)
            down = dot(hid.astype(BF), second)
            if y == 0:
                gacc[rows] = g_cin
                dacc[rows] = down
            elif y < 3:
                gacc[rows] += g_cin
                dacc[rows] += down
            else:
                gcin_out[rows] = (gacc[rows] + g_cin).astype(BF)
                down_out[rows] = (dacc[rows] + down).astype(BF)


def coarse_mlp(cins, gds, firsts, seconds):
    return pl.pallas_call(
        mlp_kernel,
        out_shape=(jax.ShapeDtypeStruct((512, 1024), BF), jax.ShapeDtypeStruct((512, 1024), BF)),
        in_specs=[VM] * 18,
        out_specs=(VM, VM),
        scratch_shapes=[
            pltpu.VMEM((512, 1024), BF),
            pltpu.VMEM((512, 1024), BF),
            pltpu.VMEM((512, 1024), F32),
            pltpu.VMEM((512, 1024), F32),
        ],
        compiler_params=params(32),
        cost_estimate=pl.CostEstimate(flops=4 * 10**9, bytes_accessed=8 * 2**20, transcendentals=10**6),
        name="coarse_mlp",
    )(*cins, *gds, *firsts, *seconds)


def g_deep_kernel(cot, w_up, out, fine, parts, acc):
    k = pl.program_id(0)

    @pl.when(k == 0)
    def _():
        set_fine(fine, cot[...].astype(F32))
        for i, part in enumerate(patch_parts(fine)):
            parts[i] = part.astype(BF)
        acc[...] = jnp.zeros_like(acc)

    acc[...] += dot_nt(parts[k], w_up[...])

    @pl.when(k == 3)
    def _():
        out[...] = acc[...].astype(BF)


def g_deep_of(cot, w_up):
    return pl.pallas_call(
        g_deep_kernel,
        grid=(4,),
        out_shape=jax.ShapeDtypeStruct((128, 1024), BF),
        in_specs=[whole((512, 512)), pl.BlockSpec((1024, 512), lambda k: (0, k))],
        out_specs=whole((128, 1024)),
        scratch_shapes=[
            pltpu.VMEM((4, 512, 128), F32),
            pltpu.VMEM((4, 128, 512), BF),
            pltpu.VMEM((128, 1024), F32),
        ],
        compiler_params=params(32),
        cost_estimate=pl.CostEstimate(flops=10**9, bytes_accessed=5 * 2**20, transcendentals=0),
        name="g_deep",
    )(cot, w_up)


def up_kernel(coarse, down_own, down_far, block, w_up, out, deep, ups, fine):
    k = pl.program_id(0)

    @pl.when(k == 0)
    def _():
        total = coarse[...].astype(F32) + down_own[...].astype(F32) + down_far[...].astype(F32)
        deep[...] = total.astype(BF)

    ups[k] = dot(deep[...], w_up[...])

    @pl.when(k == 3)
    def _():
        unpatch(fine, [ups[i] for i in range(4)])
        out[...] = (block[...].astype(F32) + get_fine(fine)).astype(BF)


def up_of(coarse, down_own, down_far, block, w_up):
    return pl.pallas_call(
        up_kernel,
        grid=(4,),
        out_shape=jax.ShapeDtypeStruct((512, 512), BF),
        in_specs=[whole((128, 1024))] * 3
        + [whole((512, 512)), pl.BlockSpec((1024, 512), lambda k: (0, k))],
        out_specs=whole((512, 512)),
        scratch_shapes=[
            pltpu.VMEM((128, 1024), BF),
            pltpu.VMEM((4, 128, 512), F32),
            pltpu.VMEM((4, 512, 128), F32),
        ],
        compiler_params=params(32),
        cost_estimate=pl.CostEstimate(flops=10**9, bytes_accessed=5 * 2**20, transcendentals=0),
        name="up",
    )(coarse, down_own, down_far, block, w_up)


def ffn_bwd_kernel(
    gcin_own, gcin_far, g_deep, coarse, gain_mlp, w_merge, block, gain_merge, cot,
    w_fc2, slope, w_fc1, resid, gain_ffn,
    g_resid_out,
    g_coarse, g_mi, fine, g_block, acc,
):
    n = pl.program_id(0)

    @pl.when(n == 0)
    def _():
        g_cin = (gcin_own[...].astype(F32) + gcin_far[...].astype(F32)).astype(BF).astype(F32)
        part = norm_back(coarse[...].astype(F32), gain_mlp[...], g_cin)
        g_coarse[...] = (g_deep[...].astype(F32) + part).astype(BF)

    @pl.when(n < 4)
    def _():
        g_mi[n] = dot_nt(g_coarse[...], w_merge[...])

    @pl.when(n == 3)
    def _():
        set_fine(fine, block[...].astype(F32))
        xhs, r = joint_normalise(patch_parts(fine))
        scaled = [g_mi[k] * gain_merge[:, 512 * k : 512 * k + 512] for k in range(4)]
        mean_s = sum(jnp.sum(s, -1, keepdims=True) for s in scaled) / 2048.0
        mean_x = sum(jnp.sum(s * x, -1, keepdims=True) for s, x in zip(scaled, xhs)) / 2048.0
        unpatch(fine, [r * (s - mean_s - x * mean_x) for s, x in zip(scaled, xhs)])
        g_block[...] = (cot[...].astype(F32) + get_fine(fine)).astype(BF)
        acc[...] = jnp.zeros_like(acc)

    @pl.when(n >= 4)
    def _():
        for m in range(2):
            rows = slice(256 * m, 256 * m + 256)
            g_hid = dot_nt(g_block[rows, :], w_fc2[...])
            g_pre = (g_hid * slope[rows, :].astype(F32)).astype(BF)
            acc[rows, :] += dot_nt(g_pre, w_fc1[...])

    @pl.when(n == 7)
    def _():
        g_fin = acc[...].astype(BF).astype(F32)
        part = norm_back(resid[...].astype(F32), gain_ffn[...], g_fin)
        g_resid_out[...] = (g_block[...].astype(F32) + part).astype(BF)


def ffn_bwd(gcin_own, gcin_far, g_deep, coarse, gain_mlp, w_merge, block, gain_merge, cot,
            w_fc2, slope, w_fc1, resid, gain_ffn):
    early = lambda n: jnp.minimum(n, 3)
    late = lambda n: jnp.maximum(n - 4, 0)
    return pl.pallas_call(
        ffn_bwd_kernel,
        grid=(8,),
        out_shape=jax.ShapeDtypeStruct((512, 512), BF),
        in_specs=[whole((128, 1024))] * 4
        + [
            whole((1, 1024)),
            pl.BlockSpec((512, 1024), lambda n: (early(n), 0)),
            whole((512, 512)),
            whole((1, 2048)),
            whole((512, 512)),
            pl.BlockSpec((512, 512), lambda n: (late(n), 0)),
            pl.BlockSpec((512, 512), lambda n: (0, late(n))),
            pl.BlockSpec((512, 512), lambda n: (0, late(n))),
            whole((512, 512)),
            whole((1, 512)),
        ],
        out_specs=whole((512, 512)),
        scratch_shapes=[
            pltpu.VMEM((128, 1024), BF),
            pltpu.VMEM((4, 128, 512), F32),
            pltpu.VMEM((4, 512, 128), F32),
            pltpu.VMEM((512, 512), BF),
            pltpu.VMEM((512, 512), F32),
        ],
        compiler_params=params(32),
        cost_estimate=pl.CostEstimate(flops=3 * 10**9, bytes_accessed=14 * 2**20, transcendentals=0),
        name="ffn_bwd",
    )(gcin_own, gcin_far, g_deep, coarse, gain_mlp, w_merge, block, gain_merge, cot,
      w_fc2, slope, w_fc1, resid, gain_ffn)


def along(axis, count, step):
    pairs = [(s, (s + step) % count) for s in range(count)]
    return lambda v: lax.ppermute(v, axis, pairs)


LAT_NEXT, LAT_PREV = along("lat", 4, 1), along("lat", 4, -1)
LON_NEXT, LON_PREV = along("lon", 32, 1), along("lon", 32, -1)


def core_swap(v):
    return lax.ppermute(v, "lat", [(0, 1), (1, 0), (2, 3), (3, 2)])


def x_swap(v):
    return lax.ppermute(v, "lat", [(0, 2), (2, 0), (1, 3), (3, 1)])


def lon_move(dx, dy, dz):
    pairs = []
    for x in range(2):
        for y in range(4):
            for z in range(4):
                to = (((x + dx) % 2) * 4 + (y + dy) % 4) * 4 + (z + dz) % 4
                pairs.append(((x * 4 + y) * 4 + z, to))
    return lambda v: lax.ppermute(v, "lon", pairs)


def spread_once(v, step):
    return [v, step(1)(v), step(-1)(v), step(2)(v)]


def spread_split(v, step):
    ahead, behind = step(1)(v), step(-1)(v)
    half = v.shape[0] // 2
    return [v, ahead, behind, step(1)(ahead[:half]), step(-1)(behind[half:])]


def gather_weights(w_first, w_second):
    both = jnp.stack([w_first.T, w_second])
    mine = lax.all_to_all(both, "lat", 1, 2, tiled=True)
    other = lon_move(1, 0, 0)(mine)
    first = jnp.concatenate([mine[0], other[0]], 0)
    second = jnp.concatenate([mine[1], other[1]], 0)
    step_y = lambda k: lon_move(0, k, 0)
    step_z = lambda k: lon_move(0, 0, k)
    first = jnp.concatenate(spread_once(first, step_z), 0)
    second = jnp.concatenate(spread_once(second, step_y), 0)
    return spread_split(first, step_y), spread_split(second, step_z)


def share(v):
    far = x_swap(v)
    return [v, core_swap(v), far, core_swap(far)]


def reduce_back(total):
    sent = core_swap(jnp.concatenate([total[128:256], total[384:512]], 0))
    own = (total[0:128].astype(F32) + sent[0:128].astype(F32)).astype(BF)
    far = (total[256:384].astype(F32) + sent[128:256].astype(F32)).astype(BF)
    return own, x_swap(far)


def on_device(
    tokens, labels, offsets, gain_attn, w_qkv, w_proj, gain_ffn, w_fc1, w_fc2,
    gain_merge, w_merge, gain_mlp, w_first, w_second, w_up, cotangent,
):
    row = lambda g: g.reshape(1, -1)
    place = jnp.concatenate([offsets, lax.axis_index("lat").astype(jnp.int32)[None]])
    slab = jnp.pad(labels.astype(BF).T, ((0, 0), (0, 512 - 32)))[None]
    own = jnp.concatenate([tokens, slab], 0)
    left, right = LON_NEXT(own[:, 8:]), LON_PREV(own[:, :8])
    strip = lambda lo: jnp.concatenate(
        [
            jnp.concatenate([v[lo : lo + 8], v[32:33]], 0) for v in (left, own, right)
        ],
        1,
    )
    up, down = LAT_NEXT(strip(24)), LAT_PREV(strip(0))
    firsts, seconds = gather_weights(w_first, w_second)
    cot = cotangent.reshape(512, 512)
    g_deep = g_deep_of(cot, w_up)
    g_deeps = share(g_deep)
    qkv, probs, resid = attn_fwd(place, left, own, right, up, down, row(gain_attn), w_qkv, w_proj)
    resid = resid.reshape(512, 512)
    slope, block, coarse, coarse_in = ffn_fwd(
        resid, row(gain_ffn), w_fc1, w_fc2, row(gain_merge), w_merge, row(gain_mlp)
    )
    g_cin, deep_down = coarse_mlp(share(coarse_in), g_deeps, firsts, seconds)
    gcin_own, gcin_far = reduce_back(g_cin)
    g_resid = ffn_bwd(
        gcin_own, gcin_far, g_deep, coarse, row(gain_mlp), w_merge, block, row(gain_merge), cot,
        w_fc2, slope, w_fc1, resid, row(gain_ffn),
    ).reshape(32, 16, 512)
    g_left, g_right = LON_NEXT(g_resid[:, 8:]), LON_PREV(g_resid[:, :8])
    g_strip = lambda lo: jnp.concatenate(
        [v[lo : lo + 8] for v in (g_left, g_resid, g_right)], 1
    )
    g_up, g_down = LAT_NEXT(g_strip(24)), LAT_PREV(g_strip(0))
    down_own, down_far = reduce_back(deep_down)
    field_out = up_of(coarse, down_own, down_far, block, w_up).reshape(32, 16, 512)
    grad_in = attn_bwd(
        place, g_left, g_resid, g_right, g_up, g_down, qkv, probs, w_proj, w_qkv, tokens,
        row(gain_attn),
    )
    return (field_out, grad_in)


def solution(mesh):
    grid = P("lat", "lon", None)
    placed = (
        grid, P("lat", "lon"), P(), P(), P(), P(), P(), P(), P(), P(), P(), P(),
        P("lat", "lon"), P("lon", "lat"), P(), grid,
    )
    return jax.shard_map(
        on_device, mesh=mesh, in_specs=placed, out_specs=(grid, grid), check_vma=False
    )
```

```python
import jax
import jax.numpy as jnp
from jax import lax
from jax.experimental import pallas as pl
from jax.experimental.pallas import tpu as pltpu
from jax.sharding import PartitionSpec as P

BF = jnp.bfloat16
F32 = jnp.float32
EPS = 1e-05
NT = (((1,), (1,)), ((), ()))
TN = (((0,), (0,)), ((), ()))
GELU_C = 0.7978845608028654
GELU_A = 0.044715


def dot(a, b):
    return jnp.dot(a, b, preferred_element_type=F32)


def dot_nt(a, b):
    return lax.dot_general(a, b, NT, preferred_element_type=F32)


def dot_tn(a, b):
    return lax.dot_general(a, b, TN, preferred_element_type=F32)


def normalise(v):
    mean = jnp.mean(v, -1, keepdims=True)
    c = v - mean
    r = lax.rsqrt(jnp.mean(c * c, -1, keepdims=True) + EPS)
    return c * r, r


def norm_back(v, gain, t):
    xh, r = normalise(v)
    s = t * gain
    return r * (s - jnp.mean(s, -1, keepdims=True) - xh * jnp.mean(s * xh, -1, keepdims=True))


def gelu_both(x):
    x2 = x * x
    t = jnp.tanh(GELU_C * x * (1.0 + GELU_A * x2))
    half = 0.5 * (1.0 + t)
    slope = half + 0.5 * x * (1.0 - t * t) * (GELU_C * (1.0 + 3.0 * GELU_A * x2))
    return x * half, slope


def head_masks():
    lane = lax.broadcasted_iota(jnp.int32, (1, 256), 1) // 64
    return [(lane == h).astype(F32).astype(BF) for h in range(4)]


def block_ones():
    r = lax.broadcasted_iota(jnp.int32, (256, 256), 0) // 64
    c = lax.broadcasted_iota(jnp.int32, (256, 256), 1) // 64
    return (r == c).astype(F32).astype(BF)


def spread(x, masks):
    return jnp.concatenate([x * m for m in masks], 0)


def collect(big, masks):
    out = None
    for h, m in enumerate(masks):
        term = big[64 * h : 64 * h + 64] * m.astype(F32)
        out = term if out is None else out + term
    return out


def fill_grid(grid, b, left, own, right, up, down):
    def moved(line):
        return pltpu.roll(line.astype(F32), 32 - b, 0)[:24]

    def row(r, carry):
        grid[8 + r] = moved(
            jnp.concatenate([left[r].astype(F32), own[r].astype(F32), right[r].astype(F32)], 0)
        )
        return carry

    lax.fori_loop(0, 32, row, 0, unroll=4)

    def edge(r, carry):
        grid[r] = moved(up[r])
        grid[40 + r] = moved(down[r])
        return carry

    lax.fori_loop(0, 8, edge, 0, unroll=2)


def place_back(back, r, a, b):
    return pltpu.roll(back[8 - a + r], 16 + b, 0)[:16]


def attn_fwd_kernel(
    place, left, own, right, up, down, gain, w_qkv, w_proj,
    qkv_out, probs_out, resid_out,
    grid, codes, back, mixed,
):
    a, b, d = place[0], place[1], place[2]
    fill_grid(grid, b, left, own, right, up, down)
    slab = jnp.concatenate([v[32].astype(F32) for v in (left, own, right)], 0)
    slab = pltpu.roll(slab, 32 - b, 0)[:24]
    first = jnp.where(d == 0, 4.0, 0.0).astype(F32)
    last = jnp.where(d == 3, 4.0, 0.0).astype(F32)
    slab_up = pltpu.roll(up[8].astype(F32) + first, 32 - b, 0)[:24]
    slab_down = pltpu.roll(down[8].astype(F32) + last, 32 - b, 0)[:24]
    for r in range(32):
        codes[8 + r] = jnp.broadcast_to(slab[:, r : r + 1], (24, 128))
    for r in range(8):
        codes[r] = jnp.broadcast_to(slab_up[:, 24 + r : 25 + r], (24, 128))
        codes[40 + r] = jnp.broadcast_to(slab_down[:, r : r + 1], (24, 128))
    masks = head_masks()
    ones = block_ones()

    def band(wi, carry):
        rows = pl.multiple_of(wi * 192, 192)
        normed = []
        for wj in range(3):
            x = grid[pl.ds(a + 8 * wi, 8), 8 * wj : 8 * wj + 8, :].reshape(64, 512)
            xh, _ = normalise(x)
            normed.append((xh * gain[...]).astype(BF))
        qkv = dot(jnp.concatenate(normed, 0), w_qkv[...]).astype(BF)
        qkv_out[pl.ds(rows, 192), :] = qkv
        for wj in range(3):
            col = codes[pl.ds(a + 8 * wi, 8), 8 * wj : 8 * wj + 8, :].reshape(64, 128)
            row = col.T[0:1, 0:64]
            same = jnp.concatenate([col, col], 1) == jnp.concatenate([row] * 4, 1)
            win = qkv[64 * wj : 64 * wj + 64]
            for c in range(2):
                lo = 256 * c
                q = win[:, lo : lo + 256]
                kbig = spread(win[:, 512 + lo : 768 + lo], masks)
                vbig = spread(win[:, 1024 + lo : 1280 + lo], masks)
                e = jnp.where(same, jnp.exp(dot_nt(q, kbig) * 0.125), 0.0)
                total = dot(e.astype(BF), ones)
                p = (e / total).astype(BF)
                probs_out[pl.ds(rows + 64 * wj, 64), lo : lo + 256] = p
                mixed[64 * wj : 64 * wj + 64, lo : lo + 256] = dot(p, vbig).astype(BF)
        att = dot(mixed[...], w_proj[...]).astype(BF).astype(F32)
        for wj in range(3):
            back[pl.ds(8 * wi, 8), 8 * wj : 8 * wj + 8, :] = att[64 * wj : 64 * wj + 64].reshape(
                8, 8, 512
            )
        return carry

    lax.fori_loop(0, 5, band, 0)

    def finish(r, carry):
        moved = place_back(back, r, a, b)
        resid_out[r] = (own[r].astype(F32) + moved).astype(BF)
        return carry

    lax.fori_loop(0, 32, finish, 0, unroll=4)


VM = pl.BlockSpec(memory_space=pltpu.VMEM)
SM = pl.BlockSpec(memory_space=pltpu.SMEM)


def params(mib):
    return pltpu.CompilerParams(vmem_limit_bytes=mib * 2**20)


def attn_fwd(place, left, own, right, up, down, gain, w_qkv, w_proj):
    return pl.pallas_call(
        attn_fwd_kernel,
        out_shape=(
            jax.ShapeDtypeStruct((960, 1536), BF),
            jax.ShapeDtypeStruct((960, 512), BF),
            jax.ShapeDtypeStruct((32, 16, 512), BF),
        ),
        in_specs=[SM] + [VM] * 8,
        out_specs=(VM, VM, VM),
        scratch_shapes=[
            pltpu.VMEM((48, 24, 512), F32),
            pltpu.VMEM((48, 24, 128), F32),
            pltpu.VMEM((40, 24, 512), F32),
            pltpu.VMEM((192, 512), BF),
        ],
        compiler_params=params(40),
        cost_estimate=pl.CostEstimate(flops=2 * 10**9, bytes_accessed=10 * 2**20, transcendentals=10**6),
        name="attn_fwd",
    )(place, left, own, right, up, down, gain, w_qkv, w_proj)


def attn_bwd_kernel(
    place, left, own, right, up, down, qkv, probs, w_proj, w_qkv, tokens, gain,
    grad_out,
    grid, back, g_qkv,
):
    a, b = place[0], place[1]
    fill_grid(grid, b, left, own, right, up, down)
    masks = head_masks()
    ones = block_ones()

    def band(wi, carry):
        rows = pl.multiple_of(wi * 192, 192)
        ups = []
        for wj in range(3):
            x = grid[pl.ds(a + 8 * wi, 8), 8 * wj : 8 * wj + 8, :].reshape(64, 512)
            ups.append(x.astype(BF))
        g_mixed = dot_nt(jnp.concatenate(ups, 0), w_proj[...]).astype(BF)
        for wj in range(3):
            at = pl.ds(rows + 64 * wj, 64)
            for c in range(2):
                lo = 256 * c
                q = qkv[at, lo : lo + 256]
                kbig = spread(qkv[at, 512 + lo : 768 + lo], masks)
                vbig = spread(qkv[at, 1024 + lo : 1280 + lo], masks)
                p = probs[at, lo : lo + 256]
                g = g_mixed[64 * wj : 64 * wj + 64, lo : lo + 256]
                g_probs = dot_nt(g, vbig)
                wide_p = p.astype(F32)
                total = dot((wide_p * g_probs).astype(BF), ones)
                g_score = (wide_p * (g_probs - total) * 0.125).astype(BF)
                g_q = dot(g_score, kbig)
                g_k = collect(dot_tn(g_score, q), masks)
                g_v = collect(dot_tn(p, g), masks)
                out = slice(64 * wj, 64 * wj + 64)
                g_qkv[out, lo : lo + 256] = g_q.astype(BF)
                g_qkv[out, 512 + lo : 768 + lo] = g_k.astype(BF)
                g_qkv[out, 1024 + lo : 1280 + lo] = g_v.astype(BF)
        g_shift = dot_nt(g_qkv[...], w_qkv[...]).astype(BF).astype(F32)
        for wj in range(3):
            back[pl.ds(8 * wi, 8), 8 * wj : 8 * wj + 8, :] = g_shift[
                64 * wj : 64 * wj + 64
            ].reshape(8, 8, 512)
        return carry

    lax.fori_loop(0, 5, band, 0)

    def finish(r, carry):
        moved = place_back(back, r, a, b)
        part = norm_back(tokens[r].astype(F32), gain[...], moved)
        grad_out[r] = (own[r].astype(F32) + part).astype(BF)
        return carry

    lax.fori_loop(0, 32, finish, 0, unroll=4)


def attn_bwd(place, left, own, right, up, down, qkv, probs, w_proj, w_qkv, tokens, gain):
    return pl.pallas_call(
        attn_bwd_kernel,
        out_shape=jax.ShapeDtypeStruct((32, 16, 512), BF),
        in_specs=[SM] + [VM] * 11,
        out_specs=VM,
        scratch_shapes=[
            pltpu.VMEM((48, 24, 512), F32),
            pltpu.VMEM((40, 24, 512), F32),
            pltpu.VMEM((192, 1536), BF),
        ],
        compiler_params=params(40),
        cost_estimate=pl.CostEstimate(flops=4 * 10**9, bytes_accessed=10 * 2**20, transcendentals=0),
        name="attn_bwd",
    )(place, left, own, right, up, down, qkv, probs, w_proj, w_qkv, tokens, gain)


def set_fine(fine, value):
    for lane in range(4):
        fine[lane] = value[:, 128 * lane : 128 * lane + 128]


def get_fine(fine):
    return jnp.concatenate([fine[lane] for lane in range(4)], 1)


def patch_parts(fine):
    parts = {}
    for s in range(2):
        lanes = [fine[lane, pl.ds(s, 256, 2), :] for lane in range(4)]
        half = jnp.concatenate(lanes, 1).reshape(16, 2, 8, 512)
        for r in range(2):
            parts[r + 2 * s] = half[:, r].reshape(128, 512)
    return [parts[k] for k in range(4)]


def unpatch(fine, parts):
    for s in range(2):
        pair = [parts[r + 2 * s].reshape(16, 1, 8, 512) for r in range(2)]
        half = jnp.concatenate(pair, 1).reshape(256, 512)
        for lane in range(4):
            fine[lane, pl.ds(s, 256, 2), :] = half[:, 128 * lane : 128 * lane + 128]


def joint_normalise(parts):
    mean = sum(jnp.sum(p, -1, keepdims=True) for p in parts) / 2048.0
    cent = [p - mean for p in parts]
    var = sum(jnp.sum(c * c, -1, keepdims=True) for c in cent) / 2048.0
    r = lax.rsqrt(var + EPS)
    return [c * r for c in cent], r


def ffn_fwd_kernel(
    resid, gain_ffn, w_fc1, w_fc2, gain_merge, w_merge, gain_mlp,
    slope_out, block_out, coarse_out, cin_out,
    ffn_in, acc, merge_in, cacc, fine,
):
    n = pl.program_id(0)

    @pl.when(n == 0)
    def _():
        xh, _ = normalise(resid[...].astype(F32))
        ffn_in[...] = (xh * gain_ffn[...]).astype(BF)
        acc[...] = resid[...].astype(F32)

    @pl.when(n < 4)
    def _():
        for m in range(2):
            rows = slice(256 * m, 256 * m + 256)
            hid, slope = gelu_both(dot(ffn_in[rows, :], w_fc1[...]))
            slope_out[rows, :] = slope.astype(BF)
            acc[rows, :] += dot(hid.astype(BF), w_fc2[...])

    @pl.when(n == 3)
    def _():
        block = acc[...].astype(BF)
        block_out[...] = block
        set_fine(fine, block.astype(F32))
        xhs, _ = joint_normalise(patch_parts(fine))
        for k in range(4):
            merge_in[k] = (xhs[k] * gain_merge[:, 512 * k : 512 * k + 512]).astype(BF)
        cacc[...] = jnp.zeros_like(cacc)

    @pl.when(n >= 4)
    def _():
        cacc[...] += dot(merge_in[n - 4], w_merge[...])

    @pl.when(n == 7)
    def _():
        coarse = cacc[...].astype(BF)
        coarse_out[...] = coarse
        xh, _ = normalise(coarse.astype(F32))
        cin_out[...] = (xh * gain_mlp[...]).astype(BF)


def whole(shape):
    return pl.BlockSpec(shape, lambda n: (0,) * len(shape))


def ffn_fwd(resid, gain_ffn, w_fc1, w_fc2, gain_merge, w_merge, gain_mlp):
    early = lambda n: jnp.minimum(n, 3)
    late = lambda n: jnp.maximum(n - 4, 0)
    return pl.pallas_call(
        ffn_fwd_kernel,
        grid=(8,),
        out_shape=(
            jax.ShapeDtypeStruct((512, 2048), BF),
            jax.ShapeDtypeStruct((512, 512), BF),
            jax.ShapeDtypeStruct((128, 1024), BF),
            jax.ShapeDtypeStruct((128, 1024), BF),
        ),
        in_specs=[
            whole((512, 512)),
            whole((1, 512)),
            pl.BlockSpec((512, 512), lambda n: (0, early(n))),
            pl.BlockSpec((512, 512), lambda n: (early(n), 0)),
            whole((1, 2048)),
            pl.BlockSpec((512, 1024), lambda n: (late(n), 0)),
            whole((1, 1024)),
        ],
        out_specs=(
            pl.BlockSpec((512, 512), lambda n: (0, early(n))),
            whole((512, 512)),
            whole((128, 1024)),
            whole((128, 1024)),
        ),
        scratch_shapes=[
            pltpu.VMEM((512, 512), BF),
            pltpu.VMEM((512, 512), F32),
            pltpu.VMEM((4, 128, 512), BF),
            pltpu.VMEM((128, 1024), F32),
            pltpu.VMEM((4, 512, 128), F32),
        ],
        compiler_params=params(32),
        cost_estimate=pl.CostEstimate(flops=3 * 10**9, bytes_accessed=12 * 2**20, transcendentals=10**6),
        name="ffn_fwd",
    )(resid, gain_ffn, w_fc1, w_fc2, gain_merge, w_merge, gain_mlp)


def second_block(b0, b1, b2, b3, b4, y):
    at = slice(64 * y, 64 * y + 64)
    fourth = b3[at] if y < 2 else b4[64 * y - 128 : 64 * y - 64]
    return jnp.concatenate([b0[at], b1[at], b2[at], fourth], 0)


def mlp_kernel(
    c0, c1, c2, c3, d0, d1, d2, d3,
    a0, a1, a2, a3, a4, b0, b1, b2, b3, b4,
    gcin_out, hid_out,
    cs, ds, gacc,
):
    for k, (c, g) in enumerate(((c0, d0), (c1, d1), (c2, d2), (c3, d3))):
        cs[128 * k : 128 * k + 128] = c[...]
        ds[128 * k : 128 * k + 128] = g[...]
    firsts = [a0[...], a1[...], a2[...], jnp.concatenate([a3[...], a4[...]], 0)]
    for y in range(4):
        first = firsts[y]
        second = second_block(b0, b1, b2, b3, b4, y)
        for m in range(2):
            rows = slice(256 * m, 256 * m + 256)
            hid, slope = gelu_both(dot_nt(cs[rows], first))
            hid_out[rows, 256 * y : 256 * y + 256] = hid.astype(BF)
            g_pre = (dot_nt(ds[rows], second) * slope).astype(BF)
            g_cin = dot(g_pre, first)
            if y == 0:
                gacc[rows] = g_cin
            elif y < 3:
                gacc[rows] += g_cin
            else:
                gcin_out[rows] = (gacc[rows] + g_cin).astype(BF)


def coarse_mlp(cins, gds, firsts, seconds):
    return pl.pallas_call(
        mlp_kernel,
        out_shape=(jax.ShapeDtypeStruct((512, 1024), BF), jax.ShapeDtypeStruct((512, 1024), BF)),
        in_specs=[VM] * 18,
        out_specs=(VM, VM),
        scratch_shapes=[
            pltpu.VMEM((512, 1024), BF),
            pltpu.VMEM((512, 1024), BF),
            pltpu.VMEM((512, 1024), F32),
        ],
        compiler_params=params(32),
        cost_estimate=pl.CostEstimate(flops=3 * 10**9, bytes_accessed=8 * 2**20, transcendentals=10**6),
        name="coarse_mlp",
    )(*cins, *gds, *firsts, *seconds)


def down_kernel(hid, b0, b1, b2, b3, b4, out):
    total = None
    for y in range(4):
        second = second_block(b0, b1, b2, b3, b4, y)
        term = dot(hid[:, 256 * y : 256 * y + 256], second)
        total = term if total is None else total + term
    out[...] = total.astype(BF)


def down_of(hid, seconds):
    return pl.pallas_call(
        down_kernel,
        out_shape=jax.ShapeDtypeStruct((512, 1024), BF),
        in_specs=[VM] * 6,
        out_specs=VM,
        compiler_params=params(32),
        cost_estimate=pl.CostEstimate(flops=10**9, bytes_accessed=5 * 2**20, transcendentals=0),
        name="down",
    )(hid, *seconds)


def g_deep_kernel(cot, w_up, out, fine, parts, acc):
    k = pl.program_id(0)

    @pl.when(k == 0)
    def _():
        set_fine(fine, cot[...].astype(F32))
        for i, part in enumerate(patch_parts(fine)):
            parts[i] = part.astype(BF)
        acc[...] = jnp.zeros_like(acc)

    acc[...] += dot_nt(parts[k], w_up[...])

    @pl.when(k == 3)
    def _():
        out[...] = acc[...].astype(BF)


def g_deep_of(cot, w_up):
    return pl.pallas_call(
        g_deep_kernel,
        grid=(4,),
        out_shape=jax.ShapeDtypeStruct((128, 1024), BF),
        in_specs=[whole((512, 512)), pl.BlockSpec((1024, 512), lambda k: (0, k))],
        out_specs=whole((128, 1024)),
        scratch_shapes=[
            pltpu.VMEM((4, 512, 128), F32),
            pltpu.VMEM((4, 128, 512), BF),
            pltpu.VMEM((128, 1024), F32),
        ],
        compiler_params=params(32),
        cost_estimate=pl.CostEstimate(flops=10**9, bytes_accessed=5 * 2**20, transcendentals=0),
        name="g_deep",
    )(cot, w_up)


def up_kernel(coarse, down_own, down_far, block, w_up, out, deep, ups, fine):
    k = pl.program_id(0)

    @pl.when(k == 0)
    def _():
        total = coarse[...].astype(F32) + down_own[...].astype(F32) + down_far[...].astype(F32)
        deep[...] = total.astype(BF)

    ups[k] = dot(deep[...], w_up[...])

    @pl.when(k == 3)
    def _():
        unpatch(fine, [ups[i] for i in range(4)])
        out[...] = (block[...].astype(F32) + get_fine(fine)).astype(BF)


def up_of(coarse, down_own, down_far, block, w_up):
    return pl.pallas_call(
        up_kernel,
        grid=(4,),
        out_shape=jax.ShapeDtypeStruct((512, 512), BF),
        in_specs=[whole((128, 1024))] * 3
        + [whole((512, 512)), pl.BlockSpec((1024, 512), lambda k: (0, k))],
        out_specs=whole((512, 512)),
        scratch_shapes=[
            pltpu.VMEM((128, 1024), BF),
            pltpu.VMEM((4, 128, 512), F32),
            pltpu.VMEM((4, 512, 128), F32),
        ],
        compiler_params=params(32),
        cost_estimate=pl.CostEstimate(flops=10**9, bytes_accessed=5 * 2**20, transcendentals=0),
        name="up",
    )(coarse, down_own, down_far, block, w_up)


def ffn_bwd_kernel(
    gcin_own, gcin_far, g_deep, coarse, gain_mlp, w_merge, block, gain_merge, cot,
    w_fc2, slope, w_fc1, resid, gain_ffn,
    g_resid_out,
    g_coarse, g_mi, fine, g_block, acc,
):
    n = pl.program_id(0)

    @pl.when(n == 0)
    def _():
        g_cin = (gcin_own[...].astype(F32) + gcin_far[...].astype(F32)).astype(BF).astype(F32)
        part = norm_back(coarse[...].astype(F32), gain_mlp[...], g_cin)
        g_coarse[...] = (g_deep[...].astype(F32) + part).astype(BF)

    @pl.when(n < 4)
    def _():
        g_mi[n] = dot_nt(g_coarse[...], w_merge[...])

    @pl.when(n == 3)
    def _():
        set_fine(fine, block[...].astype(F32))
        xhs, r = joint_normalise(patch_parts(fine))
        scaled = [g_mi[k] * gain_merge[:, 512 * k : 512 * k + 512] for k in range(4)]
        mean_s = sum(jnp.sum(s, -1, keepdims=True) for s in scaled) / 2048.0
        mean_x = sum(jnp.sum(s * x, -1, keepdims=True) for s, x in zip(scaled, xhs)) / 2048.0
        unpatch(fine, [r * (s - mean_s - x * mean_x) for s, x in zip(scaled, xhs)])
        g_block[...] = (cot[...].astype(F32) + get_fine(fine)).astype(BF)
        acc[...] = jnp.zeros_like(acc)

    @pl.when(n >= 4)
    def _():
        for m in range(2):
            rows = slice(256 * m, 256 * m + 256)
            g_hid = dot_nt(g_block[rows, :], w_fc2[...])
            g_pre = (g_hid * slope[rows, :].astype(F32)).astype(BF)
            acc[rows, :] += dot_nt(g_pre, w_fc1[...])

    @pl.when(n == 7)
    def _():
        g_fin = acc[...].astype(BF).astype(F32)
        part = norm_back(resid[...].astype(F32), gain_ffn[...], g_fin)
        g_resid_out[...] = (g_block[...].astype(F32) + part).astype(BF)


def ffn_bwd(gcin_own, gcin_far, g_deep, coarse, gain_mlp, w_merge, block, gain_merge, cot,
            w_fc2, slope, w_fc1, resid, gain_ffn):
    early = lambda n: jnp.minimum(n, 3)
    late = lambda n: jnp.maximum(n - 4, 0)
    return pl.pallas_call(
        ffn_bwd_kernel,
        grid=(8,),
        out_shape=jax.ShapeDtypeStruct((512, 512), BF),
        in_specs=[whole((128, 1024))] * 4
        + [
            whole((1, 1024)),
            pl.BlockSpec((512, 1024), lambda n: (early(n), 0)),
            whole((512, 512)),
            whole((1, 2048)),
            whole((512, 512)),
            pl.BlockSpec((512, 512), lambda n: (late(n), 0)),
            pl.BlockSpec((512, 512), lambda n: (0, late(n))),
            pl.BlockSpec((512, 512), lambda n: (0, late(n))),
            whole((512, 512)),
            whole((1, 512)),
        ],
        out_specs=whole((512, 512)),
        scratch_shapes=[
            pltpu.VMEM((128, 1024), BF),
            pltpu.VMEM((4, 128, 512), F32),
            pltpu.VMEM((4, 512, 128), F32),
            pltpu.VMEM((512, 512), BF),
            pltpu.VMEM((512, 512), F32),
        ],
        compiler_params=params(32),
        cost_estimate=pl.CostEstimate(flops=3 * 10**9, bytes_accessed=14 * 2**20, transcendentals=0),
        name="ffn_bwd",
    )(gcin_own, gcin_far, g_deep, coarse, gain_mlp, w_merge, block, gain_merge, cot,
      w_fc2, slope, w_fc1, resid, gain_ffn)


def along(axis, count, step):
    pairs = [(s, (s + step) % count) for s in range(count)]
    return lambda v: lax.ppermute(v, axis, pairs)


LAT_NEXT, LAT_PREV = along("lat", 4, 1), along("lat", 4, -1)
LON_NEXT, LON_PREV = along("lon", 32, 1), along("lon", 32, -1)


def core_swap(v):
    return lax.ppermute(v, "lat", [(0, 1), (1, 0), (2, 3), (3, 2)])


def x_swap(v):
    return lax.ppermute(v, "lat", [(0, 2), (2, 0), (1, 3), (3, 1)])


def lon_move(dx, dy, dz):
    pairs = []
    for x in range(2):
        for y in range(4):
            for z in range(4):
                to = (((x + dx) % 2) * 4 + (y + dy) % 4) * 4 + (z + dz) % 4
                pairs.append(((x * 4 + y) * 4 + z, to))
    return lambda v: lax.ppermute(v, "lon", pairs)


def after(value, *gates):
    return lax.optimization_barrier((value,) + gates)[0]


def spread_once(v, step):
    return jnp.concatenate([v, step(1)(v), step(-1)(v), step(2)(v)], 0)


def step_y(k):
    return lon_move(0, k, 0)


def step_z(k):
    return lon_move(0, 0, k)


def reduce_core(total):
    sent = core_swap(jnp.concatenate([total[128:256], total[384:512]], 0))
    own = (total[0:128].astype(F32) + sent[0:128].astype(F32)).astype(BF)
    far = (total[256:384].astype(F32) + sent[128:256].astype(F32)).astype(BF)
    return own, far


def on_device(
    tokens, labels, offsets, gain_attn, w_qkv, w_proj, gain_ffn, w_fc1, w_fc2,
    gain_merge, w_merge, gain_mlp, w_first, w_second, w_up, cotangent,
):
    row = lambda g: g.reshape(1, -1)
    place = jnp.concatenate([offsets, lax.axis_index("lat").astype(jnp.int32)[None]])
    slab = jnp.pad(labels.astype(BF).T, ((0, 0), (0, 512 - 32)))[None]
    own = jnp.concatenate([tokens, slab], 0)
    left, right = LON_NEXT(own[:, 8:]), LON_PREV(own[:, :8])
    cot = cotangent.reshape(512, 512)
    g_deep = g_deep_of(cot, w_up)
    mine = lax.all_to_all(jnp.stack([w_first.T, w_second]), "lat", 1, 2, tiled=True)
    near_deep = core_swap(g_deep)
    middle = after(own, g_deep)
    strip = lambda lo: jnp.concatenate(
        [
            jnp.concatenate([v[lo : lo + 8], v[32:33]], 0) for v in (left, middle, right)
        ],
        1,
    )
    up, down = LAT_NEXT(strip(24)), LAT_PREV(strip(0))
    mine = after(mine, left, right)
    other = lon_move(1, 0, 0)(mine)
    first = after(jnp.concatenate([mine[0], other[0]], 0), up, down)
    second = after(jnp.concatenate([mine[1], other[1]], 0), up, down)
    first = spread_once(first, step_z)
    second = spread_once(second, step_y)
    qkv, probs, resid = attn_fwd(place, left, own, right, up, down, row(gain_attn), w_qkv, w_proj)
    resid = resid.reshape(512, 512)
    first, second = after(first, resid), after(second, resid)
    first_a, first_b = step_y(1)(first), step_y(-1)(first)
    second_a, second_b = step_z(1)(second), step_z(-1)(second)
    far_deep = x_swap(after(g_deep, resid))
    slope, block, coarse, coarse_in = ffn_fwd(
        resid, row(gain_ffn), w_fc1, w_fc2, row(gain_merge), w_merge, row(gain_mlp)
    )
    far_cin = x_swap(coarse_in)
    held = (first_a, first_b, second_a, second_b)
    firsts = [
        first, first_a, first_b,
        step_y(1)(after(first_a[:128], coarse_in)), step_y(-1)(after(first_b[128:], coarse_in)),
    ]
    seconds = [
        second, second_a, second_b,
        step_z(1)(after(second_a[:128], coarse_in)), step_z(-1)(after(second_b[128:], coarse_in)),
    ]
    cins = [coarse_in, core_swap(coarse_in), far_cin, core_swap(after(far_cin, *held))]
    g_deeps = [g_deep, near_deep, far_deep, core_swap(after(far_deep, coarse_in, *held))]
    g_cin, hid = coarse_mlp(cins, g_deeps, firsts, seconds)
    gcin_own, gcin_far = reduce_core(g_cin)
    gcin_far = x_swap(gcin_far)
    down_own, down_far = reduce_core(down_of(hid, seconds))
    gcin_far, down_far = lax.optimization_barrier((gcin_far, down_far))
    down_far = x_swap(down_far)
    g_resid = ffn_bwd(
        gcin_own, gcin_far, g_deep, coarse, row(gain_mlp), w_merge, block, row(gain_merge), cot,
        w_fc2, slope, w_fc1, resid, row(gain_ffn),
    ).reshape(32, 16, 512)
    g_left, g_right = LON_NEXT(g_resid[:, 8:]), LON_PREV(g_resid[:, :8])
    g_strip = lambda lo: jnp.concatenate(
        [v[lo : lo + 8] for v in (g_left, g_resid, g_right)], 1
    )
    g_up, g_down = LAT_NEXT(g_strip(24)), LAT_PREV(g_strip(0))
    field_out = up_of(
        coarse, down_own, after(down_far, g_resid), block, w_up
    ).reshape(32, 16, 512)
    grad_in = attn_bwd(
        place, g_left, g_resid, g_right, g_up, g_down, qkv, probs, w_proj, w_qkv, tokens,
        row(gain_attn),
    )
    return (field_out, grad_in)


def solution(mesh):
    grid = P("lat", "lon", None)
    placed = (
        grid, P("lat", "lon"), P(), P(), P(), P(), P(), P(), P(), P(), P(), P(),
        P("lat", "lon"), P("lon", "lat"), P(), grid,
    )
    return jax.shard_map(
        on_device, mesh=mesh, in_specs=placed, out_specs=(grid, grid), check_vma=False
    )
```

```python
import jax
import jax.numpy as jnp
from jax import lax
from jax.experimental import pallas as pl
from jax.experimental.pallas import tpu as pltpu
from jax.sharding import PartitionSpec as P

BF = jnp.bfloat16
F32 = jnp.float32
EPS = 1e-05
NT = (((1,), (1,)), ((), ()))
TN = (((0,), (0,)), ((), ()))
GELU_C = 0.7978845608028654
GELU_A = 0.044715


def dot(a, b):
    return jnp.dot(a, b, preferred_element_type=F32)


def dot_nt(a, b):
    return lax.dot_general(a, b, NT, preferred_element_type=F32)


def dot_tn(a, b):
    return lax.dot_general(a, b, TN, preferred_element_type=F32)


def normalise(v):
    mean = jnp.mean(v, -1, keepdims=True)
    c = v - mean
    r = lax.rsqrt(jnp.mean(c * c, -1, keepdims=True) + EPS)
    return c * r, r


def norm_back(v, gain, t):
    xh, r = normalise(v)
    s = t * gain
    return r * (s - jnp.mean(s, -1, keepdims=True) - xh * jnp.mean(s * xh, -1, keepdims=True))


def gelu_both(x):
    x2 = x * x
    t = jnp.tanh(GELU_C * x * (1.0 + GELU_A * x2))
    half = 0.5 * (1.0 + t)
    slope = half + 0.5 * x * (1.0 - t * t) * (GELU_C * (1.0 + 3.0 * GELU_A * x2))
    return x * half, slope


def head_masks():
    lane = lax.broadcasted_iota(jnp.int32, (1, 256), 1) // 64
    return [(lane == h).astype(F32).astype(BF) for h in range(4)]


def block_ones():
    r = lax.broadcasted_iota(jnp.int32, (256, 256), 0) // 64
    c = lax.broadcasted_iota(jnp.int32, (256, 256), 1) // 64
    return (r == c).astype(F32).astype(BF)


def spread(x, masks):
    return jnp.concatenate([x * m for m in masks], 0)


def collect(big, masks):
    out = None
    for h, m in enumerate(masks):
        term = big[64 * h : 64 * h + 64] * m.astype(F32)
        out = term if out is None else out + term
    return out


def fill_grid(grid, b, left, own, right, up, down):
    def moved(line):
        return pltpu.roll(line.astype(F32), 32 - b, 0)[:24]

    def row(r, carry):
        grid[8 + r] = moved(
            jnp.concatenate([left[r].astype(F32), own[r].astype(F32), right[r].astype(F32)], 0)
        )
        return carry

    lax.fori_loop(0, 32, row, 0, unroll=4)

    def edge(r, carry):
        grid[r] = moved(up[r])
        grid[40 + r] = moved(down[r])
        return carry

    lax.fori_loop(0, 8, edge, 0, unroll=2)


def place_back(back, r, a, b):
    return pltpu.roll(back[8 - a + r], 16 + b, 0)[:16]


def attn_fwd_kernel(
    place, left, own, right, up, down, gain, w_qkv, w_proj,
    qkv_out, probs_out, resid_out,
    grid, codes, back, mixed,
):
    a, b, d = place[0], place[1], place[2]
    fill_grid(grid, b, left, own, right, up, down)
    slab = jnp.concatenate([v[32].astype(F32) for v in (left, own, right)], 0)
    slab = pltpu.roll(slab, 32 - b, 0)[:24]
    first = jnp.where(d == 0, 4.0, 0.0).astype(F32)
    last = jnp.where(d == 3, 4.0, 0.0).astype(F32)
    slab_up = pltpu.roll(up[8].astype(F32) + first, 32 - b, 0)[:24]
    slab_down = pltpu.roll(down[8].astype(F32) + last, 32 - b, 0)[:24]
    for r in range(32):
        codes[8 + r] = jnp.broadcast_to(slab[:, r : r + 1], (24, 128))
    for r in range(8):
        codes[r] = jnp.broadcast_to(slab_up[:, 24 + r : 25 + r], (24, 128))
        codes[40 + r] = jnp.broadcast_to(slab_down[:, r : r + 1], (24, 128))
    masks = head_masks()
    ones = block_ones()

    def band(wi, carry):
        rows = pl.multiple_of(wi * 192, 192)
        normed = []
        for wj in range(3):
            x = grid[pl.ds(a + 8 * wi, 8), 8 * wj : 8 * wj + 8, :].reshape(64, 512)
            xh, _ = normalise(x)
            normed.append((xh * gain[...]).astype(BF))
        qkv = dot(jnp.concatenate(normed, 0), w_qkv[...]).astype(BF)
        qkv_out[pl.ds(rows, 192), :] = qkv
        for wj in range(3):
            col = codes[pl.ds(a + 8 * wi, 8), 8 * wj : 8 * wj + 8, :].reshape(64, 128)
            row = col.T[0:1, 0:64]
            same = jnp.concatenate([col, col], 1) == jnp.concatenate([row] * 4, 1)
            win = qkv[64 * wj : 64 * wj + 64]
            for c in range(2):
                lo = 256 * c
                q = win[:, lo : lo + 256]
                kbig = spread(win[:, 512 + lo : 768 + lo], masks)
                vbig = spread(win[:, 1024 + lo : 1280 + lo], masks)
                e = jnp.where(same, jnp.exp(dot_nt(q, kbig) * 0.125), 0.0)
                total = dot(e.astype(BF), ones)
                p = (e / total).astype(BF)
                probs_out[pl.ds(rows + 64 * wj, 64), lo : lo + 256] = p
                mixed[64 * wj : 64 * wj + 64, lo : lo + 256] = dot(p, vbig).astype(BF)
        att = dot(mixed[...], w_proj[...]).astype(BF).astype(F32)
        for wj in range(3):
            back[pl.ds(8 * wi, 8), 8 * wj : 8 * wj + 8, :] = att[64 * wj : 64 * wj + 64].reshape(
                8, 8, 512
            )
        return carry

    lax.fori_loop(0, 5, band, 0)

    def finish(r, carry):
        moved = place_back(back, r, a, b)
        resid_out[r] = (own[r].astype(F32) + moved).astype(BF)
        return carry

    lax.fori_loop(0, 32, finish, 0, unroll=4)


VM = pl.BlockSpec(memory_space=pltpu.VMEM)
SM = pl.BlockSpec(memory_space=pltpu.SMEM)


def params(mib):
    return pltpu.CompilerParams(vmem_limit_bytes=mib * 2**20)


def attn_fwd(place, left, own, right, up, down, gain, w_qkv, w_proj):
    return pl.pallas_call(
        attn_fwd_kernel,
        out_shape=(
            jax.ShapeDtypeStruct((960, 1536), BF),
            jax.ShapeDtypeStruct((960, 512), BF),
            jax.ShapeDtypeStruct((32, 16, 512), BF),
        ),
        in_specs=[SM] + [VM] * 8,
        out_specs=(VM, VM, VM),
        scratch_shapes=[
            pltpu.VMEM((48, 24, 512), F32),
            pltpu.VMEM((48, 24, 128), F32),
            pltpu.VMEM((40, 24, 512), F32),
            pltpu.VMEM((192, 512), BF),
        ],
        compiler_params=params(40),
        cost_estimate=pl.CostEstimate(flops=2 * 10**9, bytes_accessed=10 * 2**20, transcendentals=10**6),
        name="attn_fwd",
    )(place, left, own, right, up, down, gain, w_qkv, w_proj)


def attn_bwd_kernel(
    place, left, own, right, up, down, qkv, probs, w_proj, w_qkv, tokens, gain,
    grad_out,
    grid, back, g_qkv,
):
    a, b = place[0], place[1]
    fill_grid(grid, b, left, own, right, up, down)
    masks = head_masks()
    ones = block_ones()

    def band(wi, carry):
        rows = pl.multiple_of(wi * 192, 192)
        ups = []
        for wj in range(3):
            x = grid[pl.ds(a + 8 * wi, 8), 8 * wj : 8 * wj + 8, :].reshape(64, 512)
            ups.append(x.astype(BF))
        g_mixed = dot_nt(jnp.concatenate(ups, 0), w_proj[...]).astype(BF)
        for wj in range(3):
            at = pl.ds(rows + 64 * wj, 64)
            for c in range(2):
                lo = 256 * c
                q = qkv[at, lo : lo + 256]
                kbig = spread(qkv[at, 512 + lo : 768 + lo], masks)
                vbig = spread(qkv[at, 1024 + lo : 1280 + lo], masks)
                p = probs[at, lo : lo + 256]
                g = g_mixed[64 * wj : 64 * wj + 64, lo : lo + 256]
                g_probs = dot_nt(g, vbig)
                wide_p = p.astype(F32)
                total = dot((wide_p * g_probs).astype(BF), ones)
                g_score = (wide_p * (g_probs - total) * 0.125).astype(BF)
                g_q = dot(g_score, kbig)
                g_k = collect(dot_tn(g_score, q), masks)
                g_v = collect(dot_tn(p, g), masks)
                out = slice(64 * wj, 64 * wj + 64)
                g_qkv[out, lo : lo + 256] = g_q.astype(BF)
                g_qkv[out, 512 + lo : 768 + lo] = g_k.astype(BF)
                g_qkv[out, 1024 + lo : 1280 + lo] = g_v.astype(BF)
        g_shift = dot_nt(g_qkv[...], w_qkv[...]).astype(BF).astype(F32)
        for wj in range(3):
            back[pl.ds(8 * wi, 8), 8 * wj : 8 * wj + 8, :] = g_shift[
                64 * wj : 64 * wj + 64
            ].reshape(8, 8, 512)
        return carry

    lax.fori_loop(0, 5, band, 0)

    def finish(r, carry):
        moved = place_back(back, r, a, b)
        part = norm_back(tokens[r].astype(F32), gain[...], moved)
        grad_out[r] = (own[r].astype(F32) + part).astype(BF)
        return carry

    lax.fori_loop(0, 32, finish, 0, unroll=4)


def attn_bwd(place, left, own, right, up, down, qkv, probs, w_proj, w_qkv, tokens, gain):
    return pl.pallas_call(
        attn_bwd_kernel,
        out_shape=jax.ShapeDtypeStruct((32, 16, 512), BF),
        in_specs=[SM] + [VM] * 11,
        out_specs=VM,
        scratch_shapes=[
            pltpu.VMEM((48, 24, 512), F32),
            pltpu.VMEM((40, 24, 512), F32),
            pltpu.VMEM((192, 1536), BF),
        ],
        compiler_params=params(40),
        cost_estimate=pl.CostEstimate(flops=4 * 10**9, bytes_accessed=10 * 2**20, transcendentals=0),
        name="attn_bwd",
    )(place, left, own, right, up, down, qkv, probs, w_proj, w_qkv, tokens, gain)


def set_fine(fine, value):
    for lane in range(4):
        fine[lane] = value[:, 128 * lane : 128 * lane + 128]


def get_fine(fine):
    return jnp.concatenate([fine[lane] for lane in range(4)], 1)


def patch_parts(fine):
    parts = {}
    for s in range(2):
        lanes = [fine[lane, pl.ds(s, 256, 2), :] for lane in range(4)]
        half = jnp.concatenate(lanes, 1).reshape(16, 2, 8, 512)
        for r in range(2):
            parts[r + 2 * s] = half[:, r].reshape(128, 512)
    return [parts[k] for k in range(4)]


def unpatch(fine, parts):
    for s in range(2):
        pair = [parts[r + 2 * s].reshape(16, 1, 8, 512) for r in range(2)]
        half = jnp.concatenate(pair, 1).reshape(256, 512)
        for lane in range(4):
            fine[lane, pl.ds(s, 256, 2), :] = half[:, 128 * lane : 128 * lane + 128]


def joint_normalise(parts):
    mean = sum(jnp.sum(p, -1, keepdims=True) for p in parts) / 2048.0
    cent = [p - mean for p in parts]
    var = sum(jnp.sum(c * c, -1, keepdims=True) for c in cent) / 2048.0
    r = lax.rsqrt(var + EPS)
    return [c * r for c in cent], r


def ffn_fwd_kernel(
    resid, gain_ffn, w_fc1, w_fc2, gain_merge, w_merge, gain_mlp,
    slope_out, block_out, coarse_out, cin_out,
    ffn_in, acc, merge_in, cacc, fine,
):
    n = pl.program_id(0)

    @pl.when(n == 0)
    def _():
        xh, _ = normalise(resid[...].astype(F32))
        ffn_in[...] = (xh * gain_ffn[...]).astype(BF)
        acc[...] = resid[...].astype(F32)

    @pl.when(n < 4)
    def _():
        for m in range(2):
            rows = slice(256 * m, 256 * m + 256)
            hid, slope = gelu_both(dot(ffn_in[rows, :], w_fc1[...]))
            slope_out[rows, :] = slope.astype(BF)
            acc[rows, :] += dot(hid.astype(BF), w_fc2[...])

    @pl.when(n == 3)
    def _():
        block = acc[...].astype(BF)
        block_out[...] = block
        set_fine(fine, block.astype(F32))
        xhs, _ = joint_normalise(patch_parts(fine))
        for k in range(4):
            merge_in[k] = (xhs[k] * gain_merge[:, 512 * k : 512 * k + 512]).astype(BF)
        cacc[...] = jnp.zeros_like(cacc)

    @pl.when(n >= 4)
    def _():
        cacc[...] += dot(merge_in[n - 4], w_merge[...])

    @pl.when(n == 7)
    def _():
        coarse = cacc[...].astype(BF)
        coarse_out[...] = coarse
        xh, _ = normalise(coarse.astype(F32))
        cin_out[...] = (xh * gain_mlp[...]).astype(BF)


def whole(shape):
    return pl.BlockSpec(shape, lambda n: (0,) * len(shape))


def ffn_fwd(resid, gain_ffn, w_fc1, w_fc2, gain_merge, w_merge, gain_mlp):
    early = lambda n: jnp.minimum(n, 3)
    late = lambda n: jnp.maximum(n - 4, 0)
    return pl.pallas_call(
        ffn_fwd_kernel,
        grid=(8,),
        out_shape=(
            jax.ShapeDtypeStruct((512, 2048), BF),
            jax.ShapeDtypeStruct((512, 512), BF),
            jax.ShapeDtypeStruct((128, 1024), BF),
            jax.ShapeDtypeStruct((128, 1024), BF),
        ),
        in_specs=[
            whole((512, 512)),
            whole((1, 512)),
            pl.BlockSpec((512, 512), lambda n: (0, early(n))),
            pl.BlockSpec((512, 512), lambda n: (early(n), 0)),
            whole((1, 2048)),
            pl.BlockSpec((512, 1024), lambda n: (late(n), 0)),
            whole((1, 1024)),
        ],
        out_specs=(
            pl.BlockSpec((512, 512), lambda n: (0, early(n))),
            whole((512, 512)),
            whole((128, 1024)),
            whole((128, 1024)),
        ),
        scratch_shapes=[
            pltpu.VMEM((512, 512), BF),
            pltpu.VMEM((512, 512), F32),
            pltpu.VMEM((4, 128, 512), BF),
            pltpu.VMEM((128, 1024), F32),
            pltpu.VMEM((4, 512, 128), F32),
        ],
        compiler_params=params(32),
        cost_estimate=pl.CostEstimate(flops=3 * 10**9, bytes_accessed=12 * 2**20, transcendentals=10**6),
        name="ffn_fwd",
    )(resid, gain_ffn, w_fc1, w_fc2, gain_merge, w_merge, gain_mlp)


def weight_chunk(parts, y, lo):
    blocks = [128 * k + lo for k in range(4)]
    if y < 3:
        rows = [parts[y][at : at + 64] for at in blocks]
    else:
        rows = [parts[3 + k // 2][blocks[k % 2] : blocks[k % 2] + 64] for k in range(4)]
    return jnp.concatenate(rows, 0)


def mlp_kernel(
    place, c0, c1, c2, c3, deep, w0, w1, w2, w3, w4,
    keep_out, send_out, hid_out,
    cs, gacc,
):
    me = place[2]
    spot = [pl.ds(pl.multiple_of(lax.bitwise_xor(me, k) * 128, 128), 128) for k in range(4)]
    for k, c in enumerate((c0, c1, c2, c3)):
        cs[spot[k]] = c[...]
    parts = (w0, w1, w2, w3, w4)
    for y in range(4):
        first = weight_chunk(parts, y, 0)
        second = weight_chunk(parts, y, 64)
        for m in range(2):
            rows = slice(256 * m, 256 * m + 256)
            hid, slope = gelu_both(dot_nt(cs[rows], first))
            hid_out[rows, 256 * y : 256 * y + 256] = hid.astype(BF)
            g_pre = (dot_nt(deep[rows], second) * slope).astype(BF)
            g_cin = dot(g_pre, first)
            if y == 0:
                gacc[rows] = g_cin
            else:
                gacc[rows] += g_cin
    keep_out[0:128] = gacc[spot[0]].astype(BF)
    keep_out[128:256] = gacc[spot[2]].astype(BF)
    send_out[0:128] = gacc[spot[1]].astype(BF)
    send_out[128:256] = gacc[spot[3]].astype(BF)


def coarse_mlp(place, cins, deep, parts):
    return pl.pallas_call(
        mlp_kernel,
        out_shape=(
            jax.ShapeDtypeStruct((256, 1024), BF),
            jax.ShapeDtypeStruct((256, 1024), BF),
            jax.ShapeDtypeStruct((512, 1024), BF),
        ),
        in_specs=[SM] + [VM] * 10,
        out_specs=(VM, VM, VM),
        scratch_shapes=[pltpu.VMEM((512, 1024), BF), pltpu.VMEM((512, 1024), F32)],
        compiler_params=params(32),
        cost_estimate=pl.CostEstimate(flops=3 * 10**9, bytes_accessed=8 * 2**20, transcendentals=10**6),
        name="coarse_mlp",
    )(place, *cins, deep, *parts)


def down_kernel(hid, w0, w1, w2, w3, w4, out):
    total = None
    for y in range(4):
        term = dot(hid[:, 256 * y : 256 * y + 256], weight_chunk((w0, w1, w2, w3, w4), y, 64))
        total = term if total is None else total + term
    out[...] = total.astype(BF)


def down_of(hid, parts):
    return pl.pallas_call(
        down_kernel,
        out_shape=jax.ShapeDtypeStruct((512, 1024), BF),
        in_specs=[VM] * 6,
        out_specs=VM,
        compiler_params=params(32),
        cost_estimate=pl.CostEstimate(flops=10**9, bytes_accessed=5 * 2**20, transcendentals=0),
        name="down",
    )(hid, *parts)


def g_deep_kernel(cot, w_up, out, fine, parts, acc):
    k = pl.program_id(0)

    @pl.when(k == 0)
    def _():
        set_fine(fine, cot[...].astype(F32))
        for i, part in enumerate(patch_parts(fine)):
            parts[i] = part.astype(BF)
        acc[...] = jnp.zeros_like(acc)

    acc[...] += dot_nt(parts[k], w_up[...])

    @pl.when(k == 3)
    def _():
        out[...] = acc[...].astype(BF)


def g_deep_of(cot, w_up):
    return pl.pallas_call(
        g_deep_kernel,
        grid=(4,),
        out_shape=jax.ShapeDtypeStruct((128, 1024), BF),
        in_specs=[whole((512, 512)), pl.BlockSpec((1024, 512), lambda k: (0, k))],
        out_specs=whole((128, 1024)),
        scratch_shapes=[
            pltpu.VMEM((4, 512, 128), F32),
            pltpu.VMEM((4, 128, 512), BF),
            pltpu.VMEM((128, 1024), F32),
        ],
        compiler_params=params(32),
        cost_estimate=pl.CostEstimate(flops=10**9, bytes_accessed=5 * 2**20, transcendentals=0),
        name="g_deep",
    )(cot, w_up)


def up_kernel(coarse, down, block, w_up, out, deep, ups, fine):
    k = pl.program_id(0)

    @pl.when(k == 0)
    def _():
        deep[...] = (coarse[...].astype(F32) + down[...].astype(F32)).astype(BF)

    ups[k] = dot(deep[...], w_up[...])

    @pl.when(k == 3)
    def _():
        unpatch(fine, [ups[i] for i in range(4)])
        out[...] = (block[...].astype(F32) + get_fine(fine)).astype(BF)


def up_of(coarse, down, block, w_up):
    return pl.pallas_call(
        up_kernel,
        grid=(4,),
        out_shape=jax.ShapeDtypeStruct((512, 512), BF),
        in_specs=[whole((128, 1024))] * 2
        + [whole((512, 512)), pl.BlockSpec((1024, 512), lambda k: (0, k))],
        out_specs=whole((512, 512)),
        scratch_shapes=[
            pltpu.VMEM((128, 1024), BF),
            pltpu.VMEM((4, 128, 512), F32),
            pltpu.VMEM((4, 512, 128), F32),
        ],
        compiler_params=params(32),
        cost_estimate=pl.CostEstimate(flops=10**9, bytes_accessed=5 * 2**20, transcendentals=0),
        name="up",
    )(coarse, down, block, w_up)


def ffn_bwd_kernel(
    gcin_own, gcin_near, gcin_far, g_deep, coarse, gain_mlp, w_merge, block, gain_merge, cot,
    w_fc2, slope, w_fc1, resid, gain_ffn,
    g_resid_out,
    g_coarse, g_mi, fine, g_block, acc,
):
    n = pl.program_id(0)

    @pl.when(n == 0)
    def _():
        g_cin = gcin_own[...].astype(F32) + gcin_near[...].astype(F32) + gcin_far[...].astype(F32)
        g_cin = g_cin.astype(BF).astype(F32)
        part = norm_back(coarse[...].astype(F32), gain_mlp[...], g_cin)
        g_coarse[...] = (g_deep[...].astype(F32) + part).astype(BF)

    @pl.when(n < 4)
    def _():
        g_mi[n] = dot_nt(g_coarse[...], w_merge[...])

    @pl.when(n == 3)
    def _():
        set_fine(fine, block[...].astype(F32))
        xhs, r = joint_normalise(patch_parts(fine))
        scaled = [g_mi[k] * gain_merge[:, 512 * k : 512 * k + 512] for k in range(4)]
        mean_s = sum(jnp.sum(s, -1, keepdims=True) for s in scaled) / 2048.0
        mean_x = sum(jnp.sum(s * x, -1, keepdims=True) for s, x in zip(scaled, xhs)) / 2048.0
        unpatch(fine, [r * (s - mean_s - x * mean_x) for s, x in zip(scaled, xhs)])
        g_block[...] = (cot[...].astype(F32) + get_fine(fine)).astype(BF)
        acc[...] = jnp.zeros_like(acc)

    @pl.when(n >= 4)
    def _():
        for m in range(2):
            rows = slice(256 * m, 256 * m + 256)
            g_hid = dot_nt(g_block[rows, :], w_fc2[...])
            g_pre = (g_hid * slope[rows, :].astype(F32)).astype(BF)
            acc[rows, :] += dot_nt(g_pre, w_fc1[...])

    @pl.when(n == 7)
    def _():
        g_fin = acc[...].astype(BF).astype(F32)
        part = norm_back(resid[...].astype(F32), gain_ffn[...], g_fin)
        g_resid_out[...] = (g_block[...].astype(F32) + part).astype(BF)


def ffn_bwd(gcin_own, gcin_near, gcin_far, g_deep, coarse, gain_mlp, w_merge, block, gain_merge, cot,
            w_fc2, slope, w_fc1, resid, gain_ffn):
    early = lambda n: jnp.minimum(n, 3)
    late = lambda n: jnp.maximum(n - 4, 0)
    return pl.pallas_call(
        ffn_bwd_kernel,
        grid=(8,),
        out_shape=jax.ShapeDtypeStruct((512, 512), BF),
        in_specs=[whole((128, 1024))] * 5
        + [
            whole((1, 1024)),
            pl.BlockSpec((512, 1024), lambda n: (early(n), 0)),
            whole((512, 512)),
            whole((1, 2048)),
            whole((512, 512)),
            pl.BlockSpec((512, 512), lambda n: (late(n), 0)),
            pl.BlockSpec((512, 512), lambda n: (0, late(n))),
            pl.BlockSpec((512, 512), lambda n: (0, late(n))),
            whole((512, 512)),
            whole((1, 512)),
        ],
        out_specs=whole((512, 512)),
        scratch_shapes=[
            pltpu.VMEM((128, 1024), BF),
            pltpu.VMEM((4, 128, 512), F32),
            pltpu.VMEM((4, 512, 128), F32),
            pltpu.VMEM((512, 512), BF),
            pltpu.VMEM((512, 512), F32),
        ],
        compiler_params=params(32),
        cost_estimate=pl.CostEstimate(flops=3 * 10**9, bytes_accessed=14 * 2**20, transcendentals=0),
        name="ffn_bwd",
    )(gcin_own, gcin_near, gcin_far, g_deep, coarse, gain_mlp, w_merge, block, gain_merge, cot,
      w_fc2, slope, w_fc1, resid, gain_ffn)


def along(axis, count, step):
    pairs = [(s, (s + step) % count) for s in range(count)]
    return lambda v: lax.ppermute(v, axis, pairs)


LAT_NEXT, LAT_PREV = along("lat", 4, 1), along("lat", 4, -1)
LON_NEXT, LON_PREV = along("lon", 32, 1), along("lon", 32, -1)


def core_swap(v):
    return lax.ppermute(v, "lat", [(0, 1), (1, 0), (2, 3), (3, 2)])


def x_swap(v):
    return lax.ppermute(v, "lat", [(0, 2), (2, 0), (1, 3), (3, 1)])


def x_far_swap(v):
    return lax.ppermute(v, "lon", [(k, (k + 16) % 32) for k in range(32)])


def turn(swapped, k):
    pairs = []
    for lat in range(4):
        along_y = (lat % 2 == 1) != swapped
        for lon in range(32):
            x, y, z = lon // 16, lon // 4 % 4, lon % 4
            if along_y:
                y = (y + k) % 4
            else:
                z = (z + k) % 4
            pairs.append((lat * 32 + lon, lat * 32 + (x * 4 + y) * 4 + z))
    return lambda v: lax.ppermute(v, ("lat", "lon"), pairs)


def after(value, *gates):
    return lax.optimization_barrier((value,) + gates)[0]


def on_device(
    tokens, labels, offsets, gain_attn, w_qkv, w_proj, gain_ffn, w_fc1, w_fc2,
    gain_merge, w_merge, gain_mlp, w_first, w_second, w_up, cotangent,
):
    row = lambda g: g.reshape(1, -1)
    place = jnp.concatenate([offsets, lax.axis_index("lat").astype(jnp.int32)[None]])
    slab = jnp.pad(labels.astype(BF).T, ((0, 0), (0, 512 - 32)))[None]
    own = jnp.concatenate([tokens, slab], 0)
    ends = lax.optimization_barrier((own[:, 8:], own[:, :8]))
    left, right = LON_NEXT(ends[0]), LON_PREV(ends[1])
    mine = lax.all_to_all(
        after(jnp.stack([w_first.T, w_second]), *ends), "lat", 1, 2, tiled=True
    )
    other = x_far_swap(mine)
    cot = after(cotangent.reshape(512, 512), mine)
    g_deep = g_deep_of(cot, w_up)
    deep_all = lax.all_gather(g_deep, "lat", axis=0, tiled=True)
    middle = after(own, g_deep)
    strip = lambda lo: jnp.concatenate(
        [
            jnp.concatenate([v[lo : lo + 8], v[32:33]], 0) for v in (left, middle, right)
        ],
        1,
    )
    up, down = LAT_NEXT(strip(24)), LAT_PREV(strip(0))
    seed = jnp.concatenate([mine[0], other[0], mine[1], other[1]], 0)
    seed = after(seed, up, down)
    moved = [turn(False, k)(seed) for k in (1, -1, 2)]
    qkv, probs, resid = attn_fwd(place, left, own, right, up, down, row(gain_attn), w_qkv, w_proj)
    resid = resid.reshape(512, 512)
    part = after(jnp.concatenate([seed] + moved, 0), resid)
    ahead, behind = turn(True, 1)(part), turn(True, -1)(part)
    slope, block, coarse, coarse_in = ffn_fwd(
        resid, row(gain_ffn), w_fc1, w_fc2, row(gain_merge), w_merge, row(gain_mlp)
    )
    far_cin = x_swap(coarse_in)
    near_cin = core_swap(coarse_in)
    parts = [
        part, ahead, behind,
        turn(True, 1)(after(ahead[:256], coarse_in)), turn(True, -1)(after(behind[256:], coarse_in)),
    ]
    cins = [coarse_in, near_cin, far_cin, core_swap(after(far_cin, ahead, behind))]
    keep, send, hid = coarse_mlp(place, cins, deep_all, parts)
    near = core_swap(send)
    gcin_far = x_swap((keep[128:].astype(F32) + near[128:].astype(F32)).astype(BF))
    down_all = down_of(hid, parts)
    down_sum = lax.psum_scatter(down_all, "lat", scatter_dimension=0, tiled=True)
    gcin_far = after(gcin_far, down_all)
    g_resid = ffn_bwd(
        keep, near, gcin_far, g_deep, coarse, row(gain_mlp), w_merge, block, row(gain_merge), cot,
        w_fc2, slope, w_fc1, resid, row(gain_ffn),
    ).reshape(32, 16, 512)
    g_left, g_right = LON_NEXT(g_resid[:, 8:]), LON_PREV(g_resid[:, :8])
    g_strip = lambda lo: jnp.concatenate(
        [v[lo : lo + 8] for v in (g_left, g_resid, g_right)], 1
    )
    g_up, g_down = LAT_NEXT(g_strip(24)), LAT_PREV(g_strip(0))
    field_out = up_of(coarse, down_sum, block, w_up).reshape(32, 16, 512)
    grad_in = attn_bwd(
        place, g_left, g_resid, g_right, g_up, g_down, qkv, probs, w_proj, w_qkv, tokens,
        row(gain_attn),
    )
    return (field_out, grad_in)


def solution(mesh):
    grid = P("lat", "lon", None)
    placed = (
        grid, P("lat", "lon"), P(), P(), P(), P(), P(), P(), P(), P(), P(), P(),
        P("lat", "lon"), P("lon", "lat"), P(), grid,
    )
    return jax.shard_map(
        on_device, mesh=mesh, in_specs=placed, out_specs=(grid, grid), check_vma=False
    )
```

```python
import jax
import jax.numpy as jnp
from jax import lax
from jax.experimental import pallas as pl
from jax.experimental.pallas import tpu as pltpu
from jax.sharding import PartitionSpec as P

BF = jnp.bfloat16
F32 = jnp.float32
EPS = 1e-05
NT = (((1,), (1,)), ((), ()))
TN = (((0,), (0,)), ((), ()))
GELU_C = 0.7978845608028654
GELU_A = 0.044715


def dot(a, b):
    return jnp.dot(a, b, preferred_element_type=F32)


def dot_nt(a, b):
    return lax.dot_general(a, b, NT, preferred_element_type=F32)


def dot_tn(a, b):
    return lax.dot_general(a, b, TN, preferred_element_type=F32)


def normalise(v):
    mean = jnp.mean(v, -1, keepdims=True)
    c = v - mean
    r = lax.rsqrt(jnp.mean(c * c, -1, keepdims=True) + EPS)
    return c * r, r


def norm_back(v, gain, t):
    xh, r = normalise(v)
    s = t * gain
    return r * (s - jnp.mean(s, -1, keepdims=True) - xh * jnp.mean(s * xh, -1, keepdims=True))


def gelu_both(wide):
    x = wide.astype(BF)
    x2 = x * x
    t = jnp.tanh(x * (GELU_C + GELU_C * GELU_A * x2))
    h = 0.5 * x
    slope = (0.5 + 0.5 * t) + (h - h * t * t) * (GELU_C + 3.0 * GELU_C * GELU_A * x2)
    return h + h * t, slope


def half_masks(scale):
    low = lax.broadcasted_iota(jnp.int32, (1, 128), 1) < 64
    return [jnp.where(m, scale, 0.0).astype(F32).astype(BF) for m in (low, jnp.logical_not(low))]


def spread(x, masks):
    none = jnp.zeros((64, 128), BF)
    left, right = x[:, :128], x[:, 128:]
    rows = [jnp.concatenate([left * m, none], 1) for m in masks]
    rows += [jnp.concatenate([none, right * m], 1) for m in masks]
    return jnp.concatenate(rows, 0)


def collect(big):
    low = lax.broadcasted_iota(jnp.int32, (64, 128), 1) < 64
    left = jnp.where(low, big[0:64, :128], big[64:128, :128])
    right = jnp.where(low, big[128:192, 128:], big[192:256, 128:])
    return jnp.concatenate([left, right], 1)


def fill_grid(grid, b, left, own, right, up, down):
    def rows(n, carry):
        at = pl.ds(8 * n, 8)
        line = jnp.concatenate(
            [left[at].astype(F32), own[at].astype(F32), right[at].astype(F32)], 1
        )
        grid[pl.ds(8 * n + 8, 8)] = pltpu.roll(line, 32 - b, 1)[:, :24]
        return carry

    lax.fori_loop(0, 4, rows, 0)
    grid[0:8] = pltpu.roll(up[0:8].astype(F32), 32 - b, 1)[:, :24]
    grid[40:48] = pltpu.roll(down[0:8].astype(F32), 32 - b, 1)[:, :24]


def place_back(back, n, a, b):
    return pltpu.roll(back[pl.ds(8 - a + 8 * n, 8)], 16 + b, 1)[:, :16]


def fetch(pairs, sems):
    copies = [pltpu.make_async_copy(src, dst, sems.at[k]) for k, (src, dst) in enumerate(pairs)]
    for copy in copies:
        copy.start()
    return copies


def window_of(grid, w, a):
    wi, wj = w // 3, w % 3
    return grid[pl.ds(a + 8 * wi, 8), 8 * wj : 8 * wj + 8, :].reshape(64, grid.shape[2])


def put_windows(back, n, value):
    for k in range(5):
        wi, wj = (5 * n + k) // 3, (5 * n + k) % 3
        back[8 * wi : 8 * wi + 8, 8 * wj : 8 * wj + 8, :] = value[64 * k : 64 * k + 64].reshape(
            8, 8, 512
        )


def attn_fwd_kernel(
    place, left, own, right, up, down, gain, w_qkv_hbm, w_proj_hbm,
    qkv_hbm, probs_hbm, resid_out,
    grid, codes, cols, back, mixed, qkv_out, probs_out, w_qkv, w_proj, sems,
):
    copies = fetch(((w_qkv_hbm, w_qkv), (w_proj_hbm, w_proj)), sems)
    qkv_copy = pltpu.make_async_copy(qkv_out, qkv_hbm, sems.at[2])
    probs_copy = pltpu.make_async_copy(probs_out, probs_hbm, sems.at[3])
    a, b, d = place[0], place[1], place[2]
    fill_grid(grid, b, left, own, right, up, down)
    slab = jnp.concatenate([v[32].astype(F32) for v in (left, own, right)], 0)
    slab = pltpu.roll(slab, 32 - b, 0)[:24]
    first = jnp.where(d == 0, 4.0, 0.0).astype(F32)
    last = jnp.where(d == 3, 4.0, 0.0).astype(F32)
    slab_up = pltpu.roll(up[8].astype(F32) + first, 32 - b, 0)[:24]
    slab_down = pltpu.roll(down[8].astype(F32) + last, 32 - b, 0)[:24]
    for r in range(32):
        codes[8 + r] = jnp.broadcast_to(slab[:, r : r + 1], (24, 128))
    for r in range(8):
        codes[r] = jnp.broadcast_to(slab_up[:, 24 + r : 25 + r], (24, 128))
        codes[40 + r] = jnp.broadcast_to(slab_down[:, r : r + 1], (24, 128))
    masks = half_masks(0.125)
    copies[0].wait()
    for n in range(3):
        normed = []
        for k in range(5):
            xh, _ = normalise(window_of(grid, 5 * n + k, a))
            normed.append((xh * gain[...]).astype(BF))
        qkv_out[320 * n : 320 * n + 320] = dot(jnp.concatenate(normed, 0), w_qkv[...]).astype(BF)
        for k in range(5):
            cols[5 * n + k] = window_of(codes, 5 * n + k, a)
    qkv_copy.start()

    def window(w, carry):
        at = pl.ds(pl.multiple_of(w * 64, 64), 64)
        col = cols[w]
        row = col.T[0:1, 0:64]
        same = jnp.concatenate([col, col], 1) == jnp.concatenate([row] * 4, 1)
        for c in range(2):
            lo = 256 * c
            qbig = spread(qkv_out[at, lo : lo + 256], masks)
            k = qkv_out[at, 512 + lo : 768 + lo]
            v = qkv_out[at, 1024 + lo : 1280 + lo]
            e = jnp.where(same, jnp.exp(dot_nt(k, qbig)), 0.0)
            p = (e * (1.0 / jnp.sum(e, 0, keepdims=True))).astype(BF)
            probs_out[at, lo : lo + 256] = p
            mixed[at, lo : lo + 256] = collect(dot_tn(p, v)).astype(BF)
        return carry

    lax.fori_loop(0, 15, window, 0, unroll=True)
    probs_copy.start()
    copies[1].wait()
    for n in range(3):
        att = dot(mixed[320 * n : 320 * n + 320], w_proj[...]).astype(BF).astype(F32)
        put_windows(back, n, att)

    def finish(n, carry):
        at = pl.ds(8 * n, 8)
        resid_out[at] = (own[at].astype(F32) + place_back(back, n, a, b)).astype(BF)
        return carry

    lax.fori_loop(0, 4, finish, 0, unroll=True)
    qkv_copy.wait()
    probs_copy.wait()


VM = pl.BlockSpec(memory_space=pltpu.VMEM)
SM = pl.BlockSpec(memory_space=pltpu.SMEM)
HB = pl.BlockSpec(memory_space=pltpu.HBM)


def params(mib):
    return pltpu.CompilerParams(vmem_limit_bytes=mib * 2**20)


def attn_fwd(place, left, own, right, up, down, gain, w_qkv, w_proj):
    return pl.pallas_call(
        attn_fwd_kernel,
        out_shape=(
            jax.ShapeDtypeStruct((960, 1536), BF),
            jax.ShapeDtypeStruct((960, 512), BF),
            jax.ShapeDtypeStruct((32, 16, 512), BF),
        ),
        in_specs=[SM] + [VM] * 6 + [HB] * 2,
        out_specs=(HB, HB, VM),
        scratch_shapes=[
            pltpu.VMEM((48, 24, 512), F32),
            pltpu.VMEM((48, 24, 128), F32),
            pltpu.VMEM((15, 64, 128), F32),
            pltpu.VMEM((40, 24, 512), F32),
            pltpu.VMEM((960, 512), BF),
            pltpu.VMEM((960, 1536), BF),
            pltpu.VMEM((960, 512), BF),
            pltpu.VMEM((512, 1536), BF),
            pltpu.VMEM((512, 512), BF),
            pltpu.SemaphoreType.DMA((4,)),
        ],
        compiler_params=params(32),
        cost_estimate=pl.CostEstimate(flops=2 * 10**9, bytes_accessed=10 * 2**20, transcendentals=10**6),
        name="attn_fwd",
    )(place, left, own, right, up, down, gain, w_qkv, w_proj)


def attn_bwd_kernel(
    place, left, own, right, up, down, qkv_hbm, probs_hbm, w_proj_hbm, w_qkv_hbm, tokens, gain,
    grad_out,
    grid, back, g_mixed, g_qkv, qkv, probs, w_proj, w_qkv, sems,
):
    pairs = ((w_proj_hbm, w_proj), (qkv_hbm, qkv), (probs_hbm, probs), (w_qkv_hbm, w_qkv))
    copies = fetch(pairs, sems)
    a, b = place[0], place[1]
    fill_grid(grid, b, left, own, right, up, down)
    masks, scaled = half_masks(1.0), half_masks(0.125)
    copies[0].wait()
    for n in range(3):
        ups = [window_of(grid, 5 * n + k, a).astype(BF) for k in range(5)]
        g_mixed[320 * n : 320 * n + 320] = dot_nt(jnp.concatenate(ups, 0), w_proj[...]).astype(BF)
    copies[1].wait()
    copies[2].wait()

    def window(w, carry):
        at = pl.ds(pl.multiple_of(w * 64, 64), 64)
        for c in range(2):
            lo = 256 * c
            qbig = spread(qkv[at, lo : lo + 256], scaled)
            gbig = spread(g_mixed[at, lo : lo + 256], masks)
            k = qkv[at, 512 + lo : 768 + lo]
            v = qkv[at, 1024 + lo : 1280 + lo]
            p = probs[at, lo : lo + 256]
            g_probs = dot_nt(v, gbig)
            wide_p = p.astype(F32)
            total = jnp.sum(wide_p * g_probs, 0, keepdims=True)
            g_score = (wide_p * (g_probs - total)).astype(BF)
            g_qkv[at, lo : lo + 256] = (collect(dot_tn(g_score, k)) * 0.125).astype(BF)
            g_qkv[at, 512 + lo : 768 + lo] = dot(g_score, qbig).astype(BF)
            g_qkv[at, 1024 + lo : 1280 + lo] = dot(p, gbig).astype(BF)
        return carry

    lax.fori_loop(0, 15, window, 0, unroll=True)
    copies[3].wait()
    for n in range(3):
        g_shift = dot_nt(g_qkv[320 * n : 320 * n + 320], w_qkv[...]).astype(BF).astype(F32)
        put_windows(back, n, g_shift)

    def finish(n, carry):
        at = pl.ds(8 * n, 8)
        part = norm_back(tokens[at].astype(F32), gain[...], place_back(back, n, a, b))
        grad_out[at] = (own[at].astype(F32) + part).astype(BF)
        return carry

    lax.fori_loop(0, 4, finish, 0, unroll=True)


def attn_bwd(place, left, own, right, up, down, qkv, probs, w_proj, w_qkv, tokens, gain):
    return pl.pallas_call(
        attn_bwd_kernel,
        out_shape=jax.ShapeDtypeStruct((32, 16, 512), BF),
        in_specs=[SM] + [VM] * 5 + [HB] * 4 + [VM] * 2,
        out_specs=VM,
        scratch_shapes=[
            pltpu.VMEM((48, 24, 512), F32),
            pltpu.VMEM((40, 24, 512), F32),
            pltpu.VMEM((960, 512), BF),
            pltpu.VMEM((960, 1536), BF),
            pltpu.VMEM((960, 1536), BF),
            pltpu.VMEM((960, 512), BF),
            pltpu.VMEM((512, 512), BF),
            pltpu.VMEM((512, 1536), BF),
            pltpu.SemaphoreType.DMA((4,)),
        ],
        compiler_params=params(32),
        cost_estimate=pl.CostEstimate(flops=4 * 10**9, bytes_accessed=10 * 2**20, transcendentals=0),
        name="attn_bwd",
    )(place, left, own, right, up, down, qkv, probs, w_proj, w_qkv, tokens, gain)


def set_fine(fine, value):
    for lane in range(4):
        fine[lane] = value[:, 128 * lane : 128 * lane + 128]


def get_fine(fine):
    return jnp.concatenate([fine[lane] for lane in range(4)], 1)


def patch_parts(fine):
    parts = {}
    for s in range(2):
        lanes = [fine[lane, pl.ds(s, 256, 2), :] for lane in range(4)]
        half = jnp.concatenate(lanes, 1).reshape(16, 2, 8, 512)
        for r in range(2):
            parts[r + 2 * s] = half[:, r].reshape(128, 512)
    return [parts[k] for k in range(4)]


def unpatch(fine, parts):
    for s in range(2):
        pair = [parts[r + 2 * s].reshape(16, 1, 8, 512) for r in range(2)]
        half = jnp.concatenate(pair, 1).reshape(256, 512)
        for lane in range(4):
            fine[lane, pl.ds(s, 256, 2), :] = half[:, 128 * lane : 128 * lane + 128]


def joint_normalise(parts):
    mean = sum(jnp.sum(p, -1, keepdims=True) for p in parts) / 2048.0
    cent = [p - mean for p in parts]
    var = sum(jnp.sum(c * c, -1, keepdims=True) for c in cent) / 2048.0
    r = lax.rsqrt(var + EPS)
    return [c * r for c in cent], r


def ffn_fwd_kernel(
    resid, gain_ffn, fc1_hbm, fc2_hbm, gain_merge, merge_hbm, gain_mlp,
    slope_out, block_out, coarse_out, cin_out,
    acc, fine, w_fc1, w_fc2, w_merge, sems,
):
    pairs = []
    for n in range(4):
        cut = pl.ds(512 * n, 512)
        pairs += [(fc1_hbm.at[:, cut], w_fc1.at[:, cut]), (fc2_hbm.at[cut], w_fc2.at[cut])]
    pairs += [(merge_hbm.at[pl.ds(512 * k, 512)], w_merge.at[pl.ds(512 * k, 512)]) for k in range(4)]
    copies = fetch(pairs, sems)
    xh, _ = normalise(resid[...].astype(F32))
    ffn_in = (xh * gain_ffn[...]).astype(BF)
    for n in range(4):
        cut = slice(512 * n, 512 * n + 512)
        copies[2 * n].wait()
        copies[2 * n + 1].wait()
        for m in range(2):
            rows = slice(256 * m, 256 * m + 256)
            hid, slope = gelu_both(dot(ffn_in[rows], w_fc1[:, cut]))
            slope_out[rows, cut] = slope
            term = dot(hid, w_fc2[cut, :])
            if n == 0:
                acc[rows, :] = resid[rows, :].astype(F32) + term
            else:
                acc[rows, :] += term
    block = acc[...].astype(BF)
    block_out[...] = block
    set_fine(fine, block.astype(F32))
    xhs, _ = joint_normalise(patch_parts(fine))
    coarse = None
    for k in range(4):
        cut = slice(512 * k, 512 * k + 512)
        copies[8 + k].wait()
        term = dot((xhs[k] * gain_merge[:, cut]).astype(BF), w_merge[cut, :])
        coarse = term if coarse is None else coarse + term
    coarse = coarse.astype(BF)
    coarse_out[...] = coarse
    xh, _ = normalise(coarse.astype(F32))
    cin_out[...] = (xh * gain_mlp[...]).astype(BF)


def ffn_fwd(resid, gain_ffn, w_fc1, w_fc2, gain_merge, w_merge, gain_mlp):
    return pl.pallas_call(
        ffn_fwd_kernel,
        out_shape=(
            jax.ShapeDtypeStruct((512, 2048), BF),
            jax.ShapeDtypeStruct((512, 512), BF),
            jax.ShapeDtypeStruct((128, 1024), BF),
            jax.ShapeDtypeStruct((128, 1024), BF),
        ),
        in_specs=[VM, VM, HB, HB, VM, HB, VM],
        out_specs=(VM, VM, VM, VM),
        scratch_shapes=[
            pltpu.VMEM((512, 512), F32),
            pltpu.VMEM((4, 512, 128), F32),
            pltpu.VMEM((512, 2048), BF),
            pltpu.VMEM((2048, 512), BF),
            pltpu.VMEM((2048, 1024), BF),
            pltpu.SemaphoreType.DMA((12,)),
        ],
        compiler_params=params(32),
        cost_estimate=pl.CostEstimate(flops=3 * 10**9, bytes_accessed=12 * 2**20, transcendentals=10**6),
        name="ffn_fwd",
    )(resid, gain_ffn, w_fc1, w_fc2, gain_merge, w_merge, gain_mlp)


def weight_chunk(parts, y, lo):
    blocks = [128 * k + lo for k in range(4)]
    if y < 3:
        rows = [parts[y][at : at + 64] for at in blocks]
    else:
        rows = [parts[3 + k // 2][blocks[k % 2] : blocks[k % 2] + 64] for k in range(4)]
    return jnp.concatenate(rows, 0)


def mlp_kernel(
    place, c0, c1, c2, c3, deep, w0, w1, w2, w3, w4,
    keep_out, send_out, hid_out,
    cs, gacc,
):
    me = place[2]
    spot = [pl.ds(pl.multiple_of(lax.bitwise_xor(me, k) * 128, 128), 128) for k in range(4)]
    for k, c in enumerate((c0, c1, c2, c3)):
        cs[spot[k]] = c[...]
    parts = (w0, w1, w2, w3, w4)
    for y in range(4):
        first = weight_chunk(parts, y, 0)
        second = weight_chunk(parts, y, 64)
        for m in range(2):
            rows = slice(256 * m, 256 * m + 256)
            hid, slope = gelu_both(dot_nt(cs[rows], first))
            hid_out[rows, 256 * y : 256 * y + 256] = hid
            g_pre = dot_nt(deep[rows], second).astype(BF) * slope
            g_cin = dot(g_pre, first)
            if y == 0:
                gacc[rows] = g_cin
            else:
                gacc[rows] += g_cin
    keep_out[0:128] = gacc[spot[0]].astype(BF)
    keep_out[128:256] = gacc[spot[2]].astype(BF)
    send_out[0:128] = gacc[spot[1]].astype(BF)
    send_out[128:256] = gacc[spot[3]].astype(BF)


def coarse_mlp(place, cins, deep, parts):
    return pl.pallas_call(
        mlp_kernel,
        out_shape=(
            jax.ShapeDtypeStruct((256, 1024), BF),
            jax.ShapeDtypeStruct((256, 1024), BF),
            jax.ShapeDtypeStruct((512, 1024), BF),
        ),
        in_specs=[SM] + [VM] * 10,
        out_specs=(VM, VM, VM),
        scratch_shapes=[pltpu.VMEM((512, 1024), BF), pltpu.VMEM((512, 1024), F32)],
        compiler_params=params(32),
        cost_estimate=pl.CostEstimate(flops=3 * 10**9, bytes_accessed=8 * 2**20, transcendentals=10**6),
        name="coarse_mlp",
    )(place, *cins, deep, *parts)


def down_kernel(hid, w0, w1, w2, w3, w4, out):
    total = None
    for y in range(4):
        term = dot(hid[:, 256 * y : 256 * y + 256], weight_chunk((w0, w1, w2, w3, w4), y, 64))
        total = term if total is None else total + term
    out[...] = total.astype(BF)


def down_of(hid, parts):
    return pl.pallas_call(
        down_kernel,
        out_shape=jax.ShapeDtypeStruct((512, 1024), BF),
        in_specs=[VM] * 6,
        out_specs=VM,
        compiler_params=params(32),
        cost_estimate=pl.CostEstimate(flops=10**9, bytes_accessed=5 * 2**20, transcendentals=0),
        name="down",
    )(hid, *parts)


def g_deep_kernel(cot, up_hbm, out, fine, w_up, sems):
    cuts = [pl.ds(512 * k, 512) for k in range(4)]
    copies = fetch([(up_hbm.at[:, cut], w_up.at[:, cut]) for cut in cuts], sems)
    set_fine(fine, cot[...].astype(F32))
    acc = None
    for k, part in enumerate(patch_parts(fine)):
        copies[k].wait()
        term = dot_nt(part.astype(BF), w_up[:, 512 * k : 512 * k + 512])
        acc = term if acc is None else acc + term
    out[...] = acc.astype(BF)


UP_SCRATCH = [
    pltpu.VMEM((4, 512, 128), F32),
    pltpu.VMEM((1024, 2048), BF),
    pltpu.SemaphoreType.DMA((4,)),
]


def g_deep_of(cot, w_up):
    return pl.pallas_call(
        g_deep_kernel,
        out_shape=jax.ShapeDtypeStruct((128, 1024), BF),
        in_specs=[VM, HB],
        out_specs=VM,
        scratch_shapes=UP_SCRATCH,
        compiler_params=params(32),
        cost_estimate=pl.CostEstimate(flops=10**9, bytes_accessed=5 * 2**20, transcendentals=0),
        name="g_deep",
    )(cot, w_up)


def up_kernel(coarse, down, block, up_hbm, out, fine, w_up, sems):
    cuts = [pl.ds(512 * k, 512) for k in range(4)]
    copies = fetch([(up_hbm.at[:, cut], w_up.at[:, cut]) for cut in cuts], sems)
    deep = (coarse[...].astype(F32) + down[...].astype(F32)).astype(BF)
    parts = []
    for k in range(4):
        copies[k].wait()
        parts.append(dot(deep, w_up[:, 512 * k : 512 * k + 512]))
    unpatch(fine, parts)
    out[...] = (block[...].astype(F32) + get_fine(fine)).astype(BF)


def up_of(coarse, down, block, w_up):
    return pl.pallas_call(
        up_kernel,
        out_shape=jax.ShapeDtypeStruct((512, 512), BF),
        in_specs=[VM, VM, VM, HB],
        out_specs=VM,
        scratch_shapes=UP_SCRATCH,
        compiler_params=params(32),
        cost_estimate=pl.CostEstimate(flops=10**9, bytes_accessed=5 * 2**20, transcendentals=0),
        name="up",
    )(coarse, down, block, w_up)


def ffn_bwd_kernel(
    gcin_own, gcin_near, gcin_far, g_deep, coarse, gain_mlp, merge_hbm, block, gain_merge, cot,
    fc2_hbm, slope_hbm, fc1_hbm, resid, gain_ffn,
    g_resid_out,
    fine, acc, w_merge, w_fc1, w_fc2, slope, sems,
):
    pairs = [(merge_hbm.at[pl.ds(512 * k, 512)], w_merge.at[pl.ds(512 * k, 512)]) for k in range(4)]
    for n in range(4):
        cut = pl.ds(512 * n, 512)
        pairs += [
            (fc2_hbm.at[cut], w_fc2.at[cut]),
            (slope_hbm.at[:, cut], slope.at[:, cut]),
            (fc1_hbm.at[:, cut], w_fc1.at[:, cut]),
        ]
    copies = fetch(pairs, sems)
    g_cin = gcin_own[0:128].astype(F32) + gcin_near[0:128].astype(F32) + gcin_far[...].astype(F32)
    g_cin = g_cin.astype(BF).astype(F32)
    part = norm_back(coarse[...].astype(F32), gain_mlp[...], g_cin)
    g_coarse = (g_deep[...].astype(F32) + part).astype(BF)
    set_fine(fine, block[...].astype(F32))
    xhs, r = joint_normalise(patch_parts(fine))
    scaled = []
    for k in range(4):
        cut = slice(512 * k, 512 * k + 512)
        copies[k].wait()
        scaled.append(dot_nt(g_coarse, w_merge[cut, :]) * gain_merge[:, cut])
    mean_s = sum(jnp.sum(s, -1, keepdims=True) for s in scaled) / 2048.0
    mean_x = sum(jnp.sum(s * x, -1, keepdims=True) for s, x in zip(scaled, xhs)) / 2048.0
    unpatch(fine, [r * (s - mean_s - x * mean_x) for s, x in zip(scaled, xhs)])
    g_block = (cot[...].astype(F32) + get_fine(fine)).astype(BF)
    for n in range(4):
        cut = slice(512 * n, 512 * n + 512)
        for k in range(3):
            copies[4 + 3 * n + k].wait()
        for m in range(2):
            rows = slice(256 * m, 256 * m + 256)
            g_pre = dot_nt(g_block[rows], w_fc2[cut, :]).astype(BF) * slope[rows, cut]
            term = dot_nt(g_pre, w_fc1[:, cut])
            if n == 0:
                acc[rows, :] = term
            else:
                acc[rows, :] += term
    g_fin = acc[...].astype(BF).astype(F32)
    part = norm_back(resid[...].astype(F32), gain_ffn[...], g_fin)
    g_resid_out[...] = (g_block.astype(F32) + part).astype(BF)


def ffn_bwd(gcin_own, gcin_near, gcin_far, g_deep, coarse, gain_mlp, w_merge, block, gain_merge, cot,
            w_fc2, slope, w_fc1, resid, gain_ffn):
    return pl.pallas_call(
        ffn_bwd_kernel,
        out_shape=jax.ShapeDtypeStruct((512, 512), BF),
        in_specs=[VM] * 6 + [HB, VM, VM, VM, HB, HB, HB, VM, VM],
        out_specs=VM,
        scratch_shapes=[
            pltpu.VMEM((4, 512, 128), F32),
            pltpu.VMEM((512, 512), F32),
            pltpu.VMEM((2048, 1024), BF),
            pltpu.VMEM((512, 2048), BF),
            pltpu.VMEM((2048, 512), BF),
            pltpu.VMEM((512, 2048), BF),
            pltpu.SemaphoreType.DMA((16,)),
        ],
        compiler_params=params(32),
        cost_estimate=pl.CostEstimate(flops=3 * 10**9, bytes_accessed=14 * 2**20, transcendentals=0),
        name="ffn_bwd",
    )(gcin_own, gcin_near, gcin_far, g_deep, coarse, gain_mlp, w_merge, block, gain_merge, cot,
      w_fc2, slope, w_fc1, resid, gain_ffn)


def along(axis, count, step):
    pairs = [(s, (s + step) % count) for s in range(count)]
    return lambda v: lax.ppermute(v, axis, pairs)


LAT_NEXT, LAT_PREV = along("lat", 4, 1), along("lat", 4, -1)
LON_NEXT, LON_PREV = along("lon", 32, 1), along("lon", 32, -1)


def core_swap(v):
    return lax.ppermute(v, "lat", [(0, 1), (1, 0), (2, 3), (3, 2)])


def x_swap(v):
    return lax.ppermute(v, "lat", [(0, 2), (2, 0), (1, 3), (3, 1)])


def x_far_swap(v):
    return lax.ppermute(v, "lon", [(k, (k + 16) % 32) for k in range(32)])


def turn(swapped, k):
    pairs = []
    for lat in range(4):
        along_y = (lat % 2 == 1) != swapped
        for lon in range(32):
            x, y, z = lon // 16, lon // 4 % 4, lon % 4
            if along_y:
                y = (y + k) % 4
            else:
                z = (z + k) % 4
            pairs.append((lat * 32 + lon, lat * 32 + (x * 4 + y) * 4 + z))
    return lambda v: lax.ppermute(v, ("lat", "lon"), pairs)


def after(value, *gates):
    return lax.optimization_barrier((value,) + gates)[0]


def on_device(
    tokens, labels, offsets, gain_attn, w_qkv, w_proj, gain_ffn, w_fc1, w_fc2,
    gain_merge, w_merge, gain_mlp, w_first, w_second, w_up, cotangent,
):
    row = lambda g: g.reshape(1, -1)
    place = jnp.concatenate([offsets, lax.axis_index("lat").astype(jnp.int32)[None]])
    slab = jnp.pad(labels.astype(BF).T, ((0, 0), (0, 512 - 32)))[None]
    own = jnp.concatenate([tokens, slab], 0)
    ends = lax.optimization_barrier((own[:, 8:], own[:, :8]))
    left, right = LON_NEXT(ends[0]), LON_PREV(ends[1])
    mine = lax.all_to_all(
        after(jnp.stack([w_first.T, w_second]), *ends), "lat", 1, 2, tiled=True
    )
    other = x_far_swap(mine)
    cot = after(cotangent.reshape(512, 512), mine)
    g_deep = g_deep_of(cot, w_up)
    deep_all = lax.all_gather(g_deep, "lat", axis=0, tiled=True)
    middle = after(own, g_deep)
    strip = lambda lo: jnp.concatenate(
        [
            jnp.concatenate([v[lo : lo + 8], v[32:33]], 0) for v in (left, middle, right)
        ],
        1,
    )
    up, down = LAT_NEXT(strip(24)), LAT_PREV(strip(0))
    seed = jnp.concatenate([mine[0], other[0], mine[1], other[1]], 0)
    seed = after(seed, up, down)
    moved = [turn(False, k)(seed) for k in (1, -1, 2)]
    qkv, probs, resid = attn_fwd(place, left, own, right, up, down, row(gain_attn), w_qkv, w_proj)
    resid = resid.reshape(512, 512)
    part = after(jnp.concatenate([seed] + moved, 0), resid)
    ahead, behind = turn(True, 1)(part), turn(True, -1)(part)
    slope, block, coarse, coarse_in = ffn_fwd(
        resid, row(gain_ffn), w_fc1, w_fc2, row(gain_merge), w_merge, row(gain_mlp)
    )
    far_cin = x_swap(coarse_in)
    near_cin = core_swap(coarse_in)
    parts = [
        part, ahead, behind,
        turn(True, 1)(after(ahead[:256], coarse_in)), turn(True, -1)(after(behind[256:], coarse_in)),
    ]
    cins = [coarse_in, near_cin, far_cin, core_swap(after(far_cin, ahead, behind))]
    keep, send, hid = coarse_mlp(place, cins, deep_all, parts)
    near = core_swap(send)
    gcin_far = x_swap((keep[128:].astype(F32) + near[128:].astype(F32)).astype(BF))
    down_all = down_of(hid, parts)
    down_sum = lax.psum_scatter(down_all, "lat", scatter_dimension=0, tiled=True)
    gcin_far = after(gcin_far, down_all)
    g_resid = ffn_bwd(
        keep, near, gcin_far, g_deep, coarse, row(gain_mlp), w_merge, block, row(gain_merge), cot,
        w_fc2, slope, w_fc1, resid, row(gain_ffn),
    ).reshape(32, 16, 512)
    g_left, g_right = LON_NEXT(g_resid[:, 8:]), LON_PREV(g_resid[:, :8])
    field_out = up_of(coarse, down_sum, block, w_up).reshape(32, 16, 512)
    g_middle = after(g_resid, field_out)
    g_strip = lambda lo: jnp.concatenate(
        [v[lo : lo + 8] for v in (g_left, g_middle, g_right)], 1
    )
    g_up, g_down = LAT_NEXT(g_strip(24)), LAT_PREV(g_strip(0))
    grad_in = attn_bwd(
        place, g_left, g_resid, g_right, g_up, g_down, qkv, probs, w_proj, w_qkv, tokens,
        row(gain_attn),
    )
    return (field_out, grad_in)


def solution(mesh):
    grid = P("lat", "lon", None)
    placed = (
        grid, P("lat", "lon"), P(), P(), P(), P(), P(), P(), P(), P(), P(), P(),
        P("lat", "lon"), P("lon", "lat"), P(), grid,
    )
    return jax.shard_map(
        on_device, mesh=mesh, in_specs=placed, out_specs=(grid, grid), check_vma=False
    )
```

```python
import jax
import jax.numpy as jnp
from jax import lax
from jax.experimental import pallas as pl
from jax.experimental.pallas import tpu as pltpu
from jax.sharding import PartitionSpec as P

BF = jnp.bfloat16
F32 = jnp.float32
EPS = 1e-05
NT = (((1,), (1,)), ((), ()))
TN = (((0,), (0,)), ((), ()))
GELU_C = 0.7978845608028654
GELU_A = 0.044715


def dot(a, b):
    return jnp.dot(a, b, preferred_element_type=F32)


def dot_nt(a, b):
    return lax.dot_general(a, b, NT, preferred_element_type=F32)


def dot_tn(a, b):
    return lax.dot_general(a, b, TN, preferred_element_type=F32)


def normalise(v):
    mean = jnp.mean(v, -1, keepdims=True)
    c = v - mean
    r = lax.rsqrt(jnp.mean(c * c, -1, keepdims=True) + EPS)
    return c * r, r


def norm_back(v, gain, t):
    xh, r = normalise(v)
    s = t * gain
    return r * (s - jnp.mean(s, -1, keepdims=True) - xh * jnp.mean(s * xh, -1, keepdims=True))


def gelu_both(wide):
    x = wide.astype(BF)
    x2 = x * x
    t = jnp.tanh(x * (GELU_C + GELU_C * GELU_A * x2))
    h = 0.5 * x
    slope = (0.5 + 0.5 * t) + (h - h * t * t) * (GELU_C + 3.0 * GELU_C * GELU_A * x2)
    return h + h * t, slope


def half_masks(scale):
    low = lax.broadcasted_iota(jnp.int32, (1, 128), 1) < 64
    return [jnp.where(m, scale, 0.0).astype(F32).astype(BF) for m in (low, jnp.logical_not(low))]


def spread(x, masks):
    none = jnp.zeros((64, 128), BF)
    left, right = x[:, :128], x[:, 128:]
    rows = [jnp.concatenate([left * m, none], 1) for m in masks]
    rows += [jnp.concatenate([none, right * m], 1) for m in masks]
    return jnp.concatenate(rows, 0)


def collect(big):
    low = lax.broadcasted_iota(jnp.int32, (64, 128), 1) < 64
    left = jnp.where(low, big[0:64, :128], big[64:128, :128])
    right = jnp.where(low, big[128:192, 128:], big[192:256, 128:])
    return jnp.concatenate([left, right], 1)


def fill_grid(grid, b, left, own, right, up, down):
    def rows(n, carry):
        at = pl.ds(8 * n, 8)
        line = jnp.concatenate(
            [left[at].astype(F32), own[at].astype(F32), right[at].astype(F32)], 1
        )
        grid[pl.ds(8 * n + 8, 8)] = pltpu.roll(line, 32 - b, 1)[:, :24]
        return carry

    lax.fori_loop(0, 4, rows, 0)
    grid[0:8] = pltpu.roll(up[0:8].astype(F32), 32 - b, 1)[:, :24]
    grid[40:48] = pltpu.roll(down[0:8].astype(F32), 32 - b, 1)[:, :24]


def place_back(back, n, a, b):
    return pltpu.roll(back[pl.ds(8 - a + 8 * n, 8)], 16 + b, 1)[:, :16]


def fetch(pairs, sems):
    copies = [pltpu.make_async_copy(src, dst, sems.at[k]) for k, (src, dst) in enumerate(pairs)]
    for copy in copies:
        copy.start()
    return copies


def window_of(grid, w, a):
    wi, wj = w // 3, w % 3
    return grid[pl.ds(a + 8 * wi, 8), 8 * wj : 8 * wj + 8, :].reshape(64, grid.shape[2])


def put_windows(back, n, value):
    for k in range(5):
        wi, wj = (5 * n + k) // 3, (5 * n + k) % 3
        back[8 * wi : 8 * wi + 8, 8 * wj : 8 * wj + 8, :] = value[64 * k : 64 * k + 64].reshape(
            8, 8, 512
        )


def attn_fwd_kernel(
    place, left, own, right, own_slab, up, down, gain, w_qkv_hbm, w_proj_hbm,
    qkv_hbm, probs_hbm, resid_out,
    grid, codes, cols, back, mixed, qkv_out, probs_out, w_qkv, w_proj, sems,
):
    copies = fetch(((w_qkv_hbm, w_qkv), (w_proj_hbm, w_proj)), sems)
    qkv_copy = pltpu.make_async_copy(qkv_out, qkv_hbm, sems.at[2])
    probs_copy = pltpu.make_async_copy(probs_out, probs_hbm, sems.at[3])
    a, b, d = place[0], place[1], place[2]
    fill_grid(grid, b, left, own, right, up, down)
    slab = jnp.concatenate(
        [v.astype(F32) for v in (left[32], own_slab[...], right[32])], 0
    )
    slab = pltpu.roll(slab, 32 - b, 0)[:24]
    first = jnp.where(d == 0, 4.0, 0.0).astype(F32)
    last = jnp.where(d == 3, 4.0, 0.0).astype(F32)
    slab_up = pltpu.roll(up[8].astype(F32) + first, 32 - b, 0)[:24]
    slab_down = pltpu.roll(down[8].astype(F32) + last, 32 - b, 0)[:24]
    for r in range(32):
        codes[8 + r] = jnp.broadcast_to(slab[:, r : r + 1], (24, 128))
    for r in range(8):
        codes[r] = jnp.broadcast_to(slab_up[:, 24 + r : 25 + r], (24, 128))
        codes[40 + r] = jnp.broadcast_to(slab_down[:, r : r + 1], (24, 128))
    masks = half_masks(0.125)
    copies[0].wait()
    for n in range(3):
        normed = []
        for k in range(5):
            xh, _ = normalise(window_of(grid, 5 * n + k, a))
            normed.append((xh * gain[...]).astype(BF))
        qkv_out[320 * n : 320 * n + 320] = dot(jnp.concatenate(normed, 0), w_qkv[...]).astype(BF)
        for k in range(5):
            cols[5 * n + k] = window_of(codes, 5 * n + k, a)
    qkv_copy.start()

    def window(w, carry):
        at = pl.ds(pl.multiple_of(w * 64, 64), 64)
        col = cols[w]
        row = col.T[0:1, 0:64]
        same = jnp.concatenate([col, col], 1) == jnp.concatenate([row] * 4, 1)
        for c in range(2):
            lo = 256 * c
            qbig = spread(qkv_out[at, lo : lo + 256], masks)
            k = qkv_out[at, 512 + lo : 768 + lo]
            v = qkv_out[at, 1024 + lo : 1280 + lo]
            e = jnp.where(same, jnp.exp(dot_nt(k, qbig)), 0.0)
            p = (e * (1.0 / jnp.sum(e, 0, keepdims=True))).astype(BF)
            probs_out[at, lo : lo + 256] = p
            mixed[at, lo : lo + 256] = collect(dot_tn(p, v)).astype(BF)
        return carry

    lax.fori_loop(0, 15, window, 0, unroll=True)
    probs_copy.start()
    copies[1].wait()
    for n in range(3):
        att = dot(mixed[320 * n : 320 * n + 320], w_proj[...]).astype(BF).astype(F32)
        put_windows(back, n, att)

    def finish(n, carry):
        at = pl.ds(8 * n, 8)
        resid_out[at] = (own[at].astype(F32) + place_back(back, n, a, b)).astype(BF)
        return carry

    lax.fori_loop(0, 4, finish, 0, unroll=True)
    qkv_copy.wait()
    probs_copy.wait()


VM = pl.BlockSpec(memory_space=pltpu.VMEM)
SM = pl.BlockSpec(memory_space=pltpu.SMEM)
HB = pl.BlockSpec(memory_space=pltpu.HBM)


def params(mib):
    return pltpu.CompilerParams(vmem_limit_bytes=mib * 2**20)


def attn_fwd(place, left, own, right, slab, up, down, gain, w_qkv, w_proj):
    return pl.pallas_call(
        attn_fwd_kernel,
        out_shape=(
            jax.ShapeDtypeStruct((960, 1536), BF),
            jax.ShapeDtypeStruct((960, 512), BF),
            jax.ShapeDtypeStruct((32, 16, 512), BF),
        ),
        in_specs=[SM] + [VM] * 7 + [HB] * 2,
        out_specs=(HB, HB, VM),
        scratch_shapes=[
            pltpu.VMEM((48, 24, 512), F32),
            pltpu.VMEM((48, 24, 128), F32),
            pltpu.VMEM((15, 64, 128), F32),
            pltpu.VMEM((40, 24, 512), F32),
            pltpu.VMEM((960, 512), BF),
            pltpu.VMEM((960, 1536), BF),
            pltpu.VMEM((960, 512), BF),
            pltpu.VMEM((512, 1536), BF),
            pltpu.VMEM((512, 512), BF),
            pltpu.SemaphoreType.DMA((4,)),
        ],
        compiler_params=params(32),
        cost_estimate=pl.CostEstimate(flops=2 * 10**9, bytes_accessed=10 * 2**20, transcendentals=10**6),
        name="attn_fwd",
    )(place, left, own, right, slab, up, down, gain, w_qkv, w_proj)


def attn_bwd_kernel(
    place, left, own, right, up, down, qkv_hbm, probs_hbm, w_proj_hbm, w_qkv_hbm, tokens, gain,
    grad_out,
    grid, back, g_mixed, g_qkv, qkv, probs, w_proj, w_qkv, sems,
):
    pairs = ((w_proj_hbm, w_proj), (qkv_hbm, qkv), (probs_hbm, probs), (w_qkv_hbm, w_qkv))
    copies = fetch(pairs, sems)
    a, b = place[0], place[1]
    fill_grid(grid, b, left, own, right, up, down)
    masks, scaled = half_masks(1.0), half_masks(0.125)
    copies[0].wait()
    for n in range(3):
        ups = [window_of(grid, 5 * n + k, a).astype(BF) for k in range(5)]
        g_mixed[320 * n : 320 * n + 320] = dot_nt(jnp.concatenate(ups, 0), w_proj[...]).astype(BF)
    copies[1].wait()
    copies[2].wait()

    def window(w, carry):
        at = pl.ds(pl.multiple_of(w * 64, 64), 64)
        for c in range(2):
            lo = 256 * c
            qbig = spread(qkv[at, lo : lo + 256], scaled)
            gbig = spread(g_mixed[at, lo : lo + 256], masks)
            k = qkv[at, 512 + lo : 768 + lo]
            v = qkv[at, 1024 + lo : 1280 + lo]
            p = probs[at, lo : lo + 256]
            g_probs = dot_nt(v, gbig)
            wide_p = p.astype(F32)
            total = jnp.sum(wide_p * g_probs, 0, keepdims=True)
            g_score = (wide_p * (g_probs - total)).astype(BF)
            g_qkv[at, lo : lo + 256] = (collect(dot_tn(g_score, k)) * 0.125).astype(BF)
            g_qkv[at, 512 + lo : 768 + lo] = dot(g_score, qbig).astype(BF)
            g_qkv[at, 1024 + lo : 1280 + lo] = dot(p, gbig).astype(BF)
        return carry

    lax.fori_loop(0, 15, window, 0, unroll=True)
    copies[3].wait()
    for n in range(3):
        g_shift = dot_nt(g_qkv[320 * n : 320 * n + 320], w_qkv[...]).astype(BF).astype(F32)
        put_windows(back, n, g_shift)

    def finish(n, carry):
        at = pl.ds(8 * n, 8)
        part = norm_back(tokens[at].astype(F32), gain[...], place_back(back, n, a, b))
        grad_out[at] = (own[at].astype(F32) + part).astype(BF)
        return carry

    lax.fori_loop(0, 4, finish, 0, unroll=True)


def attn_bwd(place, left, own, right, up, down, qkv, probs, w_proj, w_qkv, tokens, gain):
    return pl.pallas_call(
        attn_bwd_kernel,
        out_shape=jax.ShapeDtypeStruct((32, 16, 512), BF),
        in_specs=[SM] + [VM] * 5 + [HB] * 4 + [VM] * 2,
        out_specs=VM,
        scratch_shapes=[
            pltpu.VMEM((48, 24, 512), F32),
            pltpu.VMEM((40, 24, 512), F32),
            pltpu.VMEM((960, 512), BF),
            pltpu.VMEM((960, 1536), BF),
            pltpu.VMEM((960, 1536), BF),
            pltpu.VMEM((960, 512), BF),
            pltpu.VMEM((512, 512), BF),
            pltpu.VMEM((512, 1536), BF),
            pltpu.SemaphoreType.DMA((4,)),
        ],
        compiler_params=params(32),
        cost_estimate=pl.CostEstimate(flops=4 * 10**9, bytes_accessed=10 * 2**20, transcendentals=0),
        name="attn_bwd",
    )(place, left, own, right, up, down, qkv, probs, w_proj, w_qkv, tokens, gain)


def set_fine(fine, value):
    for lane in range(4):
        fine[lane] = value[:, 128 * lane : 128 * lane + 128]


def get_fine(fine):
    return jnp.concatenate([fine[lane] for lane in range(4)], 1)


def patch_parts(fine):
    parts = {}
    for s in range(2):
        lanes = [fine[lane, pl.ds(s, 256, 2), :] for lane in range(4)]
        half = jnp.concatenate(lanes, 1).reshape(16, 2, 8, 512)
        for r in range(2):
            parts[r + 2 * s] = half[:, r].reshape(128, 512)
    return [parts[k] for k in range(4)]


def unpatch(fine, parts):
    for s in range(2):
        pair = [parts[r + 2 * s].reshape(16, 1, 8, 512) for r in range(2)]
        half = jnp.concatenate(pair, 1).reshape(256, 512)
        for lane in range(4):
            fine[lane, pl.ds(s, 256, 2), :] = half[:, 128 * lane : 128 * lane + 128]


def joint_normalise(parts):
    mean = sum(jnp.sum(p, -1, keepdims=True) for p in parts) / 2048.0
    cent = [p - mean for p in parts]
    var = sum(jnp.sum(c * c, -1, keepdims=True) for c in cent) / 2048.0
    r = lax.rsqrt(var + EPS)
    return [c * r for c in cent], r


def ffn_fwd_kernel(
    resid, gain_ffn, fc1_hbm, fc2_hbm, gain_merge, merge_hbm, gain_mlp,
    slope_out, block_out, coarse_out, cin_out,
    acc, fine, w_fc1, w_fc2, w_merge, sems,
):
    pairs = []
    for n in range(4):
        cut = pl.ds(512 * n, 512)
        pairs += [(fc1_hbm.at[:, cut], w_fc1.at[:, cut]), (fc2_hbm.at[cut], w_fc2.at[cut])]
    pairs += [(merge_hbm.at[pl.ds(512 * k, 512)], w_merge.at[pl.ds(512 * k, 512)]) for k in range(4)]
    copies = fetch(pairs, sems)
    xh, _ = normalise(resid[...].astype(F32))
    ffn_in = (xh * gain_ffn[...]).astype(BF)
    for n in range(4):
        cut = slice(512 * n, 512 * n + 512)
        copies[2 * n].wait()
        copies[2 * n + 1].wait()
        for m in range(2):
            rows = slice(256 * m, 256 * m + 256)
            hid, slope = gelu_both(dot(ffn_in[rows], w_fc1[:, cut]))
            slope_out[rows, cut] = slope
            term = dot(hid, w_fc2[cut, :])
            if n == 0:
                acc[rows, :] = resid[rows, :].astype(F32) + term
            else:
                acc[rows, :] += term
    block = acc[...].astype(BF)
    block_out[...] = block
    set_fine(fine, block.astype(F32))
    xhs, _ = joint_normalise(patch_parts(fine))
    coarse = None
    for k in range(4):
        cut = slice(512 * k, 512 * k + 512)
        copies[8 + k].wait()
        term = dot((xhs[k] * gain_merge[:, cut]).astype(BF), w_merge[cut, :])
        coarse = term if coarse is None else coarse + term
    coarse = coarse.astype(BF)
    coarse_out[...] = coarse
    xh, _ = normalise(coarse.astype(F32))
    cin_out[...] = (xh * gain_mlp[...]).astype(BF)


def ffn_fwd(resid, gain_ffn, w_fc1, w_fc2, gain_merge, w_merge, gain_mlp):
    return pl.pallas_call(
        ffn_fwd_kernel,
        out_shape=(
            jax.ShapeDtypeStruct((512, 2048), BF),
            jax.ShapeDtypeStruct((512, 512), BF),
            jax.ShapeDtypeStruct((128, 1024), BF),
            jax.ShapeDtypeStruct((128, 1024), BF),
        ),
        in_specs=[VM, VM, HB, HB, VM, HB, VM],
        out_specs=(VM, VM, VM, VM),
        scratch_shapes=[
            pltpu.VMEM((512, 512), F32),
            pltpu.VMEM((4, 512, 128), F32),
            pltpu.VMEM((512, 2048), BF),
            pltpu.VMEM((2048, 512), BF),
            pltpu.VMEM((2048, 1024), BF),
            pltpu.SemaphoreType.DMA((12,)),
        ],
        compiler_params=params(32),
        cost_estimate=pl.CostEstimate(flops=3 * 10**9, bytes_accessed=12 * 2**20, transcendentals=10**6),
        name="ffn_fwd",
    )(resid, gain_ffn, w_fc1, w_fc2, gain_merge, w_merge, gain_mlp)


def weight_chunk(parts, y, lo):
    rows = []
    for k in range(4):
        ref, at = (parts[y], 128 * k) if y < 3 else (parts[3 + k // 2], 128 * (k % 2))
        rows += [ref[at + lo : at + lo + 32], ref[at + 64 + lo : at + 96 + lo]]
    return jnp.concatenate(rows, 0)


def mlp_kernel(
    place, c0, c1, c2, c3, d0, d1, d2, d3, w0, w1, w2, w3, w4,
    keep_out, send_out, hid_out,
    cs, deep, gacc,
):
    for k, (c, g) in enumerate(((c0, d0), (c1, d1), (c2, d2), (c3, d3))):
        cs[128 * k : 128 * k + 128] = c[...]
        deep[128 * k : 128 * k + 128] = g[...]
    parts = (w0, w1, w2, w3, w4)
    for y in range(4):
        first = weight_chunk(parts, y, 0)
        second = weight_chunk(parts, y, 32)
        for m in range(2):
            rows = slice(256 * m, 256 * m + 256)
            hid, slope = gelu_both(dot_nt(cs[rows], first))
            hid_out[rows, 256 * y : 256 * y + 256] = hid
            g_pre = dot_nt(deep[rows], second).astype(BF) * slope
            g_cin = dot(g_pre, first)
            if y == 0:
                gacc[rows] = g_cin
            else:
                gacc[rows] += g_cin
    part_out(gacc, keep_out, send_out)


def part_out(total, keep_out, send_out):
    keep_out[0:128] = total[0:128].astype(BF)
    keep_out[128:256] = total[256:384].astype(BF)
    send_out[0:128] = total[128:256].astype(BF)
    send_out[128:256] = total[384:512].astype(BF)


def coarse_mlp(place, cins, deeps, parts):
    return pl.pallas_call(
        mlp_kernel,
        out_shape=(
            jax.ShapeDtypeStruct((256, 1024), BF),
            jax.ShapeDtypeStruct((256, 1024), BF),
            jax.ShapeDtypeStruct((512, 1024), BF),
        ),
        in_specs=[SM] + [VM] * 13,
        out_specs=(VM, VM, VM),
        scratch_shapes=[
            pltpu.VMEM((512, 1024), BF),
            pltpu.VMEM((512, 1024), BF),
            pltpu.VMEM((512, 1024), F32),
        ],
        compiler_params=params(32),
        cost_estimate=pl.CostEstimate(flops=3 * 10**9, bytes_accessed=8 * 2**20, transcendentals=10**6),
        name="coarse_mlp",
    )(place, *cins, *deeps, *parts)


def down_kernel(hid, w0, w1, w2, w3, w4, keep_out, send_out):
    total = None
    for y in range(4):
        term = dot(hid[:, 256 * y : 256 * y + 256], weight_chunk((w0, w1, w2, w3, w4), y, 32))
        total = term if total is None else total + term
    part_out(total, keep_out, send_out)


def down_of(hid, parts):
    half = jax.ShapeDtypeStruct((256, 1024), BF)
    return pl.pallas_call(
        down_kernel,
        out_shape=(half, half),
        in_specs=[VM] * 6,
        out_specs=(VM, VM),
        compiler_params=params(32),
        cost_estimate=pl.CostEstimate(flops=10**9, bytes_accessed=5 * 2**20, transcendentals=0),
        name="down",
    )(hid, *parts)


def g_deep_kernel(cot, up_hbm, out, fine, w_up, sems):
    cuts = [pl.ds(512 * k, 512) for k in range(4)]
    copies = fetch([(up_hbm.at[:, cut], w_up.at[:, cut]) for cut in cuts], sems)
    set_fine(fine, cot[...].astype(F32))
    acc = None
    for k, part in enumerate(patch_parts(fine)):
        copies[k].wait()
        term = dot_nt(part.astype(BF), w_up[:, 512 * k : 512 * k + 512])
        acc = term if acc is None else acc + term
    out[...] = acc.astype(BF)


UP_SCRATCH = [
    pltpu.VMEM((4, 512, 128), F32),
    pltpu.VMEM((1024, 2048), BF),
    pltpu.SemaphoreType.DMA((4,)),
]


def g_deep_of(cot, w_up):
    return pl.pallas_call(
        g_deep_kernel,
        out_shape=jax.ShapeDtypeStruct((128, 1024), BF),
        in_specs=[VM, HB],
        out_specs=VM,
        scratch_shapes=UP_SCRATCH,
        compiler_params=params(32),
        cost_estimate=pl.CostEstimate(flops=10**9, bytes_accessed=5 * 2**20, transcendentals=0),
        name="g_deep",
    )(cot, w_up)


def up_kernel(coarse, keep, near, far, block, up_hbm, out, fine, w_up, sems):
    cuts = [pl.ds(512 * k, 512) for k in range(4)]
    copies = fetch([(up_hbm.at[:, cut], w_up.at[:, cut]) for cut in cuts], sems)
    deep = coarse[...].astype(F32) + keep[0:128].astype(F32) + near[0:128].astype(F32)
    deep = (deep + far[...].astype(F32)).astype(BF)
    parts = []
    for k in range(4):
        copies[k].wait()
        parts.append(dot(deep, w_up[:, 512 * k : 512 * k + 512]))
    unpatch(fine, parts)
    out[...] = (block[...].astype(F32) + get_fine(fine)).astype(BF)


def up_of(coarse, keep, near, far, block, w_up):
    return pl.pallas_call(
        up_kernel,
        out_shape=jax.ShapeDtypeStruct((512, 512), BF),
        in_specs=[VM] * 5 + [HB],
        out_specs=VM,
        scratch_shapes=UP_SCRATCH,
        compiler_params=params(32),
        cost_estimate=pl.CostEstimate(flops=10**9, bytes_accessed=5 * 2**20, transcendentals=0),
        name="up",
    )(coarse, keep, near, far, block, w_up)


def ffn_bwd_kernel(
    gcin_own, gcin_near, gcin_far, g_deep, coarse, gain_mlp, merge_hbm, block, gain_merge, cot,
    fc2_hbm, slope_hbm, fc1_hbm, resid, gain_ffn,
    g_resid_out, head_out, tail_out,
    fine, acc, w_merge, w_fc1, w_fc2, slope, sems,
):
    pairs = [(merge_hbm.at[pl.ds(512 * k, 512)], w_merge.at[pl.ds(512 * k, 512)]) for k in range(4)]
    for n in range(4):
        cut = pl.ds(512 * n, 512)
        pairs += [
            (fc2_hbm.at[cut], w_fc2.at[cut]),
            (slope_hbm.at[:, cut], slope.at[:, cut]),
            (fc1_hbm.at[:, cut], w_fc1.at[:, cut]),
        ]
    copies = fetch(pairs, sems)
    g_cin = gcin_own[0:128].astype(F32) + gcin_near[0:128].astype(F32) + gcin_far[...].astype(F32)
    g_cin = g_cin.astype(BF).astype(F32)
    part = norm_back(coarse[...].astype(F32), gain_mlp[...], g_cin)
    g_coarse = (g_deep[...].astype(F32) + part).astype(BF)
    set_fine(fine, block[...].astype(F32))
    xhs, r = joint_normalise(patch_parts(fine))
    scaled = []
    for k in range(4):
        cut = slice(512 * k, 512 * k + 512)
        copies[k].wait()
        scaled.append(dot_nt(g_coarse, w_merge[cut, :]) * gain_merge[:, cut])
    mean_s = sum(jnp.sum(s, -1, keepdims=True) for s in scaled) / 2048.0
    mean_x = sum(jnp.sum(s * x, -1, keepdims=True) for s, x in zip(scaled, xhs)) / 2048.0
    unpatch(fine, [r * (s - mean_s - x * mean_x) for s, x in zip(scaled, xhs)])
    g_block = (cot[...].astype(F32) + get_fine(fine)).astype(BF)
    for n in range(4):
        cut = slice(512 * n, 512 * n + 512)
        for k in range(3):
            copies[4 + 3 * n + k].wait()
        for m in range(2):
            rows = slice(256 * m, 256 * m + 256)
            g_pre = dot_nt(g_block[rows], w_fc2[cut, :]).astype(BF) * slope[rows, cut]
            term = dot_nt(g_pre, w_fc1[:, cut])
            if n == 0:
                acc[rows, :] = term
            else:
                acc[rows, :] += term
    g_fin = acc[...].astype(BF).astype(F32)
    part = norm_back(resid[...].astype(F32), gain_ffn[...], g_fin)
    total = g_block.astype(F32) + part
    g_resid_out[...] = total.astype(BF)
    lines = total.reshape(32, 16, 512)
    head_out[...] = lines[:, :8].astype(BF)
    tail_out[...] = lines[:, 8:].astype(BF)


def ffn_bwd(gcin_own, gcin_near, gcin_far, g_deep, coarse, gain_mlp, w_merge, block, gain_merge, cot,
            w_fc2, slope, w_fc1, resid, gain_ffn):
    return pl.pallas_call(
        ffn_bwd_kernel,
        out_shape=(
            jax.ShapeDtypeStruct((512, 512), BF),
            jax.ShapeDtypeStruct((32, 8, 512), BF),
            jax.ShapeDtypeStruct((32, 8, 512), BF),
        ),
        in_specs=[VM] * 6 + [HB, VM, VM, VM, HB, HB, HB, VM, VM],
        out_specs=(VM, VM, VM),
        scratch_shapes=[
            pltpu.VMEM((4, 512, 128), F32),
            pltpu.VMEM((512, 512), F32),
            pltpu.VMEM((2048, 1024), BF),
            pltpu.VMEM((512, 2048), BF),
            pltpu.VMEM((2048, 512), BF),
            pltpu.VMEM((512, 2048), BF),
            pltpu.SemaphoreType.DMA((16,)),
        ],
        compiler_params=params(32),
        cost_estimate=pl.CostEstimate(flops=3 * 10**9, bytes_accessed=14 * 2**20, transcendentals=0),
        name="ffn_bwd",
    )(gcin_own, gcin_near, gcin_far, g_deep, coarse, gain_mlp, w_merge, block, gain_merge, cot,
      w_fc2, slope, w_fc1, resid, gain_ffn)


def prep_kernel(
    place, tokens, labels, w_first, w_second,
    head_out, tail_out, slab_out, s0, s1, s2, s3,
    both,
):
    me = place[2]
    turned = labels[...].astype(F32).T
    slab = jnp.concatenate([turned, jnp.zeros((16, 480), F32)], 1)
    slab_out[...] = slab.astype(BF)
    lines = tokens[...].astype(F32)
    head_out[0:32] = lines[:, :8].astype(BF)
    tail_out[0:32] = lines[:, 8:].astype(BF)
    head_out[32] = slab[:8].astype(BF)
    tail_out[32] = slab[8:].astype(BF)
    both[0] = w_first[...].astype(F32).T.astype(BF)
    both[1] = w_second[...]
    for k, out in enumerate((s0, s1, s2, s3)):
        rows = pl.ds(pl.multiple_of(lax.bitwise_xor(me, k) * 32, 32), 32)
        out[0:32] = both[0, rows, :]
        out[32:64] = both[1, rows, :]


def prep(place, tokens, labels, w_first, w_second):
    ends = jax.ShapeDtypeStruct((33, 8, 512), BF)
    block = jax.ShapeDtypeStruct((64, 256), BF)
    return pl.pallas_call(
        prep_kernel,
        out_shape=(ends, ends, jax.ShapeDtypeStruct((16, 512), BF), block, block, block, block),
        in_specs=[SM] + [VM] * 4,
        out_specs=(VM,) * 7,
        scratch_shapes=[pltpu.VMEM((2, 128, 256), BF)],
        compiler_params=params(32),
        cost_estimate=pl.CostEstimate(flops=10**6, bytes_accessed=2 * 2**20, transcendentals=0),
        name="prep",
    )(place, tokens, labels, w_first, w_second)


def join_kernel(place, s0, s1, s2, s3, out):
    for k, block in enumerate((s0, s1, s2, s3)):
        at = pl.multiple_of(lax.bitwise_xor(place[2], k) * 256, 256)
        out[:, pl.ds(at, 256)] = block[...]


def join(place, blocks):
    return pl.pallas_call(
        join_kernel,
        out_shape=jax.ShapeDtypeStruct((64, 1024), BF),
        in_specs=[SM] + [VM] * 4,
        out_specs=VM,
        compiler_params=params(32),
        cost_estimate=pl.CostEstimate(flops=10**6, bytes_accessed=2**18, transcendentals=0),
        name="join",
    )(place, *blocks)


def strips_kernel(left, own, right, *rest):
    top_out, bottom_out = rest[-2:]
    for out, lo in ((top_out, 0), (bottom_out, 24)):
        for ref, at, wide in ((left, 0, 8), (own, 8, 16), (right, 24, 8)):
            out[0:8, at : at + wide, :] = ref[lo : lo + 8]
        if len(rest) == 3:
            out[8] = jnp.concatenate([left[32], rest[0][...], right[32]], 0)


def strips(left, own, right, *slab):
    edge = jax.ShapeDtypeStruct((8 + len(slab), 32, 512), BF)
    return pl.pallas_call(
        strips_kernel,
        out_shape=(edge, edge),
        in_specs=[VM] * (3 + len(slab)),
        out_specs=(VM, VM),
        compiler_params=params(32),
        cost_estimate=pl.CostEstimate(flops=10**6, bytes_accessed=3 * 2**20, transcendentals=0),
        name="strips",
    )(left, own, right, *slab)


def along(axis, count, step):
    pairs = [(s, (s + step) % count) for s in range(count)]
    return lambda v: lax.ppermute(v, axis, pairs)


LAT_NEXT, LAT_PREV = along("lat", 4, 1), along("lat", 4, -1)
LON_NEXT, LON_PREV = along("lon", 32, 1), along("lon", 32, -1)


def core_swap(v):
    return lax.ppermute(v, "lat", [(0, 1), (1, 0), (2, 3), (3, 2)])


def x_swap(v):
    return lax.ppermute(v, "lat", [(0, 2), (2, 0), (1, 3), (3, 1)])


def cross_swap(v):
    return lax.ppermute(v, "lat", [(0, 3), (3, 0), (1, 2), (2, 1)])


def x_far_swap(v):
    return lax.ppermute(v, "lon", [(k, (k + 16) % 32) for k in range(32)])


def turn(swapped, k):
    pairs = []
    for lat in range(4):
        along_y = (lat % 2 == 1) != swapped
        for lon in range(32):
            x, y, z = lon // 16, lon // 4 % 4, lon % 4
            if along_y:
                y = (y + k) % 4
            else:
                z = (z + k) % 4
            pairs.append((lat * 32 + lon, lat * 32 + (x * 4 + y) * 4 + z))
    return lambda v: lax.ppermute(v, ("lat", "lon"), pairs)


def after(value, *gates):
    return lax.optimization_barrier((value,) + gates)[0]


def on_device(
    tokens, labels, offsets, gain_attn, w_qkv, w_proj, gain_ffn, w_fc1, w_fc2,
    gain_merge, w_merge, gain_mlp, w_first, w_second, w_up, cotangent,
):
    row = lambda g: g.reshape(1, -1)
    place = jnp.concatenate([offsets, lax.axis_index("lat").astype(jnp.int32)[None]])
    head, tail, slab, s0, s1, s2, s3 = prep(place, tokens, labels, w_first, w_second)
    left, right = LON_NEXT(tail), LON_PREV(head)
    mine = join(place, (s0, core_swap(s1), x_swap(s2), cross_swap(s3)))
    other = x_far_swap(mine)
    cot = after(cotangent.reshape(512, 512), mine)
    g_deep = g_deep_of(cot, w_up)
    near_deep = core_swap(g_deep)
    bottom, top = strips(left, after(tokens, g_deep), right, slab)
    up, down = LAT_NEXT(top), LAT_PREV(bottom)
    seed = after(jnp.concatenate([mine, other], 0), up, down)
    moved = [turn(False, k)(seed) for k in (1, -1, 2)]
    qkv, probs, resid = attn_fwd(
        place, left, tokens, right, slab, up, down, row(gain_attn), w_qkv, w_proj
    )
    resid = resid.reshape(512, 512)
    part = after(jnp.concatenate([seed] + moved, 0), resid)
    ahead, behind = turn(True, 1)(part), turn(True, -1)(part)
    far_deep = x_swap(after(g_deep, resid))
    slope, block, coarse, coarse_in = ffn_fwd(
        resid, row(gain_ffn), w_fc1, w_fc2, row(gain_merge), w_merge, row(gain_mlp)
    )
    far_cin = x_swap(coarse_in)
    near_cin = core_swap(coarse_in)
    parts = [
        part, ahead, behind,
        turn(True, 1)(after(ahead[:256], coarse_in)), turn(True, -1)(after(behind[256:], coarse_in)),
    ]
    cins = [coarse_in, near_cin, far_cin, core_swap(after(far_cin, ahead, behind))]
    deeps = [g_deep, near_deep, far_deep, core_swap(after(far_deep, coarse_in))]
    keep, send, hid = coarse_mlp(place, cins, deeps, parts)
    near = core_swap(send)
    gcin_far = x_swap((keep[128:].astype(F32) + near[128:].astype(F32)).astype(BF))
    down_keep, down_send = down_of(hid, parts)
    down_near = core_swap(down_send)
    down_far = (down_keep[128:].astype(F32) + down_near[128:].astype(F32)).astype(BF)
    gcin_far, down_far = lax.optimization_barrier((gcin_far, down_far))
    down_far = x_swap(down_far)
    g_resid, g_head, g_tail = ffn_bwd(
        keep, near, gcin_far, g_deep, coarse, row(gain_mlp), w_merge, block, row(gain_merge), cot,
        w_fc2, slope, w_fc1, resid, row(gain_ffn),
    )
    g_resid = g_resid.reshape(32, 16, 512)
    g_left, g_right = LON_NEXT(g_tail), LON_PREV(g_head)
    field_out = up_of(coarse, down_keep, down_near, down_far, block, w_up).reshape(32, 16, 512)
    g_bottom, g_top = strips(g_left, after(g_resid, field_out), g_right)
    g_up, g_down = LAT_NEXT(g_top), LAT_PREV(g_bottom)
    grad_in = attn_bwd(
        place, g_left, g_resid, g_right, g_up, g_down, qkv, probs, w_proj, w_qkv, tokens,
        row(gain_attn),
    )
    return (field_out, grad_in)


def solution(mesh):
    grid = P("lat", "lon", None)
    placed = (
        grid, P("lat", "lon"), P(), P(), P(), P(), P(), P(), P(), P(), P(), P(),
        P("lat", "lon"), P("lon", "lat"), P(), grid,
    )
    return jax.shard_map(
        on_device, mesh=mesh, in_specs=placed, out_specs=(grid, grid), check_vma=False
    )
```

```python
import jax
import jax.numpy as jnp
from jax import lax
from jax.experimental import pallas as pl
from jax.experimental.pallas import tpu as pltpu
from jax.sharding import PartitionSpec as P

BF = jnp.bfloat16
F32 = jnp.float32
EPS = 1e-05
NT = (((1,), (1,)), ((), ()))
TN = (((0,), (0,)), ((), ()))
GELU_C = 0.7978845608028654
GELU_A = 0.044715


def dot(a, b):
    return jnp.dot(a, b, preferred_element_type=F32)


def dot_nt(a, b):
    return lax.dot_general(a, b, NT, preferred_element_type=F32)


def dot_tn(a, b):
    return lax.dot_general(a, b, TN, preferred_element_type=F32)


def normalise(v):
    mean = jnp.mean(v, -1, keepdims=True)
    c = v - mean
    r = lax.rsqrt(jnp.mean(c * c, -1, keepdims=True) + EPS)
    return c * r, r


def norm_back(v, gain, t):
    xh, r = normalise(v)
    s = t * gain
    return r * (s - jnp.mean(s, -1, keepdims=True) - xh * jnp.mean(s * xh, -1, keepdims=True))


def gelu_both(wide):
    x = wide.astype(BF)
    x2 = x * x
    t = jnp.tanh(x * (GELU_C + GELU_C * GELU_A * x2))
    h = 0.5 * x
    slope = (0.5 + 0.5 * t) + (h - h * t * t) * (GELU_C + 3.0 * GELU_C * GELU_A * x2)
    return h + h * t, slope


def half_masks(scale):
    low = lax.broadcasted_iota(jnp.int32, (1, 128), 1) < 64
    return [jnp.where(m, scale, 0.0).astype(F32).astype(BF) for m in (low, jnp.logical_not(low))]


def spread(x, masks):
    none = jnp.zeros((64, 128), BF)
    left, right = x[:, :128], x[:, 128:]
    rows = [jnp.concatenate([left * m, none], 1) for m in masks]
    rows += [jnp.concatenate([none, right * m], 1) for m in masks]
    return jnp.concatenate(rows, 0)


def collect(big):
    low = lax.broadcasted_iota(jnp.int32, (64, 128), 1) < 64
    left = jnp.where(low, big[0:64, :128], big[64:128, :128])
    right = jnp.where(low, big[128:192, 128:], big[192:256, 128:])
    return jnp.concatenate([left, right], 1)


def fill_grid(grid, b, left, own, right, up, down):
    def rows(n, carry):
        at = pl.ds(8 * n, 8)
        line = jnp.concatenate(
            [left[at].astype(F32), own[at].astype(F32), right[at].astype(F32)], 1
        )
        grid[pl.ds(8 * n + 8, 8)] = pltpu.roll(line, 32 - b, 1)[:, :24]
        return carry

    lax.fori_loop(0, 4, rows, 0)
    grid[0:8] = pltpu.roll(up[0:8].astype(F32), 32 - b, 1)[:, :24]
    grid[40:48] = pltpu.roll(down[0:8].astype(F32), 32 - b, 1)[:, :24]


def place_back(back, n, a, b):
    return pltpu.roll(back[pl.ds(8 - a + 8 * n, 8)], 16 + b, 1)[:, :16]


def fetch(pairs, sems):
    copies = [pltpu.make_async_copy(src, dst, sems.at[k]) for k, (src, dst) in enumerate(pairs)]
    for copy in copies:
        copy.start()
    return copies


def window_of(grid, w, a):
    wi, wj = w // 3, w % 3
    return grid[pl.ds(a + 8 * wi, 8), 8 * wj : 8 * wj + 8, :].reshape(64, grid.shape[2])


def put_windows(back, n, value):
    for k in range(5):
        wi, wj = (5 * n + k) // 3, (5 * n + k) % 3
        back[8 * wi : 8 * wi + 8, 8 * wj : 8 * wj + 8, :] = value[64 * k : 64 * k + 64].reshape(
            8, 8, 512
        )


def attn_fwd_kernel(
    place, left, own, right, own_slab, up, down, gain, w_qkv_hbm, w_proj_hbm,
    qkv_hbm, probs_hbm, resid_out,
    grid, codes, cols, back, mixed, qkv_out, probs_out, w_qkv, w_proj, sems,
):
    copies = fetch(((w_qkv_hbm, w_qkv), (w_proj_hbm, w_proj)), sems)
    qkv_copy = pltpu.make_async_copy(qkv_out, qkv_hbm, sems.at[2])
    probs_copy = pltpu.make_async_copy(probs_out, probs_hbm, sems.at[3])
    a, b, d = place[0], place[1], place[2]
    fill_grid(grid, b, left, own, right, up, down)
    slab = jnp.concatenate(
        [v.astype(F32) for v in (left[32], own_slab[...], right[32])], 0
    )
    slab = pltpu.roll(slab, 32 - b, 0)[:24]
    first = jnp.where(d == 0, 4.0, 0.0).astype(F32)
    last = jnp.where(d == 3, 4.0, 0.0).astype(F32)
    slab_up = pltpu.roll(up[8].astype(F32) + first, 32 - b, 0)[:24]
    slab_down = pltpu.roll(down[8].astype(F32) + last, 32 - b, 0)[:24]
    for r in range(32):
        codes[8 + r] = jnp.broadcast_to(slab[:, r : r + 1], (24, 128))
    for r in range(8):
        codes[r] = jnp.broadcast_to(slab_up[:, 24 + r : 25 + r], (24, 128))
        codes[40 + r] = jnp.broadcast_to(slab_down[:, r : r + 1], (24, 128))
    masks = half_masks(0.125)
    copies[0].wait()
    for n in range(3):
        normed = []
        for k in range(5):
            xh, _ = normalise(window_of(grid, 5 * n + k, a))
            normed.append((xh * gain[...]).astype(BF))
        qkv_out[320 * n : 320 * n + 320] = dot(jnp.concatenate(normed, 0), w_qkv[...]).astype(BF)
        for k in range(5):
            cols[5 * n + k] = window_of(codes, 5 * n + k, a)
    qkv_copy.start()

    def window(w, carry):
        at = pl.ds(pl.multiple_of(w * 64, 64), 64)
        col = cols[w]
        row = col.T[0:1, 0:64]
        same = jnp.concatenate([col, col], 1) == jnp.concatenate([row] * 4, 1)
        for c in range(2):
            lo = 256 * c
            qbig = spread(qkv_out[at, lo : lo + 256], masks)
            k = qkv_out[at, 512 + lo : 768 + lo]
            v = qkv_out[at, 1024 + lo : 1280 + lo]
            e = jnp.where(same, jnp.exp(dot_nt(k, qbig)), 0.0)
            p = (e * (1.0 / jnp.sum(e, 0, keepdims=True))).astype(BF)
            probs_out[at, lo : lo + 256] = p
            mixed[at, lo : lo + 256] = collect(dot_tn(p, v)).astype(BF)
        return carry

    lax.fori_loop(0, 15, window, 0, unroll=True)
    probs_copy.start()
    copies[1].wait()
    for n in range(3):
        att = dot(mixed[320 * n : 320 * n + 320], w_proj[...]).astype(BF).astype(F32)
        put_windows(back, n, att)

    def finish(n, carry):
        at = pl.ds(8 * n, 8)
        resid_out[at] = (own[at].astype(F32) + place_back(back, n, a, b)).astype(BF)
        return carry

    lax.fori_loop(0, 4, finish, 0, unroll=True)
    qkv_copy.wait()
    probs_copy.wait()


VM = pl.BlockSpec(memory_space=pltpu.VMEM)
SM = pl.BlockSpec(memory_space=pltpu.SMEM)
HB = pl.BlockSpec(memory_space=pltpu.HBM)


def params(mib):
    return pltpu.CompilerParams(vmem_limit_bytes=mib * 2**20)


def attn_fwd(place, left, own, right, slab, up, down, gain, w_qkv, w_proj):
    return pl.pallas_call(
        attn_fwd_kernel,
        out_shape=(
            jax.ShapeDtypeStruct((960, 1536), BF),
            jax.ShapeDtypeStruct((960, 512), BF),
            jax.ShapeDtypeStruct((32, 16, 512), BF),
        ),
        in_specs=[SM] + [VM] * 7 + [HB] * 2,
        out_specs=(HB, HB, VM),
        scratch_shapes=[
            pltpu.VMEM((48, 24, 512), F32),
            pltpu.VMEM((48, 24, 128), F32),
            pltpu.VMEM((15, 64, 128), F32),
            pltpu.VMEM((40, 24, 512), F32),
            pltpu.VMEM((960, 512), BF),
            pltpu.VMEM((960, 1536), BF),
            pltpu.VMEM((960, 512), BF),
            pltpu.VMEM((512, 1536), BF),
            pltpu.VMEM((512, 512), BF),
            pltpu.SemaphoreType.DMA((4,)),
        ],
        compiler_params=params(32),
        cost_estimate=pl.CostEstimate(flops=2 * 10**9, bytes_accessed=10 * 2**20, transcendentals=10**6),
        name="attn_fwd",
    )(place, left, own, right, slab, up, down, gain, w_qkv, w_proj)


def attn_bwd_kernel(
    place, left, own, right, up, down, qkv_hbm, probs_hbm, w_proj_hbm, w_qkv_hbm, tokens, gain,
    grad_out,
    grid, back, g_mixed, g_qkv, qkv, probs, w_proj, w_qkv, sems,
):
    pairs = ((w_proj_hbm, w_proj), (qkv_hbm, qkv), (probs_hbm, probs), (w_qkv_hbm, w_qkv))
    copies = fetch(pairs, sems)
    a, b = place[0], place[1]
    fill_grid(grid, b, left, own, right, up, down)
    masks, scaled = half_masks(1.0), half_masks(0.125)
    copies[0].wait()
    for n in range(3):
        ups = [window_of(grid, 5 * n + k, a).astype(BF) for k in range(5)]
        g_mixed[320 * n : 320 * n + 320] = dot_nt(jnp.concatenate(ups, 0), w_proj[...]).astype(BF)
    copies[1].wait()
    copies[2].wait()

    def window(w, carry):
        at = pl.ds(pl.multiple_of(w * 64, 64), 64)
        for c in range(2):
            lo = 256 * c
            qbig = spread(qkv[at, lo : lo + 256], scaled)
            gbig = spread(g_mixed[at, lo : lo + 256], masks)
            k = qkv[at, 512 + lo : 768 + lo]
            v = qkv[at, 1024 + lo : 1280 + lo]
            p = probs[at, lo : lo + 256]
            g_probs = dot_nt(v, gbig)
            wide_p = p.astype(F32)
            total = jnp.sum(wide_p * g_probs, 0, keepdims=True)
            g_score = (wide_p * (g_probs - total)).astype(BF)
            g_qkv[at, lo : lo + 256] = (collect(dot_tn(g_score, k)) * 0.125).astype(BF)
            g_qkv[at, 512 + lo : 768 + lo] = dot(g_score, qbig).astype(BF)
            g_qkv[at, 1024 + lo : 1280 + lo] = dot(p, gbig).astype(BF)
        return carry

    lax.fori_loop(0, 15, window, 0, unroll=True)
    copies[3].wait()
    for n in range(3):
        g_shift = dot_nt(g_qkv[320 * n : 320 * n + 320], w_qkv[...]).astype(BF).astype(F32)
        put_windows(back, n, g_shift)

    def finish(n, carry):
        at = pl.ds(8 * n, 8)
        part = norm_back(tokens[at].astype(F32), gain[...], place_back(back, n, a, b))
        grad_out[at] = (own[at].astype(F32) + part).astype(BF)
        return carry

    lax.fori_loop(0, 4, finish, 0, unroll=True)


def attn_bwd(place, left, own, right, up, down, qkv, probs, w_proj, w_qkv, tokens, gain):
    return pl.pallas_call(
        attn_bwd_kernel,
        out_shape=jax.ShapeDtypeStruct((32, 16, 512), BF),
        in_specs=[SM] + [VM] * 5 + [HB] * 4 + [VM] * 2,
        out_specs=VM,
        scratch_shapes=[
            pltpu.VMEM((48, 24, 512), F32),
            pltpu.VMEM((40, 24, 512), F32),
            pltpu.VMEM((960, 512), BF),
            pltpu.VMEM((960, 1536), BF),
            pltpu.VMEM((960, 1536), BF),
            pltpu.VMEM((960, 512), BF),
            pltpu.VMEM((512, 512), BF),
            pltpu.VMEM((512, 1536), BF),
            pltpu.SemaphoreType.DMA((4,)),
        ],
        compiler_params=params(32),
        cost_estimate=pl.CostEstimate(flops=4 * 10**9, bytes_accessed=10 * 2**20, transcendentals=0),
        name="attn_bwd",
    )(place, left, own, right, up, down, qkv, probs, w_proj, w_qkv, tokens, gain)


def set_fine(fine, value):
    for lane in range(4):
        fine[lane] = value[:, 128 * lane : 128 * lane + 128]


def get_fine(fine):
    return jnp.concatenate([fine[lane] for lane in range(4)], 1)


def patch_parts(fine):
    parts = {}
    for s in range(2):
        lanes = [fine[lane, pl.ds(s, 256, 2), :] for lane in range(4)]
        half = jnp.concatenate(lanes, 1).reshape(16, 2, 8, 512)
        for r in range(2):
            parts[r + 2 * s] = half[:, r].reshape(128, 512)
    return [parts[k] for k in range(4)]


def unpatch(fine, parts):
    for s in range(2):
        pair = [parts[r + 2 * s].reshape(16, 1, 8, 512) for r in range(2)]
        half = jnp.concatenate(pair, 1).reshape(256, 512)
        for lane in range(4):
            fine[lane, pl.ds(s, 256, 2), :] = half[:, 128 * lane : 128 * lane + 128]


def joint_normalise(parts):
    mean = sum(jnp.sum(p, -1, keepdims=True) for p in parts) / 2048.0
    cent = [p - mean for p in parts]
    var = sum(jnp.sum(c * c, -1, keepdims=True) for c in cent) / 2048.0
    r = lax.rsqrt(var + EPS)
    return [c * r for c in cent], r


def ffn_fwd_kernel(
    resid, gain_ffn, fc1_hbm, fc2_hbm, gain_merge, merge_hbm, gain_mlp,
    slope_out, block_out, coarse_out, cin_out,
    acc, fine, w_fc1, w_fc2, w_merge, sems,
):
    pairs = []
    for n in range(4):
        cut = pl.ds(512 * n, 512)
        pairs += [(fc1_hbm.at[:, cut], w_fc1.at[:, cut]), (fc2_hbm.at[cut], w_fc2.at[cut])]
    pairs += [(merge_hbm.at[pl.ds(512 * k, 512)], w_merge.at[pl.ds(512 * k, 512)]) for k in range(4)]
    copies = fetch(pairs, sems)
    xh, _ = normalise(resid[...].astype(F32))
    ffn_in = (xh * gain_ffn[...]).astype(BF)
    for n in range(4):
        cut = slice(512 * n, 512 * n + 512)
        copies[2 * n].wait()
        copies[2 * n + 1].wait()
        for m in range(2):
            rows = slice(256 * m, 256 * m + 256)
            hid, slope = gelu_both(dot(ffn_in[rows], w_fc1[:, cut]))
            slope_out[rows, cut] = slope
            term = dot(hid, w_fc2[cut, :])
            if n == 0:
                acc[rows, :] = resid[rows, :].astype(F32) + term
            else:
                acc[rows, :] += term
    block = acc[...].astype(BF)
    block_out[...] = block
    set_fine(fine, block.astype(F32))
    xhs, _ = joint_normalise(patch_parts(fine))
    coarse = None
    for k in range(4):
        cut = slice(512 * k, 512 * k + 512)
        copies[8 + k].wait()
        term = dot((xhs[k] * gain_merge[:, cut]).astype(BF), w_merge[cut, :])
        coarse = term if coarse is None else coarse + term
    coarse = coarse.astype(BF)
    coarse_out[...] = coarse
    xh, _ = normalise(coarse.astype(F32))
    cin_out[...] = (xh * gain_mlp[...]).astype(BF)


def ffn_fwd(resid, gain_ffn, w_fc1, w_fc2, gain_merge, w_merge, gain_mlp):
    return pl.pallas_call(
        ffn_fwd_kernel,
        out_shape=(
            jax.ShapeDtypeStruct((512, 2048), BF),
            jax.ShapeDtypeStruct((512, 512), BF),
            jax.ShapeDtypeStruct((128, 1024), BF),
            jax.ShapeDtypeStruct((128, 1024), BF),
        ),
        in_specs=[VM, VM, HB, HB, VM, HB, VM],
        out_specs=(VM, VM, VM, VM),
        scratch_shapes=[
            pltpu.VMEM((512, 512), F32),
            pltpu.VMEM((4, 512, 128), F32),
            pltpu.VMEM((512, 2048), BF),
            pltpu.VMEM((2048, 512), BF),
            pltpu.VMEM((2048, 1024), BF),
            pltpu.SemaphoreType.DMA((12,)),
        ],
        compiler_params=params(32),
        cost_estimate=pl.CostEstimate(flops=3 * 10**9, bytes_accessed=12 * 2**20, transcendentals=10**6),
        name="ffn_fwd",
    )(resid, gain_ffn, w_fc1, w_fc2, gain_merge, w_merge, gain_mlp)


def weight_chunk(parts, y, lo):
    rows = []
    for k in range(4):
        ref, at = (parts[y], 128 * k) if y < 3 else (parts[3 + k // 2], 128 * (k % 2))
        rows += [ref[at + lo : at + lo + 32], ref[at + 64 + lo : at + 96 + lo]]
    return jnp.concatenate(rows, 0)


def mlp_kernel(
    place, c0, c1, c2, c3, d0, d1, d2, d3, w0, w1, w2, w3, w4,
    keep_out, send_out, hid_out,
    cs, deep, gacc,
):
    for k, (c, g) in enumerate(((c0, d0), (c1, d1), (c2, d2), (c3, d3))):
        cs[128 * k : 128 * k + 128] = c[...]
        deep[128 * k : 128 * k + 128] = g[...]
    parts = (w0, w1, w2, w3, w4)
    for y in range(4):
        first = weight_chunk(parts, y, 0)
        second = weight_chunk(parts, y, 32)
        for m in range(2):
            rows = slice(256 * m, 256 * m + 256)
            hid, slope = gelu_both(dot_nt(cs[rows], first))
            hid_out[rows, 256 * y : 256 * y + 256] = hid
            g_pre = dot_nt(deep[rows], second).astype(BF) * slope
            g_cin = dot(g_pre, first)
            if y == 0:
                gacc[rows] = g_cin
            else:
                gacc[rows] += g_cin
    part_out(gacc, keep_out, send_out)


def part_out(total, keep_out, send_out):
    keep_out[0:128] = total[0:128].astype(BF)
    keep_out[128:256] = total[256:384].astype(BF)
    send_out[0:128] = total[128:256].astype(BF)
    send_out[128:256] = total[384:512].astype(BF)


def coarse_mlp(place, cins, deeps, parts):
    return pl.pallas_call(
        mlp_kernel,
        out_shape=(
            jax.ShapeDtypeStruct((256, 1024), BF),
            jax.ShapeDtypeStruct((256, 1024), BF),
            jax.ShapeDtypeStruct((512, 1024), BF),
        ),
        in_specs=[SM] + [VM] * 13,
        out_specs=(VM, VM, VM),
        scratch_shapes=[
            pltpu.VMEM((512, 1024), BF),
            pltpu.VMEM((512, 1024), BF),
            pltpu.VMEM((512, 1024), F32),
        ],
        compiler_params=params(32),
        cost_estimate=pl.CostEstimate(flops=3 * 10**9, bytes_accessed=8 * 2**20, transcendentals=10**6),
        name="coarse_mlp",
    )(place, *cins, *deeps, *parts)


def down_kernel(hid, w0, w1, w2, w3, w4, keep_out, send_out):
    total = None
    for y in range(4):
        term = dot(hid[:, 256 * y : 256 * y + 256], weight_chunk((w0, w1, w2, w3, w4), y, 32))
        total = term if total is None else total + term
    part_out(total, keep_out, send_out)


def down_of(hid, parts):
    half = jax.ShapeDtypeStruct((256, 1024), BF)
    return pl.pallas_call(
        down_kernel,
        out_shape=(half, half),
        in_specs=[VM] * 6,
        out_specs=(VM, VM),
        compiler_params=params(32),
        cost_estimate=pl.CostEstimate(flops=10**9, bytes_accessed=5 * 2**20, transcendentals=0),
        name="down",
    )(hid, *parts)


def g_deep_kernel(cot, up_hbm, out, fine, w_up, sems):
    cuts = [pl.ds(512 * k, 512) for k in range(4)]
    copies = fetch([(up_hbm.at[:, cut], w_up.at[:, cut]) for cut in cuts], sems)
    set_fine(fine, cot[...].astype(F32))
    acc = None
    for k, part in enumerate(patch_parts(fine)):
        copies[k].wait()
        term = dot_nt(part.astype(BF), w_up[:, 512 * k : 512 * k + 512])
        acc = term if acc is None else acc + term
    out[...] = acc.astype(BF)


UP_SCRATCH = [
    pltpu.VMEM((4, 512, 128), F32),
    pltpu.VMEM((1024, 2048), BF),
    pltpu.SemaphoreType.DMA((4,)),
]


def g_deep_of(cot, w_up):
    return pl.pallas_call(
        g_deep_kernel,
        out_shape=jax.ShapeDtypeStruct((128, 1024), BF),
        in_specs=[VM, HB],
        out_specs=VM,
        scratch_shapes=UP_SCRATCH,
        compiler_params=params(56),
        cost_estimate=pl.CostEstimate(flops=10**9, bytes_accessed=5 * 2**20, transcendentals=0),
        name="g_deep",
    )(cot, w_up)


def up_kernel(coarse, keep, near, far, block, up_hbm, out, fine, w_up, sems):
    cuts = [pl.ds(512 * k, 512) for k in range(4)]
    copies = fetch([(up_hbm.at[:, cut], w_up.at[:, cut]) for cut in cuts], sems)
    deep = coarse[...].astype(F32) + keep[0:128].astype(F32) + near[0:128].astype(F32)
    deep = (deep + far[...].astype(F32)).astype(BF)
    parts = []
    for k in range(4):
        copies[k].wait()
        parts.append(dot(deep, w_up[:, 512 * k : 512 * k + 512]))
    unpatch(fine, parts)
    out[...] = (block[...].astype(F32) + get_fine(fine)).astype(BF)


def up_of(coarse, keep, near, far, block, w_up):
    return pl.pallas_call(
        up_kernel,
        out_shape=jax.ShapeDtypeStruct((512, 512), BF),
        in_specs=[VM] * 5 + [HB],
        out_specs=VM,
        scratch_shapes=UP_SCRATCH,
        compiler_params=params(32),
        cost_estimate=pl.CostEstimate(flops=10**9, bytes_accessed=5 * 2**20, transcendentals=0),
        name="up",
    )(coarse, keep, near, far, block, w_up)


def ffn_bwd_kernel(
    gcin_own, gcin_near, gcin_far, g_deep, coarse, gain_mlp, merge_hbm, block, gain_merge, cot,
    fc2_hbm, slope_hbm, fc1_hbm, resid, gain_ffn,
    g_resid_out, head_out, tail_out,
    fine, acc, w_merge, w_fc1, w_fc2, slope, sems,
):
    pairs = [(merge_hbm.at[pl.ds(512 * k, 512)], w_merge.at[pl.ds(512 * k, 512)]) for k in range(4)]
    for n in range(4):
        cut = pl.ds(512 * n, 512)
        pairs += [
            (fc2_hbm.at[cut], w_fc2.at[cut]),
            (slope_hbm.at[:, cut], slope.at[:, cut]),
            (fc1_hbm.at[:, cut], w_fc1.at[:, cut]),
        ]
    copies = fetch(pairs, sems)
    g_cin = gcin_own[0:128].astype(F32) + gcin_near[0:128].astype(F32) + gcin_far[...].astype(F32)
    g_cin = g_cin.astype(BF).astype(F32)
    part = norm_back(coarse[...].astype(F32), gain_mlp[...], g_cin)
    g_coarse = (g_deep[...].astype(F32) + part).astype(BF)
    set_fine(fine, block[...].astype(F32))
    xhs, r = joint_normalise(patch_parts(fine))
    scaled = []
    for k in range(4):
        cut = slice(512 * k, 512 * k + 512)
        copies[k].wait()
        scaled.append(dot_nt(g_coarse, w_merge[cut, :]) * gain_merge[:, cut])
    mean_s = sum(jnp.sum(s, -1, keepdims=True) for s in scaled) / 2048.0
    mean_x = sum(jnp.sum(s * x, -1, keepdims=True) for s, x in zip(scaled, xhs)) / 2048.0
    unpatch(fine, [r * (s - mean_s - x * mean_x) for s, x in zip(scaled, xhs)])
    g_block = (cot[...].astype(F32) + get_fine(fine)).astype(BF)
    for n in range(4):
        cut = slice(512 * n, 512 * n + 512)
        for k in range(3):
            copies[4 + 3 * n + k].wait()
        for m in range(2):
            rows = slice(256 * m, 256 * m + 256)
            g_pre = dot_nt(g_block[rows], w_fc2[cut, :]).astype(BF) * slope[rows, cut]
            term = dot_nt(g_pre, w_fc1[:, cut])
            if n == 0:
                acc[rows, :] = term
            else:
                acc[rows, :] += term
    g_fin = acc[...].astype(BF).astype(F32)
    part = norm_back(resid[...].astype(F32), gain_ffn[...], g_fin)
    total = g_block.astype(F32) + part
    g_resid_out[...] = total.astype(BF)
    lines = total.reshape(32, 16, 512)
    head_out[...] = lines[:, :8].astype(BF)
    tail_out[...] = lines[:, 8:].astype(BF)


def ffn_bwd(gcin_own, gcin_near, gcin_far, g_deep, coarse, gain_mlp, w_merge, block, gain_merge, cot,
            w_fc2, slope, w_fc1, resid, gain_ffn):
    return pl.pallas_call(
        ffn_bwd_kernel,
        out_shape=(
            jax.ShapeDtypeStruct((512, 512), BF),
            jax.ShapeDtypeStruct((32, 8, 512), BF),
            jax.ShapeDtypeStruct((32, 8, 512), BF),
        ),
        in_specs=[VM] * 6 + [HB, VM, VM, VM, HB, HB, HB, VM, VM],
        out_specs=(VM, VM, VM),
        scratch_shapes=[
            pltpu.VMEM((4, 512, 128), F32),
            pltpu.VMEM((512, 512), F32),
            pltpu.VMEM((2048, 1024), BF),
            pltpu.VMEM((512, 2048), BF),
            pltpu.VMEM((2048, 512), BF),
            pltpu.VMEM((512, 2048), BF),
            pltpu.SemaphoreType.DMA((16,)),
        ],
        compiler_params=params(32),
        cost_estimate=pl.CostEstimate(flops=3 * 10**9, bytes_accessed=14 * 2**20, transcendentals=0),
        name="ffn_bwd",
    )(gcin_own, gcin_near, gcin_far, g_deep, coarse, gain_mlp, w_merge, block, gain_merge, cot,
      w_fc2, slope, w_fc1, resid, gain_ffn)


def prep_kernel(
    place, tokens, labels, w_first, w_second,
    head_out, tail_out, slab_out, s0, s1, s2, s3,
    both,
):
    me = place[2]
    turned = labels[...].astype(F32).T
    slab = jnp.concatenate([turned, jnp.zeros((16, 480), F32)], 1)
    slab_out[...] = slab.astype(BF)
    lines = tokens[...].astype(F32)
    head_out[0:32] = lines[:, :8].astype(BF)
    tail_out[0:32] = lines[:, 8:].astype(BF)
    head_out[32] = slab[:8].astype(BF)
    tail_out[32] = slab[8:].astype(BF)
    both[0] = w_first[...].astype(F32).T.astype(BF)
    both[1] = w_second[...]
    for k, out in enumerate((s0, s1, s2, s3)):
        rows = pl.ds(pl.multiple_of(lax.bitwise_xor(me, k) * 32, 32), 32)
        out[0:32] = both[0, rows, :]
        out[32:64] = both[1, rows, :]


def prep(place, tokens, labels, w_first, w_second):
    ends = jax.ShapeDtypeStruct((33, 8, 512), BF)
    block = jax.ShapeDtypeStruct((64, 256), BF)
    return pl.pallas_call(
        prep_kernel,
        out_shape=(ends, ends, jax.ShapeDtypeStruct((16, 512), BF), block, block, block, block),
        in_specs=[SM] + [VM] * 4,
        out_specs=(VM,) * 7,
        scratch_shapes=[pltpu.VMEM((2, 128, 256), BF)],
        compiler_params=params(60),
        cost_estimate=pl.CostEstimate(flops=10**6, bytes_accessed=2 * 2**20, transcendentals=0),
        name="prep",
    )(place, tokens, labels, w_first, w_second)


def join_kernel(place, s0, s1, s2, s3, out):
    for k, block in enumerate((s0, s1, s2, s3)):
        at = pl.multiple_of(lax.bitwise_xor(place[2], k) * 256, 256)
        out[:, pl.ds(at, 256)] = block[...]


def join(place, blocks):
    return pl.pallas_call(
        join_kernel,
        out_shape=jax.ShapeDtypeStruct((64, 1024), BF),
        in_specs=[SM] + [VM] * 4,
        out_specs=VM,
        compiler_params=params(32),
        cost_estimate=pl.CostEstimate(flops=10**6, bytes_accessed=2**18, transcendentals=0),
        name="join",
    )(place, *blocks)


def stack_kernel(*refs):
    for k, ref in enumerate(refs[:-1]):
        refs[-1][128 * k : 128 * k + 128] = ref[...]


def stacked(blocks):
    return pl.pallas_call(
        stack_kernel,
        out_shape=jax.ShapeDtypeStruct((512, 1024), BF),
        in_specs=[VM] * 4,
        out_specs=VM,
        compiler_params=params(32),
        cost_estimate=pl.CostEstimate(flops=10**6, bytes_accessed=2**21, transcendentals=0),
        name="stacked",
    )(*blocks)


def halves_kernel(ahead, behind, first, second):
    first[...] = ahead[0:256]
    second[...] = behind[256:512]


def halves(ahead, behind):
    half = jax.ShapeDtypeStruct((256, 1024), BF)
    return pl.pallas_call(
        halves_kernel,
        out_shape=(half, half),
        in_specs=[VM] * 2,
        out_specs=(VM, VM),
        compiler_params=params(32),
        cost_estimate=pl.CostEstimate(flops=10**6, bytes_accessed=2**21, transcendentals=0),
        name="halves",
    )(ahead, behind)


def strips_kernel(left, own, right, *rest):
    top_out, bottom_out = rest[-2:]
    for out, lo in ((top_out, 0), (bottom_out, 24)):
        for ref, at, wide in ((left, 0, 8), (own, 8, 16), (right, 24, 8)):
            out[0:8, at : at + wide, :] = ref[lo : lo + 8]
        if len(rest) == 3:
            out[8] = jnp.concatenate([left[32], rest[0][...], right[32]], 0)


def strips(left, own, right, *slab):
    edge = jax.ShapeDtypeStruct((8 + len(slab), 32, 512), BF)
    return pl.pallas_call(
        strips_kernel,
        out_shape=(edge, edge),
        in_specs=[VM] * (3 + len(slab)),
        out_specs=(VM, VM),
        compiler_params=params(32),
        cost_estimate=pl.CostEstimate(flops=10**6, bytes_accessed=3 * 2**20, transcendentals=0),
        name="strips",
    )(left, own, right, *slab)


def along(axis, count, step):
    pairs = [(s, (s + step) % count) for s in range(count)]
    return lambda v: lax.ppermute(v, axis, pairs)


LAT_NEXT, LAT_PREV = along("lat", 4, 1), along("lat", 4, -1)
LON_NEXT, LON_PREV = along("lon", 32, 1), along("lon", 32, -1)


def core_swap(v):
    return lax.ppermute(v, "lat", [(0, 1), (1, 0), (2, 3), (3, 2)])


def x_swap(v):
    return lax.ppermute(v, "lat", [(0, 2), (2, 0), (1, 3), (3, 1)])


def cross_swap(v):
    return lax.ppermute(v, "lat", [(0, 3), (3, 0), (1, 2), (2, 1)])


def x_far_swap(v):
    return lax.ppermute(v, "lon", [(k, (k + 16) % 32) for k in range(32)])


def turn(swapped, k):
    pairs = []
    for lat in range(4):
        along_y = (lat % 2 == 1) != swapped
        for lon in range(32):
            x, y, z = lon // 16, lon // 4 % 4, lon % 4
            if along_y:
                y = (y + k) % 4
            else:
                z = (z + k) % 4
            pairs.append((lat * 32 + lon, lat * 32 + (x * 4 + y) * 4 + z))
    return lambda v: lax.ppermute(v, ("lat", "lon"), pairs)


def after(value, *gates):
    return lax.optimization_barrier((value,) + gates)[0]


def on_device(
    tokens, labels, offsets, gain_attn, w_qkv, w_proj, gain_ffn, w_fc1, w_fc2,
    gain_merge, w_merge, gain_mlp, w_first, w_second, w_up, cotangent,
):
    row = lambda g: g.reshape(1, -1)
    place = jnp.concatenate([offsets, lax.axis_index("lat").astype(jnp.int32)[None]])
    head, tail, slab, s0, s1, s2, s3 = prep(place, tokens, labels, w_first, w_second)
    left, right = LON_NEXT(tail), LON_PREV(head)
    mine = join(place, (s0, core_swap(s1), x_swap(s2), cross_swap(s3)))
    other = x_far_swap(mine)
    bottom, top = strips(left, tokens, right, slab)
    up, down = LAT_NEXT(top), LAT_PREV(bottom)
    other = after(other, bottom, top)
    seed = jnp.concatenate([mine, other], 0)
    moved = [turn(False, k)(seed) for k in (1, -1, 2)]
    cot = cotangent.reshape(512, 512)
    g_deep = g_deep_of(after(cot, other, bottom, top), w_up)
    near_deep = core_swap(g_deep)
    part = stacked([after(seed, g_deep, up, down)] + moved)
    ahead, behind = turn(True, 1)(part), turn(True, -1)(part)
    qkv, probs, resid = attn_fwd(
        place, left, tokens, right, slab, after(up, part), down, row(gain_attn), w_qkv, w_proj
    )
    resid = resid.reshape(512, 512)
    far_deep = x_swap(after(g_deep, resid))
    slope, block, coarse, coarse_in = ffn_fwd(
        resid, row(gain_ffn), w_fc1, w_fc2, row(gain_merge), w_merge, row(gain_mlp)
    )
    far_cin = x_swap(coarse_in)
    near_cin = core_swap(coarse_in)
    first, second = halves(after(ahead, coarse_in), behind)
    parts = [part, ahead, behind, turn(True, 1)(first), turn(True, -1)(second)]
    cins = [coarse_in, near_cin, far_cin, core_swap(after(far_cin, first))]
    deeps = [g_deep, near_deep, far_deep, core_swap(after(far_deep, first))]
    keep, send, hid = coarse_mlp(place, cins, deeps, parts)
    near = core_swap(send)
    gcin_far = x_swap((keep[128:].astype(F32) + near[128:].astype(F32)).astype(BF))
    down_keep, down_send = down_of(hid, parts)
    down_near = core_swap(down_send)
    down_far = (down_keep[128:].astype(F32) + down_near[128:].astype(F32)).astype(BF)
    gcin_far, down_far = lax.optimization_barrier((gcin_far, down_far))
    down_far = x_swap(down_far)
    g_resid, g_head, g_tail = ffn_bwd(
        keep, near, gcin_far, g_deep, coarse, row(gain_mlp), w_merge, block, row(gain_merge), cot,
        w_fc2, slope, w_fc1, resid, row(gain_ffn),
    )
    g_resid = g_resid.reshape(32, 16, 512)
    g_left, g_right = LON_NEXT(g_tail), LON_PREV(g_head)
    field_out = up_of(coarse, down_keep, down_near, down_far, block, w_up).reshape(32, 16, 512)
    g_bottom, g_top = strips(g_left, after(g_resid, field_out), g_right)
    g_up, g_down = LAT_NEXT(g_top), LAT_PREV(g_bottom)
    grad_in = attn_bwd(
        place, g_left, g_resid, g_right, g_up, g_down, qkv, probs, w_proj, w_qkv, tokens,
        row(gain_attn),
    )
    return (field_out, grad_in)


def solution(mesh):
    grid = P("lat", "lon", None)
    placed = (
        grid, P("lat", "lon"), P(), P(), P(), P(), P(), P(), P(), P(), P(), P(),
        P("lat", "lon"), P("lon", "lat"), P(), grid,
    )
    return jax.shard_map(
        on_device, mesh=mesh, in_specs=placed, out_specs=(grid, grid), check_vma=False
    )
```

```python
import jax
import jax.numpy as jnp
from jax import lax
from jax.experimental import pallas as pl
from jax.experimental.pallas import tpu as pltpu
from jax.sharding import PartitionSpec as P

BF = jnp.bfloat16
F32 = jnp.float32
EPS = 1e-05
NT = (((1,), (1,)), ((), ()))
TN = (((0,), (0,)), ((), ()))
GELU_C = 0.7978845608028654
GELU_A = 0.044715


def dot(a, b):
    return jnp.dot(a, b, preferred_element_type=F32)


def dot_nt(a, b):
    return lax.dot_general(a, b, NT, preferred_element_type=F32)


def dot_tn(a, b):
    return lax.dot_general(a, b, TN, preferred_element_type=F32)


def normalise(v):
    mean = jnp.mean(v, -1, keepdims=True)
    c = v - mean
    r = lax.rsqrt(jnp.mean(c * c, -1, keepdims=True) + EPS)
    return c * r, r


def norm_back(v, gain, t):
    xh, r = normalise(v)
    s = t * gain
    return r * (s - jnp.mean(s, -1, keepdims=True) - xh * jnp.mean(s * xh, -1, keepdims=True))


def gelu_both(wide):
    x = wide.astype(BF)
    x2 = x * x
    t = jnp.tanh(x * (GELU_C + GELU_C * GELU_A * x2))
    h = 0.5 * x
    slope = (0.5 + 0.5 * t) + (h - h * t * t) * (GELU_C + 3.0 * GELU_C * GELU_A * x2)
    return h + h * t, slope


def half_masks(scale):
    low = lax.broadcasted_iota(jnp.int32, (1, 128), 1) < 64
    return [jnp.where(m, scale, 0.0).astype(F32).astype(BF) for m in (low, jnp.logical_not(low))]


def spread(x, masks):
    none = jnp.zeros((64, 128), BF)
    left, right = x[:, :128], x[:, 128:]
    rows = [jnp.concatenate([left * m, none], 1) for m in masks]
    rows += [jnp.concatenate([none, right * m], 1) for m in masks]
    return jnp.concatenate(rows, 0)


def collect(big):
    low = lax.broadcasted_iota(jnp.int32, (64, 128), 1) < 64
    left = jnp.where(low, big[0:64, :128], big[64:128, :128])
    right = jnp.where(low, big[128:192, 128:], big[192:256, 128:])
    return jnp.concatenate([left, right], 1)


def sides(odd, first, second):
    return jnp.where(odd, first, second), jnp.where(odd, second, first)


def fill_grid(grid, b, odd, first, own, second, up, down):
    def rows(n, carry):
        at = pl.ds(8 * n, 8)
        left, right = sides(odd, first[at].astype(F32), second[at].astype(F32))
        line = jnp.concatenate([left, own[at].astype(F32), right], 1)
        grid[pl.ds(8 * n + 8, 8)] = pltpu.roll(line, 32 - b, 1)[:, :24]
        return carry

    lax.fori_loop(0, 4, rows, 0)
    grid[0:8] = pltpu.roll(up[0:8].astype(F32), 32 - b, 1)[:, :24]
    grid[40:48] = pltpu.roll(down[0:8].astype(F32), 32 - b, 1)[:, :24]


def place_back(back, n, a, b):
    return pltpu.roll(back[pl.ds(8 - a + 8 * n, 8)], 16 + b, 1)[:, :16]


def fetch(pairs, sems):
    copies = [pltpu.make_async_copy(src, dst, sems.at[k]) for k, (src, dst) in enumerate(pairs)]
    for copy in copies:
        copy.start()
    return copies


def window_of(grid, w, a):
    wi, wj = w // 3, w % 3
    return grid[pl.ds(a + 8 * wi, 8), 8 * wj : 8 * wj + 8, :].reshape(64, grid.shape[2])


def put_windows(back, n, value):
    for k in range(5):
        wi, wj = (5 * n + k) // 3, (5 * n + k) % 3
        back[8 * wi : 8 * wi + 8, 8 * wj : 8 * wj + 8, :] = value[64 * k : 64 * k + 64].reshape(
            8, 8, 512
        )


def attn_fwd_kernel(
    place, first, own, second, own_slab, up, down, gain, w_qkv_hbm, w_proj_hbm,
    qkv_hbm, probs_hbm, resid_out,
    grid, codes, cols, back, mixed, qkv_out, probs_out, w_qkv, w_proj, sems,
):
    copies = fetch(((w_qkv_hbm, w_qkv), (w_proj_hbm, w_proj)), sems)
    qkv_copy = pltpu.make_async_copy(qkv_out, qkv_hbm, sems.at[2])
    probs_copy = pltpu.make_async_copy(probs_out, probs_hbm, sems.at[3])
    a, b, d = place[0], place[1], place[2]
    odd = place[3] == 1
    fill_grid(grid, b, odd, first, own, second, up, down)
    left, right = sides(odd, first[32].astype(F32), second[32].astype(F32))
    slab = jnp.concatenate([left, own_slab[...].astype(F32), right], 0)
    slab = pltpu.roll(slab, 32 - b, 0)[:24]
    top_code = jnp.where(d == 0, 4.0, 0.0).astype(F32)
    low_code = jnp.where(d == 3, 4.0, 0.0).astype(F32)
    slab_up = pltpu.roll(up[8].astype(F32) + top_code, 32 - b, 0)[:24]
    slab_down = pltpu.roll(down[8].astype(F32) + low_code, 32 - b, 0)[:24]
    for r in range(32):
        codes[8 + r] = jnp.broadcast_to(slab[:, r : r + 1], (24, 128))
    for r in range(8):
        codes[r] = jnp.broadcast_to(slab_up[:, 24 + r : 25 + r], (24, 128))
        codes[40 + r] = jnp.broadcast_to(slab_down[:, r : r + 1], (24, 128))
    masks = half_masks(0.125)
    copies[0].wait()
    for n in range(3):
        normed = []
        for k in range(5):
            xh, _ = normalise(window_of(grid, 5 * n + k, a))
            normed.append((xh * gain[...]).astype(BF))
        qkv_out[320 * n : 320 * n + 320] = dot(jnp.concatenate(normed, 0), w_qkv[...]).astype(BF)
        for k in range(5):
            cols[5 * n + k] = window_of(codes, 5 * n + k, a)
    qkv_copy.start()

    def window(w, carry):
        at = pl.ds(pl.multiple_of(w * 64, 64), 64)
        col = cols[w]
        row = col.T[0:1, 0:64]
        same = jnp.concatenate([col, col], 1) == jnp.concatenate([row] * 4, 1)
        for c in range(2):
            lo = 256 * c
            qbig = spread(qkv_out[at, lo : lo + 256], masks)
            k = qkv_out[at, 512 + lo : 768 + lo]
            v = qkv_out[at, 1024 + lo : 1280 + lo]
            e = jnp.where(same, jnp.exp(dot_nt(k, qbig)), 0.0)
            p = (e * (1.0 / jnp.sum(e, 0, keepdims=True))).astype(BF)
            probs_out[at, lo : lo + 256] = p
            mixed[at, lo : lo + 256] = collect(dot_tn(p, v)).astype(BF)
        return carry

    lax.fori_loop(0, 15, window, 0, unroll=True)
    probs_copy.start()
    copies[1].wait()
    for n in range(3):
        att = dot(mixed[320 * n : 320 * n + 320], w_proj[...]).astype(BF).astype(F32)
        put_windows(back, n, att)

    def finish(n, carry):
        at = pl.ds(8 * n, 8)
        resid_out[at] = (own[at].astype(F32) + place_back(back, n, a, b)).astype(BF)
        return carry

    lax.fori_loop(0, 4, finish, 0, unroll=True)
    qkv_copy.wait()
    probs_copy.wait()


VM = pl.BlockSpec(memory_space=pltpu.VMEM)
SM = pl.BlockSpec(memory_space=pltpu.SMEM)
HB = pl.BlockSpec(memory_space=pltpu.HBM)


def params(mib):
    return pltpu.CompilerParams(vmem_limit_bytes=mib * 2**20)


def attn_fwd(place, left, own, right, slab, up, down, gain, w_qkv, w_proj):
    return pl.pallas_call(
        attn_fwd_kernel,
        out_shape=(
            jax.ShapeDtypeStruct((960, 1536), BF),
            jax.ShapeDtypeStruct((960, 512), BF),
            jax.ShapeDtypeStruct((32, 16, 512), BF),
        ),
        in_specs=[SM] + [VM] * 7 + [HB] * 2,
        out_specs=(HB, HB, VM),
        scratch_shapes=[
            pltpu.VMEM((48, 24, 512), F32),
            pltpu.VMEM((48, 24, 128), F32),
            pltpu.VMEM((15, 64, 128), F32),
            pltpu.VMEM((40, 24, 512), F32),
            pltpu.VMEM((960, 512), BF),
            pltpu.VMEM((960, 1536), BF),
            pltpu.VMEM((960, 512), BF),
            pltpu.VMEM((512, 1536), BF),
            pltpu.VMEM((512, 512), BF),
            pltpu.SemaphoreType.DMA((4,)),
        ],
        compiler_params=params(56),
        cost_estimate=pl.CostEstimate(flops=2 * 10**9, bytes_accessed=10 * 2**20, transcendentals=10**6),
        name="attn_fwd",
    )(place, left, own, right, slab, up, down, gain, w_qkv, w_proj)


def attn_bwd_kernel(
    place, first, own, second, up, down, qkv_hbm, probs_hbm, w_proj_hbm, w_qkv_hbm, tokens, gain,
    grad_out,
    grid, back, g_mixed, g_qkv, qkv, probs, w_proj, w_qkv, sems,
):
    pairs = ((w_proj_hbm, w_proj), (qkv_hbm, qkv), (probs_hbm, probs), (w_qkv_hbm, w_qkv))
    copies = fetch(pairs, sems)
    a, b = place[0], place[1]
    fill_grid(grid, b, place[3] == 1, first, own, second, up, down)
    masks, scaled = half_masks(1.0), half_masks(0.125)
    copies[0].wait()
    for n in range(3):
        ups = [window_of(grid, 5 * n + k, a).astype(BF) for k in range(5)]
        g_mixed[320 * n : 320 * n + 320] = dot_nt(jnp.concatenate(ups, 0), w_proj[...]).astype(BF)
    copies[1].wait()
    copies[2].wait()

    def window(w, carry):
        at = pl.ds(pl.multiple_of(w * 64, 64), 64)
        for c in range(2):
            lo = 256 * c
            qbig = spread(qkv[at, lo : lo + 256], scaled)
            gbig = spread(g_mixed[at, lo : lo + 256], masks)
            k = qkv[at, 512 + lo : 768 + lo]
            v = qkv[at, 1024 + lo : 1280 + lo]
            p = probs[at, lo : lo + 256]
            g_probs = dot_nt(v, gbig)
            wide_p = p.astype(F32)
            total = jnp.sum(wide_p * g_probs, 0, keepdims=True)
            g_score = (wide_p * (g_probs - total)).astype(BF)
            g_qkv[at, lo : lo + 256] = (collect(dot_tn(g_score, k)) * 0.125).astype(BF)
            g_qkv[at, 512 + lo : 768 + lo] = dot(g_score, qbig).astype(BF)
            g_qkv[at, 1024 + lo : 1280 + lo] = dot(p, gbig).astype(BF)
        return carry

    lax.fori_loop(0, 15, window, 0, unroll=True)
    copies[3].wait()
    for n in range(3):
        g_shift = dot_nt(g_qkv[320 * n : 320 * n + 320], w_qkv[...]).astype(BF).astype(F32)
        put_windows(back, n, g_shift)

    def finish(n, carry):
        at = pl.ds(8 * n, 8)
        part = norm_back(tokens[at].astype(F32), gain[...], place_back(back, n, a, b))
        grad_out[at] = (own[at].astype(F32) + part).astype(BF)
        return carry

    lax.fori_loop(0, 4, finish, 0, unroll=True)


def attn_bwd(place, left, own, right, up, down, qkv, probs, w_proj, w_qkv, tokens, gain):
    return pl.pallas_call(
        attn_bwd_kernel,
        out_shape=jax.ShapeDtypeStruct((32, 16, 512), BF),
        in_specs=[SM] + [VM] * 5 + [HB] * 4 + [VM] * 2,
        out_specs=VM,
        scratch_shapes=[
            pltpu.VMEM((48, 24, 512), F32),
            pltpu.VMEM((40, 24, 512), F32),
            pltpu.VMEM((960, 512), BF),
            pltpu.VMEM((960, 1536), BF),
            pltpu.VMEM((960, 1536), BF),
            pltpu.VMEM((960, 512), BF),
            pltpu.VMEM((512, 512), BF),
            pltpu.VMEM((512, 1536), BF),
            pltpu.SemaphoreType.DMA((4,)),
        ],
        compiler_params=params(32),
        cost_estimate=pl.CostEstimate(flops=4 * 10**9, bytes_accessed=10 * 2**20, transcendentals=0),
        name="attn_bwd",
    )(place, left, own, right, up, down, qkv, probs, w_proj, w_qkv, tokens, gain)


def set_fine(fine, value):
    for lane in range(4):
        fine[lane] = value[:, 128 * lane : 128 * lane + 128]


def get_fine(fine):
    return jnp.concatenate([fine[lane] for lane in range(4)], 1)


def patch_parts(fine):
    parts = {}
    for s in range(2):
        lanes = [fine[lane, pl.ds(s, 256, 2), :] for lane in range(4)]
        half = jnp.concatenate(lanes, 1).reshape(16, 2, 8, 512)
        for r in range(2):
            parts[r + 2 * s] = half[:, r].reshape(128, 512)
    return [parts[k] for k in range(4)]


def unpatch(fine, parts):
    for s in range(2):
        pair = [parts[r + 2 * s].reshape(16, 1, 8, 512) for r in range(2)]
        half = jnp.concatenate(pair, 1).reshape(256, 512)
        for lane in range(4):
            fine[lane, pl.ds(s, 256, 2), :] = half[:, 128 * lane : 128 * lane + 128]


def joint_normalise(parts):
    mean = sum(jnp.sum(p, -1, keepdims=True) for p in parts) / 2048.0
    cent = [p - mean for p in parts]
    var = sum(jnp.sum(c * c, -1, keepdims=True) for c in cent) / 2048.0
    r = lax.rsqrt(var + EPS)
    return [c * r for c in cent], r


def ffn_fwd_kernel(
    resid, gain_ffn, fc1_hbm, fc2_hbm, gain_merge, merge_hbm, gain_mlp,
    slope_out, block_out, coarse_out, cin_out,
    acc, fine, w_fc1, w_fc2, w_merge, sems,
):
    pairs = []
    for n in range(4):
        cut = pl.ds(512 * n, 512)
        pairs += [(fc1_hbm.at[:, cut], w_fc1.at[:, cut]), (fc2_hbm.at[cut], w_fc2.at[cut])]
    pairs += [(merge_hbm.at[pl.ds(512 * k, 512)], w_merge.at[pl.ds(512 * k, 512)]) for k in range(4)]
    copies = fetch(pairs, sems)
    xh, _ = normalise(resid[...].astype(F32))
    ffn_in = (xh * gain_ffn[...]).astype(BF)
    for n in range(4):
        cut = slice(512 * n, 512 * n + 512)
        copies[2 * n].wait()
        copies[2 * n + 1].wait()
        for m in range(2):
            rows = slice(256 * m, 256 * m + 256)
            hid, slope = gelu_both(dot(ffn_in[rows], w_fc1[:, cut]))
            slope_out[rows, cut] = slope
            term = dot(hid, w_fc2[cut, :])
            if n == 0:
                acc[rows, :] = resid[rows, :].astype(F32) + term
            else:
                acc[rows, :] += term
    block = acc[...].astype(BF)
    block_out[...] = block
    set_fine(fine, block.astype(F32))
    xhs, _ = joint_normalise(patch_parts(fine))
    coarse = None
    for k in range(4):
        cut = slice(512 * k, 512 * k + 512)
        copies[8 + k].wait()
        term = dot((xhs[k] * gain_merge[:, cut]).astype(BF), w_merge[cut, :])
        coarse = term if coarse is None else coarse + term
    coarse = coarse.astype(BF)
    coarse_out[...] = coarse
    xh, _ = normalise(coarse.astype(F32))
    cin_out[...] = (xh * gain_mlp[...]).astype(BF)


def ffn_fwd(resid, gain_ffn, w_fc1, w_fc2, gain_merge, w_merge, gain_mlp):
    return pl.pallas_call(
        ffn_fwd_kernel,
        out_shape=(
            jax.ShapeDtypeStruct((512, 2048), BF),
            jax.ShapeDtypeStruct((512, 512), BF),
            jax.ShapeDtypeStruct((128, 1024), BF),
            jax.ShapeDtypeStruct((128, 1024), BF),
        ),
        in_specs=[VM, VM, HB, HB, VM, HB, VM],
        out_specs=(VM, VM, VM, VM),
        scratch_shapes=[
            pltpu.VMEM((512, 512), F32),
            pltpu.VMEM((4, 512, 128), F32),
            pltpu.VMEM((512, 2048), BF),
            pltpu.VMEM((2048, 512), BF),
            pltpu.VMEM((2048, 1024), BF),
            pltpu.SemaphoreType.DMA((12,)),
        ],
        compiler_params=params(32),
        cost_estimate=pl.CostEstimate(flops=3 * 10**9, bytes_accessed=12 * 2**20, transcendentals=10**6),
        name="ffn_fwd",
    )(resid, gain_ffn, w_fc1, w_fc2, gain_merge, w_merge, gain_mlp)


def weight_chunk(parts, y, lo):
    rows = []
    for k in range(4):
        ref, at = (parts[y], 128 * k) if y < 3 else (parts[3 + k // 2], 128 * (k % 2))
        rows += [ref[at + lo : at + lo + 32], ref[at + 64 + lo : at + 96 + lo]]
    return jnp.concatenate(rows, 0)


def mlp_kernel(
    place, c0, c1, c2, c3, d0, d1, d2, d3, w0, w1, w2, w3, w4,
    keep_out, send_out, hid_out,
    cs, deep, gacc,
):
    for k, (c, g) in enumerate(((c0, d0), (c1, d1), (c2, d2), (c3, d3))):
        cs[128 * k : 128 * k + 128] = c[...]
        deep[128 * k : 128 * k + 128] = g[...]
    parts = (w0, w1, w2, w3, w4)
    for y in range(4):
        first = weight_chunk(parts, y, 0)
        second = weight_chunk(parts, y, 32)
        for m in range(2):
            rows = slice(256 * m, 256 * m + 256)
            hid, slope = gelu_both(dot_nt(cs[rows], first))
            hid_out[rows, 256 * y : 256 * y + 256] = hid
            g_pre = dot_nt(deep[rows], second).astype(BF) * slope
            g_cin = dot(g_pre, first)
            if y == 0:
                gacc[rows] = g_cin
            else:
                gacc[rows] += g_cin
    part_out(gacc, keep_out, send_out)


def part_out(total, keep_out, send_out):
    keep_out[0:128] = total[0:128].astype(BF)
    keep_out[128:256] = total[256:384].astype(BF)
    send_out[0:128] = total[128:256].astype(BF)
    send_out[128:256] = total[384:512].astype(BF)


def coarse_mlp(place, cins, deeps, parts):
    return pl.pallas_call(
        mlp_kernel,
        out_shape=(
            jax.ShapeDtypeStruct((256, 1024), BF),
            jax.ShapeDtypeStruct((256, 1024), BF),
            jax.ShapeDtypeStruct((512, 1024), BF),
        ),
        in_specs=[SM] + [VM] * 13,
        out_specs=(VM, VM, VM),
        scratch_shapes=[
            pltpu.VMEM((512, 1024), BF),
            pltpu.VMEM((512, 1024), BF),
            pltpu.VMEM((512, 1024), F32),
        ],
        compiler_params=params(32),
        cost_estimate=pl.CostEstimate(flops=3 * 10**9, bytes_accessed=8 * 2**20, transcendentals=10**6),
        name="coarse_mlp",
    )(place, *cins, *deeps, *parts)


def down_kernel(hid, w0, w1, w2, w3, w4, keep_out, send_out):
    total = None
    for y in range(4):
        term = dot(hid[:, 256 * y : 256 * y + 256], weight_chunk((w0, w1, w2, w3, w4), y, 32))
        total = term if total is None else total + term
    part_out(total, keep_out, send_out)


def down_of(hid, parts):
    half = jax.ShapeDtypeStruct((256, 1024), BF)
    return pl.pallas_call(
        down_kernel,
        out_shape=(half, half),
        in_specs=[VM] * 6,
        out_specs=(VM, VM),
        compiler_params=params(32),
        cost_estimate=pl.CostEstimate(flops=10**9, bytes_accessed=5 * 2**20, transcendentals=0),
        name="down",
    )(hid, *parts)


def g_deep_kernel(cot, up_hbm, out, fine, w_up, sems):
    cuts = [pl.ds(256 * k, 256) for k in range(4)]
    copies = fetch([(up_hbm.at[cut], w_up.at[cut]) for cut in cuts], sems)
    set_fine(fine, cot[...].astype(F32))
    whole = jnp.concatenate([part.astype(BF) for part in patch_parts(fine)], 1)
    for k in range(4):
        copies[k].wait()
        rows = slice(256 * k, 256 * k + 256)
        out[:, rows] = dot_nt(whole, w_up[rows, :]).astype(BF)


UP_SCRATCH = [
    pltpu.VMEM((4, 512, 128), F32),
    pltpu.VMEM((1024, 2048), BF),
    pltpu.SemaphoreType.DMA((4,)),
]


def g_deep_of(cot, w_up):
    return pl.pallas_call(
        g_deep_kernel,
        out_shape=jax.ShapeDtypeStruct((128, 1024), BF),
        in_specs=[VM, HB],
        out_specs=VM,
        scratch_shapes=UP_SCRATCH,
        compiler_params=params(32),
        cost_estimate=pl.CostEstimate(flops=10**9, bytes_accessed=5 * 2**20, transcendentals=0),
        name="g_deep",
    )(cot, w_up)


def up_kernel(coarse, keep, near, far, block, up_hbm, out, fine, w_up, sems):
    cuts = [pl.ds(256 * k, 256) for k in range(4)]
    copies = fetch([(up_hbm.at[cut], w_up.at[cut]) for cut in cuts], sems)
    deep = coarse[...].astype(F32) + keep[0:128].astype(F32) + near[0:128].astype(F32)
    deep = (deep + far[...].astype(F32)).astype(BF)
    acc = None
    for k in range(4):
        copies[k].wait()
        rows = slice(256 * k, 256 * k + 256)
        term = dot(deep[:, rows], w_up[rows, :])
        acc = term if acc is None else acc + term
    unpatch(fine, [acc[:, 512 * k : 512 * k + 512] for k in range(4)])
    out[...] = (block[...].astype(F32) + get_fine(fine)).astype(BF)


def up_of(coarse, keep, near, far, block, w_up):
    return pl.pallas_call(
        up_kernel,
        out_shape=jax.ShapeDtypeStruct((512, 512), BF),
        in_specs=[VM] * 5 + [HB],
        out_specs=VM,
        scratch_shapes=UP_SCRATCH,
        compiler_params=params(32),
        cost_estimate=pl.CostEstimate(flops=10**9, bytes_accessed=5 * 2**20, transcendentals=0),
        name="up",
    )(coarse, keep, near, far, block, w_up)


def ffn_bwd_kernel(
    place, gcin_own, gcin_near, gcin_far, g_deep, coarse, gain_mlp, merge_hbm, block, gain_merge, cot,
    fc2_hbm, slope_hbm, fc1_hbm, resid, gain_ffn,
    g_resid_out, first_out, second_out,
    fine, acc, w_merge, w_fc1, w_fc2, slope, sems,
):
    pairs = [(merge_hbm.at[pl.ds(512 * k, 512)], w_merge.at[pl.ds(512 * k, 512)]) for k in range(4)]
    for n in range(4):
        cut = pl.ds(512 * n, 512)
        pairs += [
            (fc2_hbm.at[cut], w_fc2.at[cut]),
            (slope_hbm.at[:, cut], slope.at[:, cut]),
            (fc1_hbm.at[:, cut], w_fc1.at[:, cut]),
        ]
    copies = fetch(pairs, sems)
    g_cin = gcin_own[0:128].astype(F32) + gcin_near[0:128].astype(F32) + gcin_far[...].astype(F32)
    g_cin = g_cin.astype(BF).astype(F32)
    part = norm_back(coarse[...].astype(F32), gain_mlp[...], g_cin)
    g_coarse = (g_deep[...].astype(F32) + part).astype(BF)
    set_fine(fine, block[...].astype(F32))
    xhs, r = joint_normalise(patch_parts(fine))
    scaled = []
    for k in range(4):
        cut = slice(512 * k, 512 * k + 512)
        copies[k].wait()
        scaled.append(dot_nt(g_coarse, w_merge[cut, :]) * gain_merge[:, cut])
    mean_s = sum(jnp.sum(s, -1, keepdims=True) for s in scaled) / 2048.0
    mean_x = sum(jnp.sum(s * x, -1, keepdims=True) for s, x in zip(scaled, xhs)) / 2048.0
    unpatch(fine, [r * (s - mean_s - x * mean_x) for s, x in zip(scaled, xhs)])
    g_block = (cot[...].astype(F32) + get_fine(fine)).astype(BF)
    for n in range(4):
        cut = slice(512 * n, 512 * n + 512)
        for k in range(3):
            copies[4 + 3 * n + k].wait()
        for m in range(2):
            rows = slice(256 * m, 256 * m + 256)
            g_pre = dot_nt(g_block[rows], w_fc2[cut, :]).astype(BF) * slope[rows, cut]
            term = dot_nt(g_pre, w_fc1[:, cut])
            if n == 0:
                acc[rows, :] = term
            else:
                acc[rows, :] += term
    g_fin = acc[...].astype(BF).astype(F32)
    part = norm_back(resid[...].astype(F32), gain_ffn[...], g_fin)
    total = g_block.astype(F32) + part
    g_resid_out[...] = total.astype(BF)
    lines = total.reshape(32, 16, 512)
    tail, head = sides(place[3] == 1, lines[:, :8], lines[:, 8:])
    first_out[...] = tail.astype(BF)
    second_out[...] = head.astype(BF)


def ffn_bwd(place, gcin_own, gcin_near, gcin_far, g_deep, coarse, gain_mlp, w_merge, block, gain_merge, cot,
            w_fc2, slope, w_fc1, resid, gain_ffn):
    return pl.pallas_call(
        ffn_bwd_kernel,
        out_shape=(
            jax.ShapeDtypeStruct((512, 512), BF),
            jax.ShapeDtypeStruct((32, 8, 512), BF),
            jax.ShapeDtypeStruct((32, 8, 512), BF),
        ),
        in_specs=[SM] + [VM] * 6 + [HB, VM, VM, VM, HB, HB, HB, VM, VM],
        out_specs=(VM, VM, VM),
        scratch_shapes=[
            pltpu.VMEM((4, 512, 128), F32),
            pltpu.VMEM((512, 512), F32),
            pltpu.VMEM((2048, 1024), BF),
            pltpu.VMEM((512, 2048), BF),
            pltpu.VMEM((2048, 512), BF),
            pltpu.VMEM((512, 2048), BF),
            pltpu.SemaphoreType.DMA((16,)),
        ],
        compiler_params=params(32),
        cost_estimate=pl.CostEstimate(flops=3 * 10**9, bytes_accessed=14 * 2**20, transcendentals=0),
        name="ffn_bwd",
    )(place, gcin_own, gcin_near, gcin_far, g_deep, coarse, gain_mlp, w_merge, block, gain_merge, cot,
      w_fc2, slope, w_fc1, resid, gain_ffn)


def ends_kernel(tokens, turned, first_out, second_out, slab_out):
    odd = (lax.axis_index("lon") & 1) == 1
    slab = jnp.concatenate([turned[...].astype(F32), jnp.zeros((16, 480), F32)], 1)
    slab_out[...] = slab.astype(BF)
    lines = tokens[...].astype(F32)
    for at, source in ((slice(0, 32), lines), (slice(32, 33), slab.reshape(1, 16, 512))):
        tail, head = sides(odd, source[:, :8], source[:, 8:])
        first_out[at] = tail.astype(BF)
        second_out[at] = head.astype(BF)


def ends(tokens, turned):
    part = jax.ShapeDtypeStruct((33, 8, 512), BF)
    return pl.pallas_call(
        ends_kernel,
        out_shape=(part, part, jax.ShapeDtypeStruct((16, 512), BF)),
        in_specs=[VM] * 2,
        out_specs=(VM,) * 3,
        compiler_params=params(32),
        cost_estimate=pl.CostEstimate(flops=10**6, bytes_accessed=2 * 2**20, transcendentals=0),
        name="ends",
    )(tokens, turned)


def cut_kernel(place, w_first, w_second, s0, s1, s2, s3, both):
    both[0] = w_first[...].astype(F32).T.astype(BF)
    both[1] = w_second[...]
    for k, out in enumerate((s0, s1, s2, s3)):
        rows = pl.ds(pl.multiple_of(lax.bitwise_xor(place[2], k) * 32, 32), 32)
        out[0:32] = both[0, rows, :]
        out[32:64] = both[1, rows, :]


def cut(place, w_first, w_second):
    block = jax.ShapeDtypeStruct((64, 256), BF)
    return pl.pallas_call(
        cut_kernel,
        out_shape=(block,) * 4,
        in_specs=[SM] + [VM] * 2,
        out_specs=(VM,) * 4,
        scratch_shapes=[pltpu.VMEM((2, 128, 256), BF)],
        compiler_params=params(32),
        cost_estimate=pl.CostEstimate(flops=10**6, bytes_accessed=2**19, transcendentals=0),
        name="cut",
    )(place, w_first, w_second)


def join_kernel(place, s0, s1, s2, s3, out):
    for k, block in enumerate((s0, s1, s2, s3)):
        at = pl.multiple_of(lax.bitwise_xor(place[2], k) * 256, 256)
        out[:, pl.ds(at, 256)] = block[...]


def join(place, blocks):
    return pl.pallas_call(
        join_kernel,
        out_shape=jax.ShapeDtypeStruct((64, 1024), BF),
        in_specs=[SM] + [VM] * 4,
        out_specs=VM,
        compiler_params=params(32),
        cost_estimate=pl.CostEstimate(flops=10**6, bytes_accessed=2**18, transcendentals=0),
        name="join",
    )(place, *blocks)


def stack_kernel(*refs):
    for k, ref in enumerate(refs[:-1]):
        refs[-1][128 * k : 128 * k + 128] = ref[...]


def stacked(blocks):
    return pl.pallas_call(
        stack_kernel,
        out_shape=jax.ShapeDtypeStruct((512, 1024), BF),
        in_specs=[VM] * 4,
        out_specs=VM,
        compiler_params=params(32),
        cost_estimate=pl.CostEstimate(flops=10**6, bytes_accessed=2**21, transcendentals=0),
        name="stacked",
    )(*blocks)


def halves_kernel(ahead, behind, first, second):
    first[...] = ahead[0:256]
    second[...] = behind[256:512]


def halves(ahead, behind):
    half = jax.ShapeDtypeStruct((256, 1024), BF)
    return pl.pallas_call(
        halves_kernel,
        out_shape=(half, half),
        in_specs=[VM] * 2,
        out_specs=(VM, VM),
        compiler_params=params(32),
        cost_estimate=pl.CostEstimate(flops=10**6, bytes_accessed=2**21, transcendentals=0),
        name="halves",
    )(ahead, behind)


def strips_kernel(place, first, own, second, *rest):
    odd = place[3] == 1
    top_out, bottom_out = rest[-2:]
    for out, lo in ((top_out, 0), (bottom_out, 24)):
        rows = slice(lo, lo + 8)
        left, right = sides(odd, first[rows].astype(F32), second[rows].astype(F32))
        out[0:8, 0:8, :] = left.astype(BF)
        out[0:8, 8:24, :] = own[rows]
        out[0:8, 24:32, :] = right.astype(BF)
        if len(rest) == 3:
            left, right = sides(odd, first[32].astype(F32), second[32].astype(F32))
            out[8] = jnp.concatenate([left, rest[0][...].astype(F32), right], 0).astype(BF)


def strips(place, first, own, second, *slab):
    edge = jax.ShapeDtypeStruct((8 + len(slab), 32, 512), BF)
    return pl.pallas_call(
        strips_kernel,
        out_shape=(edge, edge),
        in_specs=[SM] + [VM] * (3 + len(slab)),
        out_specs=(VM, VM),
        compiler_params=params(32),
        cost_estimate=pl.CostEstimate(flops=10**6, bytes_accessed=3 * 2**20, transcendentals=0),
        name="strips",
    )(place, first, own, second, *slab)


def along(axis, count, step):
    pairs = [(s, (s + step) % count) for s in range(count)]
    return lambda v: lax.ppermute(v, axis, pairs)


LAT_NEXT, LAT_PREV = along("lat", 4, 1), along("lat", 4, -1)


def even_odd(v):
    return lax.ppermute(v, "lon", [(k, k ^ 1) for k in range(32)])


def odd_even(v):
    return lax.ppermute(v, "lon", [(k, (((k + 1) ^ 1) - 1) % 32) for k in range(32)])


def core_swap(v):
    return lax.ppermute(v, "lat", [(0, 1), (1, 0), (2, 3), (3, 2)])


def x_swap(v):
    return lax.ppermute(v, "lat", [(0, 2), (2, 0), (1, 3), (3, 1)])


def cross_swap(v):
    return lax.ppermute(v, "lat", [(0, 3), (3, 0), (1, 2), (2, 1)])


def x_far_swap(v):
    return lax.ppermute(v, "lon", [(k, (k + 16) % 32) for k in range(32)])


def turn(swapped, k):
    pairs = []
    for lat in range(4):
        along_y = (lat % 2 == 1) != swapped
        for lon in range(32):
            x, y, z = lon // 16, lon // 4 % 4, lon % 4
            if along_y:
                y = (y + k) % 4
            else:
                z = (z + k) % 4
            pairs.append((lat * 32 + lon, lat * 32 + (x * 4 + y) * 4 + z))
    return lambda v: lax.ppermute(v, ("lat", "lon"), pairs)


def after(value, *gates):
    return lax.optimization_barrier((value,) + gates)[0]


def on_device(
    tokens, labels, offsets, gain_attn, w_qkv, w_proj, gain_ffn, w_fc1, w_fc2,
    gain_merge, w_merge, gain_mlp, w_first, w_second, w_up, cotangent,
):
    row = lambda g: g.reshape(1, -1)
    first, second, slab = ends(tokens, labels.T)
    left, right = even_odd(first), odd_even(second)
    where = [lax.axis_index("lat"), lax.axis_index("lon") & 1]
    place = jnp.concatenate([after(offsets, slab), jnp.stack(where).astype(jnp.int32)])
    s0, s1, s2, s3 = cut(place, w_first, w_second)
    g_deep = g_deep_of(after(cotangent.reshape(512, 512), s0), w_up)
    near_deep = core_swap(g_deep)
    s0 = after(s0, g_deep)
    mine = join(place, (s0, core_swap(s1), x_swap(s2), cross_swap(s3)))
    other = x_far_swap(mine)
    bottom, top = strips(place, left, tokens, right, slab)
    up, down = LAT_NEXT(top), LAT_PREV(bottom)
    other = after(other, bottom, top)
    seed = jnp.concatenate([mine, other], 0)
    moved = [turn(False, k)(seed) for k in (1, -1, 2)]
    cot = cotangent.reshape(512, 512)
    part = stacked([after(seed, g_deep, up, down)] + moved)
    ahead, behind = turn(True, 1)(part), turn(True, -1)(part)
    qkv, probs, resid = attn_fwd(
        place, left, tokens, right, slab, after(up, part), down, row(gain_attn), w_qkv, w_proj
    )
    resid = resid.reshape(512, 512)
    far_deep = x_swap(after(g_deep, resid))
    slope, block, coarse, coarse_in = ffn_fwd(
        resid, row(gain_ffn), w_fc1, w_fc2, row(gain_merge), w_merge, row(gain_mlp)
    )
    far_cin = x_swap(coarse_in)
    near_cin = core_swap(coarse_in)
    fore, hind = halves(after(ahead, coarse_in), behind)
    parts = [part, ahead, behind, turn(True, 1)(fore), turn(True, -1)(hind)]
    cins = [coarse_in, near_cin, far_cin, core_swap(after(far_cin, fore))]
    deeps = [g_deep, near_deep, far_deep, core_swap(after(far_deep, fore))]
    keep, send, hid = coarse_mlp(place, cins, deeps, parts)
    near = core_swap(send)
    gcin_far = x_swap((keep[128:].astype(F32) + near[128:].astype(F32)).astype(BF))
    down_keep, down_send = down_of(hid, parts)
    down_near = core_swap(down_send)
    down_far = (down_keep[128:].astype(F32) + down_near[128:].astype(F32)).astype(BF)
    gcin_far, down_far = lax.optimization_barrier((gcin_far, down_far))
    down_far = x_swap(down_far)
    g_resid, g_first, g_second = ffn_bwd(
        place, keep, near, gcin_far, g_deep, coarse, row(gain_mlp), w_merge, block, row(gain_merge), cot,
        w_fc2, slope, w_fc1, resid, row(gain_ffn),
    )
    g_resid = g_resid.reshape(32, 16, 512)
    g_left, g_right = even_odd(g_first), odd_even(g_second)
    field_out = up_of(coarse, down_keep, down_near, down_far, block, w_up).reshape(32, 16, 512)
    g_bottom, g_top = strips(place, g_left, after(g_resid, field_out), g_right)
    g_up, g_down = LAT_NEXT(g_top), LAT_PREV(g_bottom)
    grad_in = attn_bwd(
        place, g_left, g_resid, g_right, g_up, g_down, qkv, probs, w_proj, w_qkv, tokens,
        row(gain_attn),
    )
    return (field_out, grad_in)


def solution(mesh):
    grid = P("lat", "lon", None)
    placed = (
        grid, P("lat", "lon"), P(), P(), P(), P(), P(), P(), P(), P(), P(), P(),
        P("lat", "lon"), P("lon", "lat"), P(), grid,
    )
    return jax.shard_map(
        on_device, mesh=mesh, in_specs=placed, out_specs=(grid, grid), check_vma=False
    )
```

```python
import jax
import jax.numpy as jnp
from jax import lax
from jax.experimental import pallas as pl
from jax.experimental.pallas import tpu as pltpu
from jax.sharding import PartitionSpec as P

BF = jnp.bfloat16
F32 = jnp.float32
EPS = 1e-05
NT = (((1,), (1,)), ((), ()))
TN = (((0,), (0,)), ((), ()))
GELU_C = 0.7978845608028654
GELU_A = 0.044715


def dot(a, b):
    return jnp.dot(a, b, preferred_element_type=F32)


def dot_nt(a, b):
    return lax.dot_general(a, b, NT, preferred_element_type=F32)


def dot_tn(a, b):
    return lax.dot_general(a, b, TN, preferred_element_type=F32)


def normalise(v):
    mean = jnp.mean(v, -1, keepdims=True)
    c = v - mean
    r = lax.rsqrt(jnp.mean(c * c, -1, keepdims=True) + EPS)
    return c * r, r


def norm_back(v, gain, t):
    xh, r = normalise(v)
    s = t * gain
    return r * (s - jnp.mean(s, -1, keepdims=True) - xh * jnp.mean(s * xh, -1, keepdims=True))


def gelu_both(wide):
    x = wide.astype(BF)
    x2 = x * x
    t = jnp.tanh(x * (GELU_C + GELU_C * GELU_A * x2))
    h = 0.5 * x
    slope = (0.5 + 0.5 * t) + (h - h * t * t) * (GELU_C + 3.0 * GELU_C * GELU_A * x2)
    return h + h * t, slope


def half_masks(scale):
    low = lax.broadcasted_iota(jnp.int32, (1, 128), 1) < 64
    return [jnp.where(m, scale, 0.0).astype(F32).astype(BF) for m in (low, jnp.logical_not(low))]


def spread(x, masks):
    none = jnp.zeros((64, 128), BF)
    left, right = x[:, :128], x[:, 128:]
    rows = [jnp.concatenate([left * m, none], 1) for m in masks]
    rows += [jnp.concatenate([none, right * m], 1) for m in masks]
    return jnp.concatenate(rows, 0)


def collect(big):
    low = lax.broadcasted_iota(jnp.int32, (64, 128), 1) < 64
    left = jnp.where(low, big[0:64, :128], big[64:128, :128])
    right = jnp.where(low, big[128:192, 128:], big[192:256, 128:])
    return jnp.concatenate([left, right], 1)


def sides(odd, first, second):
    return jnp.where(odd, first, second), jnp.where(odd, second, first)


def fill_grid(grid, b, odd, first, own, second, up, down):
    def rows(n, carry):
        at = pl.ds(8 * n, 8)
        left, right = sides(odd, first[at].astype(F32), second[at].astype(F32))
        line = jnp.concatenate([left, own[at].astype(F32), right], 1)
        grid[pl.ds(8 * n + 8, 8)] = pltpu.roll(line, 32 - b, 1)[:, :24]
        return carry

    lax.fori_loop(0, 4, rows, 0)
    grid[0:8] = pltpu.roll(up[0:8].astype(F32), 32 - b, 1)[:, :24]
    grid[40:48] = pltpu.roll(down[0:8].astype(F32), 32 - b, 1)[:, :24]


def place_back(back, n, a, b):
    return pltpu.roll(back[pl.ds(8 - a + 8 * n, 8)], 16 + b, 1)[:, :16]


def fetch(pairs, sems):
    copies = [pltpu.make_async_copy(src, dst, sems.at[k]) for k, (src, dst) in enumerate(pairs)]
    for copy in copies:
        copy.start()
    return copies


def window_of(grid, w, a):
    wi, wj = w // 3, w % 3
    return grid[pl.ds(a + 8 * wi, 8), 8 * wj : 8 * wj + 8, :].reshape(64, grid.shape[2])


def put_windows(back, n, value):
    for k in range(5):
        wi, wj = (5 * n + k) // 3, (5 * n + k) % 3
        back[8 * wi : 8 * wi + 8, 8 * wj : 8 * wj + 8, :] = value[64 * k : 64 * k + 64].reshape(
            8, 8, 512
        )


def attn_fwd_kernel(
    place, first, own, second, own_slab, up, down, gain, w_qkv_hbm, w_proj_hbm,
    qkv_hbm, probs_hbm, resid_out,
    grid, codes, cols, back, mixed, qkv_out, probs_out, w_qkv, w_proj, sems,
):
    copies = fetch(((w_qkv_hbm, w_qkv), (w_proj_hbm, w_proj)), sems)
    qkv_copy = pltpu.make_async_copy(qkv_out, qkv_hbm, sems.at[2])
    probs_copy = pltpu.make_async_copy(probs_out, probs_hbm, sems.at[3])
    a, b, d = place[0], place[1], place[2]
    odd = place[3] == 1
    fill_grid(grid, b, odd, first, own, second, up, down)
    left, right = sides(odd, first[32].astype(F32), second[32].astype(F32))
    slab = jnp.concatenate([left, own_slab[...].astype(F32), right], 0)
    slab = pltpu.roll(slab, 32 - b, 0)[:24]
    top_code = jnp.where(d == 0, 4.0, 0.0).astype(F32)
    low_code = jnp.where(d == 3, 4.0, 0.0).astype(F32)
    slab_up = pltpu.roll(up[8].astype(F32) + top_code, 32 - b, 0)[:24]
    slab_down = pltpu.roll(down[8].astype(F32) + low_code, 32 - b, 0)[:24]
    for r in range(32):
        codes[8 + r] = jnp.broadcast_to(slab[:, r : r + 1], (24, 128))
    for r in range(8):
        codes[r] = jnp.broadcast_to(slab_up[:, 24 + r : 25 + r], (24, 128))
        codes[40 + r] = jnp.broadcast_to(slab_down[:, r : r + 1], (24, 128))
    masks = half_masks(0.125)
    copies[0].wait()
    for n in range(3):
        normed = []
        for k in range(5):
            xh, _ = normalise(window_of(grid, 5 * n + k, a))
            normed.append((xh * gain[...]).astype(BF))
        qkv_out[320 * n : 320 * n + 320] = dot(jnp.concatenate(normed, 0), w_qkv[...]).astype(BF)
        for k in range(5):
            cols[5 * n + k] = window_of(codes, 5 * n + k, a)
    qkv_copy.start()

    def window(w, carry):
        at = pl.ds(pl.multiple_of(w * 64, 64), 64)
        col = cols[w]
        row = col.T[0:1, 0:64]
        same = jnp.concatenate([col, col], 1) == jnp.concatenate([row] * 4, 1)
        for c in range(2):
            lo = 256 * c
            qbig = spread(qkv_out[at, lo : lo + 256], masks)
            k = qkv_out[at, 512 + lo : 768 + lo]
            v = qkv_out[at, 1024 + lo : 1280 + lo]
            e = jnp.where(same, jnp.exp(dot_nt(k, qbig)), 0.0)
            p = (e * (1.0 / jnp.sum(e, 0, keepdims=True))).astype(BF)
            probs_out[at, lo : lo + 256] = p
            mixed[at, lo : lo + 256] = collect(dot_tn(p, v)).astype(BF)
        return carry

    lax.fori_loop(0, 15, window, 0, unroll=True)
    probs_copy.start()
    copies[1].wait()
    for n in range(3):
        att = dot(mixed[320 * n : 320 * n + 320], w_proj[...]).astype(BF).astype(F32)
        put_windows(back, n, att)

    def finish(n, carry):
        at = pl.ds(8 * n, 8)
        resid_out[at] = (own[at].astype(F32) + place_back(back, n, a, b)).astype(BF)
        return carry

    lax.fori_loop(0, 4, finish, 0, unroll=True)
    qkv_copy.wait()
    probs_copy.wait()


VM = pl.BlockSpec(memory_space=pltpu.VMEM)
SM = pl.BlockSpec(memory_space=pltpu.SMEM)
HB = pl.BlockSpec(memory_space=pltpu.HBM)


def params(mib):
    return pltpu.CompilerParams(vmem_limit_bytes=mib * 2**20)


def attn_fwd(place, left, own, right, slab, up, down, gain, w_qkv, w_proj):
    return pl.pallas_call(
        attn_fwd_kernel,
        out_shape=(
            jax.ShapeDtypeStruct((960, 1536), BF),
            jax.ShapeDtypeStruct((960, 512), BF),
            jax.ShapeDtypeStruct((32, 16, 512), BF),
        ),
        in_specs=[SM] + [VM] * 7 + [HB] * 2,
        out_specs=(HB, HB, VM),
        scratch_shapes=[
            pltpu.VMEM((48, 24, 512), F32),
            pltpu.VMEM((48, 24, 128), F32),
            pltpu.VMEM((15, 64, 128), F32),
            pltpu.VMEM((40, 24, 512), F32),
            pltpu.VMEM((960, 512), BF),
            pltpu.VMEM((960, 1536), BF),
            pltpu.VMEM((960, 512), BF),
            pltpu.VMEM((512, 1536), BF),
            pltpu.VMEM((512, 512), BF),
            pltpu.SemaphoreType.DMA((4,)),
        ],
        compiler_params=params(32),
        cost_estimate=pl.CostEstimate(flops=2 * 10**9, bytes_accessed=10 * 2**20, transcendentals=10**6),
        name="attn_fwd",
    )(place, left, own, right, slab, up, down, gain, w_qkv, w_proj)


def attn_bwd_kernel(
    place, first, own, second, up, down, qkv_hbm, probs_hbm, w_proj_hbm, w_qkv_hbm, tokens, gain,
    grad_out,
    grid, back, g_mixed, g_qkv, qkv, probs, w_proj, w_qkv, sems,
):
    pairs = ((w_proj_hbm, w_proj), (qkv_hbm, qkv), (probs_hbm, probs), (w_qkv_hbm, w_qkv))
    copies = fetch(pairs, sems)
    a, b = place[0], place[1]
    fill_grid(grid, b, place[3] == 1, first, own, second, up, down)
    masks, scaled = half_masks(1.0), half_masks(0.125)
    copies[0].wait()
    for n in range(3):
        ups = [window_of(grid, 5 * n + k, a).astype(BF) for k in range(5)]
        g_mixed[320 * n : 320 * n + 320] = dot_nt(jnp.concatenate(ups, 0), w_proj[...]).astype(BF)
    copies[1].wait()
    copies[2].wait()

    def window(w, carry):
        at = pl.ds(pl.multiple_of(w * 64, 64), 64)
        for c in range(2):
            lo = 256 * c
            qbig = spread(qkv[at, lo : lo + 256], scaled)
            gbig = spread(g_mixed[at, lo : lo + 256], masks)
            k = qkv[at, 512 + lo : 768 + lo]
            v = qkv[at, 1024 + lo : 1280 + lo]
            p = probs[at, lo : lo + 256]
            g_probs = dot_nt(v, gbig)
            wide_p = p.astype(F32)
            total = jnp.sum(wide_p * g_probs, 0, keepdims=True)
            g_score = (wide_p * (g_probs - total)).astype(BF)
            g_qkv[at, lo : lo + 256] = (collect(dot_tn(g_score, k)) * 0.125).astype(BF)
            g_qkv[at, 512 + lo : 768 + lo] = dot(g_score, qbig).astype(BF)
            g_qkv[at, 1024 + lo : 1280 + lo] = dot(p, gbig).astype(BF)
        return carry

    lax.fori_loop(0, 15, window, 0, unroll=True)
    copies[3].wait()
    for n in range(3):
        g_shift = dot_nt(g_qkv[320 * n : 320 * n + 320], w_qkv[...]).astype(BF).astype(F32)
        put_windows(back, n, g_shift)

    def finish(n, carry):
        at = pl.ds(8 * n, 8)
        part = norm_back(tokens[at].astype(F32), gain[...], place_back(back, n, a, b))
        grad_out[at] = (own[at].astype(F32) + part).astype(BF)
        return carry

    lax.fori_loop(0, 4, finish, 0, unroll=True)


def attn_bwd(place, left, own, right, up, down, qkv, probs, w_proj, w_qkv, tokens, gain):
    return pl.pallas_call(
        attn_bwd_kernel,
        out_shape=jax.ShapeDtypeStruct((32, 16, 512), BF),
        in_specs=[SM] + [VM] * 5 + [HB] * 4 + [VM] * 2,
        out_specs=VM,
        scratch_shapes=[
            pltpu.VMEM((48, 24, 512), F32),
            pltpu.VMEM((40, 24, 512), F32),
            pltpu.VMEM((960, 512), BF),
            pltpu.VMEM((960, 1536), BF),
            pltpu.VMEM((960, 1536), BF),
            pltpu.VMEM((960, 512), BF),
            pltpu.VMEM((512, 512), BF),
            pltpu.VMEM((512, 1536), BF),
            pltpu.SemaphoreType.DMA((4,)),
        ],
        compiler_params=params(32),
        cost_estimate=pl.CostEstimate(flops=4 * 10**9, bytes_accessed=10 * 2**20, transcendentals=0),
        name="attn_bwd",
    )(place, left, own, right, up, down, qkv, probs, w_proj, w_qkv, tokens, gain)


def set_fine(fine, value):
    for lane in range(4):
        fine[lane] = value[:, 128 * lane : 128 * lane + 128]


def get_fine(fine):
    return jnp.concatenate([fine[lane] for lane in range(4)], 1)


def patch_parts(fine):
    parts = {}
    for s in range(2):
        lanes = [fine[lane, pl.ds(s, 256, 2), :] for lane in range(4)]
        half = jnp.concatenate(lanes, 1).reshape(16, 2, 8, 512)
        for r in range(2):
            parts[r + 2 * s] = half[:, r].reshape(128, 512)
    return [parts[k] for k in range(4)]


def unpatch(fine, parts):
    for s in range(2):
        pair = [parts[r + 2 * s].reshape(16, 1, 8, 512) for r in range(2)]
        half = jnp.concatenate(pair, 1).reshape(256, 512)
        for lane in range(4):
            fine[lane, pl.ds(s, 256, 2), :] = half[:, 128 * lane : 128 * lane + 128]


def joint_normalise(parts):
    mean = sum(jnp.sum(p, -1, keepdims=True) for p in parts) / 2048.0
    cent = [p - mean for p in parts]
    var = sum(jnp.sum(c * c, -1, keepdims=True) for c in cent) / 2048.0
    r = lax.rsqrt(var + EPS)
    return [c * r for c in cent], r


def ffn_fwd_kernel(
    resid, gain_ffn, fc1_hbm, fc2_hbm, gain_merge, merge_hbm, gain_mlp,
    slope_out, block_out, coarse_out, cin_out,
    acc, fine, w_fc1, w_fc2, w_merge, sems,
):
    pairs = []
    for n in range(4):
        cut = pl.ds(512 * n, 512)
        pairs += [(fc1_hbm.at[:, cut], w_fc1.at[:, cut]), (fc2_hbm.at[cut], w_fc2.at[cut])]
    pairs += [(merge_hbm.at[pl.ds(512 * k, 512)], w_merge.at[pl.ds(512 * k, 512)]) for k in range(4)]
    copies = fetch(pairs, sems)
    xh, _ = normalise(resid[...].astype(F32))
    ffn_in = (xh * gain_ffn[...]).astype(BF)
    for n in range(4):
        cut = slice(512 * n, 512 * n + 512)
        copies[2 * n].wait()
        copies[2 * n + 1].wait()
        for m in range(2):
            rows = slice(256 * m, 256 * m + 256)
            hid, slope = gelu_both(dot(ffn_in[rows], w_fc1[:, cut]))
            slope_out[rows, cut] = slope
            term = dot(hid, w_fc2[cut, :])
            if n == 0:
                acc[rows, :] = resid[rows, :].astype(F32) + term
            else:
                acc[rows, :] += term
    block = acc[...].astype(BF)
    block_out[...] = block
    set_fine(fine, block.astype(F32))
    xhs, _ = joint_normalise(patch_parts(fine))
    coarse = None
    for k in range(4):
        cut = slice(512 * k, 512 * k + 512)
        copies[8 + k].wait()
        term = dot((xhs[k] * gain_merge[:, cut]).astype(BF), w_merge[cut, :])
        coarse = term if coarse is None else coarse + term
    coarse = coarse.astype(BF)
    coarse_out[...] = coarse
    xh, _ = normalise(coarse.astype(F32))
    cin_out[...] = (xh * gain_mlp[...]).astype(BF)


def ffn_fwd(resid, gain_ffn, w_fc1, w_fc2, gain_merge, w_merge, gain_mlp):
    return pl.pallas_call(
        ffn_fwd_kernel,
        out_shape=(
            jax.ShapeDtypeStruct((512, 2048), BF),
            jax.ShapeDtypeStruct((512, 512), BF),
            jax.ShapeDtypeStruct((128, 1024), BF),
            jax.ShapeDtypeStruct((128, 1024), BF),
        ),
        in_specs=[VM, VM, HB, HB, VM, HB, VM],
        out_specs=(VM, VM, VM, VM),
        scratch_shapes=[
            pltpu.VMEM((512, 512), F32),
            pltpu.VMEM((4, 512, 128), F32),
            pltpu.VMEM((512, 2048), BF),
            pltpu.VMEM((2048, 512), BF),
            pltpu.VMEM((2048, 1024), BF),
            pltpu.SemaphoreType.DMA((12,)),
        ],
        compiler_params=params(32),
        cost_estimate=pl.CostEstimate(flops=3 * 10**9, bytes_accessed=12 * 2**20, transcendentals=10**6),
        name="ffn_fwd",
    )(resid, gain_ffn, w_fc1, w_fc2, gain_merge, w_merge, gain_mlp)


def weight_chunk(parts, y, lo):
    rows = []
    for k in range(4):
        ref, at = (parts[y], 128 * k) if y < 3 else (parts[3 + k // 2], 128 * (k % 2))
        rows += [ref[at + lo : at + lo + 32], ref[at + 64 + lo : at + 96 + lo]]
    return jnp.concatenate(rows, 0)


def mlp_kernel(
    place, c0, c1, c2, c3, d0, d1, d2, d3, w0, w1, w2, w3, w4,
    keep_out, send_out, hid_out,
    cs, deep, gacc,
):
    for k, (c, g) in enumerate(((c0, d0), (c1, d1), (c2, d2), (c3, d3))):
        cs[128 * k : 128 * k + 128] = c[...]
        deep[128 * k : 128 * k + 128] = g[...]
    parts = (w0, w1, w2, w3, w4)
    for y in range(4):
        first = weight_chunk(parts, y, 0)
        second = weight_chunk(parts, y, 32)
        for m in range(2):
            rows = slice(256 * m, 256 * m + 256)
            hid, slope = gelu_both(dot_nt(cs[rows], first))
            hid_out[rows, 256 * y : 256 * y + 256] = hid
            g_pre = dot_nt(deep[rows], second).astype(BF) * slope
            g_cin = dot(g_pre, first)
            if y == 0:
                gacc[rows] = g_cin
            else:
                gacc[rows] += g_cin
    part_out(gacc, keep_out, send_out)


def part_out(total, keep_out, send_out):
    keep_out[0:128] = total[0:128].astype(BF)
    keep_out[128:256] = total[256:384].astype(BF)
    send_out[0:128] = total[128:256].astype(BF)
    send_out[128:256] = total[384:512].astype(BF)


def coarse_mlp(place, cins, deeps, parts):
    return pl.pallas_call(
        mlp_kernel,
        out_shape=(
            jax.ShapeDtypeStruct((256, 1024), BF),
            jax.ShapeDtypeStruct((256, 1024), BF),
            jax.ShapeDtypeStruct((512, 1024), BF),
        ),
        in_specs=[SM] + [VM] * 13,
        out_specs=(VM, VM, VM),
        scratch_shapes=[
            pltpu.VMEM((512, 1024), BF),
            pltpu.VMEM((512, 1024), BF),
            pltpu.VMEM((512, 1024), F32),
        ],
        compiler_params=params(32),
        cost_estimate=pl.CostEstimate(flops=3 * 10**9, bytes_accessed=8 * 2**20, transcendentals=10**6),
        name="coarse_mlp",
    )(place, *cins, *deeps, *parts)


def down_kernel(hid, w0, w1, w2, w3, w4, keep_out, send_out):
    total = None
    for y in range(4):
        term = dot(hid[:, 256 * y : 256 * y + 256], weight_chunk((w0, w1, w2, w3, w4), y, 32))
        total = term if total is None else total + term
    part_out(total, keep_out, send_out)


def down_of(hid, parts):
    half = jax.ShapeDtypeStruct((256, 1024), BF)
    return pl.pallas_call(
        down_kernel,
        out_shape=(half, half),
        in_specs=[VM] * 6,
        out_specs=(VM, VM),
        compiler_params=params(32),
        cost_estimate=pl.CostEstimate(flops=10**9, bytes_accessed=5 * 2**20, transcendentals=0),
        name="down",
    )(hid, *parts)


def g_deep_kernel(cot, up_hbm, out, fine, w_up, sems):
    cuts = [pl.ds(256 * k, 256) for k in range(4)]
    copies = fetch([(up_hbm.at[cut], w_up.at[cut]) for cut in cuts], sems)
    set_fine(fine, cot[...].astype(F32))
    whole = jnp.concatenate([part.astype(BF) for part in patch_parts(fine)], 1)
    for k in range(4):
        copies[k].wait()
        rows = slice(256 * k, 256 * k + 256)
        out[:, rows] = dot_nt(whole, w_up[rows, :]).astype(BF)


UP_SCRATCH = [
    pltpu.VMEM((4, 512, 128), F32),
    pltpu.VMEM((1024, 2048), BF),
    pltpu.SemaphoreType.DMA((4,)),
]


def g_deep_of(cot, w_up):
    return pl.pallas_call(
        g_deep_kernel,
        out_shape=jax.ShapeDtypeStruct((128, 1024), BF),
        in_specs=[VM, HB],
        out_specs=VM,
        scratch_shapes=UP_SCRATCH,
        compiler_params=params(32),
        cost_estimate=pl.CostEstimate(flops=10**9, bytes_accessed=5 * 2**20, transcendentals=0),
        name="g_deep",
    )(cot, w_up)


def up_kernel(coarse, keep, near, far, block, up_hbm, out, fine, w_up, sems):
    cuts = [pl.ds(256 * k, 256) for k in range(4)]
    copies = fetch([(up_hbm.at[cut], w_up.at[cut]) for cut in cuts], sems)
    deep = coarse[...].astype(F32) + keep[0:128].astype(F32) + near[0:128].astype(F32)
    deep = (deep + far[...].astype(F32)).astype(BF)
    acc = None
    for k in range(4):
        copies[k].wait()
        rows = slice(256 * k, 256 * k + 256)
        term = dot(deep[:, rows], w_up[rows, :])
        acc = term if acc is None else acc + term
    unpatch(fine, [acc[:, 512 * k : 512 * k + 512] for k in range(4)])
    out[...] = (block[...].astype(F32) + get_fine(fine)).astype(BF)


def up_of(coarse, keep, near, far, block, w_up):
    return pl.pallas_call(
        up_kernel,
        out_shape=jax.ShapeDtypeStruct((512, 512), BF),
        in_specs=[VM] * 5 + [HB],
        out_specs=VM,
        scratch_shapes=UP_SCRATCH,
        compiler_params=params(32),
        cost_estimate=pl.CostEstimate(flops=10**9, bytes_accessed=5 * 2**20, transcendentals=0),
        name="up",
    )(coarse, keep, near, far, block, w_up)


def ffn_bwd_kernel(
    place, gcin_own, gcin_near, gcin_far, g_deep, coarse, gain_mlp, merge_hbm, block, gain_merge, cot,
    fc2_hbm, slope_hbm, fc1_hbm, resid, gain_ffn,
    g_resid_out, first_out, second_out,
    fine, acc, w_merge, w_fc1, w_fc2, slope, sems,
):
    pairs = [(merge_hbm.at[pl.ds(512 * k, 512)], w_merge.at[pl.ds(512 * k, 512)]) for k in range(4)]
    for n in range(4):
        cut = pl.ds(512 * n, 512)
        pairs += [
            (fc2_hbm.at[cut], w_fc2.at[cut]),
            (slope_hbm.at[:, cut], slope.at[:, cut]),
            (fc1_hbm.at[:, cut], w_fc1.at[:, cut]),
        ]
    copies = fetch(pairs, sems)
    g_cin = gcin_own[0:128].astype(F32) + gcin_near[0:128].astype(F32) + gcin_far[...].astype(F32)
    g_cin = g_cin.astype(BF).astype(F32)
    part = norm_back(coarse[...].astype(F32), gain_mlp[...], g_cin)
    g_coarse = (g_deep[...].astype(F32) + part).astype(BF)
    set_fine(fine, block[...].astype(F32))
    xhs, r = joint_normalise(patch_parts(fine))
    scaled = []
    for k in range(4):
        cut = slice(512 * k, 512 * k + 512)
        copies[k].wait()
        scaled.append(dot_nt(g_coarse, w_merge[cut, :]) * gain_merge[:, cut])
    mean_s = sum(jnp.sum(s, -1, keepdims=True) for s in scaled) / 2048.0
    mean_x = sum(jnp.sum(s * x, -1, keepdims=True) for s, x in zip(scaled, xhs)) / 2048.0
    unpatch(fine, [r * (s - mean_s - x * mean_x) for s, x in zip(scaled, xhs)])
    g_block = (cot[...].astype(F32) + get_fine(fine)).astype(BF)
    for n in range(4):
        cut = slice(512 * n, 512 * n + 512)
        for k in range(3):
            copies[4 + 3 * n + k].wait()
        for m in range(2):
            rows = slice(256 * m, 256 * m + 256)
            g_pre = dot_nt(g_block[rows], w_fc2[cut, :]).astype(BF) * slope[rows, cut]
            term = dot_nt(g_pre, w_fc1[:, cut])
            if n == 0:
                acc[rows, :] = term
            else:
                acc[rows, :] += term
    g_fin = acc[...].astype(BF).astype(F32)
    part = norm_back(resid[...].astype(F32), gain_ffn[...], g_fin)
    total = g_block.astype(F32) + part
    g_resid_out[...] = total.astype(BF)
    lines = total.reshape(32, 16, 512)
    tail, head = sides(place[3] == 1, lines[:, :8], lines[:, 8:])
    first_out[...] = tail.astype(BF)
    second_out[...] = head.astype(BF)


def ffn_bwd(place, gcin_own, gcin_near, gcin_far, g_deep, coarse, gain_mlp, w_merge, block, gain_merge, cot,
            w_fc2, slope, w_fc1, resid, gain_ffn):
    return pl.pallas_call(
        ffn_bwd_kernel,
        out_shape=(
            jax.ShapeDtypeStruct((512, 512), BF),
            jax.ShapeDtypeStruct((32, 8, 512), BF),
            jax.ShapeDtypeStruct((32, 8, 512), BF),
        ),
        in_specs=[SM] + [VM] * 6 + [HB, VM, VM, VM, HB, HB, HB, VM, VM],
        out_specs=(VM, VM, VM),
        scratch_shapes=[
            pltpu.VMEM((4, 512, 128), F32),
            pltpu.VMEM((512, 512), F32),
            pltpu.VMEM((2048, 1024), BF),
            pltpu.VMEM((512, 2048), BF),
            pltpu.VMEM((2048, 512), BF),
            pltpu.VMEM((512, 2048), BF),
            pltpu.SemaphoreType.DMA((16,)),
        ],
        compiler_params=params(32),
        cost_estimate=pl.CostEstimate(flops=3 * 10**9, bytes_accessed=14 * 2**20, transcendentals=0),
        name="ffn_bwd",
    )(place, gcin_own, gcin_near, gcin_far, g_deep, coarse, gain_mlp, w_merge, block, gain_merge, cot,
      w_fc2, slope, w_fc1, resid, gain_ffn)


def ends_kernel(tokens, turned, first_out, second_out, slab_out):
    odd = (lax.axis_index("lon") & 1) == 1
    slab = jnp.concatenate([turned[...].astype(F32), jnp.zeros((16, 480), F32)], 1)
    slab_out[...] = slab.astype(BF)
    lines = tokens[...].astype(F32)
    for at, source in ((slice(0, 32), lines), (slice(32, 33), slab.reshape(1, 16, 512))):
        tail, head = sides(odd, source[:, :8], source[:, 8:])
        first_out[at] = tail.astype(BF)
        second_out[at] = head.astype(BF)


def ends(tokens, turned):
    part = jax.ShapeDtypeStruct((33, 8, 512), BF)
    return pl.pallas_call(
        ends_kernel,
        out_shape=(part, part, jax.ShapeDtypeStruct((16, 512), BF)),
        in_specs=[VM] * 2,
        out_specs=(VM,) * 3,
        compiler_params=params(32),
        cost_estimate=pl.CostEstimate(flops=10**6, bytes_accessed=2 * 2**20, transcendentals=0),
        name="ends",
    )(tokens, turned)


def cut_kernel(w_first, w_second, s0, s1, s2, s3, both):
    me = lax.axis_index("lat")
    both[0] = w_first[...].astype(F32).T.astype(BF)
    both[1] = w_second[...]
    for k, out in enumerate((s0, s1, s2, s3)):
        rows = pl.ds(pl.multiple_of(lax.bitwise_xor(me, k) * 32, 32), 32)
        out[0:32] = both[0, rows, :]
        out[32:64] = both[1, rows, :]


def cut(w_first, w_second):
    block = jax.ShapeDtypeStruct((64, 256), BF)
    return pl.pallas_call(
        cut_kernel,
        out_shape=(block,) * 4,
        in_specs=[VM] * 2,
        out_specs=(VM,) * 4,
        scratch_shapes=[pltpu.VMEM((2, 128, 256), BF)],
        compiler_params=params(32),
        cost_estimate=pl.CostEstimate(flops=10**6, bytes_accessed=2**19, transcendentals=0),
        name="cut",
    )(w_first, w_second)


def join_kernel(place, s0, s1, s2, s3, out):
    for k, block in enumerate((s0, s1, s2, s3)):
        at = pl.multiple_of(lax.bitwise_xor(place[2], k) * 256, 256)
        out[:, pl.ds(at, 256)] = block[...]


def join(place, blocks):
    return pl.pallas_call(
        join_kernel,
        out_shape=jax.ShapeDtypeStruct((64, 1024), BF),
        in_specs=[SM] + [VM] * 4,
        out_specs=VM,
        compiler_params=params(32),
        cost_estimate=pl.CostEstimate(flops=10**6, bytes_accessed=2**18, transcendentals=0),
        name="join",
    )(place, *blocks)


def stack_kernel(*refs):
    for k, ref in enumerate(refs[:-1]):
        refs[-1][128 * k : 128 * k + 128] = ref[...]


def stacked(blocks):
    return pl.pallas_call(
        stack_kernel,
        out_shape=jax.ShapeDtypeStruct((512, 1024), BF),
        in_specs=[VM] * 4,
        out_specs=VM,
        compiler_params=params(32),
        cost_estimate=pl.CostEstimate(flops=10**6, bytes_accessed=2**21, transcendentals=0),
        name="stacked",
    )(*blocks)


def halves_kernel(ahead, behind, first, second):
    first[...] = ahead[0:256]
    second[...] = behind[256:512]


def halves(ahead, behind):
    half = jax.ShapeDtypeStruct((256, 1024), BF)
    return pl.pallas_call(
        halves_kernel,
        out_shape=(half, half),
        in_specs=[VM] * 2,
        out_specs=(VM, VM),
        compiler_params=params(32),
        cost_estimate=pl.CostEstimate(flops=10**6, bytes_accessed=2**21, transcendentals=0),
        name="halves",
    )(ahead, behind)


def strips_kernel(place, first, own, second, *rest):
    odd = place[3] == 1
    top_out, bottom_out = rest[-2:]
    for out, lo in ((top_out, 0), (bottom_out, 24)):
        rows = slice(lo, lo + 8)
        left, right = sides(odd, first[rows].astype(F32), second[rows].astype(F32))
        out[0:8, 0:8, :] = left.astype(BF)
        out[0:8, 8:24, :] = own[rows]
        out[0:8, 24:32, :] = right.astype(BF)
        if len(rest) == 3:
            left, right = sides(odd, first[32].astype(F32), second[32].astype(F32))
            out[8] = jnp.concatenate([left, rest[0][...].astype(F32), right], 0).astype(BF)


def strips(place, first, own, second, *slab):
    edge = jax.ShapeDtypeStruct((8 + len(slab), 32, 512), BF)
    return pl.pallas_call(
        strips_kernel,
        out_shape=(edge, edge),
        in_specs=[SM] + [VM] * (3 + len(slab)),
        out_specs=(VM, VM),
        compiler_params=params(32),
        cost_estimate=pl.CostEstimate(flops=10**6, bytes_accessed=3 * 2**20, transcendentals=0),
        name="strips",
    )(place, first, own, second, *slab)


def along(axis, count, step):
    pairs = [(s, (s + step) % count) for s in range(count)]
    return lambda v: lax.ppermute(v, axis, pairs)


LAT_NEXT, LAT_PREV = along("lat", 4, 1), along("lat", 4, -1)


def even_odd(v):
    return lax.ppermute(v, "lon", [(k, k ^ 1) for k in range(32)])


def odd_even(v):
    return lax.ppermute(v, "lon", [(k, (((k + 1) ^ 1) - 1) % 32) for k in range(32)])


def core_swap(v):
    return lax.ppermute(v, "lat", [(0, 1), (1, 0), (2, 3), (3, 2)])


def x_swap(v):
    return lax.ppermute(v, "lat", [(0, 2), (2, 0), (1, 3), (3, 1)])


def cross_swap(v):
    return lax.ppermute(v, "lat", [(0, 3), (3, 0), (1, 2), (2, 1)])


def x_far_swap(v):
    return lax.ppermute(v, "lon", [(k, (k + 16) % 32) for k in range(32)])


def turn(swapped, k):
    pairs = []
    for lat in range(4):
        along_y = (lat % 2 == 1) != swapped
        for lon in range(32):
            x, y, z = lon // 16, lon // 4 % 4, lon % 4
            if along_y:
                y = (y + k) % 4
            else:
                z = (z + k) % 4
            pairs.append((lat * 32 + lon, lat * 32 + (x * 4 + y) * 4 + z))
    return lambda v: lax.ppermute(v, ("lat", "lon"), pairs)


def after(value, *gates):
    return lax.optimization_barrier((value,) + gates)[0]


def on_device(
    tokens, labels, offsets, gain_attn, w_qkv, w_proj, gain_ffn, w_fc1, w_fc2,
    gain_merge, w_merge, gain_mlp, w_first, w_second, w_up, cotangent,
):
    row = lambda g: g.reshape(1, -1)
    s0, s1, s2, s3 = cut(w_first, w_second)
    s1, s2, s3 = core_swap(s1), x_swap(s2), cross_swap(s3)
    first, second, slab = ends(after(tokens, s0), labels.T)
    left, right = even_odd(first), odd_even(second)
    where = [lax.axis_index("lat"), lax.axis_index("lon") & 1]
    place = jnp.concatenate([after(offsets, slab), jnp.stack(where).astype(jnp.int32)])
    mine = join(place, (s0, s1, s2, s3))
    other = x_far_swap(mine)
    cot = cotangent.reshape(512, 512)
    g_deep = g_deep_of(after(cot, mine), w_up)
    near_deep = core_swap(g_deep)
    seed = jnp.concatenate([mine, after(other, g_deep)], 0)
    moved = [turn(False, k)(seed) for k in (1, -1, 2)]
    bottom, top = strips(place, left, after(tokens, seed), right, slab)
    up, down = LAT_NEXT(top), LAT_PREV(bottom)
    part = stacked([after(seed, up, down)] + moved)
    ahead, behind = turn(True, 1)(part), turn(True, -1)(part)
    qkv, probs, resid = attn_fwd(
        place, left, tokens, right, slab, after(up, part), down, row(gain_attn), w_qkv, w_proj
    )
    resid = resid.reshape(512, 512)
    far_deep = x_swap(after(g_deep, resid))
    slope, block, coarse, coarse_in = ffn_fwd(
        resid, row(gain_ffn), w_fc1, w_fc2, row(gain_merge), w_merge, row(gain_mlp)
    )
    fore, hind = halves(after(ahead, coarse_in), behind)
    far_cin = x_swap(coarse_in)
    near_cin = core_swap(coarse_in)
    parts = [part, ahead, behind, turn(True, 1)(fore), turn(True, -1)(hind)]
    cins = [coarse_in, near_cin, far_cin, core_swap(far_cin)]
    deeps = [g_deep, near_deep, far_deep, core_swap(after(far_deep, coarse_in))]
    keep, send, hid = coarse_mlp(place, cins, deeps, parts)
    near = core_swap(send)
    gcin_far = x_swap((keep[128:].astype(F32) + near[128:].astype(F32)).astype(BF))
    down_keep, down_send = down_of(hid, parts)
    down_near = core_swap(down_send)
    down_far = (down_keep[128:].astype(F32) + down_near[128:].astype(F32)).astype(BF)
    gcin_far, down_far = lax.optimization_barrier((gcin_far, down_far))
    down_far = x_swap(down_far)
    g_resid, g_first, g_second = ffn_bwd(
        place, keep, near, gcin_far, g_deep, coarse, row(gain_mlp), w_merge, block, row(gain_merge), cot,
        w_fc2, slope, w_fc1, resid, row(gain_ffn),
    )
    g_resid = g_resid.reshape(32, 16, 512)
    g_left, g_right = even_odd(g_first), odd_even(g_second)
    field_out = up_of(coarse, down_keep, down_near, down_far, block, w_up).reshape(32, 16, 512)
    g_bottom, g_top = strips(place, g_left, after(g_resid, field_out), g_right)
    g_up, g_down = LAT_NEXT(g_top), LAT_PREV(g_bottom)
    grad_in = attn_bwd(
        place, g_left, g_resid, g_right, g_up, g_down, qkv, probs, w_proj, w_qkv, tokens,
        row(gain_attn),
    )
    return (field_out, grad_in)


def solution(mesh):
    grid = P("lat", "lon", None)
    placed = (
        grid, P("lat", "lon"), P(), P(), P(), P(), P(), P(), P(), P(), P(), P(),
        P("lat", "lon"), P("lon", "lat"), P(), grid,
    )
    return jax.shard_map(
        on_device, mesh=mesh, in_specs=placed, out_specs=(grid, grid), check_vma=False
    )
```

```python
import jax
import jax.numpy as jnp
from jax import lax
from jax.experimental import pallas as pl
from jax.experimental.pallas import tpu as pltpu
from jax.sharding import PartitionSpec as P

BF = jnp.bfloat16
F32 = jnp.float32
EPS = 1e-05
NT = (((1,), (1,)), ((), ()))
TN = (((0,), (0,)), ((), ()))
GELU_C = 0.7978845608028654
GELU_A = 0.044715


def dot(a, b):
    return jnp.dot(a, b, preferred_element_type=F32)


def dot_nt(a, b):
    return lax.dot_general(a, b, NT, preferred_element_type=F32)


def dot_tn(a, b):
    return lax.dot_general(a, b, TN, preferred_element_type=F32)


def normalise(v):
    mean = jnp.mean(v, -1, keepdims=True)
    c = v - mean
    r = lax.rsqrt(jnp.mean(c * c, -1, keepdims=True) + EPS)
    return c * r, r


def norm_back(v, gain, t):
    xh, r = normalise(v)
    s = t * gain
    return r * (s - jnp.mean(s, -1, keepdims=True) - xh * jnp.mean(s * xh, -1, keepdims=True))


def gelu_both(wide):
    x = wide.astype(BF)
    x2 = x * x
    t = jnp.tanh(x * (GELU_C + GELU_C * GELU_A * x2))
    h = 0.5 * x
    slope = (0.5 + 0.5 * t) + (h - h * t * t) * (GELU_C + 3.0 * GELU_C * GELU_A * x2)
    return h + h * t, slope


def half_masks(scale):
    low = lax.broadcasted_iota(jnp.int32, (1, 128), 1) < 64
    return [jnp.where(m, scale, 0.0).astype(F32).astype(BF) for m in (low, jnp.logical_not(low))]


def spread(x, masks):
    none = jnp.zeros((64, 128), BF)
    left, right = x[:, :128], x[:, 128:]
    rows = [jnp.concatenate([left * m, none], 1) for m in masks]
    rows += [jnp.concatenate([none, right * m], 1) for m in masks]
    return jnp.concatenate(rows, 0)


def collect(big):
    low = lax.broadcasted_iota(jnp.int32, (64, 128), 1) < 64
    left = jnp.where(low, big[0:64, :128], big[64:128, :128])
    right = jnp.where(low, big[128:192, 128:], big[192:256, 128:])
    return jnp.concatenate([left, right], 1)


def sides(odd, first, second):
    return jnp.where(odd, first, second), jnp.where(odd, second, first)


def shifted_cols(lines, b):
    return pltpu.roll(lines, 32 - b, 1)[:, :24]


def fill_middle(grid, b, odd, first, own, second):
    def rows(n, carry):
        at = pl.ds(8 * n, 8)
        left, right = sides(odd, first[at].astype(F32), second[at].astype(F32))
        grid[at] = shifted_cols(jnp.concatenate([left, own[at].astype(F32), right], 1), b)
        return carry

    lax.fori_loop(0, 4, rows, 0)


def fill_edges(grid, b, edges):
    for n, edge in enumerate(edges):
        grid[8 * n : 8 * n + 8] = shifted_cols(edge[0:8].astype(F32), b)


def slab_cols(slab, b):
    return pltpu.roll(slab, 32 - b, 0)[:24]


def place_back(back, n, a, b):
    return pltpu.roll(back[pl.ds(8 - a + 8 * n, 8)], 16 + b, 1)[:, :16]


def fetch(pairs, sems):
    copies = [pltpu.make_async_copy(src, dst, sems.at[k]) for k, (src, dst) in enumerate(pairs)]
    for copy in copies:
        copy.start()
    return copies


def windows_of(grid, base, a):
    lines = grid[pl.ds(a + base, 8)]
    return [lines[:, 8 * k : 8 * k + 8].reshape(64, grid.shape[2]) for k in range(3)]


def put_windows(back, row, value):
    for k in range(3):
        part = value[64 * k : 64 * k + 64].reshape(8, 8, 512)
        back[row : row + 8, 8 * k : 8 * k + 8, :] = part


def fwd_windows(grid, codes, cols, mixed, qkv, probs, gain, w_qkv, bases, a, after_qkv):
    for n, base in enumerate(bases):
        normed = [(normalise(x)[0] * gain[...]).astype(BF) for x in windows_of(grid, base, a)]
        qkv[192 * n : 192 * n + 192] = dot(jnp.concatenate(normed, 0), w_qkv[...]).astype(BF)
        for k, col in enumerate(windows_of(codes, base, a)):
            cols[3 * n + k] = col
    after_qkv()
    masks = half_masks(0.125)

    def window(w, carry):
        at = pl.ds(pl.multiple_of(w * 64, 64), 64)
        col = cols[w]
        row = col.T[0:1, 0:64]
        same = jnp.concatenate([col, col], 1) == jnp.concatenate([row] * 4, 1)
        for c in range(2):
            lo = 256 * c
            qbig = spread(qkv[at, lo : lo + 256], masks)
            k = qkv[at, 512 + lo : 768 + lo]
            v = qkv[at, 1024 + lo : 1280 + lo]
            e = jnp.where(same, jnp.exp(dot_nt(k, qbig)), 0.0)
            p = (e * (1.0 / jnp.sum(e, 0, keepdims=True))).astype(BF)
            probs[at, lo : lo + 256] = p
            mixed[at, lo : lo + 256] = collect(dot_tn(p, v)).astype(BF)
        return carry

    lax.fori_loop(0, 3 * len(bases), window, 0, unroll=True)


def fwd_middle_kernel(
    place, first, own, second, own_slab, gain, w_qkv_hbm, w_proj_hbm,
    qkv_hbm, probs_hbm, back,
    grid, codes, cols, mixed, qkv, probs, w_qkv, w_proj, sems,
):
    copies = fetch(((w_qkv_hbm, w_qkv), (w_proj_hbm, w_proj)), sems)
    qkv_copy = pltpu.make_async_copy(qkv, qkv_hbm, sems.at[2])
    probs_copy = pltpu.make_async_copy(probs, probs_hbm, sems.at[3])
    a, b = place[0], place[1]
    odd = place[3] == 1
    fill_middle(grid, b, odd, first, own, second)
    left, right = sides(odd, first[32].astype(F32), second[32].astype(F32))
    slab = slab_cols(jnp.concatenate([left, own_slab[...].astype(F32), right], 0), b)
    for r in range(32):
        codes[r] = jnp.broadcast_to(slab[:, r : r + 1], (24, 128))
    copies[0].wait()
    bases = (0, 8, 16)
    fwd_windows(grid, codes, cols, mixed, qkv, probs, gain, w_qkv, bases, a, qkv_copy.start)
    probs_copy.start()
    copies[1].wait()
    for n in range(3):
        att = dot(mixed[192 * n : 192 * n + 192], w_proj[...]).astype(BF).astype(F32)
        put_windows(back, 8 * n, att)
    qkv_copy.wait()
    probs_copy.wait()


def fwd_edge_kernel(
    place, up, bottom, top, down, own, middle, gain, w_qkv_hbm, w_proj_hbm,
    qkv_hbm, probs_hbm, resid_out,
    grid, codes, cols, mixed, qkv, probs, w_qkv, w_proj, back, sems,
):
    copies = fetch(((w_qkv_hbm, w_qkv), (w_proj_hbm, w_proj)), sems)
    qkv_copy = pltpu.make_async_copy(qkv, qkv_hbm, sems.at[2])
    probs_copy = pltpu.make_async_copy(probs, probs_hbm, sems.at[3])
    a, b, d = place[0], place[1], place[2]
    edges = (up, bottom, top, down)
    fill_edges(grid, b, edges)
    extra = (jnp.where(d == 0, 4.0, 0.0), 0.0, 0.0, jnp.where(d == 3, 4.0, 0.0))
    for n, (edge, lane, code) in enumerate(zip(edges, (24, 0, 24, 0), extra)):
        slab = slab_cols(edge[8].astype(F32) + code, b)
        for r in range(8):
            codes[8 * n + r] = jnp.broadcast_to(slab[:, lane + r : lane + r + 1], (24, 128))
    copies[0].wait()
    bases = (0, 16)
    fwd_windows(grid, codes, cols, mixed, qkv, probs, gain, w_qkv, bases, a, qkv_copy.start)
    probs_copy.start()
    back[8:32] = middle[...]
    copies[1].wait()
    for n in range(2):
        att = dot(mixed[192 * n : 192 * n + 192], w_proj[...]).astype(BF).astype(F32)
        put_windows(back, 32 * n, att)
    for n in range(4):
        at = slice(8 * n, 8 * n + 8)
        resid_out[at] = (own[at].astype(F32) + place_back(back, n, a, b)).astype(BF)
    qkv_copy.wait()
    probs_copy.wait()


def bwd_windows(grid, g_mixed, g_qkv, qkv, probs, w_proj, bases, a, ready):
    for n, base in enumerate(bases):
        ups = jnp.concatenate([x.astype(BF) for x in windows_of(grid, base, a)], 0)
        g_mixed[192 * n : 192 * n + 192] = dot_nt(ups, w_proj[...]).astype(BF)
    ready()
    masks, scaled = half_masks(1.0), half_masks(0.125)

    def window(w, carry):
        at = pl.ds(pl.multiple_of(w * 64, 64), 64)
        for c in range(2):
            lo = 256 * c
            qbig = spread(qkv[at, lo : lo + 256], scaled)
            gbig = spread(g_mixed[at, lo : lo + 256], masks)
            k = qkv[at, 512 + lo : 768 + lo]
            v = qkv[at, 1024 + lo : 1280 + lo]
            p = probs[at, lo : lo + 256]
            g_probs = dot_nt(v, gbig)
            wide_p = p.astype(F32)
            total = jnp.sum(wide_p * g_probs, 0, keepdims=True)
            g_score = (wide_p * (g_probs - total)).astype(BF)
            g_qkv[at, lo : lo + 256] = (collect(dot_tn(g_score, k)) * 0.125).astype(BF)
            g_qkv[at, 512 + lo : 768 + lo] = dot(g_score, qbig).astype(BF)
            g_qkv[at, 1024 + lo : 1280 + lo] = dot(p, gbig).astype(BF)
        return carry

    lax.fori_loop(0, 3 * len(bases), window, 0, unroll=True)


def bwd_middle_kernel(
    place, first, own, second, qkv_hbm, probs_hbm, w_proj_hbm, w_qkv_hbm,
    back,
    grid, g_mixed, g_qkv, qkv, probs, w_proj, w_qkv, sems,
):
    pairs = ((w_proj_hbm, w_proj), (qkv_hbm, qkv), (probs_hbm, probs), (w_qkv_hbm, w_qkv))
    copies = fetch(pairs, sems)

    def ready():
        copies[1].wait()
        copies[2].wait()

    a, b = place[0], place[1]
    fill_middle(grid, b, place[3] == 1, first, own, second)
    copies[0].wait()
    bwd_windows(grid, g_mixed, g_qkv, qkv, probs, w_proj, (0, 8, 16), a, ready)
    copies[3].wait()
    for n in range(3):
        g_shift = dot_nt(g_qkv[192 * n : 192 * n + 192], w_qkv[...]).astype(BF).astype(F32)
        put_windows(back, 8 * n, g_shift)


def bwd_edge_kernel(
    place, up, bottom, top, down, own, middle, qkv_hbm, probs_hbm, w_proj_hbm, w_qkv_hbm,
    tokens, gain,
    grad_out,
    grid, g_mixed, g_qkv, qkv, probs, w_proj, w_qkv, back, sems,
):
    pairs = ((w_proj_hbm, w_proj), (qkv_hbm, qkv), (probs_hbm, probs), (w_qkv_hbm, w_qkv))
    copies = fetch(pairs, sems)

    def ready():
        copies[1].wait()
        copies[2].wait()

    a, b = place[0], place[1]
    fill_edges(grid, b, (up, bottom, top, down))
    copies[0].wait()
    bwd_windows(grid, g_mixed, g_qkv, qkv, probs, w_proj, (0, 16), a, ready)
    back[8:32] = middle[...]
    copies[3].wait()
    for n in range(2):
        g_shift = dot_nt(g_qkv[192 * n : 192 * n + 192], w_qkv[...]).astype(BF).astype(F32)
        put_windows(back, 32 * n, g_shift)
    for n in range(4):
        at = slice(8 * n, 8 * n + 8)
        part = norm_back(tokens[at].astype(F32), gain[...], place_back(back, n, a, b))
        grad_out[at] = (own[at].astype(F32) + part).astype(BF)


VM = pl.BlockSpec(memory_space=pltpu.VMEM)
SM = pl.BlockSpec(memory_space=pltpu.SMEM)
HB = pl.BlockSpec(memory_space=pltpu.HBM)


def params(mib):
    return pltpu.CompilerParams(vmem_limit_bytes=mib * 2**20)


def attn_scratch(rows, backward):
    shapes = [(32, 24, 512, F32)]
    if not backward:
        shapes += [(32, 24, 128, F32), (rows // 64, 64, 128, F32), (rows, 512, BF)]
    else:
        shapes += [(rows, 512, BF), (rows, 1536, BF)]
    shapes += [(rows, 1536, BF), (rows, 512, BF)]
    shapes += [(512, 512, BF), (512, 1536, BF)] if backward else [(512, 1536, BF), (512, 512, BF)]
    if rows == 384:
        shapes += [(40, 24, 512, F32)]
    return [pltpu.VMEM(shape[:-1], shape[-1]) for shape in shapes] + [pltpu.SemaphoreType.DMA((4,))]


MIDDLE = jax.ShapeDtypeStruct((24, 24, 512), F32)
FINE = jax.ShapeDtypeStruct((32, 16, 512), BF)


def attention(kernel, name, rows, backward, specs, outs, out_specs, flops, operands):
    return pl.pallas_call(
        kernel,
        out_shape=outs,
        in_specs=specs,
        out_specs=out_specs,
        scratch_shapes=attn_scratch(rows, backward),
        compiler_params=params(32),
        cost_estimate=pl.CostEstimate(flops=flops, bytes_accessed=6 * 2**20, transcendentals=10**5),
        name=name,
    )(*operands)


def kept(rows):
    return (jax.ShapeDtypeStruct((rows, 1536), BF), jax.ShapeDtypeStruct((rows, 512), BF))


def fwd_middle(*operands):
    return attention(
        fwd_middle_kernel, "fwd_middle", 576, False, [SM] + [VM] * 5 + [HB] * 2,
        kept(576) + (MIDDLE,), (HB, HB, VM), 10**9, operands,
    )


def fwd_edge(*operands):
    return attention(
        fwd_edge_kernel, "fwd_edge", 384, False, [SM] + [VM] * 7 + [HB] * 2,
        kept(384) + (FINE,), (HB, HB, VM), 10**9, operands,
    )


def bwd_middle(*operands):
    return attention(
        bwd_middle_kernel, "bwd_middle", 576, True, [SM] + [VM] * 3 + [HB] * 4,
        MIDDLE, VM, 2 * 10**9, operands,
    )


def bwd_edge(*operands):
    return attention(
        bwd_edge_kernel, "bwd_edge", 384, True, [SM] + [VM] * 6 + [HB] * 4 + [VM] * 2,
        FINE, VM, 2 * 10**9, operands,
    )


def set_fine(fine, value):
    for lane in range(4):
        fine[lane] = value[:, 128 * lane : 128 * lane + 128]


def get_fine(fine):
    return jnp.concatenate([fine[lane] for lane in range(4)], 1)


def patch_parts(fine):
    parts = {}
    for s in range(2):
        lanes = [fine[lane, pl.ds(s, 256, 2), :] for lane in range(4)]
        half = jnp.concatenate(lanes, 1).reshape(16, 2, 8, 512)
        for r in range(2):
            parts[r + 2 * s] = half[:, r].reshape(128, 512)
    return [parts[k] for k in range(4)]


def unpatch(fine, parts):
    for s in range(2):
        pair = [parts[r + 2 * s].reshape(16, 1, 8, 512) for r in range(2)]
        half = jnp.concatenate(pair, 1).reshape(256, 512)
        for lane in range(4):
            fine[lane, pl.ds(s, 256, 2), :] = half[:, 128 * lane : 128 * lane + 128]


def joint_normalise(parts):
    mean = sum(jnp.sum(p, -1, keepdims=True) for p in parts) / 2048.0
    cent = [p - mean for p in parts]
    var = sum(jnp.sum(c * c, -1, keepdims=True) for c in cent) / 2048.0
    r = lax.rsqrt(var + EPS)
    return [c * r for c in cent], r


def ffn_fwd_kernel(
    resid, gain_ffn, fc1_hbm, fc2_hbm, gain_merge, merge_hbm, gain_mlp,
    slope_out, block_out, coarse_out, cin_out,
    acc, fine, w_fc1, w_fc2, w_merge, sems,
):
    pairs = []
    for n in range(4):
        cut = pl.ds(512 * n, 512)
        pairs += [(fc1_hbm.at[:, cut], w_fc1.at[:, cut]), (fc2_hbm.at[cut], w_fc2.at[cut])]
    pairs += [(merge_hbm.at[pl.ds(512 * k, 512)], w_merge.at[pl.ds(512 * k, 512)]) for k in range(4)]
    copies = fetch(pairs, sems)
    xh, _ = normalise(resid[...].astype(F32))
    ffn_in = (xh * gain_ffn[...]).astype(BF)
    for n in range(4):
        cut = slice(512 * n, 512 * n + 512)
        copies[2 * n].wait()
        copies[2 * n + 1].wait()
        for m in range(2):
            rows = slice(256 * m, 256 * m + 256)
            hid, slope = gelu_both(dot(ffn_in[rows], w_fc1[:, cut]))
            slope_out[rows, cut] = slope
            term = dot(hid, w_fc2[cut, :])
            if n == 0:
                acc[rows, :] = resid[rows, :].astype(F32) + term
            else:
                acc[rows, :] += term
    block = acc[...].astype(BF)
    block_out[...] = block
    set_fine(fine, block.astype(F32))
    xhs, _ = joint_normalise(patch_parts(fine))
    coarse = None
    for k in range(4):
        cut = slice(512 * k, 512 * k + 512)
        copies[8 + k].wait()
        term = dot((xhs[k] * gain_merge[:, cut]).astype(BF), w_merge[cut, :])
        coarse = term if coarse is None else coarse + term
    coarse = coarse.astype(BF)
    coarse_out[...] = coarse
    xh, _ = normalise(coarse.astype(F32))
    cin_out[...] = (xh * gain_mlp[...]).astype(BF)


def ffn_fwd(resid, gain_ffn, w_fc1, w_fc2, gain_merge, w_merge, gain_mlp):
    return pl.pallas_call(
        ffn_fwd_kernel,
        out_shape=(
            jax.ShapeDtypeStruct((512, 2048), BF),
            jax.ShapeDtypeStruct((512, 512), BF),
            jax.ShapeDtypeStruct((128, 1024), BF),
            jax.ShapeDtypeStruct((128, 1024), BF),
        ),
        in_specs=[VM, VM, HB, HB, VM, HB, VM],
        out_specs=(VM, VM, VM, VM),
        scratch_shapes=[
            pltpu.VMEM((512, 512), F32),
            pltpu.VMEM((4, 512, 128), F32),
            pltpu.VMEM((512, 2048), BF),
            pltpu.VMEM((2048, 512), BF),
            pltpu.VMEM((2048, 1024), BF),
            pltpu.SemaphoreType.DMA((12,)),
        ],
        compiler_params=params(32),
        cost_estimate=pl.CostEstimate(flops=3 * 10**9, bytes_accessed=12 * 2**20, transcendentals=10**6),
        name="ffn_fwd",
    )(resid, gain_ffn, w_fc1, w_fc2, gain_merge, w_merge, gain_mlp)


def weight_chunk(parts, y, lo):
    rows = []
    for k in range(4):
        ref, at = (parts[y], 128 * k) if y < 3 else (parts[3 + k // 2], 128 * (k % 2))
        rows += [ref[at + lo : at + lo + 32], ref[at + 64 + lo : at + 96 + lo]]
    return jnp.concatenate(rows, 0)


def mlp_kernel(
    place, c0, c1, c2, c3, d0, d1, d2, d3, w0, w1, w2, w3, w4,
    keep_out, send_out, hid_out,
    cs, deep, gacc,
):
    for k, (c, g) in enumerate(((c0, d0), (c1, d1), (c2, d2), (c3, d3))):
        cs[128 * k : 128 * k + 128] = c[...]
        deep[128 * k : 128 * k + 128] = g[...]
    parts = (w0, w1, w2, w3, w4)
    for y in range(4):
        first = weight_chunk(parts, y, 0)
        second = weight_chunk(parts, y, 32)
        for m in range(2):
            rows = slice(256 * m, 256 * m + 256)
            hid, slope = gelu_both(dot_nt(cs[rows], first))
            hid_out[rows, 256 * y : 256 * y + 256] = hid
            g_pre = dot_nt(deep[rows], second).astype(BF) * slope
            g_cin = dot(g_pre, first)
            if y == 0:
                gacc[rows] = g_cin
            else:
                gacc[rows] += g_cin
    part_out(gacc, keep_out, send_out)


def part_out(total, keep_out, send_out):
    keep_out[0:128] = total[0:128].astype(BF)
    keep_out[128:256] = total[256:384].astype(BF)
    send_out[0:128] = total[128:256].astype(BF)
    send_out[128:256] = total[384:512].astype(BF)


def coarse_mlp(place, cins, deeps, parts):
    return pl.pallas_call(
        mlp_kernel,
        out_shape=(
            jax.ShapeDtypeStruct((256, 1024), BF),
            jax.ShapeDtypeStruct((256, 1024), BF),
            jax.ShapeDtypeStruct((512, 1024), BF),
        ),
        in_specs=[SM] + [VM] * 13,
        out_specs=(VM, VM, VM),
        scratch_shapes=[
            pltpu.VMEM((512, 1024), BF),
            pltpu.VMEM((512, 1024), BF),
            pltpu.VMEM((512, 1024), F32),
        ],
        compiler_params=params(32),
        cost_estimate=pl.CostEstimate(flops=3 * 10**9, bytes_accessed=8 * 2**20, transcendentals=10**6),
        name="coarse_mlp",
    )(place, *cins, *deeps, *parts)


def down_kernel(hid, w0, w1, w2, w3, w4, keep_out, send_out):
    total = None
    for y in range(4):
        term = dot(hid[:, 256 * y : 256 * y + 256], weight_chunk((w0, w1, w2, w3, w4), y, 32))
        total = term if total is None else total + term
    part_out(total, keep_out, send_out)


def down_of(hid, parts):
    half = jax.ShapeDtypeStruct((256, 1024), BF)
    return pl.pallas_call(
        down_kernel,
        out_shape=(half, half),
        in_specs=[VM] * 6,
        out_specs=(VM, VM),
        compiler_params=params(32),
        cost_estimate=pl.CostEstimate(flops=10**9, bytes_accessed=5 * 2**20, transcendentals=0),
        name="down",
    )(hid, *parts)


def g_deep_kernel(cot, up_hbm, out, fine, w_up, sems):
    cuts = [pl.ds(256 * k, 256) for k in range(4)]
    copies = fetch([(up_hbm.at[cut], w_up.at[cut]) for cut in cuts], sems)
    set_fine(fine, cot[...].astype(F32))
    whole = jnp.concatenate([part.astype(BF) for part in patch_parts(fine)], 1)
    for k in range(4):
        copies[k].wait()
        rows = slice(256 * k, 256 * k + 256)
        out[:, rows] = dot_nt(whole, w_up[rows, :]).astype(BF)


UP_SCRATCH = [
    pltpu.VMEM((4, 512, 128), F32),
    pltpu.VMEM((1024, 2048), BF),
    pltpu.SemaphoreType.DMA((4,)),
]


def g_deep_of(cot, w_up):
    return pl.pallas_call(
        g_deep_kernel,
        out_shape=jax.ShapeDtypeStruct((128, 1024), BF),
        in_specs=[VM, HB],
        out_specs=VM,
        scratch_shapes=UP_SCRATCH,
        compiler_params=params(32),
        cost_estimate=pl.CostEstimate(flops=10**9, bytes_accessed=5 * 2**20, transcendentals=0),
        name="g_deep",
    )(cot, w_up)


def up_kernel(coarse, keep, near, far, block, up_hbm, out, fine, w_up, sems):
    cuts = [pl.ds(256 * k, 256) for k in range(4)]
    copies = fetch([(up_hbm.at[cut], w_up.at[cut]) for cut in cuts], sems)
    deep = coarse[...].astype(F32) + keep[0:128].astype(F32) + near[0:128].astype(F32)
    deep = (deep + far[...].astype(F32)).astype(BF)
    acc = None
    for k in range(4):
        copies[k].wait()
        rows = slice(256 * k, 256 * k + 256)
        term = dot(deep[:, rows], w_up[rows, :])
        acc = term if acc is None else acc + term
    unpatch(fine, [acc[:, 512 * k : 512 * k + 512] for k in range(4)])
    out[...] = (block[...].astype(F32) + get_fine(fine)).astype(BF)


def up_of(coarse, keep, near, far, block, w_up):
    return pl.pallas_call(
        up_kernel,
        out_shape=jax.ShapeDtypeStruct((512, 512), BF),
        in_specs=[VM] * 5 + [HB],
        out_specs=VM,
        scratch_shapes=UP_SCRATCH,
        compiler_params=params(32),
        cost_estimate=pl.CostEstimate(flops=10**9, bytes_accessed=5 * 2**20, transcendentals=0),
        name="up",
    )(coarse, keep, near, far, block, w_up)


def ffn_bwd_kernel(
    place, gcin_own, gcin_near, gcin_far, g_deep, coarse, gain_mlp, merge_hbm, block, gain_merge, cot,
    fc2_hbm, slope_hbm, fc1_hbm, resid, gain_ffn,
    g_resid_out, first_out, second_out,
    fine, acc, w_merge, w_fc1, w_fc2, slope, sems,
):
    pairs = [(merge_hbm.at[pl.ds(512 * k, 512)], w_merge.at[pl.ds(512 * k, 512)]) for k in range(4)]
    for n in range(4):
        cut = pl.ds(512 * n, 512)
        pairs += [
            (fc2_hbm.at[cut], w_fc2.at[cut]),
            (slope_hbm.at[:, cut], slope.at[:, cut]),
            (fc1_hbm.at[:, cut], w_fc1.at[:, cut]),
        ]
    copies = fetch(pairs, sems)
    g_cin = gcin_own[0:128].astype(F32) + gcin_near[0:128].astype(F32) + gcin_far[...].astype(F32)
    g_cin = g_cin.astype(BF).astype(F32)
    part = norm_back(coarse[...].astype(F32), gain_mlp[...], g_cin)
    g_coarse = (g_deep[...].astype(F32) + part).astype(BF)
    set_fine(fine, block[...].astype(F32))
    xhs, r = joint_normalise(patch_parts(fine))
    scaled = []
    for k in range(4):
        cut = slice(512 * k, 512 * k + 512)
        copies[k].wait()
        scaled.append(dot_nt(g_coarse, w_merge[cut, :]) * gain_merge[:, cut])
    mean_s = sum(jnp.sum(s, -1, keepdims=True) for s in scaled) / 2048.0
    mean_x = sum(jnp.sum(s * x, -1, keepdims=True) for s, x in zip(scaled, xhs)) / 2048.0
    unpatch(fine, [r * (s - mean_s - x * mean_x) for s, x in zip(scaled, xhs)])
    g_block = (cot[...].astype(F32) + get_fine(fine)).astype(BF)
    for n in range(4):
        cut = slice(512 * n, 512 * n + 512)
        for k in range(3):
            copies[4 + 3 * n + k].wait()
        for m in range(2):
            rows = slice(256 * m, 256 * m + 256)
            g_pre = dot_nt(g_block[rows], w_fc2[cut, :]).astype(BF) * slope[rows, cut]
            term = dot_nt(g_pre, w_fc1[:, cut])
            if n == 0:
                acc[rows, :] = term
            else:
                acc[rows, :] += term
    g_fin = acc[...].astype(BF).astype(F32)
    part = norm_back(resid[...].astype(F32), gain_ffn[...], g_fin)
    total = g_block.astype(F32) + part
    g_resid_out[...] = total.astype(BF)
    lines = total.reshape(32, 16, 512)
    tail, head = sides(place[3] == 1, lines[:, :8], lines[:, 8:])
    first_out[...] = tail.astype(BF)
    second_out[...] = head.astype(BF)


def ffn_bwd(place, gcin_own, gcin_near, gcin_far, g_deep, coarse, gain_mlp, w_merge, block, gain_merge, cot,
            w_fc2, slope, w_fc1, resid, gain_ffn):
    return pl.pallas_call(
        ffn_bwd_kernel,
        out_shape=(
            jax.ShapeDtypeStruct((512, 512), BF),
            jax.ShapeDtypeStruct((32, 8, 512), BF),
            jax.ShapeDtypeStruct((32, 8, 512), BF),
        ),
        in_specs=[SM] + [VM] * 6 + [HB, VM, VM, VM, HB, HB, HB, VM, VM],
        out_specs=(VM, VM, VM),
        scratch_shapes=[
            pltpu.VMEM((4, 512, 128), F32),
            pltpu.VMEM((512, 512), F32),
            pltpu.VMEM((2048, 1024), BF),
            pltpu.VMEM((512, 2048), BF),
            pltpu.VMEM((2048, 512), BF),
            pltpu.VMEM((512, 2048), BF),
            pltpu.SemaphoreType.DMA((16,)),
        ],
        compiler_params=params(32),
        cost_estimate=pl.CostEstimate(flops=3 * 10**9, bytes_accessed=14 * 2**20, transcendentals=0),
        name="ffn_bwd",
    )(place, gcin_own, gcin_near, gcin_far, g_deep, coarse, gain_mlp, w_merge, block, gain_merge, cot,
      w_fc2, slope, w_fc1, resid, gain_ffn)


def ends_kernel(tokens, turned, first_out, second_out, slab_out):
    odd = (lax.axis_index("lon") & 1) == 1
    slab = jnp.concatenate([turned[...].astype(F32), jnp.zeros((16, 480), F32)], 1)
    slab_out[...] = slab.astype(BF)
    lines = tokens[...].astype(F32)
    for at, source in ((slice(0, 32), lines), (slice(32, 33), slab.reshape(1, 16, 512))):
        tail, head = sides(odd, source[:, :8], source[:, 8:])
        first_out[at] = tail.astype(BF)
        second_out[at] = head.astype(BF)


def ends(tokens, turned):
    part = jax.ShapeDtypeStruct((33, 8, 512), BF)
    return pl.pallas_call(
        ends_kernel,
        out_shape=(part, part, jax.ShapeDtypeStruct((16, 512), BF)),
        in_specs=[VM] * 2,
        out_specs=(VM,) * 3,
        compiler_params=params(32),
        cost_estimate=pl.CostEstimate(flops=10**6, bytes_accessed=2 * 2**20, transcendentals=0),
        name="ends",
    )(tokens, turned)


def cut_kernel(w_first, w_second, s0, s1, s2, s3, both):
    me = lax.axis_index("lat")
    both[0] = w_first[...].astype(F32).T.astype(BF)
    both[1] = w_second[...]
    for k, out in enumerate((s0, s1, s2, s3)):
        rows = pl.ds(pl.multiple_of(lax.bitwise_xor(me, k) * 32, 32), 32)
        out[0:32] = both[0, rows, :]
        out[32:64] = both[1, rows, :]


def cut(w_first, w_second):
    block = jax.ShapeDtypeStruct((64, 256), BF)
    return pl.pallas_call(
        cut_kernel,
        out_shape=(block,) * 4,
        in_specs=[VM] * 2,
        out_specs=(VM,) * 4,
        scratch_shapes=[pltpu.VMEM((2, 128, 256), BF)],
        compiler_params=params(32),
        cost_estimate=pl.CostEstimate(flops=10**6, bytes_accessed=2**19, transcendentals=0),
        name="cut",
    )(w_first, w_second)


def join_kernel(place, s0, s1, s2, s3, out):
    for k, block in enumerate((s0, s1, s2, s3)):
        at = pl.multiple_of(lax.bitwise_xor(place[2], k) * 256, 256)
        out[:, pl.ds(at, 256)] = block[...]


def join(place, blocks):
    return pl.pallas_call(
        join_kernel,
        out_shape=jax.ShapeDtypeStruct((64, 1024), BF),
        in_specs=[SM] + [VM] * 4,
        out_specs=VM,
        compiler_params=params(32),
        cost_estimate=pl.CostEstimate(flops=10**6, bytes_accessed=2**18, transcendentals=0),
        name="join",
    )(place, *blocks)


def stack_kernel(*refs):
    for k, ref in enumerate(refs[:-1]):
        refs[-1][128 * k : 128 * k + 128] = ref[...]


def stacked(blocks):
    return pl.pallas_call(
        stack_kernel,
        out_shape=jax.ShapeDtypeStruct((512, 1024), BF),
        in_specs=[VM] * 4,
        out_specs=VM,
        compiler_params=params(32),
        cost_estimate=pl.CostEstimate(flops=10**6, bytes_accessed=2**21, transcendentals=0),
        name="stacked",
    )(*blocks)


def halves_kernel(ahead, behind, first, second):
    first[...] = ahead[0:256]
    second[...] = behind[256:512]


def halves(ahead, behind):
    half = jax.ShapeDtypeStruct((256, 1024), BF)
    return pl.pallas_call(
        halves_kernel,
        out_shape=(half, half),
        in_specs=[VM] * 2,
        out_specs=(VM, VM),
        compiler_params=params(32),
        cost_estimate=pl.CostEstimate(flops=10**6, bytes_accessed=2**21, transcendentals=0),
        name="halves",
    )(ahead, behind)


def strips_kernel(place, first, own, second, *rest):
    odd = place[3] == 1
    top_out, bottom_out = rest[-2:]
    for out, lo in ((top_out, 0), (bottom_out, 24)):
        rows = slice(lo, lo + 8)
        left, right = sides(odd, first[rows].astype(F32), second[rows].astype(F32))
        out[0:8, 0:8, :] = left.astype(BF)
        out[0:8, 8:24, :] = own[rows]
        out[0:8, 24:32, :] = right.astype(BF)
        if len(rest) == 3:
            left, right = sides(odd, first[32].astype(F32), second[32].astype(F32))
            out[8] = jnp.concatenate([left, rest[0][...].astype(F32), right], 0).astype(BF)


def strips(place, first, own, second, *slab):
    edge = jax.ShapeDtypeStruct((8 + len(slab), 32, 512), BF)
    return pl.pallas_call(
        strips_kernel,
        out_shape=(edge, edge),
        in_specs=[SM] + [VM] * (3 + len(slab)),
        out_specs=(VM, VM),
        compiler_params=params(32),
        cost_estimate=pl.CostEstimate(flops=10**6, bytes_accessed=3 * 2**20, transcendentals=0),
        name="strips",
    )(place, first, own, second, *slab)


def along(axis, count, step):
    pairs = [(s, (s + step) % count) for s in range(count)]
    return lambda v: lax.ppermute(v, axis, pairs)


LAT_NEXT, LAT_PREV = along("lat", 4, 1), along("lat", 4, -1)


def even_odd(v):
    return lax.ppermute(v, "lon", [(k, k ^ 1) for k in range(32)])


def odd_even(v):
    return lax.ppermute(v, "lon", [(k, (((k + 1) ^ 1) - 1) % 32) for k in range(32)])


def core_swap(v):
    return lax.ppermute(v, "lat", [(0, 1), (1, 0), (2, 3), (3, 2)])


def x_swap(v):
    return lax.ppermute(v, "lat", [(0, 2), (2, 0), (1, 3), (3, 1)])


def cross_swap(v):
    return lax.ppermute(v, "lat", [(0, 3), (3, 0), (1, 2), (2, 1)])


def x_far_swap(v):
    return lax.ppermute(v, "lon", [(k, (k + 16) % 32) for k in range(32)])


def turn(swapped, k):
    pairs = []
    for lat in range(4):
        along_y = (lat % 2 == 1) != swapped
        for lon in range(32):
            x, y, z = lon // 16, lon // 4 % 4, lon % 4
            if along_y:
                y = (y + k) % 4
            else:
                z = (z + k) % 4
            pairs.append((lat * 32 + lon, lat * 32 + (x * 4 + y) * 4 + z))
    return lambda v: lax.ppermute(v, ("lat", "lon"), pairs)


def after(value, *gates):
    return lax.optimization_barrier((value,) + gates)[0]


def on_device(
    tokens, labels, offsets, gain_attn, w_qkv, w_proj, gain_ffn, w_fc1, w_fc2,
    gain_merge, w_merge, gain_mlp, w_first, w_second, w_up, cotangent,
):
    row = lambda g: g.reshape(1, -1)
    s0, s1, s2, s3 = cut(w_first, w_second)
    s1, s2, s3 = core_swap(s1), x_swap(s2), cross_swap(s3)
    first, second, slab = ends(after(tokens, s0), labels.T)
    left, right = even_odd(first), odd_even(second)
    where = [lax.axis_index("lat"), lax.axis_index("lon") & 1]
    place = jnp.concatenate([after(offsets, slab), jnp.stack(where).astype(jnp.int32)])
    mine = join(place, (s0, s1, s2, s3))
    other = x_far_swap(mine)
    cot = cotangent.reshape(512, 512)
    g_deep = g_deep_of(after(cot, mine), w_up)
    near_deep = core_swap(g_deep)
    seed = jnp.concatenate([mine, after(other, g_deep)], 0)
    moved = [turn(False, k)(seed) for k in (1, -1, 2)]
    bottom, top = strips(place, left, after(tokens, seed), right, slab)
    up, down = LAT_NEXT(top), LAT_PREV(bottom)
    gain = row(gain_attn)
    qkv_mid, probs_mid, middle = fwd_middle(
        place, left, tokens, right, slab, gain, w_qkv, w_proj
    )
    part = stacked([after(seed, up, down, middle)] + moved)
    ahead, behind = turn(True, 1)(part), turn(True, -1)(part)
    qkv_edge, probs_edge, resid = fwd_edge(
        place, after(up, part), bottom, top, down, tokens, middle, gain, w_qkv, w_proj
    )
    resid = resid.reshape(512, 512)
    far_deep = x_swap(after(g_deep, resid))
    slope, block, coarse, coarse_in = ffn_fwd(
        resid, row(gain_ffn), w_fc1, w_fc2, row(gain_merge), w_merge, row(gain_mlp)
    )
    fore, hind = halves(after(ahead, coarse_in), behind)
    far_cin = x_swap(coarse_in)
    near_cin = core_swap(coarse_in)
    parts = [part, ahead, behind, turn(True, 1)(fore), turn(True, -1)(hind)]
    cins = [coarse_in, near_cin, far_cin, core_swap(far_cin)]
    deeps = [g_deep, near_deep, far_deep, core_swap(after(far_deep, coarse_in))]
    keep, send, hid = coarse_mlp(place, cins, deeps, parts)
    near = core_swap(send)
    gcin_far = x_swap((keep[128:].astype(F32) + near[128:].astype(F32)).astype(BF))
    down_keep, down_send = down_of(hid, parts)
    down_near = core_swap(down_send)
    down_far = (down_keep[128:].astype(F32) + down_near[128:].astype(F32)).astype(BF)
    gcin_far, down_far = lax.optimization_barrier((gcin_far, down_far))
    down_far = x_swap(down_far)
    g_resid, g_first, g_second = ffn_bwd(
        place, keep, near, gcin_far, g_deep, coarse, row(gain_mlp), w_merge, block, row(gain_merge), cot,
        w_fc2, slope, w_fc1, resid, row(gain_ffn),
    )
    g_resid = g_resid.reshape(32, 16, 512)
    g_left, g_right = even_odd(g_first), odd_even(g_second)
    field_out = up_of(coarse, down_keep, down_near, down_far, block, w_up).reshape(32, 16, 512)
    g_bottom, g_top = strips(place, g_left, after(g_resid, field_out), g_right)
    g_up, g_down = LAT_NEXT(g_top), LAT_PREV(g_bottom)
    g_middle = bwd_middle(place, g_left, g_resid, g_right, qkv_mid, probs_mid, w_proj, w_qkv)
    grad_in = bwd_edge(
        place, g_up, g_bottom, g_top, g_down, g_resid, g_middle, qkv_edge, probs_edge,
        w_proj, w_qkv, tokens, gain,
    )
    return (field_out, grad_in)


def solution(mesh):
    grid = P("lat", "lon", None)
    placed = (
        grid, P("lat", "lon"), P(), P(), P(), P(), P(), P(), P(), P(), P(), P(),
        P("lat", "lon"), P("lon", "lat"), P(), grid,
    )
    return jax.shard_map(
        on_device, mesh=mesh, in_specs=placed, out_specs=(grid, grid), check_vma=False
    )
```

```python
import jax
import jax.numpy as jnp
from jax import lax
from jax.experimental import pallas as pl
from jax.experimental.pallas import tpu as pltpu
from jax.sharding import PartitionSpec as P

BF = jnp.bfloat16
F32 = jnp.float32
EPS = 1e-05
NT = (((1,), (1,)), ((), ()))
TN = (((0,), (0,)), ((), ()))
GELU_C = 0.7978845608028654
GELU_A = 0.044715


def dot(a, b):
    return jnp.dot(a, b, preferred_element_type=F32)


def dot_nt(a, b):
    return lax.dot_general(a, b, NT, preferred_element_type=F32)


def dot_tn(a, b):
    return lax.dot_general(a, b, TN, preferred_element_type=F32)


def normalise(v):
    mean = jnp.mean(v, -1, keepdims=True)
    c = v - mean
    r = lax.rsqrt(jnp.mean(c * c, -1, keepdims=True) + EPS)
    return c * r, r


def norm_back(v, gain, t):
    xh, r = normalise(v)
    s = t * gain
    return r * (s - jnp.mean(s, -1, keepdims=True) - xh * jnp.mean(s * xh, -1, keepdims=True))


def gelu_both(wide):
    x = wide.astype(BF)
    x2 = x * x
    t = jnp.tanh(x * (GELU_C + GELU_C * GELU_A * x2))
    h = 0.5 * x
    slope = (0.5 + 0.5 * t) + (h - h * t * t) * (GELU_C + 3.0 * GELU_C * GELU_A * x2)
    return h + h * t, slope


def half_masks(scale):
    low = lax.broadcasted_iota(jnp.int32, (1, 128), 1) < 64
    return [jnp.where(m, scale, 0.0).astype(F32).astype(BF) for m in (low, jnp.logical_not(low))]


def spread(x, masks):
    none = jnp.zeros((64, 128), BF)
    left, right = x[:, :128], x[:, 128:]
    rows = [jnp.concatenate([left * m, none], 1) for m in masks]
    rows += [jnp.concatenate([none, right * m], 1) for m in masks]
    return jnp.concatenate(rows, 0)


def collect(big):
    low = lax.broadcasted_iota(jnp.int32, (64, 128), 1) < 64
    left = jnp.where(low, big[0:64, :128], big[64:128, :128])
    right = jnp.where(low, big[128:192, 128:], big[192:256, 128:])
    return jnp.concatenate([left, right], 1)


def sides(odd, first, second):
    return jnp.where(odd, first, second), jnp.where(odd, second, first)


def shifted_cols(lines, b):
    return pltpu.roll(lines, 32 - b, 1)[:, :24]


def fill_middle(grid, b, odd, first, own, second):
    def rows(n, carry):
        at = pl.ds(8 * n, 8)
        left, right = sides(odd, first[at].astype(F32), second[at].astype(F32))
        grid[at] = shifted_cols(jnp.concatenate([left, own[at].astype(F32), right], 1), b)
        return carry

    lax.fori_loop(0, 4, rows, 0)


def fill_edges(grid, b, edges):
    for n, edge in enumerate(edges):
        grid[8 * n : 8 * n + 8] = shifted_cols(edge[0:8].astype(F32), b)


def slab_cols(slab, b):
    return pltpu.roll(slab, 32 - b, 0)[:24]


def place_back(back, n, a, b):
    return pltpu.roll(back[pl.ds(8 - a + 8 * n, 8)], 16 + b, 1)[:, :16]


def fetch(pairs, sems):
    copies = [pltpu.make_async_copy(src, dst, sems.at[k]) for k, (src, dst) in enumerate(pairs)]
    for copy in copies:
        copy.start()
    return copies


def windows_of(grid, base, a):
    lines = grid[pl.ds(a + base, 8)]
    return [lines[:, 8 * k : 8 * k + 8].reshape(64, grid.shape[2]) for k in range(3)]


def put_windows(back, row, value):
    for k in range(3):
        part = value[64 * k : 64 * k + 64].reshape(8, 8, 512)
        back[row : row + 8, 8 * k : 8 * k + 8, :] = part


def fwd_windows(grid, codes, cols, mixed, qkv, probs, gain, w_qkv, bases, a, after_qkv):
    for n, base in enumerate(bases):
        normed = [(normalise(x)[0] * gain[...]).astype(BF) for x in windows_of(grid, base, a)]
        qkv[192 * n : 192 * n + 192] = dot(jnp.concatenate(normed, 0), w_qkv[...]).astype(BF)
        for k, col in enumerate(windows_of(codes, base, a)):
            cols[3 * n + k] = col
    after_qkv()
    masks = half_masks(0.125)

    def window(w, carry):
        at = pl.ds(pl.multiple_of(w * 64, 64), 64)
        col = cols[w]
        row = col.T[0:1, 0:64]
        same = jnp.concatenate([col, col], 1) == jnp.concatenate([row] * 4, 1)
        for c in range(2):
            lo = 256 * c
            qbig = spread(qkv[at, lo : lo + 256], masks)
            k = qkv[at, 512 + lo : 768 + lo]
            v = qkv[at, 1024 + lo : 1280 + lo]
            e = jnp.where(same, jnp.exp(dot_nt(k, qbig)), 0.0)
            p = (e * (1.0 / jnp.sum(e, 0, keepdims=True))).astype(BF)
            probs[at, lo : lo + 256] = p
            mixed[at, lo : lo + 256] = collect(dot_tn(p, v)).astype(BF)
        return carry

    lax.fori_loop(0, 3 * len(bases), window, 0, unroll=True)


def fwd_middle_kernel(
    place, first, own, second, own_slab, gain, w_qkv_hbm, w_proj_hbm,
    qkv_hbm, probs_hbm, back,
    grid, codes, cols, mixed, qkv, probs, w_qkv, w_proj, sems,
):
    copies = fetch(((w_qkv_hbm, w_qkv), (w_proj_hbm, w_proj)), sems)
    qkv_copy = pltpu.make_async_copy(qkv, qkv_hbm, sems.at[2])
    probs_copy = pltpu.make_async_copy(probs, probs_hbm, sems.at[3])
    a, b = place[0], place[1]
    odd = place[3] == 1
    fill_middle(grid, b, odd, first, own, second)
    left, right = sides(odd, first[32].astype(F32), second[32].astype(F32))
    slab = slab_cols(jnp.concatenate([left, own_slab[...].astype(F32), right], 0), b)
    for r in range(32):
        codes[r] = jnp.broadcast_to(slab[:, r : r + 1], (24, 128))
    copies[0].wait()
    bases = (0, 8, 16)
    fwd_windows(grid, codes, cols, mixed, qkv, probs, gain, w_qkv, bases, a, qkv_copy.start)
    probs_copy.start()
    copies[1].wait()
    for n in range(3):
        att = dot(mixed[192 * n : 192 * n + 192], w_proj[...]).astype(BF).astype(F32)
        put_windows(back, 8 * n, att)
    qkv_copy.wait()
    probs_copy.wait()


def fwd_edge_kernel(
    place, up, bottom, top, down, own, middle, gain, w_qkv_hbm, w_proj_hbm,
    qkv_hbm, probs_hbm, resid_out,
    grid, codes, cols, mixed, qkv, probs, w_qkv, w_proj, back, sems,
):
    copies = fetch(((w_qkv_hbm, w_qkv), (w_proj_hbm, w_proj)), sems)
    qkv_copy = pltpu.make_async_copy(qkv, qkv_hbm, sems.at[2])
    probs_copy = pltpu.make_async_copy(probs, probs_hbm, sems.at[3])
    a, b, d = place[0], place[1], place[2]
    edges = (up, bottom, top, down)
    fill_edges(grid, b, edges)
    extra = (jnp.where(d == 0, 4.0, 0.0), 0.0, 0.0, jnp.where(d == 3, 4.0, 0.0))
    for n, (edge, lane, code) in enumerate(zip(edges, (24, 0, 24, 0), extra)):
        slab = slab_cols(edge[8].astype(F32) + code, b)
        for r in range(8):
            codes[8 * n + r] = jnp.broadcast_to(slab[:, lane + r : lane + r + 1], (24, 128))
    copies[0].wait()
    bases = (0, 16)
    fwd_windows(grid, codes, cols, mixed, qkv, probs, gain, w_qkv, bases, a, qkv_copy.start)
    probs_copy.start()
    back[8:32] = middle[...]
    copies[1].wait()
    for n in range(2):
        att = dot(mixed[192 * n : 192 * n + 192], w_proj[...]).astype(BF).astype(F32)
        put_windows(back, 32 * n, att)
    for n in range(4):
        at = slice(8 * n, 8 * n + 8)
        resid_out[at] = (own[at].astype(F32) + place_back(back, n, a, b)).astype(BF)
    qkv_copy.wait()
    probs_copy.wait()


def bwd_windows(grid, g_mixed, g_qkv, qkv, probs, w_proj, bases, a, ready):
    for n, base in enumerate(bases):
        ups = jnp.concatenate([x.astype(BF) for x in windows_of(grid, base, a)], 0)
        g_mixed[192 * n : 192 * n + 192] = dot_nt(ups, w_proj[...]).astype(BF)
    ready()
    masks, scaled = half_masks(1.0), half_masks(0.125)

    def window(w, carry):
        at = pl.ds(pl.multiple_of(w * 64, 64), 64)
        for c in range(2):
            lo = 256 * c
            qbig = spread(qkv[at, lo : lo + 256], scaled)
            gbig = spread(g_mixed[at, lo : lo + 256], masks)
            k = qkv[at, 512 + lo : 768 + lo]
            v = qkv[at, 1024 + lo : 1280 + lo]
            p = probs[at, lo : lo + 256]
            g_probs = dot_nt(v, gbig)
            wide_p = p.astype(F32)
            total = jnp.sum(wide_p * g_probs, 0, keepdims=True)
            g_score = (wide_p * (g_probs - total)).astype(BF)
            g_qkv[at, lo : lo + 256] = (collect(dot_tn(g_score, k)) * 0.125).astype(BF)
            g_qkv[at, 512 + lo : 768 + lo] = dot(g_score, qbig).astype(BF)
            g_qkv[at, 1024 + lo : 1280 + lo] = dot(p, gbig).astype(BF)
        return carry

    lax.fori_loop(0, 3 * len(bases), window, 0, unroll=True)


def bwd_middle_kernel(
    place, first, own, second, qkv_hbm, probs_hbm, w_proj_hbm, w_qkv_hbm,
    back,
    grid, g_mixed, g_qkv, qkv, probs, w_proj, w_qkv, sems,
):
    pairs = ((w_proj_hbm, w_proj), (qkv_hbm, qkv), (probs_hbm, probs), (w_qkv_hbm, w_qkv))
    copies = fetch(pairs, sems)

    def ready():
        copies[1].wait()
        copies[2].wait()

    a, b = place[0], place[1]
    fill_middle(grid, b, place[3] == 1, first, own, second)
    copies[0].wait()
    bwd_windows(grid, g_mixed, g_qkv, qkv, probs, w_proj, (0, 8, 16), a, ready)
    copies[3].wait()
    for n in range(3):
        g_shift = dot_nt(g_qkv[192 * n : 192 * n + 192], w_qkv[...]).astype(BF).astype(F32)
        put_windows(back, 8 * n, g_shift)


def bwd_edge_kernel(
    place, up, bottom, top, down, own, middle, qkv_hbm, probs_hbm, w_proj_hbm, w_qkv_hbm,
    tokens, gain,
    grad_out,
    grid, g_mixed, g_qkv, qkv, probs, w_proj, w_qkv, back, sems,
):
    pairs = ((w_proj_hbm, w_proj), (qkv_hbm, qkv), (probs_hbm, probs), (w_qkv_hbm, w_qkv))
    copies = fetch(pairs, sems)

    def ready():
        copies[1].wait()
        copies[2].wait()

    a, b = place[0], place[1]
    fill_edges(grid, b, (up, bottom, top, down))
    copies[0].wait()
    bwd_windows(grid, g_mixed, g_qkv, qkv, probs, w_proj, (0, 16), a, ready)
    back[8:32] = middle[...]
    copies[3].wait()
    for n in range(2):
        g_shift = dot_nt(g_qkv[192 * n : 192 * n + 192], w_qkv[...]).astype(BF).astype(F32)
        put_windows(back, 32 * n, g_shift)
    for n in range(4):
        at = slice(8 * n, 8 * n + 8)
        part = norm_back(tokens[at].astype(F32), gain[...], place_back(back, n, a, b))
        grad_out[at] = (own[at].astype(F32) + part).astype(BF)


VM = pl.BlockSpec(memory_space=pltpu.VMEM)
SM = pl.BlockSpec(memory_space=pltpu.SMEM)
HB = pl.BlockSpec(memory_space=pltpu.HBM)


def params(mib):
    return pltpu.CompilerParams(vmem_limit_bytes=mib * 2**20)


def attn_scratch(rows, backward):
    shapes = [(32, 24, 512, F32)]
    if not backward:
        shapes += [(32, 24, 128, F32), (rows // 64, 64, 128, F32), (rows, 512, BF)]
    else:
        shapes += [(rows, 512, BF), (rows, 1536, BF)]
    shapes += [(rows, 1536, BF), (rows, 512, BF)]
    shapes += [(512, 512, BF), (512, 1536, BF)] if backward else [(512, 1536, BF), (512, 512, BF)]
    if rows == 384:
        shapes += [(40, 24, 512, F32)]
    return [pltpu.VMEM(shape[:-1], shape[-1]) for shape in shapes] + [pltpu.SemaphoreType.DMA((4,))]


MIDDLE = jax.ShapeDtypeStruct((24, 24, 512), F32)
FINE = jax.ShapeDtypeStruct((32, 16, 512), BF)


def attention(kernel, name, rows, backward, specs, outs, out_specs, flops, operands):
    return pl.pallas_call(
        kernel,
        out_shape=outs,
        in_specs=specs,
        out_specs=out_specs,
        scratch_shapes=attn_scratch(rows, backward),
        compiler_params=params(32),
        cost_estimate=pl.CostEstimate(flops=flops, bytes_accessed=6 * 2**20, transcendentals=10**5),
        name=name,
    )(*operands)


def kept(rows):
    return (jax.ShapeDtypeStruct((rows, 1536), BF), jax.ShapeDtypeStruct((rows, 512), BF))


def fwd_middle(*operands):
    return attention(
        fwd_middle_kernel, "fwd_middle", 576, False, [SM] + [VM] * 5 + [HB] * 2,
        kept(576) + (MIDDLE,), (HB, HB, VM), 10**9, operands,
    )


def fwd_edge(*operands):
    return attention(
        fwd_edge_kernel, "fwd_edge", 384, False, [SM] + [VM] * 7 + [HB] * 2,
        kept(384) + (FINE,), (HB, HB, VM), 10**9, operands,
    )


def bwd_middle(*operands):
    return attention(
        bwd_middle_kernel, "bwd_middle", 576, True, [SM] + [VM] * 3 + [HB] * 4,
        MIDDLE, VM, 2 * 10**9, operands,
    )


def bwd_edge(*operands):
    return attention(
        bwd_edge_kernel, "bwd_edge", 384, True, [SM] + [VM] * 6 + [HB] * 4 + [VM] * 2,
        FINE, VM, 2 * 10**9, operands,
    )


def set_fine(fine, value):
    for lane in range(4):
        fine[lane] = value[:, 128 * lane : 128 * lane + 128]


def get_fine(fine):
    return jnp.concatenate([fine[lane] for lane in range(4)], 1)


def patch_parts(fine):
    parts = {}
    for s in range(2):
        lanes = [fine[lane, pl.ds(s, 256, 2), :] for lane in range(4)]
        half = jnp.concatenate(lanes, 1).reshape(16, 2, 8, 512)
        for r in range(2):
            parts[r + 2 * s] = half[:, r].reshape(128, 512)
    return [parts[k] for k in range(4)]


def unpatch(fine, parts):
    for s in range(2):
        pair = [parts[r + 2 * s].reshape(16, 1, 8, 512) for r in range(2)]
        half = jnp.concatenate(pair, 1).reshape(256, 512)
        for lane in range(4):
            fine[lane, pl.ds(s, 256, 2), :] = half[:, 128 * lane : 128 * lane + 128]


def joint_normalise(parts):
    mean = sum(jnp.sum(p, -1, keepdims=True) for p in parts) / 2048.0
    cent = [p - mean for p in parts]
    var = sum(jnp.sum(c * c, -1, keepdims=True) for c in cent) / 2048.0
    r = lax.rsqrt(var + EPS)
    return [c * r for c in cent], r


def ffn_fwd_kernel(
    resid, gain_ffn, fc1_hbm, fc2_hbm, gain_merge, merge_hbm, gain_mlp,
    slope_out, block_out, coarse_out, cin_out,
    acc, fine, w_fc1, w_fc2, w_merge, sems,
):
    pairs = []
    for n in range(4):
        cut = pl.ds(512 * n, 512)
        pairs += [(fc1_hbm.at[:, cut], w_fc1.at[:, cut]), (fc2_hbm.at[cut], w_fc2.at[cut])]
    pairs += [(merge_hbm.at[pl.ds(512 * k, 512)], w_merge.at[pl.ds(512 * k, 512)]) for k in range(4)]
    copies = fetch(pairs, sems)
    xh, _ = normalise(resid[...].astype(F32))
    ffn_in = (xh * gain_ffn[...]).astype(BF)
    for n in range(4):
        cut = slice(512 * n, 512 * n + 512)
        copies[2 * n].wait()
        copies[2 * n + 1].wait()
        for m in range(2):
            rows = slice(256 * m, 256 * m + 256)
            hid, slope = gelu_both(dot(ffn_in[rows], w_fc1[:, cut]))
            slope_out[rows, cut] = slope
            term = dot(hid, w_fc2[cut, :])
            if n == 0:
                acc[rows, :] = resid[rows, :].astype(F32) + term
            else:
                acc[rows, :] += term
    block = acc[...].astype(BF)
    block_out[...] = block
    set_fine(fine, block.astype(F32))
    xhs, _ = joint_normalise(patch_parts(fine))
    coarse = None
    for k in range(4):
        cut = slice(512 * k, 512 * k + 512)
        copies[8 + k].wait()
        term = dot((xhs[k] * gain_merge[:, cut]).astype(BF), w_merge[cut, :])
        coarse = term if coarse is None else coarse + term
    coarse = coarse.astype(BF)
    coarse_out[...] = coarse
    xh, _ = normalise(coarse.astype(F32))
    cin_out[...] = (xh * gain_mlp[...]).astype(BF)


def ffn_fwd(resid, gain_ffn, w_fc1, w_fc2, gain_merge, w_merge, gain_mlp):
    return pl.pallas_call(
        ffn_fwd_kernel,
        out_shape=(
            jax.ShapeDtypeStruct((512, 2048), BF),
            jax.ShapeDtypeStruct((512, 512), BF),
            jax.ShapeDtypeStruct((128, 1024), BF),
            jax.ShapeDtypeStruct((128, 1024), BF),
        ),
        in_specs=[VM, VM, HB, HB, VM, HB, VM],
        out_specs=(VM, VM, VM, VM),
        scratch_shapes=[
            pltpu.VMEM((512, 512), F32),
            pltpu.VMEM((4, 512, 128), F32),
            pltpu.VMEM((512, 2048), BF),
            pltpu.VMEM((2048, 512), BF),
            pltpu.VMEM((2048, 1024), BF),
            pltpu.SemaphoreType.DMA((12,)),
        ],
        compiler_params=params(32),
        cost_estimate=pl.CostEstimate(flops=3 * 10**9, bytes_accessed=12 * 2**20, transcendentals=10**6),
        name="ffn_fwd",
    )(resid, gain_ffn, w_fc1, w_fc2, gain_merge, w_merge, gain_mlp)


def weight_chunk(parts, y, lo):
    rows = []
    for k in range(4):
        ref, at = (parts[y], 128 * k) if y < 3 else (parts[3 + k // 2], 128 * (k % 2))
        rows += [ref[at + lo : at + lo + 32], ref[at + 64 + lo : at + 96 + lo]]
    return jnp.concatenate(rows, 0)


def mlp_kernel(
    c0, c1, d0, d1, w0, w1, w2, w3, w4,
    keep_out, send_out, hid_out,
    cs, deep, gacc,
):
    for k, (c, g) in enumerate(((c0, d0), (c1, d1))):
        cs[128 * k : 128 * k + 128] = c[...]
        deep[128 * k : 128 * k + 128] = g[...]
    parts = (w0, w1, w2, w3, w4)
    for y in range(4):
        first = weight_chunk(parts, y, 0)
        second = weight_chunk(parts, y, 32)
        hid, slope = gelu_both(dot_nt(cs[...], first))
        hid_out[:, 256 * y : 256 * y + 256] = hid
        g_pre = dot_nt(deep[...], second).astype(BF) * slope
        g_cin = dot(g_pre, first)
        if y == 0:
            gacc[...] = g_cin
        else:
            gacc[...] += g_cin
    keep_out[...] = gacc[0:128].astype(BF)
    send_out[...] = gacc[128:256].astype(BF)


QUARTER = jax.ShapeDtypeStruct((128, 1024), BF)


def coarse_mlp(cins, deeps, parts, name):
    return pl.pallas_call(
        mlp_kernel,
        out_shape=(QUARTER, QUARTER, jax.ShapeDtypeStruct((256, 1024), BF)),
        in_specs=[VM] * 9,
        out_specs=(VM, VM, VM),
        scratch_shapes=[
            pltpu.VMEM((256, 1024), BF),
            pltpu.VMEM((256, 1024), BF),
            pltpu.VMEM((256, 1024), F32),
        ],
        compiler_params=params(32),
        cost_estimate=pl.CostEstimate(flops=2 * 10**9, bytes_accessed=6 * 2**20, transcendentals=10**6),
        name=name,
    )(*cins, *deeps, *parts)


def down_kernel(near, far, w0, w1, w2, w3, w4, near_keep, send, far_keep):
    near_sum, far_sum = None, None
    for y in range(4):
        cols = slice(256 * y, 256 * y + 256)
        second = weight_chunk((w0, w1, w2, w3, w4), y, 32)
        near_term, far_term = dot(near[:, cols], second), dot(far[:, cols], second)
        near_sum = near_term if near_sum is None else near_sum + near_term
        far_sum = far_term if far_sum is None else far_sum + far_term
    near_keep[...] = near_sum[0:128].astype(BF)
    send[0:128] = near_sum[128:256].astype(BF)
    far_keep[...] = far_sum[0:128].astype(BF)
    send[128:256] = far_sum[128:256].astype(BF)


def down_of(near, far, parts):
    return pl.pallas_call(
        down_kernel,
        out_shape=(QUARTER, jax.ShapeDtypeStruct((256, 1024), BF), QUARTER),
        in_specs=[VM] * 7,
        out_specs=(VM,) * 3,
        compiler_params=params(32),
        cost_estimate=pl.CostEstimate(flops=10**9, bytes_accessed=5 * 2**20, transcendentals=0),
        name="down",
    )(near, far, *parts)


def g_deep_kernel(cot, up_hbm, out, fine, w_up, sems):
    cuts = [pl.ds(256 * k, 256) for k in range(4)]
    copies = fetch([(up_hbm.at[cut], w_up.at[cut]) for cut in cuts], sems)
    set_fine(fine, cot[...].astype(F32))
    whole = jnp.concatenate([part.astype(BF) for part in patch_parts(fine)], 1)
    for k in range(4):
        copies[k].wait()
        rows = slice(256 * k, 256 * k + 256)
        out[:, rows] = dot_nt(whole, w_up[rows, :]).astype(BF)


UP_SCRATCH = [
    pltpu.VMEM((4, 512, 128), F32),
    pltpu.VMEM((1024, 2048), BF),
    pltpu.SemaphoreType.DMA((4,)),
]


def g_deep_of(cot, w_up):
    return pl.pallas_call(
        g_deep_kernel,
        out_shape=jax.ShapeDtypeStruct((128, 1024), BF),
        in_specs=[VM, HB],
        out_specs=VM,
        scratch_shapes=UP_SCRATCH,
        compiler_params=params(32),
        cost_estimate=pl.CostEstimate(flops=10**9, bytes_accessed=5 * 2**20, transcendentals=0),
        name="g_deep",
    )(cot, w_up)


def up_kernel(coarse, keep, near, far, block, up_hbm, out, fine, w_up, sems):
    cuts = [pl.ds(256 * k, 256) for k in range(4)]
    copies = fetch([(up_hbm.at[cut], w_up.at[cut]) for cut in cuts], sems)
    deep = coarse[...].astype(F32) + keep[...].astype(F32) + near[0:128].astype(F32)
    deep = (deep + far[...].astype(F32)).astype(BF)
    acc = None
    for k in range(4):
        copies[k].wait()
        rows = slice(256 * k, 256 * k + 256)
        term = dot(deep[:, rows], w_up[rows, :])
        acc = term if acc is None else acc + term
    unpatch(fine, [acc[:, 512 * k : 512 * k + 512] for k in range(4)])
    out[...] = (block[...].astype(F32) + get_fine(fine)).astype(BF)


def up_of(coarse, keep, near, far, block, w_up):
    return pl.pallas_call(
        up_kernel,
        out_shape=jax.ShapeDtypeStruct((512, 512), BF),
        in_specs=[VM] * 5 + [HB],
        out_specs=VM,
        scratch_shapes=UP_SCRATCH,
        compiler_params=params(32),
        cost_estimate=pl.CostEstimate(flops=10**9, bytes_accessed=5 * 2**20, transcendentals=0),
        name="up",
    )(coarse, keep, near, far, block, w_up)


def ffn_bwd_kernel(
    place, gcin_own, gcin_near, gcin_far, g_deep, coarse, gain_mlp, merge_hbm, block, gain_merge, cot,
    fc2_hbm, slope_hbm, fc1_hbm, resid, gain_ffn,
    g_resid_out, first_out, second_out,
    fine, acc, w_merge, w_fc1, w_fc2, slope, sems,
):
    pairs = [(merge_hbm.at[pl.ds(512 * k, 512)], w_merge.at[pl.ds(512 * k, 512)]) for k in range(4)]
    for n in range(4):
        cut = pl.ds(512 * n, 512)
        pairs += [
            (fc2_hbm.at[cut], w_fc2.at[cut]),
            (slope_hbm.at[:, cut], slope.at[:, cut]),
            (fc1_hbm.at[:, cut], w_fc1.at[:, cut]),
        ]
    copies = fetch(pairs, sems)
    g_cin = gcin_own[...].astype(F32) + gcin_near[...].astype(F32) + gcin_far[...].astype(F32)
    g_cin = g_cin.astype(BF).astype(F32)
    part = norm_back(coarse[...].astype(F32), gain_mlp[...], g_cin)
    g_coarse = (g_deep[...].astype(F32) + part).astype(BF)
    set_fine(fine, block[...].astype(F32))
    xhs, r = joint_normalise(patch_parts(fine))
    scaled = []
    for k in range(4):
        cut = slice(512 * k, 512 * k + 512)
        copies[k].wait()
        scaled.append(dot_nt(g_coarse, w_merge[cut, :]) * gain_merge[:, cut])
    mean_s = sum(jnp.sum(s, -1, keepdims=True) for s in scaled) / 2048.0
    mean_x = sum(jnp.sum(s * x, -1, keepdims=True) for s, x in zip(scaled, xhs)) / 2048.0
    unpatch(fine, [r * (s - mean_s - x * mean_x) for s, x in zip(scaled, xhs)])
    g_block = (cot[...].astype(F32) + get_fine(fine)).astype(BF)
    for n in range(4):
        cut = slice(512 * n, 512 * n + 512)
        for k in range(3):
            copies[4 + 3 * n + k].wait()
        for m in range(2):
            rows = slice(256 * m, 256 * m + 256)
            g_pre = dot_nt(g_block[rows], w_fc2[cut, :]).astype(BF) * slope[rows, cut]
            term = dot_nt(g_pre, w_fc1[:, cut])
            if n == 0:
                acc[rows, :] = term
            else:
                acc[rows, :] += term
    g_fin = acc[...].astype(BF).astype(F32)
    part = norm_back(resid[...].astype(F32), gain_ffn[...], g_fin)
    total = g_block.astype(F32) + part
    g_resid_out[...] = total.astype(BF)
    lines = total.reshape(32, 16, 512)
    tail, head = sides(place[3] == 1, lines[:, :8], lines[:, 8:])
    first_out[...] = tail.astype(BF)
    second_out[...] = head.astype(BF)


def ffn_bwd(place, gcin_own, gcin_near, gcin_far, g_deep, coarse, gain_mlp, w_merge, block, gain_merge, cot,
            w_fc2, slope, w_fc1, resid, gain_ffn):
    return pl.pallas_call(
        ffn_bwd_kernel,
        out_shape=(
            jax.ShapeDtypeStruct((512, 512), BF),
            jax.ShapeDtypeStruct((32, 8, 512), BF),
            jax.ShapeDtypeStruct((32, 8, 512), BF),
        ),
        in_specs=[SM] + [VM] * 6 + [HB, VM, VM, VM, HB, HB, HB, VM, VM],
        out_specs=(VM, VM, VM),
        scratch_shapes=[
            pltpu.VMEM((4, 512, 128), F32),
            pltpu.VMEM((512, 512), F32),
            pltpu.VMEM((2048, 1024), BF),
            pltpu.VMEM((512, 2048), BF),
            pltpu.VMEM((2048, 512), BF),
            pltpu.VMEM((512, 2048), BF),
            pltpu.SemaphoreType.DMA((16,)),
        ],
        compiler_params=params(32),
        cost_estimate=pl.CostEstimate(flops=3 * 10**9, bytes_accessed=14 * 2**20, transcendentals=0),
        name="ffn_bwd",
    )(place, gcin_own, gcin_near, gcin_far, g_deep, coarse, gain_mlp, w_merge, block, gain_merge, cot,
      w_fc2, slope, w_fc1, resid, gain_ffn)


def ends_kernel(tokens, turned, first_out, second_out, slab_out):
    odd = (lax.axis_index("lon") & 1) == 1
    slab = jnp.concatenate([turned[...].astype(F32), jnp.zeros((16, 480), F32)], 1)
    slab_out[...] = slab.astype(BF)
    lines = tokens[...].astype(F32)
    for at, source in ((slice(0, 32), lines), (slice(32, 33), slab.reshape(1, 16, 512))):
        tail, head = sides(odd, source[:, :8], source[:, 8:])
        first_out[at] = tail.astype(BF)
        second_out[at] = head.astype(BF)


def ends(tokens, turned):
    part = jax.ShapeDtypeStruct((33, 8, 512), BF)
    return pl.pallas_call(
        ends_kernel,
        out_shape=(part, part, jax.ShapeDtypeStruct((16, 512), BF)),
        in_specs=[VM] * 2,
        out_specs=(VM,) * 3,
        compiler_params=params(32),
        cost_estimate=pl.CostEstimate(flops=10**6, bytes_accessed=2 * 2**20, transcendentals=0),
        name="ends",
    )(tokens, turned)


def cut_kernel(w_first, w_second, s0, s1, s2, s3, both):
    me = lax.axis_index("lat")
    both[0] = w_first[...].astype(F32).T.astype(BF)
    both[1] = w_second[...]
    for k, out in enumerate((s0, s1, s2, s3)):
        rows = pl.ds(pl.multiple_of(lax.bitwise_xor(me, k) * 32, 32), 32)
        out[0:32] = both[0, rows, :]
        out[32:64] = both[1, rows, :]


def cut(w_first, w_second):
    block = jax.ShapeDtypeStruct((64, 256), BF)
    return pl.pallas_call(
        cut_kernel,
        out_shape=(block,) * 4,
        in_specs=[VM] * 2,
        out_specs=(VM,) * 4,
        scratch_shapes=[pltpu.VMEM((2, 128, 256), BF)],
        compiler_params=params(32),
        cost_estimate=pl.CostEstimate(flops=10**6, bytes_accessed=2**19, transcendentals=0),
        name="cut",
    )(w_first, w_second)


def join_kernel(place, s0, s1, s2, s3, out):
    for k, block in enumerate((s0, s1, s2, s3)):
        at = pl.multiple_of(lax.bitwise_xor(place[2], k) * 256, 256)
        out[:, pl.ds(at, 256)] = block[...]


def join(place, blocks):
    return pl.pallas_call(
        join_kernel,
        out_shape=jax.ShapeDtypeStruct((64, 1024), BF),
        in_specs=[SM] + [VM] * 4,
        out_specs=VM,
        compiler_params=params(32),
        cost_estimate=pl.CostEstimate(flops=10**6, bytes_accessed=2**18, transcendentals=0),
        name="join",
    )(place, *blocks)


def stack_kernel(*refs):
    for k, ref in enumerate(refs[:-1]):
        refs[-1][128 * k : 128 * k + 128] = ref[...]


def stacked(blocks):
    return pl.pallas_call(
        stack_kernel,
        out_shape=jax.ShapeDtypeStruct((512, 1024), BF),
        in_specs=[VM] * 4,
        out_specs=VM,
        compiler_params=params(32),
        cost_estimate=pl.CostEstimate(flops=10**6, bytes_accessed=2**21, transcendentals=0),
        name="stacked",
    )(*blocks)


def halves_kernel(ahead, behind, first, second):
    first[...] = ahead[0:256]
    second[...] = behind[256:512]


def halves(ahead, behind):
    half = jax.ShapeDtypeStruct((256, 1024), BF)
    return pl.pallas_call(
        halves_kernel,
        out_shape=(half, half),
        in_specs=[VM] * 2,
        out_specs=(VM, VM),
        compiler_params=params(32),
        cost_estimate=pl.CostEstimate(flops=10**6, bytes_accessed=2**21, transcendentals=0),
        name="halves",
    )(ahead, behind)


def strips_kernel(place, first, own, second, *rest):
    odd = place[3] == 1
    top_out, bottom_out = rest[-2:]
    for out, lo in ((top_out, 0), (bottom_out, 24)):
        rows = slice(lo, lo + 8)
        left, right = sides(odd, first[rows].astype(F32), second[rows].astype(F32))
        out[0:8, 0:8, :] = left.astype(BF)
        out[0:8, 8:24, :] = own[rows]
        out[0:8, 24:32, :] = right.astype(BF)
        if len(rest) == 3:
            left, right = sides(odd, first[32].astype(F32), second[32].astype(F32))
            out[8] = jnp.concatenate([left, rest[0][...].astype(F32), right], 0).astype(BF)


def strips(place, first, own, second, *slab):
    edge = jax.ShapeDtypeStruct((8 + len(slab), 32, 512), BF)
    return pl.pallas_call(
        strips_kernel,
        out_shape=(edge, edge),
        in_specs=[SM] + [VM] * (3 + len(slab)),
        out_specs=(VM, VM),
        compiler_params=params(32),
        cost_estimate=pl.CostEstimate(flops=10**6, bytes_accessed=3 * 2**20, transcendentals=0),
        name="strips",
    )(place, first, own, second, *slab)


def along(axis, count, step):
    pairs = [(s, (s + step) % count) for s in range(count)]
    return lambda v: lax.ppermute(v, axis, pairs)


LAT_NEXT, LAT_PREV = along("lat", 4, 1), along("lat", 4, -1)


def even_odd(v):
    return lax.ppermute(v, "lon", [(k, k ^ 1) for k in range(32)])


def odd_even(v):
    return lax.ppermute(v, "lon", [(k, (((k + 1) ^ 1) - 1) % 32) for k in range(32)])


def core_swap(v):
    return lax.ppermute(v, "lat", [(0, 1), (1, 0), (2, 3), (3, 2)])


def x_swap(v):
    return lax.ppermute(v, "lat", [(0, 2), (2, 0), (1, 3), (3, 1)])


def cross_swap(v):
    return lax.ppermute(v, "lat", [(0, 3), (3, 0), (1, 2), (2, 1)])


def x_far_swap(v):
    return lax.ppermute(v, "lon", [(k, (k + 16) % 32) for k in range(32)])


def turn(swapped, k):
    pairs = []
    for lat in range(4):
        along_y = (lat % 2 == 1) != swapped
        for lon in range(32):
            x, y, z = lon // 16, lon // 4 % 4, lon % 4
            if along_y:
                y = (y + k) % 4
            else:
                z = (z + k) % 4
            pairs.append((lat * 32 + lon, lat * 32 + (x * 4 + y) * 4 + z))
    return lambda v: lax.ppermute(v, ("lat", "lon"), pairs)


def after(value, *gates):
    return lax.optimization_barrier((value,) + gates)[0]


def on_device(
    tokens, labels, offsets, gain_attn, w_qkv, w_proj, gain_ffn, w_fc1, w_fc2,
    gain_merge, w_merge, gain_mlp, w_first, w_second, w_up, cotangent,
):
    row = lambda g: g.reshape(1, -1)
    s0, s1, s2, s3 = cut(w_first, w_second)
    s1, s2, s3 = core_swap(s1), x_swap(s2), cross_swap(s3)
    first, second, slab = ends(after(tokens, s0), labels.T)
    left, right = even_odd(first), odd_even(second)
    where = [lax.axis_index("lat"), lax.axis_index("lon") & 1]
    place = jnp.concatenate([after(offsets, slab), jnp.stack(where).astype(jnp.int32)])
    mine = join(place, (s0, s1, s2, s3))
    other = x_far_swap(mine)
    cot = cotangent.reshape(512, 512)
    g_deep = g_deep_of(after(cot, mine), w_up)
    near_deep = core_swap(g_deep)
    seed = jnp.concatenate([mine, after(other, g_deep)], 0)
    moved = [turn(False, k)(seed) for k in (1, -1, 2)]
    bottom, top = strips(place, left, after(tokens, seed), right, slab)
    up, down = LAT_NEXT(top), LAT_PREV(bottom)
    gain = row(gain_attn)
    qkv_mid, probs_mid, middle = fwd_middle(
        place, left, tokens, right, slab, gain, w_qkv, w_proj
    )
    part = stacked([after(seed, up, down, middle)] + moved)
    ahead, behind = turn(True, 1)(part), turn(True, -1)(part)
    qkv_edge, probs_edge, resid = fwd_edge(
        place, after(up, part), bottom, top, down, tokens, middle, gain, w_qkv, w_proj
    )
    resid = resid.reshape(512, 512)
    far_deep = x_swap(after(g_deep, resid))
    slope, block, coarse, coarse_in = ffn_fwd(
        resid, row(gain_ffn), w_fc1, w_fc2, row(gain_merge), w_merge, row(gain_mlp)
    )
    fore, hind = halves(after(ahead, coarse_in), behind)
    far_cin = x_swap(coarse_in)
    near_cin = core_swap(coarse_in)
    parts = [part, ahead, behind, turn(True, 1)(fore), turn(True, -1)(hind)]
    cross_cin = core_swap(far_cin)
    cross_deep = core_swap(after(far_deep, coarse_in))
    far_keep, far_send, far_hid = coarse_mlp(
        (far_cin, cross_cin), (far_deep, cross_deep), parts, "far_mlp"
    )
    far_near = core_swap(far_send)
    far_sum = (far_keep.astype(F32) + far_near.astype(F32)).astype(BF)
    gcin_far = x_swap(far_sum)
    keep, send, near_hid = coarse_mlp(
        (after(coarse_in, far_sum), near_cin), (g_deep, near_deep), parts, "near_mlp"
    )
    near = core_swap(send)
    down_keep, down_send, down_far = down_of(near_hid, far_hid, parts)
    down_near = core_swap(down_send)
    down_far = (down_far.astype(F32) + down_near[128:].astype(F32)).astype(BF)
    gcin_far, down_far = lax.optimization_barrier((gcin_far, down_far))
    down_far = x_swap(down_far)
    g_resid, g_first, g_second = ffn_bwd(
        place, keep, near, gcin_far, g_deep, coarse, row(gain_mlp), w_merge, block, row(gain_merge), cot,
        w_fc2, slope, w_fc1, resid, row(gain_ffn),
    )
    g_resid = g_resid.reshape(32, 16, 512)
    g_left, g_right = even_odd(g_first), odd_even(g_second)
    field_out = up_of(coarse, down_keep, down_near, down_far, block, w_up).reshape(32, 16, 512)
    g_bottom, g_top = strips(place, g_left, after(g_resid, field_out), g_right)
    g_up, g_down = LAT_NEXT(g_top), LAT_PREV(g_bottom)
    g_middle = bwd_middle(place, g_left, g_resid, g_right, qkv_mid, probs_mid, w_proj, w_qkv)
    grad_in = bwd_edge(
        place, g_up, g_bottom, g_top, g_down, g_resid, g_middle, qkv_edge, probs_edge,
        w_proj, w_qkv, tokens, gain,
    )
    return (field_out, grad_in)


def solution(mesh):
    grid = P("lat", "lon", None)
    placed = (
        grid, P("lat", "lon"), P(), P(), P(), P(), P(), P(), P(), P(), P(), P(),
        P("lat", "lon"), P("lon", "lat"), P(), grid,
    )
    return jax.shard_map(
        on_device, mesh=mesh, in_specs=placed, out_specs=(grid, grid), check_vma=False
    )
```

```python
import jax
import jax.numpy as jnp
from jax import lax
from jax.experimental import pallas as pl
from jax.experimental.pallas import tpu as pltpu
from jax.sharding import PartitionSpec as P

BF = jnp.bfloat16
F32 = jnp.float32
EPS = 1e-05
NT = (((1,), (1,)), ((), ()))
TN = (((0,), (0,)), ((), ()))
GELU_C = 0.7978845608028654
GELU_A = 0.044715


def dot(a, b):
    return jnp.dot(a, b, preferred_element_type=F32)


def dot_nt(a, b):
    return lax.dot_general(a, b, NT, preferred_element_type=F32)


def dot_tn(a, b):
    return lax.dot_general(a, b, TN, preferred_element_type=F32)


def normalise(v):
    mean = jnp.mean(v, -1, keepdims=True)
    c = v - mean
    r = lax.rsqrt(jnp.mean(c * c, -1, keepdims=True) + EPS)
    return c * r, r


def norm_back(v, gain, t):
    xh, r = normalise(v)
    s = t * gain
    return r * (s - jnp.mean(s, -1, keepdims=True) - xh * jnp.mean(s * xh, -1, keepdims=True))


def gelu_both(wide):
    x = wide.astype(BF)
    x2 = x * x
    t = jnp.tanh(x * (GELU_C + GELU_C * GELU_A * x2))
    h = 0.5 * x
    slope = (0.5 + 0.5 * t) + (h - h * t * t) * (GELU_C + 3.0 * GELU_C * GELU_A * x2)
    return h + h * t, slope


def half_masks(scale):
    low = lax.broadcasted_iota(jnp.int32, (1, 128), 1) < 64
    return [jnp.where(m, scale, 0.0).astype(F32).astype(BF) for m in (low, jnp.logical_not(low))]


def spread(x, masks):
    none = jnp.zeros((64, 128), BF)
    left, right = x[:, :128], x[:, 128:]
    rows = [jnp.concatenate([left * m, none], 1) for m in masks]
    rows += [jnp.concatenate([none, right * m], 1) for m in masks]
    return jnp.concatenate(rows, 0)


def collect(big):
    low = lax.broadcasted_iota(jnp.int32, (64, 128), 1) < 64
    left = jnp.where(low, big[0:64, :128], big[64:128, :128])
    right = jnp.where(low, big[128:192, 128:], big[192:256, 128:])
    return jnp.concatenate([left, right], 1)


def sides(odd, first, second):
    return jnp.where(odd, first, second), jnp.where(odd, second, first)


def shifted_cols(lines, b):
    return pltpu.roll(lines, 32 - b, 1)[:, :24]


def fill_middle(grid, b, odd, first, own, second):
    def rows(n, carry):
        at = pl.ds(8 * n, 8)
        left, right = sides(odd, first[at].astype(F32), second[at].astype(F32))
        grid[at] = shifted_cols(jnp.concatenate([left, own[at].astype(F32), right], 1), b)
        return carry

    lax.fori_loop(0, 4, rows, 0)


def fill_edges(grid, b, edges):
    for n, edge in enumerate(edges):
        grid[8 * n : 8 * n + 8] = shifted_cols(edge[0:8].astype(F32), b)


def slab_cols(slab, b):
    return pltpu.roll(slab, 32 - b, 0)[:24]


def place_back(back, n, a, b):
    return pltpu.roll(back[pl.ds(8 - a + 8 * n, 8)], 16 + b, 1)[:, :16]


def windows_of(grid, base, a):
    lines = grid[pl.ds(a + base, 8)]
    return [lines[:, 8 * k : 8 * k + 8].reshape(64, grid.shape[2]) for k in range(3)]


def put_windows(back, row, value):
    for k in range(3):
        part = value[64 * k : 64 * k + 64].reshape(8, 8, 512)
        back[row : row + 8, 8 * k : 8 * k + 8, :] = part


def fwd_windows(grid, codes, cols, mixed, qkv, probs, gain, w_qkv, bases, a):
    for n, base in enumerate(bases):
        normed = [(normalise(x)[0] * gain[...]).astype(BF) for x in windows_of(grid, base, a)]
        qkv[192 * n : 192 * n + 192] = dot(jnp.concatenate(normed, 0), w_qkv[...]).astype(BF)
        for k, col in enumerate(windows_of(codes, base, a)):
            cols[3 * n + k] = col
    masks = half_masks(0.125)

    def window(w, carry):
        at = pl.ds(pl.multiple_of(w * 64, 64), 64)
        col = cols[w]
        row = col.T[0:1, 0:64]
        same = jnp.concatenate([col, col], 1) == jnp.concatenate([row] * 4, 1)
        for c in range(2):
            lo = 256 * c
            qbig = spread(qkv[at, lo : lo + 256], masks)
            k = qkv[at, 512 + lo : 768 + lo]
            v = qkv[at, 1024 + lo : 1280 + lo]
            e = jnp.where(same, jnp.exp(dot_nt(k, qbig)), 0.0)
            p = (e * (1.0 / jnp.sum(e, 0, keepdims=True))).astype(BF)
            probs[at, lo : lo + 256] = p
            mixed[at, lo : lo + 256] = collect(dot_tn(p, v)).astype(BF)
        return carry

    lax.fori_loop(0, 3 * len(bases), window, 0, unroll=True)


def fwd_middle_kernel(
    place, first, own, second, own_slab, gain, w_qkv, w_proj,
    qkv, probs, back,
    grid, codes, cols, mixed,
):
    a, b = place[0], place[1]
    odd = place[3] == 1
    fill_middle(grid, b, odd, first, own, second)
    left, right = sides(odd, first[32].astype(F32), second[32].astype(F32))
    slab = slab_cols(jnp.concatenate([left, own_slab[...].astype(F32), right], 0), b)
    for r in range(32):
        codes[r] = jnp.broadcast_to(slab[:, r : r + 1], (24, 128))
    bases = (0, 8, 16)
    fwd_windows(grid, codes, cols, mixed, qkv, probs, gain, w_qkv, bases, a)
    for n in range(3):
        att = dot(mixed[192 * n : 192 * n + 192], w_proj[...]).astype(BF).astype(F32)
        put_windows(back, 8 * n, att)


def fwd_edge_kernel(
    place, up, bottom, top, down, own, middle, gain, w_qkv, w_proj,
    qkv, probs, resid_out,
    grid, codes, cols, mixed, back,
):
    a, b, d = place[0], place[1], place[2]
    edges = (up, bottom, top, down)
    fill_edges(grid, b, edges)
    extra = (jnp.where(d == 0, 4.0, 0.0), 0.0, 0.0, jnp.where(d == 3, 4.0, 0.0))
    for n, (edge, lane, code) in enumerate(zip(edges, (24, 0, 24, 0), extra)):
        slab = slab_cols(edge[8].astype(F32) + code, b)
        for r in range(8):
            codes[8 * n + r] = jnp.broadcast_to(slab[:, lane + r : lane + r + 1], (24, 128))
    bases = (0, 16)
    fwd_windows(grid, codes, cols, mixed, qkv, probs, gain, w_qkv, bases, a)
    back[8:32] = middle[...]
    for n in range(2):
        att = dot(mixed[192 * n : 192 * n + 192], w_proj[...]).astype(BF).astype(F32)
        put_windows(back, 32 * n, att)
    for n in range(4):
        at = slice(8 * n, 8 * n + 8)
        resid_out[at] = (own[at].astype(F32) + place_back(back, n, a, b)).astype(BF)


def bwd_windows(grid, g_mixed, g_qkv, qkv, probs, w_proj, bases, a):
    for n, base in enumerate(bases):
        ups = jnp.concatenate([x.astype(BF) for x in windows_of(grid, base, a)], 0)
        g_mixed[192 * n : 192 * n + 192] = dot_nt(ups, w_proj[...]).astype(BF)
    masks, scaled = half_masks(1.0), half_masks(0.125)

    def window(w, carry):
        at = pl.ds(pl.multiple_of(w * 64, 64), 64)
        for c in range(2):
            lo = 256 * c
            qbig = spread(qkv[at, lo : lo + 256], scaled)
            gbig = spread(g_mixed[at, lo : lo + 256], masks)
            k = qkv[at, 512 + lo : 768 + lo]
            v = qkv[at, 1024 + lo : 1280 + lo]
            p = probs[at, lo : lo + 256]
            g_probs = dot_nt(v, gbig)
            wide_p = p.astype(F32)
            total = jnp.sum(wide_p * g_probs, 0, keepdims=True)
            g_score = (wide_p * (g_probs - total)).astype(BF)
            g_qkv[at, lo : lo + 256] = (collect(dot_tn(g_score, k)) * 0.125).astype(BF)
            g_qkv[at, 512 + lo : 768 + lo] = dot(g_score, qbig).astype(BF)
            g_qkv[at, 1024 + lo : 1280 + lo] = dot(p, gbig).astype(BF)
        return carry

    lax.fori_loop(0, 3 * len(bases), window, 0, unroll=True)


def bwd_middle_kernel(
    place, first, own, second, qkv, probs, w_proj, w_qkv,
    back,
    grid, g_mixed, g_qkv,
):

    a, b = place[0], place[1]
    fill_middle(grid, b, place[3] == 1, first, own, second)
    bwd_windows(grid, g_mixed, g_qkv, qkv, probs, w_proj, (0, 8, 16), a)
    for n in range(3):
        g_shift = dot_nt(g_qkv[192 * n : 192 * n + 192], w_qkv[...]).astype(BF).astype(F32)
        put_windows(back, 8 * n, g_shift)


def bwd_edge_kernel(
    place, up, bottom, top, down, own, middle, qkv, probs, w_proj, w_qkv,
    tokens, gain,
    grad_out,
    grid, g_mixed, g_qkv, back,
):

    a, b = place[0], place[1]
    fill_edges(grid, b, (up, bottom, top, down))
    bwd_windows(grid, g_mixed, g_qkv, qkv, probs, w_proj, (0, 16), a)
    back[8:32] = middle[...]
    for n in range(2):
        g_shift = dot_nt(g_qkv[192 * n : 192 * n + 192], w_qkv[...]).astype(BF).astype(F32)
        put_windows(back, 32 * n, g_shift)
    for n in range(4):
        at = slice(8 * n, 8 * n + 8)
        part = norm_back(tokens[at].astype(F32), gain[...], place_back(back, n, a, b))
        grad_out[at] = (own[at].astype(F32) + part).astype(BF)


VM = pl.BlockSpec(memory_space=pltpu.VMEM)
SM = pl.BlockSpec(memory_space=pltpu.SMEM)


def params(mib):
    return pltpu.CompilerParams(vmem_limit_bytes=mib * 2**20)


def attn_scratch(rows, backward):
    shapes = [(32, 24, 512, F32)]
    if not backward:
        shapes += [(32, 24, 128, F32), (rows // 64, 64, 128, F32), (rows, 512, BF)]
    else:
        shapes += [(rows, 512, BF), (rows, 1536, BF)]
    if rows == 384:
        shapes += [(40, 24, 512, F32)]
    return [pltpu.VMEM(shape[:-1], shape[-1]) for shape in shapes]


MIDDLE = jax.ShapeDtypeStruct((24, 24, 512), F32)
FINE = jax.ShapeDtypeStruct((32, 16, 512), BF)


def attention(kernel, name, rows, backward, specs, outs, out_specs, flops, operands):
    return pl.pallas_call(
        kernel,
        out_shape=outs,
        in_specs=specs,
        out_specs=out_specs,
        scratch_shapes=attn_scratch(rows, backward),
        compiler_params=params(32),
        cost_estimate=pl.CostEstimate(flops=flops, bytes_accessed=6 * 2**20, transcendentals=10**5),
        name=name,
    )(*operands)


def kept(rows):
    return (jax.ShapeDtypeStruct((rows, 1536), BF), jax.ShapeDtypeStruct((rows, 512), BF))


def fwd_middle(*operands):
    return attention(
        fwd_middle_kernel, "fwd_middle", 576, False, [SM] + [VM] * 7,
        kept(576) + (MIDDLE,), (VM, VM, VM), 10**9, operands,
    )


def fwd_edge(*operands):
    return attention(
        fwd_edge_kernel, "fwd_edge", 384, False, [SM] + [VM] * 9,
        kept(384) + (FINE,), (VM, VM, VM), 10**9, operands,
    )


def bwd_middle(*operands):
    return attention(
        bwd_middle_kernel, "bwd_middle", 576, True, [SM] + [VM] * 7,
        MIDDLE, VM, 2 * 10**9, operands,
    )


def bwd_edge(*operands):
    return attention(
        bwd_edge_kernel, "bwd_edge", 384, True, [SM] + [VM] * 12,
        FINE, VM, 2 * 10**9, operands,
    )


def set_fine(fine, value):
    for lane in range(4):
        fine[lane] = value[:, 128 * lane : 128 * lane + 128]


def get_fine(fine):
    return jnp.concatenate([fine[lane] for lane in range(4)], 1)


def patch_parts(fine):
    parts = {}
    for s in range(2):
        lanes = [fine[lane, pl.ds(s, 256, 2), :] for lane in range(4)]
        half = jnp.concatenate(lanes, 1).reshape(16, 2, 8, 512)
        for r in range(2):
            parts[r + 2 * s] = half[:, r].reshape(128, 512)
    return [parts[k] for k in range(4)]


def unpatch(fine, parts):
    for s in range(2):
        pair = [parts[r + 2 * s].reshape(16, 1, 8, 512) for r in range(2)]
        half = jnp.concatenate(pair, 1).reshape(256, 512)
        for lane in range(4):
            fine[lane, pl.ds(s, 256, 2), :] = half[:, 128 * lane : 128 * lane + 128]


def joint_normalise(parts):
    mean = sum(jnp.sum(p, -1, keepdims=True) for p in parts) / 2048.0
    cent = [p - mean for p in parts]
    var = sum(jnp.sum(c * c, -1, keepdims=True) for c in cent) / 2048.0
    r = lax.rsqrt(var + EPS)
    return [c * r for c in cent], r


def ffn_fwd_kernel(
    resid, gain_ffn, w_fc1, w_fc2, gain_merge, w_merge, gain_mlp,
    slope_out, block_out, coarse_out, cin_out,
    acc, fine,
):
    xh, _ = normalise(resid[...].astype(F32))
    ffn_in = (xh * gain_ffn[...]).astype(BF)
    for n in range(4):
        cut = slice(512 * n, 512 * n + 512)
        for m in range(2):
            rows = slice(256 * m, 256 * m + 256)
            hid, slope = gelu_both(dot(ffn_in[rows], w_fc1[:, cut]))
            slope_out[rows, cut] = slope
            term = dot(hid, w_fc2[cut, :])
            if n == 0:
                acc[rows, :] = resid[rows, :].astype(F32) + term
            else:
                acc[rows, :] += term
    block = acc[...].astype(BF)
    block_out[...] = block
    set_fine(fine, block.astype(F32))
    xhs, _ = joint_normalise(patch_parts(fine))
    coarse = None
    for k in range(4):
        cut = slice(512 * k, 512 * k + 512)
        term = dot((xhs[k] * gain_merge[:, cut]).astype(BF), w_merge[cut, :])
        coarse = term if coarse is None else coarse + term
    coarse = coarse.astype(BF)
    coarse_out[...] = coarse
    xh, _ = normalise(coarse.astype(F32))
    cin_out[...] = (xh * gain_mlp[...]).astype(BF)


def ffn_fwd(resid, gain_ffn, w_fc1, w_fc2, gain_merge, w_merge, gain_mlp):
    return pl.pallas_call(
        ffn_fwd_kernel,
        out_shape=(
            jax.ShapeDtypeStruct((512, 2048), BF),
            jax.ShapeDtypeStruct((512, 512), BF),
            jax.ShapeDtypeStruct((128, 1024), BF),
            jax.ShapeDtypeStruct((128, 1024), BF),
        ),
        in_specs=[VM] * 7,
        out_specs=(VM, VM, VM, VM),
        scratch_shapes=[
            pltpu.VMEM((512, 512), F32),
            pltpu.VMEM((4, 512, 128), F32),
        ],
        compiler_params=params(32),
        cost_estimate=pl.CostEstimate(flops=3 * 10**9, bytes_accessed=12 * 2**20, transcendentals=10**6),
        name="ffn_fwd",
    )(resid, gain_ffn, w_fc1, w_fc2, gain_merge, w_merge, gain_mlp)


def weight_chunk(parts, y, lo):
    rows = []
    for k in range(4):
        ref, at = (parts[y], 128 * k) if y < 3 else (parts[3 + k // 2], 128 * (k % 2))
        rows += [ref[at + lo : at + lo + 32], ref[at + 64 + lo : at + 96 + lo]]
    return jnp.concatenate(rows, 0)


def mlp_kernel(
    place, c0, c1, c2, c3, d0, d1, d2, d3, w0, w1, w2, w3, w4,
    keep_out, send_out, hid_out,
    cs, deep, gacc,
):
    for k, (c, g) in enumerate(((c0, d0), (c1, d1), (c2, d2), (c3, d3))):
        cs[128 * k : 128 * k + 128] = c[...]
        deep[128 * k : 128 * k + 128] = g[...]
    parts = (w0, w1, w2, w3, w4)
    for y in range(4):
        first = weight_chunk(parts, y, 0)
        second = weight_chunk(parts, y, 32)
        for m in range(2):
            rows = slice(256 * m, 256 * m + 256)
            hid, slope = gelu_both(dot_nt(cs[rows], first))
            hid_out[rows, 256 * y : 256 * y + 256] = hid
            g_pre = dot_nt(deep[rows], second).astype(BF) * slope
            g_cin = dot(g_pre, first)
            if y == 0:
                gacc[rows] = g_cin
            else:
                gacc[rows] += g_cin
    part_out(gacc, keep_out, send_out)


def part_out(total, keep_out, send_out):
    keep_out[0:128] = total[0:128].astype(BF)
    keep_out[128:256] = total[256:384].astype(BF)
    send_out[0:128] = total[128:256].astype(BF)
    send_out[128:256] = total[384:512].astype(BF)


def coarse_mlp(place, cins, deeps, parts):
    return pl.pallas_call(
        mlp_kernel,
        out_shape=(
            jax.ShapeDtypeStruct((256, 1024), BF),
            jax.ShapeDtypeStruct((256, 1024), BF),
            jax.ShapeDtypeStruct((512, 1024), BF),
        ),
        in_specs=[SM] + [VM] * 13,
        out_specs=(VM, VM, VM),
        scratch_shapes=[
            pltpu.VMEM((512, 1024), BF),
            pltpu.VMEM((512, 1024), BF),
            pltpu.VMEM((512, 1024), F32),
        ],
        compiler_params=params(32),
        cost_estimate=pl.CostEstimate(flops=3 * 10**9, bytes_accessed=8 * 2**20, transcendentals=10**6),
        name="coarse_mlp",
    )(place, *cins, *deeps, *parts)


def down_kernel(hid, w0, w1, w2, w3, w4, keep_out, send_out):
    total = None
    for y in range(4):
        term = dot(hid[:, 256 * y : 256 * y + 256], weight_chunk((w0, w1, w2, w3, w4), y, 32))
        total = term if total is None else total + term
    part_out(total, keep_out, send_out)


def down_of(hid, parts):
    half = jax.ShapeDtypeStruct((256, 1024), BF)
    return pl.pallas_call(
        down_kernel,
        out_shape=(half, half),
        in_specs=[VM] * 6,
        out_specs=(VM, VM),
        compiler_params=params(32),
        cost_estimate=pl.CostEstimate(flops=10**9, bytes_accessed=5 * 2**20, transcendentals=0),
        name="down",
    )(hid, *parts)


def g_deep_kernel(cot, w_up, out, fine):
    set_fine(fine, cot[...].astype(F32))
    whole = jnp.concatenate([part.astype(BF) for part in patch_parts(fine)], 1)
    for k in range(4):
        rows = slice(256 * k, 256 * k + 256)
        out[:, rows] = dot_nt(whole, w_up[rows, :]).astype(BF)


UP_SCRATCH = [
    pltpu.VMEM((4, 512, 128), F32),
]


def g_deep_of(cot, w_up):
    return pl.pallas_call(
        g_deep_kernel,
        out_shape=jax.ShapeDtypeStruct((128, 1024), BF),
        in_specs=[VM, VM],
        out_specs=VM,
        scratch_shapes=UP_SCRATCH,
        compiler_params=params(32),
        cost_estimate=pl.CostEstimate(flops=10**9, bytes_accessed=5 * 2**20, transcendentals=0),
        name="g_deep",
    )(cot, w_up)


def up_kernel(coarse, keep, near, far, block, w_up, out, fine):
    deep = coarse[...].astype(F32) + keep[0:128].astype(F32) + near[0:128].astype(F32)
    deep = (deep + far[...].astype(F32)).astype(BF)
    acc = None
    for k in range(4):
        rows = slice(256 * k, 256 * k + 256)
        term = dot(deep[:, rows], w_up[rows, :])
        acc = term if acc is None else acc + term
    unpatch(fine, [acc[:, 512 * k : 512 * k + 512] for k in range(4)])
    out[...] = (block[...].astype(F32) + get_fine(fine)).astype(BF)


def up_of(coarse, keep, near, far, block, w_up):
    return pl.pallas_call(
        up_kernel,
        out_shape=jax.ShapeDtypeStruct((512, 512), BF),
        in_specs=[VM] * 6,
        out_specs=VM,
        scratch_shapes=UP_SCRATCH,
        compiler_params=params(32),
        cost_estimate=pl.CostEstimate(flops=10**9, bytes_accessed=5 * 2**20, transcendentals=0),
        name="up",
    )(coarse, keep, near, far, block, w_up)


def ffn_bwd_kernel(
    place, gcin_own, gcin_near, gcin_far, g_deep, coarse, gain_mlp, w_merge, block, gain_merge, cot,
    w_fc2, slope, w_fc1, resid, gain_ffn,
    g_resid_out, first_out, second_out,
    fine, acc,
):
    g_cin = gcin_own[0:128].astype(F32) + gcin_near[0:128].astype(F32) + gcin_far[...].astype(F32)
    g_cin = g_cin.astype(BF).astype(F32)
    part = norm_back(coarse[...].astype(F32), gain_mlp[...], g_cin)
    g_coarse = (g_deep[...].astype(F32) + part).astype(BF)
    set_fine(fine, block[...].astype(F32))
    xhs, r = joint_normalise(patch_parts(fine))
    scaled = []
    for k in range(4):
        cut = slice(512 * k, 512 * k + 512)
        scaled.append(dot_nt(g_coarse, w_merge[cut, :]) * gain_merge[:, cut])
    mean_s = sum(jnp.sum(s, -1, keepdims=True) for s in scaled) / 2048.0
    mean_x = sum(jnp.sum(s * x, -1, keepdims=True) for s, x in zip(scaled, xhs)) / 2048.0
    unpatch(fine, [r * (s - mean_s - x * mean_x) for s, x in zip(scaled, xhs)])
    g_block = (cot[...].astype(F32) + get_fine(fine)).astype(BF)
    for n in range(4):
        cut = slice(512 * n, 512 * n + 512)
        for m in range(2):
            rows = slice(256 * m, 256 * m + 256)
            g_pre = dot_nt(g_block[rows], w_fc2[cut, :]).astype(BF) * slope[rows, cut]
            term = dot_nt(g_pre, w_fc1[:, cut])
            if n == 0:
                acc[rows, :] = term
            else:
                acc[rows, :] += term
    g_fin = acc[...].astype(BF).astype(F32)
    part = norm_back(resid[...].astype(F32), gain_ffn[...], g_fin)
    total = g_block.astype(F32) + part
    g_resid_out[...] = total.astype(BF)
    lines = total.reshape(32, 16, 512)
    tail, head = sides(place[3] == 1, lines[:, :8], lines[:, 8:])
    first_out[...] = tail.astype(BF)
    second_out[...] = head.astype(BF)


def ffn_bwd(place, gcin_own, gcin_near, gcin_far, g_deep, coarse, gain_mlp, w_merge, block, gain_merge, cot,
            w_fc2, slope, w_fc1, resid, gain_ffn):
    return pl.pallas_call(
        ffn_bwd_kernel,
        out_shape=(
            jax.ShapeDtypeStruct((512, 512), BF),
            jax.ShapeDtypeStruct((32, 8, 512), BF),
            jax.ShapeDtypeStruct((32, 8, 512), BF),
        ),
        in_specs=[SM] + [VM] * 15,
        out_specs=(VM, VM, VM),
        scratch_shapes=[
            pltpu.VMEM((4, 512, 128), F32),
            pltpu.VMEM((512, 512), F32),
        ],
        compiler_params=params(32),
        cost_estimate=pl.CostEstimate(flops=3 * 10**9, bytes_accessed=14 * 2**20, transcendentals=0),
        name="ffn_bwd",
    )(place, gcin_own, gcin_near, gcin_far, g_deep, coarse, gain_mlp, w_merge, block, gain_merge, cot,
      w_fc2, slope, w_fc1, resid, gain_ffn)


def ends_kernel(tokens, turned, first_out, second_out, slab_out):
    odd = (lax.axis_index("lon") & 1) == 1
    slab = jnp.concatenate([turned[...].astype(F32), jnp.zeros((16, 480), F32)], 1)
    slab_out[...] = slab.astype(BF)
    lines = tokens[...].astype(F32)
    for at, source in ((slice(0, 32), lines), (slice(32, 33), slab.reshape(1, 16, 512))):
        tail, head = sides(odd, source[:, :8], source[:, 8:])
        first_out[at] = tail.astype(BF)
        second_out[at] = head.astype(BF)


def ends(tokens, turned):
    part = jax.ShapeDtypeStruct((33, 8, 512), BF)
    return pl.pallas_call(
        ends_kernel,
        out_shape=(part, part, jax.ShapeDtypeStruct((16, 512), BF)),
        in_specs=[VM] * 2,
        out_specs=(VM,) * 3,
        compiler_params=params(32),
        cost_estimate=pl.CostEstimate(flops=10**6, bytes_accessed=2 * 2**20, transcendentals=0),
        name="ends",
    )(tokens, turned)


def cut_kernel(w_first, w_second, s0, s1, s2, s3, both):
    me = lax.axis_index("lat")
    both[0] = w_first[...].astype(F32).T.astype(BF)
    both[1] = w_second[...]
    for k, out in enumerate((s0, s1, s2, s3)):
        rows = pl.ds(pl.multiple_of(lax.bitwise_xor(me, k) * 32, 32), 32)
        out[0:32] = both[0, rows, :]
        out[32:64] = both[1, rows, :]


def cut(w_first, w_second):
    block = jax.ShapeDtypeStruct((64, 256), BF)
    return pl.pallas_call(
        cut_kernel,
        out_shape=(block,) * 4,
        in_specs=[VM] * 2,
        out_specs=(VM,) * 4,
        scratch_shapes=[pltpu.VMEM((2, 128, 256), BF)],
        compiler_params=params(32),
        cost_estimate=pl.CostEstimate(flops=10**6, bytes_accessed=2**19, transcendentals=0),
        name="cut",
    )(w_first, w_second)


def join_kernel(place, s0, s1, s2, s3, out):
    for k, block in enumerate((s0, s1, s2, s3)):
        at = pl.multiple_of(lax.bitwise_xor(place[2], k) * 256, 256)
        out[:, pl.ds(at, 256)] = block[...]


def join(place, blocks):
    return pl.pallas_call(
        join_kernel,
        out_shape=jax.ShapeDtypeStruct((64, 1024), BF),
        in_specs=[SM] + [VM] * 4,
        out_specs=VM,
        compiler_params=params(32),
        cost_estimate=pl.CostEstimate(flops=10**6, bytes_accessed=2**18, transcendentals=0),
        name="join",
    )(place, *blocks)


def stack_kernel(*refs):
    for k, ref in enumerate(refs[:-1]):
        refs[-1][128 * k : 128 * k + 128] = ref[...]


def stacked(blocks):
    return pl.pallas_call(
        stack_kernel,
        out_shape=jax.ShapeDtypeStruct((512, 1024), BF),
        in_specs=[VM] * 4,
        out_specs=VM,
        compiler_params=params(32),
        cost_estimate=pl.CostEstimate(flops=10**6, bytes_accessed=2**21, transcendentals=0),
        name="stacked",
    )(*blocks)


def halves_kernel(ahead, behind, first, second):
    first[...] = ahead[0:256]
    second[...] = behind[256:512]


def halves(ahead, behind):
    half = jax.ShapeDtypeStruct((256, 1024), BF)
    return pl.pallas_call(
        halves_kernel,
        out_shape=(half, half),
        in_specs=[VM] * 2,
        out_specs=(VM, VM),
        compiler_params=params(32),
        cost_estimate=pl.CostEstimate(flops=10**6, bytes_accessed=2**21, transcendentals=0),
        name="halves",
    )(ahead, behind)


def strips_kernel(place, first, own, second, *rest):
    odd = place[3] == 1
    top_out, bottom_out = rest[-2:]
    for out, lo in ((top_out, 0), (bottom_out, 24)):
        rows = slice(lo, lo + 8)
        left, right = sides(odd, first[rows].astype(F32), second[rows].astype(F32))
        out[0:8, 0:8, :] = left.astype(BF)
        out[0:8, 8:24, :] = own[rows]
        out[0:8, 24:32, :] = right.astype(BF)
        if len(rest) == 3:
            left, right = sides(odd, first[32].astype(F32), second[32].astype(F32))
            out[8] = jnp.concatenate([left, rest[0][...].astype(F32), right], 0).astype(BF)


def strips(place, first, own, second, *slab):
    edge = jax.ShapeDtypeStruct((8 + len(slab), 32, 512), BF)
    return pl.pallas_call(
        strips_kernel,
        out_shape=(edge, edge),
        in_specs=[SM] + [VM] * (3 + len(slab)),
        out_specs=(VM, VM),
        compiler_params=params(32),
        cost_estimate=pl.CostEstimate(flops=10**6, bytes_accessed=3 * 2**20, transcendentals=0),
        name="strips",
    )(place, first, own, second, *slab)


def along(axis, count, step):
    pairs = [(s, (s + step) % count) for s in range(count)]
    return lambda v: lax.ppermute(v, axis, pairs)


LAT_NEXT, LAT_PREV = along("lat", 4, 1), along("lat", 4, -1)


def even_odd(v):
    return lax.ppermute(v, "lon", [(k, k ^ 1) for k in range(32)])


def odd_even(v):
    return lax.ppermute(v, "lon", [(k, (((k + 1) ^ 1) - 1) % 32) for k in range(32)])


def core_swap(v):
    return lax.ppermute(v, "lat", [(0, 1), (1, 0), (2, 3), (3, 2)])


def x_swap(v):
    return lax.ppermute(v, "lat", [(0, 2), (2, 0), (1, 3), (3, 1)])


def cross_swap(v):
    return lax.ppermute(v, "lat", [(0, 3), (3, 0), (1, 2), (2, 1)])


def x_far_swap(v):
    return lax.ppermute(v, "lon", [(k, (k + 16) % 32) for k in range(32)])


def turn(swapped, k):
    pairs = []
    for lat in range(4):
        along_y = (lat % 2 == 1) != swapped
        for lon in range(32):
            x, y, z = lon // 16, lon // 4 % 4, lon % 4
            if along_y:
                y = (y + k) % 4
            else:
                z = (z + k) % 4
            pairs.append((lat * 32 + lon, lat * 32 + (x * 4 + y) * 4 + z))
    return lambda v: lax.ppermute(v, ("lat", "lon"), pairs)


def after(value, *gates):
    return lax.optimization_barrier((value,) + gates)[0]


def on_device(
    tokens, labels, offsets, gain_attn, w_qkv, w_proj, gain_ffn, w_fc1, w_fc2,
    gain_merge, w_merge, gain_mlp, w_first, w_second, w_up, cotangent,
):
    row = lambda g: g.reshape(1, -1)
    s0, s1, s2, s3 = cut(w_first, w_second)
    s1, s2, s3 = core_swap(s1), x_swap(s2), cross_swap(s3)
    first, second, slab = ends(after(tokens, s0), labels.T)
    left, right = even_odd(first), odd_even(second)
    where = [lax.axis_index("lat"), lax.axis_index("lon") & 1]
    place = jnp.concatenate([after(offsets, slab), jnp.stack(where).astype(jnp.int32)])
    mine = join(place, (s0, s1, s2, s3))
    other = x_far_swap(mine)
    cot = cotangent.reshape(512, 512)
    g_deep = g_deep_of(after(cot, mine), w_up)
    near_deep = core_swap(g_deep)
    seed = jnp.concatenate([mine, after(other, g_deep)], 0)
    moved = [turn(False, k)(seed) for k in (1, -1, 2)]
    bottom, top = strips(place, left, after(tokens, seed), right, slab)
    up, down = LAT_NEXT(top), LAT_PREV(bottom)
    gain = row(gain_attn)
    qkv_mid, probs_mid, middle = fwd_middle(
        place, left, tokens, right, slab, gain, w_qkv, w_proj
    )
    part = stacked([after(seed, up, down, middle)] + moved)
    ahead, behind = turn(True, 1)(part), turn(True, -1)(part)
    qkv_edge, probs_edge, resid = fwd_edge(
        place, after(up, part), bottom, top, down, tokens, middle, gain, w_qkv, w_proj
    )
    resid = resid.reshape(512, 512)
    far_deep = x_swap(after(g_deep, resid))
    slope, block, coarse, coarse_in = ffn_fwd(
        resid, row(gain_ffn), w_fc1, w_fc2, row(gain_merge), w_merge, row(gain_mlp)
    )
    fore, hind = halves(after(ahead, coarse_in), behind)
    far_cin = x_swap(coarse_in)
    near_cin = core_swap(coarse_in)
    parts = [part, ahead, behind, turn(True, 1)(fore), turn(True, -1)(hind)]
    cins = [coarse_in, near_cin, far_cin, core_swap(far_cin)]
    deeps = [g_deep, near_deep, far_deep, core_swap(after(far_deep, coarse_in))]
    keep, send, hid = coarse_mlp(place, cins, deeps, parts)
    near = core_swap(send)
    gcin_far = x_swap((keep[128:].astype(F32) + near[128:].astype(F32)).astype(BF))
    down_keep, down_send = down_of(hid, parts)
    down_near = core_swap(down_send)
    down_far = (down_keep[128:].astype(F32) + down_near[128:].astype(F32)).astype(BF)
    gcin_far, down_far = lax.optimization_barrier((gcin_far, down_far))
    down_far = x_swap(down_far)
    g_resid, g_first, g_second = ffn_bwd(
        place, keep, near, gcin_far, g_deep, coarse, row(gain_mlp), w_merge, block, row(gain_merge), cot,
        w_fc2, slope, w_fc1, resid, row(gain_ffn),
    )
    g_resid = g_resid.reshape(32, 16, 512)
    g_left, g_right = even_odd(g_first), odd_even(g_second)
    field_out = up_of(coarse, down_keep, down_near, down_far, block, w_up).reshape(32, 16, 512)
    g_bottom, g_top = strips(place, g_left, after(g_resid, field_out), g_right)
    g_up, g_down = LAT_NEXT(g_top), LAT_PREV(g_bottom)
    g_middle = bwd_middle(place, g_left, g_resid, g_right, qkv_mid, probs_mid, w_proj, w_qkv)
    grad_in = bwd_edge(
        place, g_up, g_bottom, g_top, g_down, g_resid, g_middle, qkv_edge, probs_edge,
        w_proj, w_qkv, tokens, gain,
    )
    return (field_out, grad_in)


def solution(mesh):
    grid = P("lat", "lon", None)
    placed = (
        grid, P("lat", "lon"), P(), P(), P(), P(), P(), P(), P(), P(), P(), P(),
        P("lat", "lon"), P("lon", "lat"), P(), grid,
    )
    return jax.shard_map(
        on_device, mesh=mesh, in_specs=placed, out_specs=(grid, grid), check_vma=False
    )
```

```python
import jax
import jax.numpy as jnp
from jax import lax
from jax.experimental import pallas as pl
from jax.experimental.pallas import tpu as pltpu
from jax.sharding import PartitionSpec as P

BF = jnp.bfloat16
F32 = jnp.float32
EPS = 1e-05
NT = (((1,), (1,)), ((), ()))
TN = (((0,), (0,)), ((), ()))
GELU_C = 0.7978845608028654
GELU_A = 0.044715


def dot(a, b):
    return jnp.dot(a, b, preferred_element_type=F32)


def dot_nt(a, b):
    return lax.dot_general(a, b, NT, preferred_element_type=F32)


def dot_tn(a, b):
    return lax.dot_general(a, b, TN, preferred_element_type=F32)


def normalise(v):
    mean = jnp.mean(v, -1, keepdims=True)
    c = v - mean
    r = lax.rsqrt(jnp.mean(c * c, -1, keepdims=True) + EPS)
    return c * r, r


def norm_back(v, gain, t):
    xh, r = normalise(v)
    s = t * gain
    return r * (s - jnp.mean(s, -1, keepdims=True) - xh * jnp.mean(s * xh, -1, keepdims=True))


def gelu_both(wide):
    x = wide.astype(BF)
    x2 = x * x
    t = jnp.tanh(x * (GELU_C + GELU_C * GELU_A * x2))
    h = 0.5 * x
    slope = (0.5 + 0.5 * t) + (h - h * t * t) * (GELU_C + 3.0 * GELU_C * GELU_A * x2)
    return h + h * t, slope


def half_masks(scale):
    low = lax.broadcasted_iota(jnp.int32, (1, 128), 1) < 64
    return [jnp.where(m, scale, 0.0).astype(F32).astype(BF) for m in (low, jnp.logical_not(low))]


def spread(x, masks):
    none = jnp.zeros((64, 128), BF)
    left, right = x[:, :128], x[:, 128:]
    rows = [jnp.concatenate([left * m, none], 1) for m in masks]
    rows += [jnp.concatenate([none, right * m], 1) for m in masks]
    return jnp.concatenate(rows, 0)


def collect(big):
    low = lax.broadcasted_iota(jnp.int32, (64, 128), 1) < 64
    left = jnp.where(low, big[0:64, :128], big[64:128, :128])
    right = jnp.where(low, big[128:192, 128:], big[192:256, 128:])
    return jnp.concatenate([left, right], 1)


def sides(odd, first, second):
    return jnp.where(odd, first, second), jnp.where(odd, second, first)


def shifted_cols(lines, b):
    return pltpu.roll(lines, 32 - b, 1)[:, :24]


def fill_middle(grid, b, odd, first, own, second):
    def rows(n, carry):
        at = pl.ds(8 * n, 8)
        left, right = sides(odd, first[at].astype(F32), second[at].astype(F32))
        grid[at] = shifted_cols(jnp.concatenate([left, own[at].astype(F32), right], 1), b)
        return carry

    lax.fori_loop(0, 4, rows, 0)


def fill_edges(grid, b, edges):
    for n, edge in enumerate(edges):
        grid[8 * n : 8 * n + 8] = shifted_cols(edge[0:8].astype(F32), b)


def slab_cols(slab, b):
    return pltpu.roll(slab, 32 - b, 0)[:24]


def place_back(back, n, a, b):
    return pltpu.roll(back[pl.ds(8 - a + 8 * n, 8)], 16 + b, 1)[:, :16]


def windows_of(grid, base, a):
    lines = grid[pl.ds(a + base, 8)]
    return [lines[:, 8 * k : 8 * k + 8].reshape(64, grid.shape[2]) for k in range(3)]


def put_windows(back, row, value):
    for k in range(3):
        part = value[64 * k : 64 * k + 64].reshape(8, 8, 512)
        back[row : row + 8, 8 * k : 8 * k + 8, :] = part


def fwd_windows(grid, codes, cols, mixed, qkv, probs, gain, w_qkv, bases, a):
    for n, base in enumerate(bases):
        normed = [(normalise(x)[0] * gain[...]).astype(BF) for x in windows_of(grid, base, a)]
        qkv[192 * n : 192 * n + 192] = dot(jnp.concatenate(normed, 0), w_qkv[...]).astype(BF)
        for k, col in enumerate(windows_of(codes, base, a)):
            cols[3 * n + k] = col
    masks = half_masks(0.125)

    def window(w, carry):
        at = pl.ds(pl.multiple_of(w * 64, 64), 64)
        col = cols[w]
        row = col.T[0:1, 0:64]
        same = jnp.concatenate([col, col], 1) == jnp.concatenate([row] * 4, 1)
        for c in range(2):
            lo = 256 * c
            qbig = spread(qkv[at, lo : lo + 256], masks)
            k = qkv[at, 512 + lo : 768 + lo]
            v = qkv[at, 1024 + lo : 1280 + lo]
            e = jnp.where(same, jnp.exp(dot_nt(k, qbig)), 0.0)
            p = (e * (1.0 / jnp.sum(e, 0, keepdims=True))).astype(BF)
            probs[at, lo : lo + 256] = p
            mixed[at, lo : lo + 256] = collect(dot_tn(p, v)).astype(BF)
        return carry

    lax.fori_loop(0, 3 * len(bases), window, 0, unroll=True)


def fwd_middle_kernel(
    place, first, own, second, own_slab, gain, w_qkv, w_proj,
    qkv, probs, back,
    grid, codes, cols, mixed,
):
    a, b = place[0], place[1]
    odd = place[3] == 1
    fill_middle(grid, b, odd, first, own, second)
    left, right = sides(odd, first[32].astype(F32), second[32].astype(F32))
    slab = slab_cols(jnp.concatenate([left, own_slab[...].astype(F32), right], 0), b)
    for r in range(32):
        codes[r] = jnp.broadcast_to(slab[:, r : r + 1], (24, 128))
    bases = (0, 8, 16)
    fwd_windows(grid, codes, cols, mixed, qkv, probs, gain, w_qkv, bases, a)
    for n in range(3):
        att = dot(mixed[192 * n : 192 * n + 192], w_proj[...]).astype(BF).astype(F32)
        put_windows(back, 8 * n, att)


def fwd_edge_kernel(
    place, up, bottom, top, down, own, middle, gain, w_qkv, w_proj,
    qkv, probs, resid_out,
    grid, codes, cols, mixed, back,
):
    a, b, d = place[0], place[1], place[2]
    edges = (up, bottom, top, down)
    fill_edges(grid, b, edges)
    extra = (jnp.where(d == 0, 4.0, 0.0), 0.0, 0.0, jnp.where(d == 3, 4.0, 0.0))
    for n, (edge, lane, code) in enumerate(zip(edges, (24, 0, 24, 0), extra)):
        slab = slab_cols(edge[8].astype(F32) + code, b)
        for r in range(8):
            codes[8 * n + r] = jnp.broadcast_to(slab[:, lane + r : lane + r + 1], (24, 128))
    bases = (0, 16)
    fwd_windows(grid, codes, cols, mixed, qkv, probs, gain, w_qkv, bases, a)
    back[8:32] = middle[...]
    for n in range(2):
        att = dot(mixed[192 * n : 192 * n + 192], w_proj[...]).astype(BF).astype(F32)
        put_windows(back, 32 * n, att)
    for n in range(4):
        at = slice(8 * n, 8 * n + 8)
        resid_out[at] = (own[at].astype(F32) + place_back(back, n, a, b)).astype(BF)


def bwd_windows(grid, g_mixed, g_qkv, qkv, probs, w_proj, bases, a):
    for n, base in enumerate(bases):
        ups = jnp.concatenate([x.astype(BF) for x in windows_of(grid, base, a)], 0)
        g_mixed[192 * n : 192 * n + 192] = dot_nt(ups, w_proj[...]).astype(BF)
    masks, scaled = half_masks(1.0), half_masks(0.125)

    def window(w, carry):
        at = pl.ds(pl.multiple_of(w * 64, 64), 64)
        for c in range(2):
            lo = 256 * c
            qbig = spread(qkv[at, lo : lo + 256], scaled)
            gbig = spread(g_mixed[at, lo : lo + 256], masks)
            k = qkv[at, 512 + lo : 768 + lo]
            v = qkv[at, 1024 + lo : 1280 + lo]
            p = probs[at, lo : lo + 256]
            g_probs = dot_nt(v, gbig)
            wide_p = p.astype(F32)
            total = jnp.sum(wide_p * g_probs, 0, keepdims=True)
            g_score = (wide_p * (g_probs - total)).astype(BF)
            g_qkv[at, lo : lo + 256] = (collect(dot_tn(g_score, k)) * 0.125).astype(BF)
            g_qkv[at, 512 + lo : 768 + lo] = dot(g_score, qbig).astype(BF)
            g_qkv[at, 1024 + lo : 1280 + lo] = dot(p, gbig).astype(BF)
        return carry

    lax.fori_loop(0, 3 * len(bases), window, 0, unroll=True)


def bwd_middle_kernel(
    place, first, own, second, qkv, probs, w_proj, w_qkv,
    back,
    grid, g_mixed, g_qkv,
):

    a, b = place[0], place[1]
    fill_middle(grid, b, place[3] == 1, first, own, second)
    bwd_windows(grid, g_mixed, g_qkv, qkv, probs, w_proj, (0, 8, 16), a)
    for n in range(3):
        g_shift = dot_nt(g_qkv[192 * n : 192 * n + 192], w_qkv[...]).astype(BF).astype(F32)
        put_windows(back, 8 * n, g_shift)


def bwd_edge_kernel(
    place, up, bottom, top, down, own, middle, qkv, probs, w_proj, w_qkv,
    tokens, gain,
    grad_out,
    grid, g_mixed, g_qkv, back,
):

    a, b = place[0], place[1]
    fill_edges(grid, b, (up, bottom, top, down))
    bwd_windows(grid, g_mixed, g_qkv, qkv, probs, w_proj, (0, 16), a)
    back[8:32] = middle[...]
    for n in range(2):
        g_shift = dot_nt(g_qkv[192 * n : 192 * n + 192], w_qkv[...]).astype(BF).astype(F32)
        put_windows(back, 32 * n, g_shift)
    for n in range(4):
        at = slice(8 * n, 8 * n + 8)
        part = norm_back(tokens[at].astype(F32), gain[...], place_back(back, n, a, b))
        grad_out[at] = (own[at].astype(F32) + part).astype(BF)


VM = pl.BlockSpec(memory_space=pltpu.VMEM)
SM = pl.BlockSpec(memory_space=pltpu.SMEM)


def params(mib):
    return pltpu.CompilerParams(vmem_limit_bytes=mib * 2**20)


def attn_scratch(rows, backward):
    shapes = [(32, 24, 512, F32)]
    if not backward:
        shapes += [(32, 24, 128, F32), (rows // 64, 64, 128, F32), (rows, 512, BF)]
    else:
        shapes += [(rows, 512, BF), (rows, 1536, BF)]
    if rows == 384:
        shapes += [(40, 24, 512, F32)]
    return [pltpu.VMEM(shape[:-1], shape[-1]) for shape in shapes]


MIDDLE = jax.ShapeDtypeStruct((24, 24, 512), F32)
FINE = jax.ShapeDtypeStruct((32, 16, 512), BF)


def attention(kernel, name, rows, backward, specs, outs, out_specs, flops, operands):
    return pl.pallas_call(
        kernel,
        out_shape=outs,
        in_specs=specs,
        out_specs=out_specs,
        scratch_shapes=attn_scratch(rows, backward),
        compiler_params=params(32),
        cost_estimate=pl.CostEstimate(flops=flops, bytes_accessed=6 * 2**20, transcendentals=10**5),
        name=name,
    )(*operands)


def kept(rows):
    return (jax.ShapeDtypeStruct((rows, 1536), BF), jax.ShapeDtypeStruct((rows, 512), BF))


def fwd_middle(*operands):
    return attention(
        fwd_middle_kernel, "fwd_middle", 576, False, [SM] + [VM] * 7,
        kept(576) + (MIDDLE,), (VM, VM, VM), 10**9, operands,
    )


def fwd_edge(*operands):
    return attention(
        fwd_edge_kernel, "fwd_edge", 384, False, [SM] + [VM] * 9,
        kept(384) + (FINE,), (VM, VM, VM), 10**9, operands,
    )


def bwd_middle(*operands):
    return attention(
        bwd_middle_kernel, "bwd_middle", 576, True, [SM] + [VM] * 7,
        MIDDLE, VM, 2 * 10**9, operands,
    )


def bwd_edge(*operands):
    return attention(
        bwd_edge_kernel, "bwd_edge", 384, True, [SM] + [VM] * 12,
        FINE, VM, 2 * 10**9, operands,
    )


def set_fine(fine, value):
    for lane in range(4):
        fine[lane] = value[:, 128 * lane : 128 * lane + 128]


def get_fine(fine):
    return jnp.concatenate([fine[lane] for lane in range(4)], 1)


def patch_parts(fine):
    parts = {}
    for s in range(2):
        lanes = [fine[lane, pl.ds(s, 256, 2), :] for lane in range(4)]
        half = jnp.concatenate(lanes, 1).reshape(16, 2, 8, 512)
        for r in range(2):
            parts[r + 2 * s] = half[:, r].reshape(128, 512)
    return [parts[k] for k in range(4)]


def unpatch(fine, parts):
    for s in range(2):
        pair = [parts[r + 2 * s].reshape(16, 1, 8, 512) for r in range(2)]
        half = jnp.concatenate(pair, 1).reshape(256, 512)
        for lane in range(4):
            fine[lane, pl.ds(s, 256, 2), :] = half[:, 128 * lane : 128 * lane + 128]


def joint_normalise(parts):
    mean = sum(jnp.sum(p, -1, keepdims=True) for p in parts) / 2048.0
    cent = [p - mean for p in parts]
    var = sum(jnp.sum(c * c, -1, keepdims=True) for c in cent) / 2048.0
    r = lax.rsqrt(var + EPS)
    return [c * r for c in cent], r


def ffn_fwd_kernel(
    resid, gain_ffn, w_fc1, w_fc2, gain_merge, w_merge, gain_mlp,
    slope_out, block_out, coarse_out, cin_out,
    acc, fine,
):
    xh, _ = normalise(resid[...].astype(F32))
    ffn_in = (xh * gain_ffn[...]).astype(BF)
    for n in range(4):
        cut = slice(512 * n, 512 * n + 512)
        for m in range(2):
            rows = slice(256 * m, 256 * m + 256)
            hid, slope = gelu_both(dot(ffn_in[rows], w_fc1[:, cut]))
            slope_out[rows, cut] = slope
            term = dot(hid, w_fc2[cut, :])
            if n == 0:
                acc[rows, :] = resid[rows, :].astype(F32) + term
            else:
                acc[rows, :] += term
    block = acc[...].astype(BF)
    block_out[...] = block
    set_fine(fine, block.astype(F32))
    xhs, _ = joint_normalise(patch_parts(fine))
    coarse = None
    for k in range(4):
        cut = slice(512 * k, 512 * k + 512)
        term = dot((xhs[k] * gain_merge[:, cut]).astype(BF), w_merge[cut, :])
        coarse = term if coarse is None else coarse + term
    coarse = coarse.astype(BF)
    coarse_out[...] = coarse
    xh, _ = normalise(coarse.astype(F32))
    cin_out[...] = (xh * gain_mlp[...]).astype(BF)


def ffn_fwd(resid, gain_ffn, w_fc1, w_fc2, gain_merge, w_merge, gain_mlp):
    return pl.pallas_call(
        ffn_fwd_kernel,
        out_shape=(
            jax.ShapeDtypeStruct((512, 2048), BF),
            jax.ShapeDtypeStruct((512, 512), BF),
            jax.ShapeDtypeStruct((128, 1024), BF),
            jax.ShapeDtypeStruct((128, 1024), BF),
        ),
        in_specs=[VM] * 7,
        out_specs=(VM, VM, VM, VM),
        scratch_shapes=[
            pltpu.VMEM((512, 512), F32),
            pltpu.VMEM((4, 512, 128), F32),
        ],
        compiler_params=params(32),
        cost_estimate=pl.CostEstimate(flops=3 * 10**9, bytes_accessed=12 * 2**20, transcendentals=10**6),
        name="ffn_fwd",
    )(resid, gain_ffn, w_fc1, w_fc2, gain_merge, w_merge, gain_mlp)


def weight_chunk(parts, y, lo):
    rows = []
    for k in range(4):
        ref, at = (parts[y], 128 * k) if y < 3 else (parts[3 + k // 2], 128 * (k % 2))
        rows += [ref[at + lo : at + lo + 32], ref[at + 64 + lo : at + 96 + lo]]
    return jnp.concatenate(rows, 0)


def mlp_kernel(
    place, c0, c1, c2, c3, d0, d1, d2, d3, w0, w1, w2, w3, w4,
    keep_out, send_out, hid_out,
    cs, deep, gacc,
):
    for k, (c, g) in enumerate(((c0, d0), (c1, d1), (c2, d2), (c3, d3))):
        cs[128 * k : 128 * k + 128] = c[...]
        deep[128 * k : 128 * k + 128] = g[...]
    parts = (w0, w1, w2, w3, w4)
    for y in range(4):
        first = weight_chunk(parts, y, 0)
        second = weight_chunk(parts, y, 32)
        for m in range(2):
            rows = slice(256 * m, 256 * m + 256)
            hid, slope = gelu_both(dot_nt(cs[rows], first))
            hid_out[rows, 256 * y : 256 * y + 256] = hid
            g_pre = dot_nt(deep[rows], second).astype(BF) * slope
            g_cin = dot(g_pre, first)
            if y == 0:
                gacc[rows] = g_cin
            else:
                gacc[rows] += g_cin
    part_out(gacc, keep_out, send_out)


def part_out(total, keep_out, send_out):
    keep_out[0:128] = total[0:128].astype(BF)
    keep_out[128:256] = total[256:384].astype(BF)
    send_out[0:128] = total[128:256].astype(BF)
    send_out[128:256] = total[384:512].astype(BF)


def coarse_mlp(place, cins, deeps, parts):
    return pl.pallas_call(
        mlp_kernel,
        out_shape=(
            jax.ShapeDtypeStruct((256, 1024), BF),
            jax.ShapeDtypeStruct((256, 1024), BF),
            jax.ShapeDtypeStruct((512, 1024), BF),
        ),
        in_specs=[SM] + [VM] * 13,
        out_specs=(VM, VM, VM),
        scratch_shapes=[
            pltpu.VMEM((512, 1024), BF),
            pltpu.VMEM((512, 1024), BF),
            pltpu.VMEM((512, 1024), F32),
        ],
        compiler_params=params(32),
        cost_estimate=pl.CostEstimate(flops=3 * 10**9, bytes_accessed=8 * 2**20, transcendentals=10**6),
        name="coarse_mlp",
    )(place, *cins, *deeps, *parts)


def down_kernel(hid, w0, w1, w2, w3, w4, keep_out, send_out):
    total = None
    for y in range(4):
        term = dot(hid[:, 256 * y : 256 * y + 256], weight_chunk((w0, w1, w2, w3, w4), y, 32))
        total = term if total is None else total + term
    part_out(total, keep_out, send_out)


def down_of(hid, parts):
    half = jax.ShapeDtypeStruct((256, 1024), BF)
    return pl.pallas_call(
        down_kernel,
        out_shape=(half, half),
        in_specs=[VM] * 6,
        out_specs=(VM, VM),
        compiler_params=params(32),
        cost_estimate=pl.CostEstimate(flops=10**9, bytes_accessed=5 * 2**20, transcendentals=0),
        name="down",
    )(hid, *parts)


def g_deep_kernel(cot, w_up, out, fine):
    set_fine(fine, cot[...].astype(F32))
    whole = jnp.concatenate([part.astype(BF) for part in patch_parts(fine)], 1)
    for k in range(4):
        rows = slice(256 * k, 256 * k + 256)
        out[:, rows] = dot_nt(whole, w_up[rows, :]).astype(BF)


UP_SCRATCH = [
    pltpu.VMEM((4, 512, 128), F32),
]


def g_deep_of(cot, w_up):
    return pl.pallas_call(
        g_deep_kernel,
        out_shape=jax.ShapeDtypeStruct((128, 1024), BF),
        in_specs=[VM, VM],
        out_specs=VM,
        scratch_shapes=UP_SCRATCH,
        compiler_params=params(32),
        cost_estimate=pl.CostEstimate(flops=10**9, bytes_accessed=5 * 2**20, transcendentals=0),
        name="g_deep",
    )(cot, w_up)


def up_kernel(coarse, keep, near, far, block, w_up, out, fine):
    deep = coarse[...].astype(F32) + keep[0:128].astype(F32) + near[0:128].astype(F32)
    deep = (deep + far[...].astype(F32)).astype(BF)
    acc = None
    for k in range(4):
        rows = slice(256 * k, 256 * k + 256)
        term = dot(deep[:, rows], w_up[rows, :])
        acc = term if acc is None else acc + term
    unpatch(fine, [acc[:, 512 * k : 512 * k + 512] for k in range(4)])
    out[...] = (block[...].astype(F32) + get_fine(fine)).astype(BF)


def up_of(coarse, keep, near, far, block, w_up):
    return pl.pallas_call(
        up_kernel,
        out_shape=jax.ShapeDtypeStruct((512, 512), BF),
        in_specs=[VM] * 6,
        out_specs=VM,
        scratch_shapes=UP_SCRATCH,
        compiler_params=params(32),
        cost_estimate=pl.CostEstimate(flops=10**9, bytes_accessed=5 * 2**20, transcendentals=0),
        name="up",
    )(coarse, keep, near, far, block, w_up)


def ffn_bwd_kernel(
    place, gcin_own, gcin_near, gcin_far, g_deep, coarse, gain_mlp, w_merge, block, gain_merge, cot,
    w_fc2, slope, w_fc1, resid, gain_ffn,
    g_resid_out, first_out, second_out,
    fine, acc,
):
    g_cin = gcin_own[0:128].astype(F32) + gcin_near[0:128].astype(F32) + gcin_far[...].astype(F32)
    g_cin = g_cin.astype(BF).astype(F32)
    part = norm_back(coarse[...].astype(F32), gain_mlp[...], g_cin)
    g_coarse = (g_deep[...].astype(F32) + part).astype(BF)
    set_fine(fine, block[...].astype(F32))
    xhs, r = joint_normalise(patch_parts(fine))
    scaled = []
    for k in range(4):
        cut = slice(512 * k, 512 * k + 512)
        scaled.append(dot_nt(g_coarse, w_merge[cut, :]) * gain_merge[:, cut])
    mean_s = sum(jnp.sum(s, -1, keepdims=True) for s in scaled) / 2048.0
    mean_x = sum(jnp.sum(s * x, -1, keepdims=True) for s, x in zip(scaled, xhs)) / 2048.0
    unpatch(fine, [r * (s - mean_s - x * mean_x) for s, x in zip(scaled, xhs)])
    g_block = (cot[...].astype(F32) + get_fine(fine)).astype(BF)
    for n in range(4):
        cut = slice(512 * n, 512 * n + 512)
        for m in range(2):
            rows = slice(256 * m, 256 * m + 256)
            g_pre = dot_nt(g_block[rows], w_fc2[cut, :]).astype(BF) * slope[rows, cut]
            term = dot_nt(g_pre, w_fc1[:, cut])
            if n == 0:
                acc[rows, :] = term
            else:
                acc[rows, :] += term
    g_fin = acc[...].astype(BF).astype(F32)
    part = norm_back(resid[...].astype(F32), gain_ffn[...], g_fin)
    total = g_block.astype(F32) + part
    g_resid_out[...] = total.astype(BF)
    lines = total.reshape(32, 16, 512)
    tail, head = sides(place[3] == 1, lines[:, :8], lines[:, 8:])
    first_out[...] = tail.astype(BF)
    second_out[...] = head.astype(BF)


def ffn_bwd(place, gcin_own, gcin_near, gcin_far, g_deep, coarse, gain_mlp, w_merge, block, gain_merge, cot,
            w_fc2, slope, w_fc1, resid, gain_ffn):
    return pl.pallas_call(
        ffn_bwd_kernel,
        out_shape=(
            jax.ShapeDtypeStruct((512, 512), BF),
            jax.ShapeDtypeStruct((32, 8, 512), BF),
            jax.ShapeDtypeStruct((32, 8, 512), BF),
        ),
        in_specs=[SM] + [VM] * 15,
        out_specs=(VM, VM, VM),
        scratch_shapes=[
            pltpu.VMEM((4, 512, 128), F32),
            pltpu.VMEM((512, 512), F32),
        ],
        compiler_params=params(32),
        cost_estimate=pl.CostEstimate(flops=3 * 10**9, bytes_accessed=14 * 2**20, transcendentals=0),
        name="ffn_bwd",
    )(place, gcin_own, gcin_near, gcin_far, g_deep, coarse, gain_mlp, w_merge, block, gain_merge, cot,
      w_fc2, slope, w_fc1, resid, gain_ffn)


def prep_kernel(
    tokens, turned, w_first, w_second,
    first_out, second_out, slab_out, s0, s1, s2, s3,
    both,
):
    me = lax.axis_index("lat")
    odd = (lax.axis_index("lon") & 1) == 1
    slab = jnp.concatenate([turned[...].astype(F32), jnp.zeros((16, 480), F32)], 1)
    slab_out[...] = slab.astype(BF)
    lines = tokens[...].astype(F32)
    for at, source in ((slice(0, 32), lines), (slice(32, 33), slab.reshape(1, 16, 512))):
        tail, head = sides(odd, source[:, :8], source[:, 8:])
        first_out[at] = tail.astype(BF)
        second_out[at] = head.astype(BF)
    both[0] = w_first[...].astype(F32).T.astype(BF)
    both[1] = w_second[...]
    for k, out in enumerate((s0, s1, s2, s3)):
        rows = pl.ds(pl.multiple_of(lax.bitwise_xor(me, k) * 32, 32), 32)
        out[0:32] = both[0, rows, :]
        out[32:64] = both[1, rows, :]


def prep(tokens, turned, w_first, w_second):
    part = jax.ShapeDtypeStruct((33, 8, 512), BF)
    block = jax.ShapeDtypeStruct((64, 256), BF)
    return pl.pallas_call(
        prep_kernel,
        out_shape=(part, part, jax.ShapeDtypeStruct((16, 512), BF)) + (block,) * 4,
        in_specs=[VM] * 4,
        out_specs=(VM,) * 7,
        scratch_shapes=[pltpu.VMEM((2, 128, 256), BF)],
        compiler_params=params(60),
        cost_estimate=pl.CostEstimate(flops=10**6, bytes_accessed=2 * 2**20, transcendentals=0),
        name="prep",
    )(tokens, turned, w_first, w_second)


def join_kernel(place, s0, s1, s2, s3, out):
    for k, block in enumerate((s0, s1, s2, s3)):
        at = pl.multiple_of(lax.bitwise_xor(place[2], k) * 256, 256)
        out[:, pl.ds(at, 256)] = block[...]


def join(place, blocks):
    return pl.pallas_call(
        join_kernel,
        out_shape=jax.ShapeDtypeStruct((64, 1024), BF),
        in_specs=[SM] + [VM] * 4,
        out_specs=VM,
        compiler_params=params(32),
        cost_estimate=pl.CostEstimate(flops=10**6, bytes_accessed=2**18, transcendentals=0),
        name="join",
    )(place, *blocks)


def stack_kernel(*refs):
    for k, ref in enumerate(refs[:-1]):
        refs[-1][128 * k : 128 * k + 128] = ref[...]


def stacked(blocks):
    return pl.pallas_call(
        stack_kernel,
        out_shape=jax.ShapeDtypeStruct((512, 1024), BF),
        in_specs=[VM] * 4,
        out_specs=VM,
        compiler_params=params(32),
        cost_estimate=pl.CostEstimate(flops=10**6, bytes_accessed=2**21, transcendentals=0),
        name="stacked",
    )(*blocks)


def halves_kernel(ahead, behind, first, second):
    first[...] = ahead[0:256]
    second[...] = behind[256:512]


def halves(ahead, behind):
    half = jax.ShapeDtypeStruct((256, 1024), BF)
    return pl.pallas_call(
        halves_kernel,
        out_shape=(half, half),
        in_specs=[VM] * 2,
        out_specs=(VM, VM),
        compiler_params=params(32),
        cost_estimate=pl.CostEstimate(flops=10**6, bytes_accessed=2**21, transcendentals=0),
        name="halves",
    )(ahead, behind)


def strips_kernel(place, first, own, second, *rest):
    odd = place[3] == 1
    top_out, bottom_out = rest[-2:]
    for out, lo in ((top_out, 0), (bottom_out, 24)):
        rows = slice(lo, lo + 8)
        left, right = sides(odd, first[rows].astype(F32), second[rows].astype(F32))
        out[0:8, 0:8, :] = left.astype(BF)
        out[0:8, 8:24, :] = own[rows]
        out[0:8, 24:32, :] = right.astype(BF)
        if len(rest) == 3:
            left, right = sides(odd, first[32].astype(F32), second[32].astype(F32))
            out[8] = jnp.concatenate([left, rest[0][...].astype(F32), right], 0).astype(BF)


def strips(place, first, own, second, *slab):
    edge = jax.ShapeDtypeStruct((8 + len(slab), 32, 512), BF)
    return pl.pallas_call(
        strips_kernel,
        out_shape=(edge, edge),
        in_specs=[SM] + [VM] * (3 + len(slab)),
        out_specs=(VM, VM),
        compiler_params=params(32),
        cost_estimate=pl.CostEstimate(flops=10**6, bytes_accessed=3 * 2**20, transcendentals=0),
        name="strips",
    )(place, first, own, second, *slab)


def along(axis, count, step):
    pairs = [(s, (s + step) % count) for s in range(count)]
    return lambda v: lax.ppermute(v, axis, pairs)


LAT_NEXT, LAT_PREV = along("lat", 4, 1), along("lat", 4, -1)


def even_odd(v):
    return lax.ppermute(v, "lon", [(k, k ^ 1) for k in range(32)])


def odd_even(v):
    return lax.ppermute(v, "lon", [(k, (((k + 1) ^ 1) - 1) % 32) for k in range(32)])


def core_swap(v):
    return lax.ppermute(v, "lat", [(0, 1), (1, 0), (2, 3), (3, 2)])


def x_swap(v):
    return lax.ppermute(v, "lat", [(0, 2), (2, 0), (1, 3), (3, 1)])


def cross_swap(v):
    return lax.ppermute(v, "lat", [(0, 3), (3, 0), (1, 2), (2, 1)])


def x_far_swap(v):
    return lax.ppermute(v, "lon", [(k, (k + 16) % 32) for k in range(32)])


def turn(swapped, k):
    pairs = []
    for lat in range(4):
        along_y = (lat % 2 == 1) != swapped
        for lon in range(32):
            x, y, z = lon // 16, lon // 4 % 4, lon % 4
            if along_y:
                y = (y + k) % 4
            else:
                z = (z + k) % 4
            pairs.append((lat * 32 + lon, lat * 32 + (x * 4 + y) * 4 + z))
    return lambda v: lax.ppermute(v, ("lat", "lon"), pairs)


def after(value, *gates):
    return lax.optimization_barrier((value,) + gates)[0]


def on_device(
    tokens, labels, offsets, gain_attn, w_qkv, w_proj, gain_ffn, w_fc1, w_fc2,
    gain_merge, w_merge, gain_mlp, w_first, w_second, w_up, cotangent,
):
    row = lambda g: g.reshape(1, -1)
    first, second, slab, s0, s1, s2, s3 = prep(tokens, labels.T, w_first, w_second)
    s1, s2, s3 = core_swap(s1), x_swap(s2), cross_swap(s3)
    left, right = even_odd(first), odd_even(second)
    where = [lax.axis_index("lat"), lax.axis_index("lon") & 1]
    place = jnp.concatenate([after(offsets, slab), jnp.stack(where).astype(jnp.int32)])
    mine = join(place, (s0, s1, s2, s3))
    other = x_far_swap(mine)
    cot = cotangent.reshape(512, 512)
    g_deep = g_deep_of(after(cot, mine), w_up)
    near_deep = core_swap(g_deep)
    seed = jnp.concatenate([mine, after(other, g_deep)], 0)
    moved = [turn(False, k)(seed) for k in (1, -1, 2)]
    bottom, top = strips(place, left, after(tokens, seed), right, slab)
    up, down = LAT_NEXT(top), LAT_PREV(bottom)
    gain = row(gain_attn)
    qkv_mid, probs_mid, middle = fwd_middle(
        place, left, tokens, right, slab, gain, w_qkv, w_proj
    )
    part = stacked([after(seed, up, down, middle)] + moved)
    ahead, behind = turn(True, 1)(part), turn(True, -1)(part)
    qkv_edge, probs_edge, resid = fwd_edge(
        place, after(up, part), bottom, top, down, tokens, middle, gain, w_qkv, w_proj
    )
    resid = resid.reshape(512, 512)
    far_deep = x_swap(after(g_deep, resid))
    slope, block, coarse, coarse_in = ffn_fwd(
        resid, row(gain_ffn), w_fc1, w_fc2, row(gain_merge), w_merge, row(gain_mlp)
    )
    fore, hind = halves(after(ahead, coarse_in), behind)
    far_cin = x_swap(coarse_in)
    near_cin = core_swap(coarse_in)
    parts = [part, ahead, behind, turn(True, 1)(fore), turn(True, -1)(hind)]
    cins = [coarse_in, near_cin, far_cin, core_swap(far_cin)]
    deeps = [g_deep, near_deep, far_deep, core_swap(after(far_deep, coarse_in))]
    keep, send, hid = coarse_mlp(place, cins, deeps, parts)
    near = core_swap(send)
    gcin_far = x_swap((keep[128:].astype(F32) + near[128:].astype(F32)).astype(BF))
    down_keep, down_send = down_of(hid, parts)
    down_near = core_swap(down_send)
    down_far = (down_keep[128:].astype(F32) + down_near[128:].astype(F32)).astype(BF)
    gcin_far, down_far = lax.optimization_barrier((gcin_far, down_far))
    down_far = x_swap(down_far)
    g_resid, g_first, g_second = ffn_bwd(
        place, keep, near, gcin_far, g_deep, coarse, row(gain_mlp), w_merge, block, row(gain_merge), cot,
        w_fc2, slope, w_fc1, resid, row(gain_ffn),
    )
    g_resid = g_resid.reshape(32, 16, 512)
    g_left, g_right = even_odd(g_first), odd_even(g_second)
    field_out = up_of(coarse, down_keep, down_near, down_far, block, w_up).reshape(32, 16, 512)
    g_bottom, g_top = strips(place, g_left, after(g_resid, field_out), g_right)
    g_up, g_down = LAT_NEXT(g_top), LAT_PREV(g_bottom)
    g_middle = bwd_middle(place, g_left, g_resid, g_right, qkv_mid, probs_mid, w_proj, w_qkv)
    grad_in = bwd_edge(
        place, g_up, g_bottom, g_top, g_down, g_resid, g_middle, qkv_edge, probs_edge,
        w_proj, w_qkv, tokens, gain,
    )
    return (field_out, grad_in)


def solution(mesh):
    grid = P("lat", "lon", None)
    placed = (
        grid, P("lat", "lon"), P(), P(), P(), P(), P(), P(), P(), P(), P(), P(),
        P("lat", "lon"), P("lon", "lat"), P(), grid,
    )
    return jax.shard_map(
        on_device, mesh=mesh, in_specs=placed, out_specs=(grid, grid), check_vma=False
    )
```

```python
import jax
import jax.numpy as jnp
from jax import lax
from jax.experimental import pallas as pl
from jax.experimental.pallas import tpu as pltpu
from jax.sharding import PartitionSpec as P

BF = jnp.bfloat16
F32 = jnp.float32
EPS = 1e-05
NT = (((1,), (1,)), ((), ()))
TN = (((0,), (0,)), ((), ()))
GELU_C = 0.7978845608028654
GELU_A = 0.044715


def dot(a, b):
    return jnp.dot(a, b, preferred_element_type=F32)


def dot_nt(a, b):
    return lax.dot_general(a, b, NT, preferred_element_type=F32)


def dot_tn(a, b):
    return lax.dot_general(a, b, TN, preferred_element_type=F32)


def normalise(v):
    mean = jnp.mean(v, -1, keepdims=True)
    c = v - mean
    r = lax.rsqrt(jnp.mean(c * c, -1, keepdims=True) + EPS)
    return c * r, r


def norm_back(v, gain, t):
    xh, r = normalise(v)
    s = t * gain
    return r * (s - jnp.mean(s, -1, keepdims=True) - xh * jnp.mean(s * xh, -1, keepdims=True))


def gelu_both(wide):
    x = wide.astype(BF)
    x2 = x * x
    t = jnp.tanh(x * (GELU_C + GELU_C * GELU_A * x2))
    h = 0.5 * x
    slope = (0.5 + 0.5 * t) + (h - h * t * t) * (GELU_C + 3.0 * GELU_C * GELU_A * x2)
    return h + h * t, slope


def half_masks(scale):
    low = lax.broadcasted_iota(jnp.int32, (1, 128), 1) < 64
    return [jnp.where(m, scale, 0.0).astype(F32).astype(BF) for m in (low, jnp.logical_not(low))]


def spread(x, masks):
    none = jnp.zeros((64, 128), BF)
    left, right = x[:, :128], x[:, 128:]
    rows = [jnp.concatenate([left * m, none], 1) for m in masks]
    rows += [jnp.concatenate([none, right * m], 1) for m in masks]
    return jnp.concatenate(rows, 0)


def collect(big):
    low = lax.broadcasted_iota(jnp.int32, (64, 128), 1) < 64
    left = jnp.where(low, big[0:64, :128], big[64:128, :128])
    right = jnp.where(low, big[128:192, 128:], big[192:256, 128:])
    return jnp.concatenate([left, right], 1)


def sides(odd, first, second):
    return jnp.where(odd, first, second), jnp.where(odd, second, first)


def shifted_cols(lines, b):
    return pltpu.roll(lines, 32 - b, 1)[:, :24]


def fill_middle(grid, b, odd, first, own, second):
    def rows(n, carry):
        at = pl.ds(8 * n, 8)
        left, right = sides(odd, first[at].astype(F32), second[at].astype(F32))
        grid[at] = shifted_cols(jnp.concatenate([left, own[at].astype(F32), right], 1), b)
        return carry

    lax.fori_loop(0, 4, rows, 0)


def fill_edges(grid, b, edges):
    for n, edge in enumerate(edges):
        grid[8 * n : 8 * n + 8] = shifted_cols(edge[0:8].astype(F32), b)


def slab_cols(slab, b):
    return pltpu.roll(slab, 32 - b, 0)[:24]


def place_back(back, n, a, b):
    return pltpu.roll(back[pl.ds(8 - a + 8 * n, 8)], 16 + b, 1)[:, :16]


def windows_of(grid, base, a):
    lines = grid[pl.ds(a + base, 8)]
    return [lines[:, 8 * k : 8 * k + 8].reshape(64, grid.shape[2]) for k in range(3)]


def put_windows(back, row, value):
    for k in range(3):
        part = value[64 * k : 64 * k + 64].reshape(8, 8, 512)
        back[row : row + 8, 8 * k : 8 * k + 8, :] = part


def fwd_windows(grid, codes, cols, mixed, qkv, probs, gain, w_qkv, bases, a):
    for n, base in enumerate(bases):
        normed = [(normalise(x)[0] * gain[...]).astype(BF) for x in windows_of(grid, base, a)]
        qkv[192 * n : 192 * n + 192] = dot(jnp.concatenate(normed, 0), w_qkv[...]).astype(BF)
        for k, col in enumerate(windows_of(codes, base, a)):
            cols[3 * n + k] = col
    masks = half_masks(0.125)

    def window(w, carry):
        at = pl.ds(pl.multiple_of(w * 64, 64), 64)
        col = cols[w]
        row = col.T[0:1, 0:64]
        same = jnp.concatenate([col, col], 1) == jnp.concatenate([row] * 4, 1)
        for c in range(2):
            lo = 256 * c
            qbig = spread(qkv[at, lo : lo + 256], masks)
            k = qkv[at, 512 + lo : 768 + lo]
            v = qkv[at, 1024 + lo : 1280 + lo]
            e = jnp.where(same, jnp.exp(dot_nt(k, qbig)), 0.0)
            p = (e * (1.0 / jnp.sum(e, 0, keepdims=True))).astype(BF)
            probs[at, lo : lo + 256] = p
            mixed[at, lo : lo + 256] = collect(dot_tn(p, v)).astype(BF)
        return carry

    lax.fori_loop(0, 3 * len(bases), window, 0, unroll=True)


def fwd_middle_kernel(
    place, first, own, second, own_slab, gain, w_qkv, w_proj,
    qkv, probs, back,
    grid, codes, cols, mixed,
):
    a, b = place[0], place[1]
    odd = place[3] == 1
    fill_middle(grid, b, odd, first, own, second)
    left, right = sides(odd, first[32].astype(F32), second[32].astype(F32))
    slab = slab_cols(jnp.concatenate([left, own_slab[...].astype(F32), right], 0), b)
    for r in range(32):
        codes[r] = jnp.broadcast_to(slab[:, r : r + 1], (24, 128))
    bases = (0, 8, 16)
    fwd_windows(grid, codes, cols, mixed, qkv, probs, gain, w_qkv, bases, a)
    for n in range(3):
        att = dot(mixed[192 * n : 192 * n + 192], w_proj[...]).astype(BF).astype(F32)
        put_windows(back, 8 * n, att)


def fwd_edge_kernel(
    place, up, bottom, top, down, own, middle, gain, w_qkv, w_proj,
    qkv, probs, resid_out,
    grid, codes, cols, mixed, back,
):
    a, b, d = place[0], place[1], place[2]
    edges = (up, bottom, top, down)
    fill_edges(grid, b, edges)
    extra = (jnp.where(d == 0, 4.0, 0.0), 0.0, 0.0, jnp.where(d == 3, 4.0, 0.0))
    for n, (edge, lane, code) in enumerate(zip(edges, (24, 0, 24, 0), extra)):
        slab = slab_cols(edge[8].astype(F32) + code, b)
        for r in range(8):
            codes[8 * n + r] = jnp.broadcast_to(slab[:, lane + r : lane + r + 1], (24, 128))
    bases = (0, 16)
    fwd_windows(grid, codes, cols, mixed, qkv, probs, gain, w_qkv, bases, a)
    back[8:32] = middle[...]
    for n in range(2):
        att = dot(mixed[192 * n : 192 * n + 192], w_proj[...]).astype(BF).astype(F32)
        put_windows(back, 32 * n, att)
    for n in range(4):
        at = slice(8 * n, 8 * n + 8)
        resid_out[at] = (own[at].astype(F32) + place_back(back, n, a, b)).astype(BF)


def bwd_windows(ups, g_mixed, g_qkv, qkv, probs, w_proj, kept_at):
    for n in range(len(ups) // 3):
        group = jnp.concatenate([x.astype(BF) for x in ups[3 * n : 3 * n + 3]], 0)
        g_mixed[192 * n : 192 * n + 192] = dot_nt(group, w_proj[...]).astype(BF)
    masks, scaled = half_masks(1.0), half_masks(0.125)
    for n, w in enumerate(kept_at):
        at, out = slice(64 * w, 64 * w + 64), slice(64 * n, 64 * n + 64)
        for c in range(2):
            lo = 256 * c
            qbig = spread(qkv[at, lo : lo + 256], scaled)
            gbig = spread(g_mixed[out, lo : lo + 256], masks)
            k = qkv[at, 512 + lo : 768 + lo]
            v = qkv[at, 1024 + lo : 1280 + lo]
            p = probs[at, lo : lo + 256]
            g_probs = dot_nt(v, gbig)
            wide_p = p.astype(F32)
            total = jnp.sum(wide_p * g_probs, 0, keepdims=True)
            g_score = (wide_p * (g_probs - total)).astype(BF)
            g_qkv[out, lo : lo + 256] = (collect(dot_tn(g_score, k)) * 0.125).astype(BF)
            g_qkv[out, 512 + lo : 768 + lo] = dot(g_score, qbig).astype(BF)
            g_qkv[out, 1024 + lo : 1280 + lo] = dot(p, gbig).astype(BF)


def bwd_center_kernel(place, own, qkv, probs, w_proj, w_qkv, center, grid, g_mixed, g_qkv):
    a, b = place[0], place[1]
    for n in range(4):
        at = slice(8 * n, 8 * n + 8)
        grid[at] = pltpu.roll(own[at].astype(F32), 16 - b, 1)[:, :8]
    ups = [grid[pl.ds(a + base, 8)].reshape(64, 512) for base in (0, 8, 16)]
    bwd_windows(ups, g_mixed, g_qkv, qkv, probs, w_proj, (1, 4, 7))
    g_shift = dot_nt(g_qkv[...], w_qkv[...]).astype(BF).astype(F32)
    center[...] = g_shift.reshape(24, 8, 512)


def bwd_middle_kernel(
    place, first, own, second, center, qkv, probs, w_proj, w_qkv,
    back,
    grid, g_mixed, g_qkv,
):
    a, b = place[0], place[1]
    fill_middle(grid, b, place[3] == 1, first, own, second)
    ups = []
    for base in (0, 8, 16):
        ups += windows_of(grid, base, a)[::2]
    bwd_windows(ups, g_mixed, g_qkv, qkv, probs, w_proj, (0, 2, 3, 5, 6, 8))
    back[:, 8:16, :] = center[...]
    for n in range(2):
        g_shift = dot_nt(g_qkv[192 * n : 192 * n + 192], w_qkv[...]).astype(BF).astype(F32)
        for k in range(3):
            row, side = 8 * ((3 * n + k) // 2), 16 * ((3 * n + k) % 2)
            part = g_shift[64 * k : 64 * k + 64].reshape(8, 8, 512)
            back[row : row + 8, side : side + 8, :] = part


def bwd_edge_kernel(
    place, up, bottom, top, down, own, middle, qkv, probs, w_proj, w_qkv,
    tokens, gain,
    grad_out,
    grid, g_mixed, g_qkv, back,
):

    a, b = place[0], place[1]
    fill_edges(grid, b, (up, bottom, top, down))
    ups = windows_of(grid, 0, a) + windows_of(grid, 16, a)
    bwd_windows(ups, g_mixed, g_qkv, qkv, probs, w_proj, range(6))
    back[8:32] = middle[...]
    for n in range(2):
        g_shift = dot_nt(g_qkv[192 * n : 192 * n + 192], w_qkv[...]).astype(BF).astype(F32)
        put_windows(back, 32 * n, g_shift)
    for n in range(4):
        at = slice(8 * n, 8 * n + 8)
        part = norm_back(tokens[at].astype(F32), gain[...], place_back(back, n, a, b))
        grad_out[at] = (own[at].astype(F32) + part).astype(BF)


VM = pl.BlockSpec(memory_space=pltpu.VMEM)
SM = pl.BlockSpec(memory_space=pltpu.SMEM)


def params(mib):
    return pltpu.CompilerParams(vmem_limit_bytes=mib * 2**20)


def attn_scratch(rows, backward):
    shapes = [(32, 8 if rows == 192 else 24, 512, F32)]
    if not backward:
        shapes += [(32, 24, 128, F32), (rows // 64, 64, 128, F32), (rows, 512, BF)]
    else:
        shapes += [(rows // 192 * 192, 512, BF), (rows // 192 * 192, 1536, BF)]
    if rows == 384:
        shapes += [(40, 24, 512, F32)]
    return [pltpu.VMEM(shape[:-1], shape[-1]) for shape in shapes]


MIDDLE = jax.ShapeDtypeStruct((24, 24, 512), F32)
FINE = jax.ShapeDtypeStruct((32, 16, 512), BF)


def attention(kernel, name, rows, backward, specs, outs, out_specs, flops, operands):
    return pl.pallas_call(
        kernel,
        out_shape=outs,
        in_specs=specs,
        out_specs=out_specs,
        scratch_shapes=attn_scratch(rows, backward),
        compiler_params=params(32),
        cost_estimate=pl.CostEstimate(flops=flops, bytes_accessed=6 * 2**20, transcendentals=10**5),
        name=name,
    )(*operands)


def kept(rows):
    return (jax.ShapeDtypeStruct((rows, 1536), BF), jax.ShapeDtypeStruct((rows, 512), BF))


def fwd_middle(*operands):
    return attention(
        fwd_middle_kernel, "fwd_middle", 576, False, [SM] + [VM] * 7,
        kept(576) + (MIDDLE,), (VM, VM, VM), 10**9, operands,
    )


def fwd_edge(*operands):
    return attention(
        fwd_edge_kernel, "fwd_edge", 384, False, [SM] + [VM] * 9,
        kept(384) + (FINE,), (VM, VM, VM), 10**9, operands,
    )


def bwd_center(*operands):
    return attention(
        bwd_center_kernel, "bwd_center", 192, True, [SM] + [VM] * 5,
        jax.ShapeDtypeStruct((24, 8, 512), F32), VM, 10**9, operands,
    )


def bwd_middle(*operands):
    return attention(
        bwd_middle_kernel, "bwd_middle", 385, True, [SM] + [VM] * 8,
        MIDDLE, VM, 2 * 10**9, operands,
    )


def bwd_edge(*operands):
    return attention(
        bwd_edge_kernel, "bwd_edge", 384, True, [SM] + [VM] * 12,
        FINE, VM, 2 * 10**9, operands,
    )


def set_fine(fine, value):
    for lane in range(4):
        fine[lane] = value[:, 128 * lane : 128 * lane + 128]


def get_fine(fine):
    return jnp.concatenate([fine[lane] for lane in range(4)], 1)


def patch_parts(fine):
    parts = {}
    for s in range(2):
        lanes = [fine[lane, pl.ds(s, 256, 2), :] for lane in range(4)]
        half = jnp.concatenate(lanes, 1).reshape(16, 2, 8, 512)
        for r in range(2):
            parts[r + 2 * s] = half[:, r].reshape(128, 512)
    return [parts[k] for k in range(4)]


def unpatch(fine, parts):
    for s in range(2):
        pair = [parts[r + 2 * s].reshape(16, 1, 8, 512) for r in range(2)]
        half = jnp.concatenate(pair, 1).reshape(256, 512)
        for lane in range(4):
            fine[lane, pl.ds(s, 256, 2), :] = half[:, 128 * lane : 128 * lane + 128]


def joint_normalise(parts):
    mean = sum(jnp.sum(p, -1, keepdims=True) for p in parts) / 2048.0
    cent = [p - mean for p in parts]
    var = sum(jnp.sum(c * c, -1, keepdims=True) for c in cent) / 2048.0
    r = lax.rsqrt(var + EPS)
    return [c * r for c in cent], r


def ffn_fwd_kernel(
    resid, gain_ffn, w_fc1, w_fc2, gain_merge, w_merge, gain_mlp,
    slope_out, block_out, coarse_out, cin_out,
    acc, fine,
):
    xh, _ = normalise(resid[...].astype(F32))
    ffn_in = (xh * gain_ffn[...]).astype(BF)
    for n in range(4):
        cut = slice(512 * n, 512 * n + 512)
        for m in range(2):
            rows = slice(256 * m, 256 * m + 256)
            hid, slope = gelu_both(dot(ffn_in[rows], w_fc1[:, cut]))
            slope_out[rows, cut] = slope
            term = dot(hid, w_fc2[cut, :])
            if n == 0:
                acc[rows, :] = resid[rows, :].astype(F32) + term
            else:
                acc[rows, :] += term
    block = acc[...].astype(BF)
    block_out[...] = block
    set_fine(fine, block.astype(F32))
    xhs, _ = joint_normalise(patch_parts(fine))
    coarse = None
    for k in range(4):
        cut = slice(512 * k, 512 * k + 512)
        term = dot((xhs[k] * gain_merge[:, cut]).astype(BF), w_merge[cut, :])
        coarse = term if coarse is None else coarse + term
    coarse = coarse.astype(BF)
    coarse_out[...] = coarse
    xh, _ = normalise(coarse.astype(F32))
    cin_out[...] = (xh * gain_mlp[...]).astype(BF)


def ffn_fwd(resid, gain_ffn, w_fc1, w_fc2, gain_merge, w_merge, gain_mlp):
    return pl.pallas_call(
        ffn_fwd_kernel,
        out_shape=(
            jax.ShapeDtypeStruct((512, 2048), BF),
            jax.ShapeDtypeStruct((512, 512), BF),
            jax.ShapeDtypeStruct((128, 1024), BF),
            jax.ShapeDtypeStruct((128, 1024), BF),
        ),
        in_specs=[VM] * 7,
        out_specs=(VM, VM, VM, VM),
        scratch_shapes=[
            pltpu.VMEM((512, 512), F32),
            pltpu.VMEM((4, 512, 128), F32),
        ],
        compiler_params=params(32),
        cost_estimate=pl.CostEstimate(flops=3 * 10**9, bytes_accessed=12 * 2**20, transcendentals=10**6),
        name="ffn_fwd",
    )(resid, gain_ffn, w_fc1, w_fc2, gain_merge, w_merge, gain_mlp)


def weight_chunk(parts, y, lo):
    rows = []
    for k in range(4):
        ref, at = (parts[y], 128 * k) if y < 3 else (parts[3 + k // 2], 128 * (k % 2))
        rows += [ref[at + lo : at + lo + 32], ref[at + 64 + lo : at + 96 + lo]]
    return jnp.concatenate(rows, 0)


def mlp_kernel(
    place, c0, c1, c2, c3, d0, d1, d2, d3, w0, w1, w2, w3, w4,
    keep_out, send_out, hid_out,
    cs, deep, gacc,
):
    for k, (c, g) in enumerate(((c0, d0), (c1, d1), (c2, d2), (c3, d3))):
        cs[128 * k : 128 * k + 128] = c[...]
        deep[128 * k : 128 * k + 128] = g[...]
    parts = (w0, w1, w2, w3, w4)
    for y in range(4):
        first = weight_chunk(parts, y, 0)
        second = weight_chunk(parts, y, 32)
        for m in range(2):
            rows = slice(256 * m, 256 * m + 256)
            hid, slope = gelu_both(dot_nt(cs[rows], first))
            hid_out[rows, 256 * y : 256 * y + 256] = hid
            g_pre = dot_nt(deep[rows], second).astype(BF) * slope
            g_cin = dot(g_pre, first)
            if y == 0:
                gacc[rows] = g_cin
            else:
                gacc[rows] += g_cin
    part_out(gacc, keep_out, send_out)


def part_out(total, keep_out, send_out):
    keep_out[0:128] = total[0:128].astype(BF)
    keep_out[128:256] = total[256:384].astype(BF)
    send_out[0:128] = total[128:256].astype(BF)
    send_out[128:256] = total[384:512].astype(BF)


def coarse_mlp(place, cins, deeps, parts):
    return pl.pallas_call(
        mlp_kernel,
        out_shape=(
            jax.ShapeDtypeStruct((256, 1024), BF),
            jax.ShapeDtypeStruct((256, 1024), BF),
            jax.ShapeDtypeStruct((512, 1024), BF),
        ),
        in_specs=[SM] + [VM] * 13,
        out_specs=(VM, VM, VM),
        scratch_shapes=[
            pltpu.VMEM((512, 1024), BF),
            pltpu.VMEM((512, 1024), BF),
            pltpu.VMEM((512, 1024), F32),
        ],
        compiler_params=params(32),
        cost_estimate=pl.CostEstimate(flops=3 * 10**9, bytes_accessed=8 * 2**20, transcendentals=10**6),
        name="coarse_mlp",
    )(place, *cins, *deeps, *parts)


def down_kernel(hid, w0, w1, w2, w3, w4, keep_out, send_out):
    total = None
    for y in range(4):
        term = dot(hid[:, 256 * y : 256 * y + 256], weight_chunk((w0, w1, w2, w3, w4), y, 32))
        total = term if total is None else total + term
    part_out(total, keep_out, send_out)


def down_of(hid, parts):
    half = jax.ShapeDtypeStruct((256, 1024), BF)
    return pl.pallas_call(
        down_kernel,
        out_shape=(half, half),
        in_specs=[VM] * 6,
        out_specs=(VM, VM),
        compiler_params=params(32),
        cost_estimate=pl.CostEstimate(flops=10**9, bytes_accessed=5 * 2**20, transcendentals=0),
        name="down",
    )(hid, *parts)


def g_deep_kernel(cot, w_up, out, fine):
    set_fine(fine, cot[...].astype(F32))
    whole = jnp.concatenate([part.astype(BF) for part in patch_parts(fine)], 1)
    for k in range(4):
        rows = slice(256 * k, 256 * k + 256)
        out[:, rows] = dot_nt(whole, w_up[rows, :]).astype(BF)


UP_SCRATCH = [
    pltpu.VMEM((4, 512, 128), F32),
]


def g_deep_of(cot, w_up):
    return pl.pallas_call(
        g_deep_kernel,
        out_shape=jax.ShapeDtypeStruct((128, 1024), BF),
        in_specs=[VM, VM],
        out_specs=VM,
        scratch_shapes=UP_SCRATCH,
        compiler_params=params(32),
        cost_estimate=pl.CostEstimate(flops=10**9, bytes_accessed=5 * 2**20, transcendentals=0),
        name="g_deep",
    )(cot, w_up)


def up_kernel(coarse, keep, near, far, block, w_up, out, fine):
    deep = coarse[...].astype(F32) + keep[0:128].astype(F32) + near[0:128].astype(F32)
    deep = (deep + far[...].astype(F32)).astype(BF)
    acc = None
    for k in range(4):
        rows = slice(256 * k, 256 * k + 256)
        term = dot(deep[:, rows], w_up[rows, :])
        acc = term if acc is None else acc + term
    unpatch(fine, [acc[:, 512 * k : 512 * k + 512] for k in range(4)])
    out[...] = (block[...].astype(F32) + get_fine(fine)).astype(BF)


def up_of(coarse, keep, near, far, block, w_up):
    return pl.pallas_call(
        up_kernel,
        out_shape=jax.ShapeDtypeStruct((512, 512), BF),
        in_specs=[VM] * 6,
        out_specs=VM,
        scratch_shapes=UP_SCRATCH,
        compiler_params=params(32),
        cost_estimate=pl.CostEstimate(flops=10**9, bytes_accessed=5 * 2**20, transcendentals=0),
        name="up",
    )(coarse, keep, near, far, block, w_up)


def ffn_bwd_kernel(
    place, gcin_own, gcin_near, gcin_far, g_deep, coarse, gain_mlp, w_merge, block, gain_merge, cot,
    w_fc2, slope, w_fc1, resid, gain_ffn,
    g_resid_out, first_out, second_out,
    fine, acc,
):
    g_cin = gcin_own[0:128].astype(F32) + gcin_near[0:128].astype(F32) + gcin_far[...].astype(F32)
    g_cin = g_cin.astype(BF).astype(F32)
    part = norm_back(coarse[...].astype(F32), gain_mlp[...], g_cin)
    g_coarse = (g_deep[...].astype(F32) + part).astype(BF)
    set_fine(fine, block[...].astype(F32))
    xhs, r = joint_normalise(patch_parts(fine))
    scaled = []
    for k in range(4):
        cut = slice(512 * k, 512 * k + 512)
        scaled.append(dot_nt(g_coarse, w_merge[cut, :]) * gain_merge[:, cut])
    mean_s = sum(jnp.sum(s, -1, keepdims=True) for s in scaled) / 2048.0
    mean_x = sum(jnp.sum(s * x, -1, keepdims=True) for s, x in zip(scaled, xhs)) / 2048.0
    unpatch(fine, [r * (s - mean_s - x * mean_x) for s, x in zip(scaled, xhs)])
    g_block = (cot[...].astype(F32) + get_fine(fine)).astype(BF)
    for n in range(4):
        cut = slice(512 * n, 512 * n + 512)
        for m in range(2):
            rows = slice(256 * m, 256 * m + 256)
            g_pre = dot_nt(g_block[rows], w_fc2[cut, :]).astype(BF) * slope[rows, cut]
            term = dot_nt(g_pre, w_fc1[:, cut])
            if n == 0:
                acc[rows, :] = term
            else:
                acc[rows, :] += term
    g_fin = acc[...].astype(BF).astype(F32)
    part = norm_back(resid[...].astype(F32), gain_ffn[...], g_fin)
    total = g_block.astype(F32) + part
    g_resid_out[...] = total.astype(BF)
    lines = total.reshape(32, 16, 512)
    tail, head = sides(place[3] == 1, lines[:, :8], lines[:, 8:])
    first_out[...] = tail.astype(BF)
    second_out[...] = head.astype(BF)


def ffn_bwd(place, gcin_own, gcin_near, gcin_far, g_deep, coarse, gain_mlp, w_merge, block, gain_merge, cot,
            w_fc2, slope, w_fc1, resid, gain_ffn):
    return pl.pallas_call(
        ffn_bwd_kernel,
        out_shape=(
            jax.ShapeDtypeStruct((512, 512), BF),
            jax.ShapeDtypeStruct((32, 8, 512), BF),
            jax.ShapeDtypeStruct((32, 8, 512), BF),
        ),
        in_specs=[SM] + [VM] * 15,
        out_specs=(VM, VM, VM),
        scratch_shapes=[
            pltpu.VMEM((4, 512, 128), F32),
            pltpu.VMEM((512, 512), F32),
        ],
        compiler_params=params(32),
        cost_estimate=pl.CostEstimate(flops=3 * 10**9, bytes_accessed=14 * 2**20, transcendentals=0),
        name="ffn_bwd",
    )(place, gcin_own, gcin_near, gcin_far, g_deep, coarse, gain_mlp, w_merge, block, gain_merge, cot,
      w_fc2, slope, w_fc1, resid, gain_ffn)


def prep_kernel(
    tokens, turned, w_first, w_second,
    first_out, second_out, slab_out, s0, s1, s2, s3,
    both,
):
    me = lax.axis_index("lat")
    odd = (lax.axis_index("lon") & 1) == 1
    slab = jnp.concatenate([turned[...].astype(F32), jnp.zeros((16, 480), F32)], 1)
    slab_out[...] = slab.astype(BF)
    lines = tokens[...].astype(F32)
    for at, source in ((slice(0, 32), lines), (slice(32, 33), slab.reshape(1, 16, 512))):
        tail, head = sides(odd, source[:, :8], source[:, 8:])
        first_out[at] = tail.astype(BF)
        second_out[at] = head.astype(BF)
    both[0] = w_first[...].astype(F32).T.astype(BF)
    both[1] = w_second[...]
    for k, out in enumerate((s0, s1, s2, s3)):
        rows = pl.ds(pl.multiple_of(lax.bitwise_xor(me, k) * 32, 32), 32)
        out[0:32] = both[0, rows, :]
        out[32:64] = both[1, rows, :]


def prep(tokens, turned, w_first, w_second):
    part = jax.ShapeDtypeStruct((33, 8, 512), BF)
    block = jax.ShapeDtypeStruct((64, 256), BF)
    return pl.pallas_call(
        prep_kernel,
        out_shape=(part, part, jax.ShapeDtypeStruct((16, 512), BF)) + (block,) * 4,
        in_specs=[VM] * 4,
        out_specs=(VM,) * 7,
        scratch_shapes=[pltpu.VMEM((2, 128, 256), BF)],
        compiler_params=params(60),
        cost_estimate=pl.CostEstimate(flops=10**6, bytes_accessed=2 * 2**20, transcendentals=0),
        name="prep",
    )(tokens, turned, w_first, w_second)


def join_kernel(place, s0, s1, s2, s3, out):
    for k, block in enumerate((s0, s1, s2, s3)):
        at = pl.multiple_of(lax.bitwise_xor(place[2], k) * 256, 256)
        out[:, pl.ds(at, 256)] = block[...]


def join(place, blocks):
    return pl.pallas_call(
        join_kernel,
        out_shape=jax.ShapeDtypeStruct((64, 1024), BF),
        in_specs=[SM] + [VM] * 4,
        out_specs=VM,
        compiler_params=params(32),
        cost_estimate=pl.CostEstimate(flops=10**6, bytes_accessed=2**18, transcendentals=0),
        name="join",
    )(place, *blocks)


def stack_kernel(*refs):
    for k, ref in enumerate(refs[:-1]):
        refs[-1][128 * k : 128 * k + 128] = ref[...]


def stacked(blocks):
    return pl.pallas_call(
        stack_kernel,
        out_shape=jax.ShapeDtypeStruct((512, 1024), BF),
        in_specs=[VM] * 4,
        out_specs=VM,
        compiler_params=params(32),
        cost_estimate=pl.CostEstimate(flops=10**6, bytes_accessed=2**21, transcendentals=0),
        name="stacked",
    )(*blocks)


def halves_kernel(ahead, behind, first, second):
    first[...] = ahead[0:256]
    second[...] = behind[256:512]


def halves(ahead, behind):
    half = jax.ShapeDtypeStruct((256, 1024), BF)
    return pl.pallas_call(
        halves_kernel,
        out_shape=(half, half),
        in_specs=[VM] * 2,
        out_specs=(VM, VM),
        compiler_params=params(32),
        cost_estimate=pl.CostEstimate(flops=10**6, bytes_accessed=2**21, transcendentals=0),
        name="halves",
    )(ahead, behind)


def strips_kernel(place, first, own, second, *rest):
    odd = place[3] == 1
    top_out, bottom_out = rest[-2:]
    for out, lo in ((top_out, 0), (bottom_out, 24)):
        rows = slice(lo, lo + 8)
        left, right = sides(odd, first[rows].astype(F32), second[rows].astype(F32))
        out[0:8, 0:8, :] = left.astype(BF)
        out[0:8, 8:24, :] = own[rows]
        out[0:8, 24:32, :] = right.astype(BF)
        if len(rest) == 3:
            left, right = sides(odd, first[32].astype(F32), second[32].astype(F32))
            out[8] = jnp.concatenate([left, rest[0][...].astype(F32), right], 0).astype(BF)


def strips(place, first, own, second, *slab):
    edge = jax.ShapeDtypeStruct((8 + len(slab), 32, 512), BF)
    return pl.pallas_call(
        strips_kernel,
        out_shape=(edge, edge),
        in_specs=[SM] + [VM] * (3 + len(slab)),
        out_specs=(VM, VM),
        compiler_params=params(32),
        cost_estimate=pl.CostEstimate(flops=10**6, bytes_accessed=3 * 2**20, transcendentals=0),
        name="strips",
    )(place, first, own, second, *slab)


def along(axis, count, step):
    pairs = [(s, (s + step) % count) for s in range(count)]
    return lambda v: lax.ppermute(v, axis, pairs)


LAT_NEXT, LAT_PREV = along("lat", 4, 1), along("lat", 4, -1)


def even_odd(v):
    return lax.ppermute(v, "lon", [(k, k ^ 1) for k in range(32)])


def odd_even(v):
    return lax.ppermute(v, "lon", [(k, (((k + 1) ^ 1) - 1) % 32) for k in range(32)])


def core_swap(v):
    return lax.ppermute(v, "lat", [(0, 1), (1, 0), (2, 3), (3, 2)])


def x_swap(v):
    return lax.ppermute(v, "lat", [(0, 2), (2, 0), (1, 3), (3, 1)])


def cross_swap(v):
    return lax.ppermute(v, "lat", [(0, 3), (3, 0), (1, 2), (2, 1)])


def x_far_swap(v):
    return lax.ppermute(v, "lon", [(k, (k + 16) % 32) for k in range(32)])


def turn(swapped, k):
    pairs = []
    for lat in range(4):
        along_y = (lat % 2 == 1) != swapped
        for lon in range(32):
            x, y, z = lon // 16, lon // 4 % 4, lon % 4
            if along_y:
                y = (y + k) % 4
            else:
                z = (z + k) % 4
            pairs.append((lat * 32 + lon, lat * 32 + (x * 4 + y) * 4 + z))
    return lambda v: lax.ppermute(v, ("lat", "lon"), pairs)


def after(value, *gates):
    return lax.optimization_barrier((value,) + gates)[0]


def on_device(
    tokens, labels, offsets, gain_attn, w_qkv, w_proj, gain_ffn, w_fc1, w_fc2,
    gain_merge, w_merge, gain_mlp, w_first, w_second, w_up, cotangent,
):
    row = lambda g: g.reshape(1, -1)
    first, second, slab, s0, s1, s2, s3 = prep(tokens, labels.T, w_first, w_second)
    s1, s2, s3 = core_swap(s1), x_swap(s2), cross_swap(s3)
    left, right = even_odd(first), odd_even(second)
    where = [lax.axis_index("lat"), lax.axis_index("lon") & 1]
    place = jnp.concatenate([after(offsets, slab), jnp.stack(where).astype(jnp.int32)])
    mine = join(place, (s0, s1, s2, s3))
    other = x_far_swap(mine)
    cot = cotangent.reshape(512, 512)
    g_deep = g_deep_of(after(cot, mine), w_up)
    near_deep = core_swap(g_deep)
    seed = jnp.concatenate([mine, after(other, g_deep)], 0)
    moved = [turn(False, k)(seed) for k in (1, -1, 2)]
    bottom, top = strips(place, left, after(tokens, seed), right, slab)
    up, down = LAT_NEXT(top), LAT_PREV(bottom)
    gain = row(gain_attn)
    qkv_mid, probs_mid, middle = fwd_middle(
        place, left, tokens, right, slab, gain, w_qkv, w_proj
    )
    part = stacked([after(seed, up, down, middle)] + moved)
    ahead, behind = turn(True, 1)(part), turn(True, -1)(part)
    qkv_edge, probs_edge, resid = fwd_edge(
        place, after(up, part), bottom, top, down, tokens, middle, gain, w_qkv, w_proj
    )
    resid = resid.reshape(512, 512)
    far_deep = x_swap(after(g_deep, resid))
    slope, block, coarse, coarse_in = ffn_fwd(
        resid, row(gain_ffn), w_fc1, w_fc2, row(gain_merge), w_merge, row(gain_mlp)
    )
    fore, hind = halves(after(ahead, coarse_in), behind)
    far_cin = x_swap(coarse_in)
    near_cin = core_swap(coarse_in)
    parts = [part, ahead, behind, turn(True, 1)(fore), turn(True, -1)(hind)]
    cins = [coarse_in, near_cin, far_cin, core_swap(far_cin)]
    deeps = [g_deep, near_deep, far_deep, core_swap(after(far_deep, coarse_in))]
    keep, send, hid = coarse_mlp(place, cins, deeps, parts)
    near = core_swap(send)
    gcin_far = x_swap((keep[128:].astype(F32) + near[128:].astype(F32)).astype(BF))
    down_keep, down_send = down_of(hid, parts)
    down_near = core_swap(down_send)
    down_far = (down_keep[128:].astype(F32) + down_near[128:].astype(F32)).astype(BF)
    gcin_far, down_far = lax.optimization_barrier((gcin_far, down_far))
    down_far = x_swap(down_far)
    g_resid, g_first, g_second = ffn_bwd(
        place, keep, near, gcin_far, g_deep, coarse, row(gain_mlp), w_merge, block, row(gain_merge), cot,
        w_fc2, slope, w_fc1, resid, row(gain_ffn),
    )
    g_resid = g_resid.reshape(32, 16, 512)
    g_left, g_right = even_odd(g_first), odd_even(g_second)
    field_out = up_of(coarse, down_keep, down_near, down_far, block, w_up).reshape(32, 16, 512)
    g_center = bwd_center(place, g_resid, qkv_mid, probs_mid, w_proj, w_qkv)
    g_bottom, g_top = strips(place, g_left, after(g_resid, field_out, g_center), g_right)
    g_up, g_down = LAT_NEXT(g_top), LAT_PREV(g_bottom)
    g_middle = bwd_middle(
        place, g_left, g_resid, g_right, g_center, qkv_mid, probs_mid, w_proj, w_qkv
    )
    grad_in = bwd_edge(
        place, g_up, g_bottom, g_top, g_down, g_resid, g_middle, qkv_edge, probs_edge,
        w_proj, w_qkv, tokens, gain,
    )
    return (field_out, grad_in)


def solution(mesh):
    grid = P("lat", "lon", None)
    placed = (
        grid, P("lat", "lon"), P(), P(), P(), P(), P(), P(), P(), P(), P(), P(),
        P("lat", "lon"), P("lon", "lat"), P(), grid,
    )
    return jax.shard_map(
        on_device, mesh=mesh, in_specs=placed, out_specs=(grid, grid), check_vma=False
    )
```
